32 devices in a mesh: utt: 2 (over y), tm: 16 (over z, x, core).
Axes of the slice: x: 2, y: 2, z: 4, core: 2. Of those that a mesh axis runs over, the one named last changes fastest.
Arguments:
- stem: bfloat16 [4096, 1280], P(('utt', 'tm')), parts along dimension 0, may hold values from -8 to 8
- norm_gain: float32 [1280], replicated, may hold values from 0.25 to 1.75
- qkv_weight: bfloat16 [1280, 3840], P('tm'), may hold values from -0.2934839 to 0.2934839
- segment_ids: int32 [4096], P(('utt', 'tm')), parts along dimension 0, may hold values from 1 to 5, as said below
- dec_queries: bfloat16 [64, 1280], P(('utt', 'tm')), parts along dimension 0, may hold values from -9 to 9
- stretch_mask: int32 [64, 16], P(('utt', 'tm')), parts along dimension 0, may hold values 0 or 1
Outputs:
- memory: bfloat16 [4096, 1280], P(('utt', 'tm')), parts along dimension 0
- cross_out: bfloat16 [64, 1280], P(('utt', 'tm')), parts along dimension 0
The draws below stay inside these ranges and needn't reach their ends.
There are 2 independent parts, one for each index of `utt`. The reference program is written for one: setup_inputs(seed, part) draws one part's arguments, and reference() takes and returns one part's arrays. A program takes and returns all parts, laid end to end along the dimension named above; an argument that names none is the same for every part. Nothing has to cross between parts.
Inputs may be any that keep to these rules, and one draw needn't show every extreme that they name: `segment_ids`: ids start at 1 and rise by one from run to run; each id covers one contiguous run of at most 512 positions, and the last run is exactly 512 positions long.
All inputs are finite; a program needn't handle non-finite values. No bound on the sum of `stretch_mask` on one device may be relied on, other than what follows from the above.
Results may differ from the reference program's by a relative error of at most 0.0062.
Values may be sent and summed in bfloat16 or wider, within the bound.
No kernel may reach another device: no remote copies, remote signals or barrier semaphores. Data moves between devices by JAX's collectives and lax.ppermute only.
A program may use at most 64 MiB of HBM per device.

```python
import jax
import jax.numpy as jnp
from jax import lax

H = 20
HD = 64
D = 1280
POS_DEV = 128
DTOK_DEV = 2
WINDOW = 512
POS = 2048
DTOK = 32
STRETCHES = 16
N_TM = 16


def loud_pattern(key):
    flips = jax.random.bernoulli(jax.random.fold_in(key, 7), 0.5, (D,))
    return jnp.where(flips, 1.0, -1.0).astype(jnp.float32)


def loud_rows(key, count, share, lowest):
    pattern = loud_pattern(key)
    noise_key, pick_key, level_key = jax.random.split(key, 3)
    noise = jnp.clip(jax.random.normal(noise_key, (count, D), jnp.float32), -4.0, 4.0)
    loud = jax.random.bernoulli(pick_key, share, (count, 1))
    amplitude = lowest + 1.5 * jax.random.randint(level_key, (count, 1), 0, 3).astype(jnp.float32)
    return jnp.where(loud, amplitude * pattern[None, :] + 0.6 * noise, noise)


def draw_stem(key, part):
    return loud_rows(jax.random.fold_in(key, 11), POS, 1.0 / 32.0, 2.5).astype(jnp.bfloat16)


def draw_dec_queries(key, part):
    return loud_rows(jax.random.fold_in(key, 13), DTOK, 1.0 / 8.0, 3.0).astype(jnp.bfloat16)


def draw_qkv_weight(key, part):
    base_key = jax.random.fold_in(key, 0)
    whole = jnp.clip(jax.random.normal(base_key, (D, 3 * D), jnp.float32), -4.0, 4.0) * D ** (-0.5)
    return whole.astype(jnp.bfloat16)


def draw_segment_ids(key, part):
    runs = (N_TM - 4) // 3
    margin = POS_DEV // 4
    shifts = jax.random.randint(key, (runs - 1,), -margin, margin + 1, dtype=jnp.int32)
    marks = jnp.arange(1, runs, dtype=jnp.int32)
    inner = marks * ((N_TM - 4) * POS_DEV) // runs + shifts
    cuts = jnp.concatenate([inner, jnp.full((1,), POS - 4 * POS_DEV, jnp.int32)])
    places = jnp.arange(POS, dtype=jnp.int32)
    passed = jnp.sum((places[:, None] >= cuts[None, :]).astype(jnp.int32), axis=1)
    return (passed + 1).astype(jnp.int32)


def place_ends(values, own_key, least, top_value):
    shape = values.shape
    index_at = [jax.random.randint(jax.random.fold_in(own_key, axis), (), 0, shape[axis]) for axis in range(len(shape))]
    values = values.at[tuple(index_at)].set(least)
    longest = shape.index(max(shape))
    index_at[longest] = (index_at[longest] + 1) % shape[longest]
    return values.at[tuple(index_at)].set(top_value)


def setup_inputs(seed: int = 0, part: int = 0) -> dict:
    streams_of = jax.random.split(jax.random.key(seed), 7)
    own_keys = jax.random.split(jax.random.fold_in(streams_of[6], part), 7)
    return {
        "stem": draw_stem(jax.random.fold_in(jax.random.fold_in(streams_of[6], part), 71), part),
        "norm_gain": jnp.clip(1.0 + 0.15 * jax.random.normal(streams_of[1], (D,), jnp.float32), 0.25, 1.75),
        "qkv_weight": draw_qkv_weight(jax.random.fold_in(streams_of[6], 71), part),
        "segment_ids": draw_segment_ids(jax.random.fold_in(jax.random.fold_in(streams_of[6], part), 71), part),
        "dec_queries": draw_dec_queries(jax.random.fold_in(jax.random.fold_in(streams_of[6], part), 71), part),
        "stretch_mask": place_ends((jax.random.randint(own_keys[5], (DTOK, STRETCHES), 0, 2) < 1).astype(jnp.int32), jax.random.fold_in(own_keys[5], 1), 0, 1),
    }


def layer_norm(stem, norm_gain):
    values = stem.astype(jnp.float32)
    mean = lax.optimization_barrier(jnp.mean(values, axis=-1, keepdims=True))
    var = lax.optimization_barrier(jnp.mean((values - mean) ** 2, axis=-1, keepdims=True))
    return ((values - mean) * lax.rsqrt(var + 1e-05) * norm_gain).astype(jnp.bfloat16)

def reference(stem, norm_gain, qkv_weight, segment_ids, dec_queries, stretch_mask):
    scale = HD ** (-0.5)
    normed = layer_norm(stem, norm_gain)
    projected = jnp.dot(normed, qkv_weight, preferred_element_type=jnp.float32).astype(jnp.bfloat16)
    queries = projected[:, :D]
    keyvals = projected[:, D:]
    zero_rows = jnp.zeros((WINDOW, 2 * D), jnp.bfloat16)
    padded = jnp.concatenate([zero_rows, keyvals, zero_rows], axis=0)
    zero_ids = jnp.full((WINDOW,), -1, jnp.int32)
    seg_padded = jnp.concatenate([zero_ids, segment_ids.astype(jnp.int32), zero_ids], axis=0)
    extent = 2 * WINDOW + POS_DEV

    def block(index):
        start = (index * POS_DEV).astype(jnp.int32)
        qblock = lax.dynamic_slice_in_dim(queries, start, POS_DEV, 0).reshape(POS_DEV, H, HD).astype(jnp.float32)
        kvblock = lax.dynamic_slice_in_dim(padded, start, extent, 0)
        keys = kvblock[:, :D].reshape(extent, H, HD).astype(jnp.float32)
        values = kvblock[:, D:].reshape(extent, H, HD).astype(jnp.float32)
        seg_q = lax.dynamic_slice_in_dim(segment_ids.astype(jnp.int32), start, POS_DEV, 0)
        seg_k = lax.dynamic_slice_in_dim(seg_padded, start, extent, 0)
        scores = jnp.einsum('qhd,khd->hqk', qblock, keys) * scale
        same = seg_q[:, None] == seg_k[None, :]
        scores = jnp.where(same[None], scores, jnp.float32(-1e+30))
        top = lax.optimization_barrier(jnp.max(scores, axis=-1, keepdims=True))
        raised = jnp.exp(scores - top)
        probs = (raised / lax.optimization_barrier(jnp.sum(raised, axis=-1, keepdims=True))).astype(jnp.bfloat16)
        context = jnp.einsum('hqk,khd->qhd', probs.astype(jnp.float32), values)
        return context.reshape(POS_DEV, D)
    contexts = lax.map(block, jnp.arange(N_TM, dtype=jnp.int32)).reshape(POS, D)
    memory = (stem.astype(jnp.float32) + contexts).astype(jnp.bfloat16)
    owner = jnp.arange(DTOK, dtype=jnp.int32) // DTOK_DEV
    stretch_index = jnp.arange(N_TM, dtype=jnp.int32)
    allowed = (stretch_mask == 1) | (owner[:, None] == stretch_index[None, :])
    head_queries = jnp.transpose(dec_queries.reshape(DTOK, H, HD), (1, 0, 2))
    head_memory = jnp.transpose(memory.reshape(POS, H, HD), (1, 0, 2))

    def one_head(pair):
        query, mem = pair
        cross = jnp.dot(query, mem.T, preferred_element_type=jnp.float32) * scale
        cross = cross.reshape(DTOK, N_TM, POS_DEV)
        top = lax.optimization_barrier(jnp.max(cross, axis=-1))
        raised = jnp.where(allowed[:, :, None], jnp.exp(cross - top[:, :, None]), jnp.float32(0.0))
        den = lax.optimization_barrier(jnp.sum(raised, axis=-1))
        num = jnp.einsum('tcp,cpd->tcd', raised.astype(jnp.bfloat16).astype(jnp.float32), mem.reshape(N_TM, POS_DEV, HD).astype(jnp.float32))
        top_masked = jnp.where(allowed, top, jnp.float32(-1e+30))
        best = lax.optimization_barrier(jnp.max(top_masked, axis=1))
        factor = jnp.exp(top_masked - best[:, None])
        total = lax.optimization_barrier(jnp.sum(factor[:, :, None] * num, axis=1))
        return total / lax.optimization_barrier(jnp.sum(factor * den, axis=1))[:, None]
    heads_out = lax.map(one_head, (head_queries, head_memory))
    cross_out = jnp.transpose(heads_out, (1, 0, 2)).reshape(DTOK, D).astype(jnp.bfloat16)
    return (memory, cross_out)
```

```python
import functools

import jax
import jax.numpy as jnp
from jax import lax
from jax.experimental import pallas as pl
from jax.experimental.pallas import tpu as pltpu
from jax.sharding import PartitionSpec as P

HD = 64
WIDE = 256
GROUP = 320
BF = jnp.bfloat16
F32 = jnp.float32
LOW = -1e30
VMEM = pl.BlockSpec(memory_space=pltpu.VMEM)
SMEM = pl.BlockSpec(memory_space=pltpu.SMEM)


def send(block, route):
    return lax.ppermute(block, "tm", route)


def swap(block, n, mask):
    return send(block, [(d, d ^ mask) for d in range(n)])


def group_of(array, g):
    return array[:, WIDE * g : WIDE * g + WIDE], array[:, 1024 + HD * g : 1024 + HD * g + HD]


def weight_group(weight, g):
    width = weight.shape[1] // 3
    parts = [group_of(weight[:, i * width : (i + 1) * width], g) for i in range(3)]
    (q0, q1), (k0, k1), (v0, v1) = parts
    return jnp.concatenate([q0, k0, v0, k1, v1, q1], axis=1)


def token_group(queries, mask, g):
    wide, tail = group_of(queries, g)
    tokens, blocks = mask.shape
    gap = jnp.zeros((tokens, HD), BF)
    return jnp.concatenate([wide, tail, gap, mask.astype(BF)], axis=1)


def encoder_kernel(n_blocks, n_parts, depth, places, gain, *refs):
    blocks = refs[:n_blocks]
    parts = refs[n_blocks : n_blocks + n_parts]
    memory, normed, weight, ids, residual, queries, keyvals = refs[n_blocks + n_parts :]
    group = places[n_blocks + n_parts + 1]
    halo_on = places[n_blocks + n_parts]

    ids[...] = jnp.zeros_like(ids)
    for i, part in enumerate(parts):
        row = pl.multiple_of(places[n_blocks + i] * depth, 16)
        weight[pl.ds(row, depth), :] = part[:depth, :]

    for i, block in enumerate(blocks):
        place = pl.multiple_of(places[i], 128)
        values = block[:128, :].astype(F32)
        mean = jnp.mean(values, axis=-1, keepdims=True)
        centred = values - mean
        var = jnp.mean(centred * centred, axis=-1, keepdims=True)
        normed[pl.ds(place, 128), :] = (centred * lax.rsqrt(var + 1e-05) * gain[...]).astype(BF)
        marks = block[128:136, :256].astype(F32)
        found = marks[:, :128] * 128.0 + marks[:, 128:]
        if i >= 8:
            found = found * halo_on.astype(F32)
        ids[:, pl.ds(place, 128)] = found

        if i < 8:

            @pl.when(place // 512 == 1)
            def _():
                row = pl.multiple_of(place - 512, 128)
                residual[pl.ds(row, 128), :WIDE] = block[
                    :128, pl.ds(pl.multiple_of(group * WIDE, 128), WIDE)
                ]
                slab = block[:128, pl.ds(pl.multiple_of(1024 + group // 2 * 128, 128), 128)]
                odd = jnp.broadcast_to(lax.rem(group, 2), (128, HD)) == 1
                residual[pl.ds(row, 128), WIDE:] = jnp.where(odd, slab[:, HD:], slab[:, :HD])

    def project(step, carry):
        row = pl.multiple_of(step * 256, 256)
        rows = normed[pl.ds(row, 256), :]
        keyvals[pl.ds(row, 256), :] = jnp.dot(
            rows, weight[:, 256:896], preferred_element_type=F32
        ).astype(BF)
        return carry

    lax.fori_loop(0, 6, project, 0)

    def project_queries(step, carry):
        row = pl.multiple_of(step * 256, 256)
        rows = normed[pl.ds(row + 512, 256), :]
        queries[pl.ds(row, 256), :WIDE] = (
            jnp.dot(rows, weight[:, :WIDE], preferred_element_type=F32).astype(BF)
        )
        tail = jnp.dot(rows, weight[:, 896:960], preferred_element_type=F32).astype(BF)
        queries[pl.ds(row, 256), WIDE:] = jnp.concatenate([tail, jnp.zeros_like(tail)], axis=1)
        return carry

    lax.fori_loop(0, 2, project_queries, 0)

    def attend(step, carry):
        row = pl.multiple_of(step * 128, 128)
        mine = jnp.broadcast_to(ids[0:1, pl.ds(row + 512, 128)], (128, 128)).T[:, 0:1]
        wide = ids[0:1, pl.ds(row, 1152)]
        bias = jnp.where(mine == wide, 0.0, LOW)
        lane = lax.broadcasted_iota(jnp.int32, (128, 128), 1)
        contexts = []
        for slab in range(3):
            query = queries[pl.ds(row, 128), 128 * slab : 128 * slab + 128] * BF(0.125)
            if slab < 2:
                none = jnp.zeros_like(query)
                heads = [jnp.where(lane < HD, query, none), jnp.where(lane < HD, none, query)]
                keys = keyvals[pl.ds(row, 1152), 128 * slab : 128 * slab + 128]
                vals = keyvals[pl.ds(row, 1152), WIDE + 128 * slab : WIDE + 128 * slab + 128]
            else:
                heads = [query]
                keys = vals = keyvals[pl.ds(row, 1152), 512:640]
            outs = []
            for head in heads:
                scores = lax.dot_general(
                    head, keys, (((1,), (1,)), ((), ())), preferred_element_type=F32
                )
                scores = scores + bias
                raised = jnp.exp(scores - jnp.max(scores, axis=-1, keepdims=True))
                total = jnp.sum(raised, axis=-1, keepdims=True)
                out = jnp.dot(raised.astype(BF), vals, preferred_element_type=F32)
                outs.append(out / total)
            if slab < 2:
                context = jnp.where(lane < HD, outs[0], outs[1])
                stem = residual[pl.ds(row, 128), 128 * slab : 128 * slab + 128].astype(F32)
                memory[pl.ds(row, 128), 128 * slab : 128 * slab + 128] = (stem + context).astype(BF)
            else:
                stem = residual[pl.ds(row, 128), WIDE:].astype(F32)
                memory[pl.ds(row, 128), WIDE:] = (stem + outs[0][:, HD:]).astype(BF)
        return carry

    lax.fori_loop(0, 4, attend, 0)


def encoder(places, gain, blocks, parts, depth):
    body = functools.partial(encoder_kernel, len(blocks), len(parts), depth)
    return pl.pallas_call(
        body,
        out_shape=jax.ShapeDtypeStruct((512, GROUP), BF),
        in_specs=[SMEM] + [VMEM] * (1 + len(blocks) + len(parts)),
        out_specs=VMEM,
        scratch_shapes=[
            pltpu.VMEM((1536, 1280), BF),
            pltpu.VMEM((1280, 960), BF),
            pltpu.VMEM((8, 1536), F32),
            pltpu.VMEM((512, GROUP), BF),
            pltpu.VMEM((512, 384), BF),
            pltpu.VMEM((1536, 640), BF),
        ],
        compiler_params=pltpu.CompilerParams(vmem_limit_bytes=48 * 1024 * 1024),
    )(places, gain, *blocks, *parts)


def spread(columns, rows, slab):
    lane = lax.broadcasted_iota(jnp.int32, (rows, 128), 1)
    return jnp.where(lane < HD, columns[2 * slab], columns[min(2 * slab + 1, 4)])


def cross_kernel(place, memory, tokens, out):
    count = tokens.shape[0]
    blocks = tokens.shape[1] - 384
    first = place[0]
    me = place[1]
    spot = lax.broadcasted_iota(jnp.int32, (count, blocks), 1)
    asked = tokens[:, 384:].astype(F32)
    order = lax.broadcasted_iota(jnp.int32, (count, 1), 0)
    half = count // 2
    relative = 2 * (lax.rem(order, half) // 2) + order // half
    owner = relative ^ me
    allowed = []
    for b in range(4):
        ask = jnp.sum(jnp.where(spot == first + b, asked, 0.0), axis=-1, keepdims=True)
        allowed.append((ask > 0.5) | (owner == first + b))
    lane = lax.broadcasted_iota(jnp.int32, (count, 128), 1)
    bias = jnp.concatenate(
        [jnp.broadcast_to(jnp.where(a, 0.0, LOW), (count, 128)) for a in allowed], axis=1
    )
    stats = jnp.zeros((count, 128), F32)
    for slab in range(3):
        query = tokens[:, 128 * slab : 128 * slab + 128] * BF(0.125)
        if slab < 2:
            none = jnp.zeros_like(query)
            heads = [jnp.where(lane < HD, query, none), jnp.where(lane < HD, none, query)]
            held = memory[:, 128 * slab : 128 * slab + 128]
        else:
            heads = [query[:, :HD]]
            held = memory[:, WIDE:]
        outs = []
        for i, head in enumerate(heads):
            cross = lax.dot_general(
                head, held, (((1,), (1,)), ((), ())), preferred_element_type=F32
            )
            cross = jnp.where(bias < 0.0, LOW, cross)
            top = jnp.max(cross, axis=-1, keepdims=True)
            raised = jnp.where(bias < 0.0, 0.0, jnp.exp(cross - top))
            den = jnp.sum(raised, axis=-1, keepdims=True)
            outs.append(jnp.dot(raised.astype(BF), held, preferred_element_type=F32))
            stats = jnp.where(lane == 2 * slab + i, top, stats)
            stats = jnp.where(lane == 8 + 2 * slab + i, den, stats)
        if slab < 2:
            out[:, 128 * slab : 128 * slab + 128] = jnp.where(lane < HD, outs[0], outs[1])
        else:
            out[:, WIDE:384] = jnp.concatenate([outs[0], jnp.zeros_like(outs[0])], axis=1)
    out[:, 384:] = stats


def cross_partial(place, memory, tokens):
    return pl.pallas_call(
        cross_kernel,
        out_shape=jax.ShapeDtypeStruct((tokens.shape[0], 512), F32),
        in_specs=[SMEM, VMEM, VMEM],
        out_specs=VMEM,
    )(place, memory, tokens)


def merge_kernel(last, mine, theirs, out):
    rows = theirs.shape[0]
    ours = mine[:rows, 384:]
    other = theirs[:, 384:]
    lane = lax.broadcasted_iota(jnp.int32, (rows, 128), 1)
    stats = jnp.zeros((rows, 128), F32)
    left, right, dens = [], [], []
    for head in range(5):
        a, b = ours[:, head : head + 1], other[:, head : head + 1]
        best = jnp.maximum(a, b)
        a, b = jnp.exp(a - best), jnp.exp(b - best)
        den = a * ours[:, 8 + head : 9 + head] + b * other[:, 8 + head : 9 + head]
        left.append(a)
        right.append(b)
        dens.append(den)
        stats = jnp.where(lane == head, best, stats)
        stats = jnp.where(lane == 8 + head, den, stats)
    for slab in range(3):
        span = slice(128 * slab, 128 * slab + 128)
        total = spread(left, rows, slab) * mine[:rows, span] + spread(right, rows, slab) * theirs[:, span]
        if last:
            out[:, span] = (total / spread(dens, rows, slab)).astype(BF)
        else:
            out[:, span] = total
    if not last:
        out[:, 384:] = stats


def merge(mine, theirs, last):
    rows = theirs.shape[0]
    shape = jax.ShapeDtypeStruct((rows, 384), BF) if last else jax.ShapeDtypeStruct((rows, 512), F32)
    return pl.pallas_call(
        functools.partial(merge_kernel, last),
        out_shape=shape,
        in_specs=[VMEM, VMEM],
        out_specs=VMEM,
    )(mine, theirs)


def gather_groups(pieces, group):
    wide, tail = [], []
    for g in range(4):
        turn = group ^ g
        piece = jnp.where(
            turn < 2,
            jnp.where(turn == 0, pieces[0], pieces[1]),
            jnp.where(turn == 2, pieces[2], pieces[3]),
        )
        wide.append(piece[:, :WIDE])
        tail.append(piece[:, WIDE:GROUP])
    return jnp.concatenate(wide + tail, axis=1)


def on_device(stem, norm_gain, qkv_weight, segment_ids, dec_queries, stretch_mask):
    n = lax.axis_size("tm")
    layers = n // 4
    me = lax.axis_index("tm")
    z, x, c = me // 4, (me // 2) % 2, me % 2
    p, k = z % 2, z // 2
    quarter = 2 * k + c
    group = 2 * p + x
    depth = qkv_weight.shape[0]

    digits = jnp.concatenate([segment_ids // 128, segment_ids % 128]).astype(BF)
    extra = jnp.zeros((8, stem.shape[1]), BF).at[0, :256].set(digits)
    own = jnp.concatenate([stem, extra], axis=0)

    steps = [1 if i % 2 else -1 for i in range(layers)]
    near = [
        (4 * i + j, 4 * (i + s) + j)
        for i, s in enumerate(steps)
        for j in range(4)
        if 0 <= i + s < layers
    ]
    far = [
        (4 * i + j, 4 * (i + 2 * s) + j)
        for i, s in enumerate(steps)
        for j in range(4)
        if 0 <= i + 2 * s < layers
    ]
    pair = swap(own, n, 4)
    halo_near = send(own, near)
    halo_far = send(own, far)
    own_x = swap(own, n, 2)
    pair_x = swap(pair, n, 2)
    if layers == 4:
        halo = jnp.where((z == 1) | (z == 2), halo_near, halo_far)
        halo_x = swap(halo, n, 2)
        halo_on = (c != k).astype(jnp.int32)
        halo_c, halo_xc = swap(halo, n, 1), swap(halo_x, n, 1)
    else:
        left = jnp.where(p == 0, halo_near, halo_far)
        right = jnp.where(p == 0, halo_far, halo_near)
        left_x, right_x = swap(left, n, 2), swap(right, n, 2)
        halo = jnp.where(c == 0, left, right)
        halo_x = jnp.where(c == 0, left_x, right_x)
        halo_c = swap(jnp.where(c == 0, right, left), n, 1)
        halo_xc = swap(jnp.where(c == 0, right_x, left_x), n, 1)
        halo_on = jnp.int32(1)
    blocks = [own, swap(own, n, 1), own_x, swap(own_x, n, 1)]
    blocks += [pair, swap(pair, n, 1), pair_x, swap(pair_x, n, 1)]
    blocks += [halo, halo_c, halo_x, halo_xc]
    starts = [512 * (p - c + 1), 512 * (2 - p - c), 1024 * c]
    inner = [128 * (2 * x + c), 128 * (2 * x + 1 - c), 128 * (2 - 2 * x + c), 128 * (3 - 2 * x - c)]
    places = [s + i for s in starts for i in inner]

    if depth % 16 == 0 and layers == 4:
        payload = jnp.stack(
            [
                jnp.concatenate(
                    [
                        weight_group(qkv_weight, g),
                        jnp.pad(
                            token_group(dec_queries, stretch_mask, g),
                            ((0, 6), (0, 960 - 384 - stretch_mask.shape[1])),
                        ),
                    ],
                    axis=0,
                )
                for g in range(4)
            ]
        )
        chosen = [
            [
                lax.dynamic_index_in_dim(payload, 2 * (p ^ a) + (x ^ b), 0, keepdims=False)
                for b in range(2)
            ]
            for a in range(2)
        ]
        parts = {}
        for far_z in (3, 2, 1, 0):
            for far_x in (1, 0):
                mask = 4 * far_z + 2 * far_x
                part = chosen[far_z % 2][far_x]
                if mask:
                    part = swap(part, n, mask)
                parts[mask] = part
                parts[mask + 1] = swap(part, n, 1)
        order = [m for core in range(2) for m in range(core, n, 2)]
        tokens = jnp.concatenate(
            [parts[m][depth : depth + 2, : 384 + stretch_mask.shape[1]] for m in order], axis=0
        )
        part_places = [me ^ m for m in order]
        weights = [parts[m] for m in order]
    else:
        whole = lax.all_gather(qkv_weight, "tm", axis=0, tiled=True)
        grouped = jnp.stack([weight_group(whole, g) for g in range(4)])
        weights = [lax.dynamic_index_in_dim(grouped, group, 0, keepdims=False)]
        part_places = [jnp.int32(0)]
        depth = whole.shape[0]
        packed = jnp.stack([token_group(dec_queries, stretch_mask, g) for g in range(4)])
        every = lax.all_gather(packed, "tm", axis=1, tiled=True)
        every = lax.dynamic_index_in_dim(every, group, 0, keepdims=False)
        order = jnp.array([m for core in range(2) for m in range(core, n, 2)], jnp.int32)
        rows = 2 * (order ^ me)
        tokens = jnp.take(every, jnp.stack([rows, rows + 1], axis=1).reshape(-1), axis=0)

    table = jnp.stack([jnp.asarray(v, jnp.int32) for v in places + part_places + [halo_on, group]])
    held = encoder(table, norm_gain.reshape(1, -1), blocks, weights, depth)

    pieces = []
    for turn in range(2):
        rows = lax.dynamic_slice_in_dim(held, 256 * (x ^ turn), 256, 0)
        route = [
            (
                8 * (d // 8) + 4 * (d // 4 % 2) + (d & 2) + (d & 1),
                8 * (d // 8) + 4 * (d & 1) + ((d & 2) ^ (2 * turn)) + (d // 4 % 2),
            )
            for d in range(n)
        ]
        got = send(rows, route)
        keep = lax.dynamic_slice_in_dim(got, 128 * c, 128, 0)
        give = swap(lax.dynamic_slice_in_dim(got, 128 * (1 - c), 128, 0), n, 1)
        pieces.append((keep, give))
    memory = gather_groups(
        [pieces[0][0], pieces[1][0], pieces[0][1], pieces[1][1]], 2 * c + x
    )

    place = jnp.stack([4 * quarter, me]).astype(jnp.int32)
    partial = cross_partial(place, held, tokens)
    bits = [1]
    step = n // 2
    while step >= 8:
        bits.append(step)
        step //= 2
    for i, bit in enumerate(bits):
        half = partial.shape[0] // 2
        theirs = swap(partial[half:], n, bit)
        partial = merge(partial, theirs, i == len(bits) - 1)
    final = [partial[0:2]]
    for i in (1, 2, 3):
        final.append(swap(partial[2 * i : 2 * i + 2], n, 2 * i))
    cross_out = gather_groups(final, group)
    return (memory, cross_out)


def solution(mesh):
    placed = (
        P(("utt", "tm"), None),
        P(),
        P("tm", None),
        P(("utt", "tm")),
        P(("utt", "tm"), None),
        P(("utt", "tm"), None),
    )
    return jax.shard_map(
        on_device,
        mesh=mesh,
        in_specs=placed,
        out_specs=(P(("utt", "tm"), None), P(("utt", "tm"), None)),
        check_vma=False,
    )
```

```python
import functools

import jax
import jax.numpy as jnp
from jax import lax
from jax.experimental import pallas as pl
from jax.experimental.pallas import tpu as pltpu
from jax.sharding import PartitionSpec as P

HD = 64
WIDE = 256
GROUP = 320
BF = jnp.bfloat16
F32 = jnp.float32
LOW = -1e30
VMEM = pl.BlockSpec(memory_space=pltpu.VMEM)
SMEM = pl.BlockSpec(memory_space=pltpu.SMEM)


def send(block, route):
    return lax.ppermute(block, "tm", route)


def swap(block, n, mask):
    return send(block, [(d, d ^ mask) for d in range(n)])


def scalars(values):
    return jnp.stack([jnp.asarray(v, jnp.int32) for v in values])


def group_of(array, g):
    return array[:, WIDE * g : WIDE * g + WIDE], array[:, 1024 + HD * g : 1024 + HD * g + HD]


def weight_group(weight, g):
    width = weight.shape[1] // 3
    parts = [group_of(weight[:, i * width : (i + 1) * width], g) for i in range(3)]
    (q0, q1), (k0, k1), (v0, v1) = parts
    return jnp.concatenate([q0, k0, v0, k1, v1, q1], axis=1)


def token_group(queries, mask, g):
    wide, tail = group_of(queries, g)
    heads = [wide[:, HD * i : HD * i + HD] for i in range(4)] + [tail]
    asked = jnp.pad(mask.astype(BF), ((0, 0), (0, HD - mask.shape[1])))
    return jnp.concatenate(heads + [asked], axis=0)


def norm_kernel(places, gain, *refs):
    blocks, (normed, ids, residual) = refs[:4], refs[4:]
    group = places[4]
    real = places[5].astype(F32)
    ids[...] = jnp.zeros_like(ids)
    for i, block in enumerate(blocks):
        place = pl.multiple_of(places[i], 128)
        values = block[:128, :].astype(F32)
        mean = jnp.mean(values, axis=-1, keepdims=True)
        centred = values - mean
        var = jnp.mean(centred * centred, axis=-1, keepdims=True)
        normed[pl.ds(place, 128), :] = (centred * lax.rsqrt(var + 1e-05) * gain[...]).astype(BF)
        marks = block[128:136, :256].astype(F32)
        ids[:, pl.ds(place, 128)] = (marks[:, :128] * 128.0 + marks[:, 128:]) * real
        residual[pl.ds(place, 128), :WIDE] = block[
            :128, pl.ds(pl.multiple_of(group * WIDE, 128), WIDE)
        ]
        slab = block[:128, pl.ds(pl.multiple_of(1024 + group // 2 * 128, 128), 128)]
        odd = jnp.broadcast_to(lax.rem(group, 2), (128, HD)) == 1
        residual[pl.ds(place, 128), WIDE:] = jnp.where(odd, slab[:, HD:], slab[:, :HD])


def norm_layer(places, gain, blocks):
    return pl.pallas_call(
        norm_kernel,
        out_shape=(
            jax.ShapeDtypeStruct((512, 1280), BF),
            jax.ShapeDtypeStruct((8, 512), F32),
            jax.ShapeDtypeStruct((512, GROUP), BF),
        ),
        in_specs=[SMEM] + [VMEM] * 5,
        out_specs=(VMEM, VMEM, VMEM),
        compiler_params=pltpu.CompilerParams(vmem_limit_bytes=16 * 1024 * 1024),
    )(places, gain, *blocks)


def encoder_kernel(n_parts, depth, places, *refs):
    layers = [refs[3 * i : 3 * i + 3] for i in range(3)]
    parts = refs[9 : 9 + n_parts]
    memory, weight, ids, residual, queries, keyvals = refs[9 + n_parts :]

    for i, part in enumerate(parts):
        row = pl.multiple_of(places[3 + i] * depth, 16)
        weight[pl.ds(row, depth), :] = part[...]

    for i, (normed, marks, kept) in enumerate(layers):
        place = pl.multiple_of(places[i], 512)
        ids[:, pl.ds(place, 512)] = marks[...]

        def project(step, carry):
            row = pl.multiple_of(step * 256, 256)
            to = pl.multiple_of(place + row, 256)
            keyvals[pl.ds(to, 256), :] = jnp.dot(
                normed[pl.ds(row, 256), :], weight[:, 256:896], preferred_element_type=F32
            ).astype(BF)
            return carry

        lax.fori_loop(0, 2, project, 0)
        if i < 2:

            @pl.when(place == 512)
            def _():
                residual[...] = kept[...]

                def project_queries(step, carry):
                    row = pl.multiple_of(step * 256, 256)
                    rows = normed[pl.ds(row, 256), :]
                    queries[pl.ds(row, 256), :WIDE] = jnp.dot(
                        rows, weight[:, :WIDE], preferred_element_type=F32
                    ).astype(BF)
                    tail = jnp.dot(rows, weight[:, 896:], preferred_element_type=F32).astype(BF)
                    lane = lax.broadcasted_iota(jnp.int32, tail.shape, 1)
                    queries[pl.ds(row, 256), WIDE:] = jnp.where(lane < HD, tail, jnp.zeros_like(tail))
                    return carry

                lax.fori_loop(0, 2, project_queries, 0)

    def attend(step, carry):
        row = pl.multiple_of(step * 128, 128)
        mine = jnp.broadcast_to(ids[0:1, pl.ds(row + 512, 128)], (128, 128)).T[:, 0:1]
        wide = ids[0:1, pl.ds(row, 1152)]
        bias = jnp.where(mine == wide, 0.0, LOW)
        lane = lax.broadcasted_iota(jnp.int32, (128, 128), 1)
        for slab in range(3):
            query = queries[pl.ds(row, 128), 128 * slab : 128 * slab + 128] * BF(0.125)
            if slab < 2:
                none = jnp.zeros_like(query)
                heads = [jnp.where(lane < HD, query, none), jnp.where(lane < HD, none, query)]
                keys = keyvals[pl.ds(row, 1152), 128 * slab : 128 * slab + 128]
                vals = keyvals[pl.ds(row, 1152), WIDE + 128 * slab : WIDE + 128 * slab + 128]
            else:
                heads = [query]
                keys = vals = keyvals[pl.ds(row, 1152), 512:640]
            outs = []
            for head in heads:
                scores = lax.dot_general(
                    head, keys, (((1,), (1,)), ((), ())), preferred_element_type=F32
                )
                scores = scores + bias
                raised = jnp.exp(scores - jnp.max(scores, axis=-1, keepdims=True))
                total = jnp.sum(raised, axis=-1, keepdims=True)
                out = jnp.dot(raised.astype(BF), vals, preferred_element_type=F32)
                outs.append(out / total)
            if slab < 2:
                context = jnp.where(lane < HD, outs[0], outs[1])
                stem = residual[pl.ds(row, 128), 128 * slab : 128 * slab + 128].astype(F32)
                memory[pl.ds(row, 128), 128 * slab : 128 * slab + 128] = (stem + context).astype(BF)
            else:
                stem = residual[pl.ds(row, 128), WIDE:].astype(F32)
                memory[pl.ds(row, 128), WIDE:] = (stem + outs[0][:, HD:]).astype(BF)
        return carry

    lax.fori_loop(0, 4, attend, 0)


def encoder(places, layers, parts, depth):
    return pl.pallas_call(
        functools.partial(encoder_kernel, len(parts), depth),
        out_shape=jax.ShapeDtypeStruct((512, GROUP), BF),
        in_specs=[SMEM] + [VMEM] * (9 + len(parts)),
        out_specs=VMEM,
        scratch_shapes=[
            pltpu.VMEM((1280, 1024), BF),
            pltpu.VMEM((8, 1536), F32),
            pltpu.VMEM((512, GROUP), BF),
            pltpu.VMEM((512, 384), BF),
            pltpu.VMEM((1536, 640), BF),
        ],
        compiler_params=pltpu.CompilerParams(vmem_limit_bytes=20 * 1024 * 1024),
    )(places, *[a for layer in layers for a in layer], *parts)


def spread(columns, rows, slab):
    lane = lax.broadcasted_iota(jnp.int32, (rows, 128), 1)
    return jnp.where(lane < HD, columns[2 * slab], columns[min(2 * slab + 1, 4)])


def cross_kernel(chips, place, memory, *refs):
    parts, (out, tokens) = refs[:-2], refs[-2:]
    first, me, core, straight = place[0], place[1], place[2], place[3]
    count = out.shape[0]
    half = count // 2
    if chips:
        for i in range(len(parts) // 2):
            here, there = parts[2 * i][:24, 960:], parts[2 * i + 1][:24, 960:]
            rows = jnp.where(jnp.broadcast_to(straight, (24, HD)) == 1, here.astype(F32), there.astype(F32))
            for h in range(6):
                low, high = rows[4 * h : 4 * h + 2], rows[4 * h + 2 : 4 * h + 4]
                flip = jnp.broadcast_to(core, (2, HD)) == 1
                tokens[h, 2 * i : 2 * i + 2, :] = jnp.where(flip, high, low)
                tokens[h, half + 2 * i : half + 2 * i + 2, :] = jnp.where(flip, low, high)
    else:
        tokens[...] = parts[0][...].astype(F32)
    blocks = HD
    spot = lax.broadcasted_iota(jnp.int32, (count, blocks), 1)
    order = lax.broadcasted_iota(jnp.int32, (count, 1), 0)
    relative = 2 * (lax.rem(order, half) // 2) + order // half
    owner = relative ^ me
    allowed = []
    for b in range(4):
        ask = jnp.sum(jnp.where(spot == first + b, tokens[5], 0.0), axis=-1, keepdims=True)
        allowed.append((ask > 0.5) | (owner == first + b))
    lane = lax.broadcasted_iota(jnp.int32, (count, 128), 1)
    bias = jnp.concatenate(
        [jnp.broadcast_to(jnp.where(a, 0.0, LOW), (count, 128)) for a in allowed], axis=1
    )
    stats = jnp.zeros((count, 128), F32)
    for slab in range(3):
        heads = [(tokens[h] * 0.125).astype(BF) for h in range(2 * slab, min(2 * slab + 2, 5))]
        none = jnp.zeros_like(heads[0])
        if slab < 2:
            heads = [
                jnp.concatenate([heads[0], none], axis=1),
                jnp.concatenate([none, heads[1]], axis=1),
            ]
            held = memory[:, 128 * slab : 128 * slab + 128]
        else:
            held = memory[:, WIDE:]
        outs = []
        for i, head in enumerate(heads):
            cross = lax.dot_general(
                head, held, (((1,), (1,)), ((), ())), preferred_element_type=F32
            )
            cross = jnp.where(bias < 0.0, LOW, cross)
            top = jnp.max(cross, axis=-1, keepdims=True)
            raised = jnp.where(bias < 0.0, 0.0, jnp.exp(cross - top))
            den = jnp.sum(raised, axis=-1, keepdims=True)
            outs.append(jnp.dot(raised.astype(BF), held, preferred_element_type=F32))
            stats = jnp.where(lane == 2 * slab + i, top, stats)
            stats = jnp.where(lane == 8 + 2 * slab + i, den, stats)
        if slab < 2:
            out[:, 128 * slab : 128 * slab + 128] = jnp.where(lane < HD, outs[0], outs[1])
        else:
            out[:, WIDE:384] = jnp.concatenate([outs[0], jnp.zeros_like(outs[0])], axis=1)
    out[:, 384:] = stats


def cross_partial(place, memory, parts, count, chips):
    return pl.pallas_call(
        functools.partial(cross_kernel, chips),
        out_shape=jax.ShapeDtypeStruct((count, 512), F32),
        in_specs=[SMEM] + [VMEM] * (1 + len(parts)),
        out_specs=VMEM,
        scratch_shapes=[pltpu.VMEM((6, count, HD), F32)],
    )(place, memory, *parts)


def merge_kernel(last, mine, theirs, out):
    rows = theirs.shape[0]
    ours = mine[:rows, 384:]
    other = theirs[:, 384:]
    lane = lax.broadcasted_iota(jnp.int32, (rows, 128), 1)
    stats = jnp.zeros((rows, 128), F32)
    left, right, dens = [], [], []
    for head in range(5):
        a, b = ours[:, head : head + 1], other[:, head : head + 1]
        best = jnp.maximum(a, b)
        a, b = jnp.exp(a - best), jnp.exp(b - best)
        den = a * ours[:, 8 + head : 9 + head] + b * other[:, 8 + head : 9 + head]
        left.append(a)
        right.append(b)
        dens.append(den)
        stats = jnp.where(lane == head, best, stats)
        stats = jnp.where(lane == 8 + head, den, stats)
    for slab in range(3):
        span = slice(128 * slab, 128 * slab + 128)
        total = spread(left, rows, slab) * mine[:rows, span] + spread(right, rows, slab) * theirs[:, span]
        if last:
            out[:, span] = (total / spread(dens, rows, slab)).astype(BF)
        else:
            out[:, span] = total
    if not last:
        out[:, 384:] = stats


def merge(mine, theirs, last):
    rows = theirs.shape[0]
    shape = jax.ShapeDtypeStruct((rows, 384), BF) if last else jax.ShapeDtypeStruct((rows, 512), F32)
    return pl.pallas_call(
        functools.partial(merge_kernel, last),
        out_shape=shape,
        in_specs=[VMEM, VMEM],
        out_specs=VMEM,
    )(mine, theirs)


def gather_groups(pieces, group):
    wide, tail = [], []
    for g in range(4):
        turn = group ^ g
        piece = jnp.where(
            turn < 2,
            jnp.where(turn == 0, pieces[0], pieces[1]),
            jnp.where(turn == 2, pieces[2], pieces[3]),
        )
        wide.append(piece[:, :WIDE])
        tail.append(piece[:, WIDE:GROUP])
    return jnp.concatenate(wide + tail, axis=1)


def on_device(stem, norm_gain, qkv_weight, segment_ids, dec_queries, stretch_mask):
    n = lax.axis_size("tm")
    layers = n // 4
    me = lax.axis_index("tm")
    z, x, c = me // 4, (me // 2) % 2, me % 2
    p, k = z % 2, z // 2
    quarter = 2 * k + c
    group = 2 * p + x
    depth = qkv_weight.shape[0]

    digits = jnp.concatenate([segment_ids // 128, segment_ids % 128]).astype(BF)
    extra = jnp.zeros((8, stem.shape[1]), BF).at[0, :256].set(digits)
    own = jnp.concatenate([stem, extra], axis=0)

    steps = [1 if i % 2 else -1 for i in range(layers)]
    near = [
        (4 * i + j, 4 * (i + s) + j)
        for i, s in enumerate(steps)
        for j in range(4)
        if 0 <= i + s < layers
    ]
    far = [
        (4 * i + j, 4 * (i + 2 * s) + j)
        for i, s in enumerate(steps)
        for j in range(4)
        if 0 <= i + 2 * s < layers
    ]
    pair = swap(own, n, 4)
    halo_near = send(own, near)
    halo_far = send(own, far)
    own_x = swap(own, n, 2)
    pair_x = swap(pair, n, 2)
    if layers == 4:
        halo = jnp.where((z == 1) | (z == 2), halo_near, halo_far)
        halo_x = swap(halo, n, 2)
        halo_on = (c != k).astype(jnp.int32)
        halo_c, halo_xc = swap(halo, n, 1), swap(halo_x, n, 1)
    else:
        left = jnp.where(p == 0, halo_near, halo_far)
        right = jnp.where(p == 0, halo_far, halo_near)
        left_x, right_x = swap(left, n, 2), swap(right, n, 2)
        halo = jnp.where(c == 0, left, right)
        halo_x = jnp.where(c == 0, left_x, right_x)
        halo_c = swap(jnp.where(c == 0, right, left), n, 1)
        halo_xc = swap(jnp.where(c == 0, right_x, left_x), n, 1)
        halo_on = jnp.int32(1)
    own_layer = [own, swap(own, n, 1), own_x, swap(own_x, n, 1)]
    pair_layer = [pair, swap(pair, n, 1), pair_x, swap(pair_x, n, 1)]
    halo_layer = [halo, halo_c, halo_x, halo_xc]
    inner = [128 * (2 * x + c), 128 * (2 * x + 1 - c), 128 * (2 - 2 * x + c), 128 * (3 - 2 * x - c)]
    gain = norm_gain.reshape(1, -1)
    layered = []
    for blocks, real in ((own_layer, 1), (pair_layer, 1), (halo_layer, halo_on)):
        layered.append(norm_layer(scalars(inner + [group, real]), gain, blocks))
    places = [512 * (p - c + 1), 512 * (2 - p - c), 1024 * c]

    utts = lax.axis_size("utt")
    straight = (c == lax.axis_index("utt") % 2).astype(jnp.int32)
    if depth % 16 == 0 and layers == 4 and utts % 2 == 0:
        carriers = [(u, d) for u in range(utts) for d in range(n) if d % 2 == u % 2]

        def carry(block, turn_u, turn_d):
            route = [(u * n + d, (u ^ turn_u) * n + (d ^ turn_d)) for u, d in carriers]
            return lax.ppermute(block, ("utt", "tm"), route)

        small = jnp.stack([token_group(dec_queries, stretch_mask, g) for g in range(4)])
        other = swap(small, n, 1)
        both = jnp.stack(
            [jnp.where(c == 0, small, other), jnp.where(c == 0, other, small)], axis=1
        )
        both = both.reshape(4, 2, 6, 2, HD).transpose(0, 2, 1, 3, 4).reshape(4, 24, HD)
        both = jnp.pad(both, ((0, 0), (0, depth - 24), (0, 0)))
        payload = jnp.stack(
            [
                jnp.concatenate([weight_group(qkv_weight, g), both[g]], axis=1)
                for g in (0, 2, 1, 3)
            ]
        ).reshape(2, 2, depth, 1024)
        mine = lax.dynamic_index_in_dim(payload, x, 0, keepdims=False)
        across = carry(lax.dynamic_index_in_dim(payload, 1 - x, 0, keepdims=False), 0, 2)
        ready = [
            jnp.concatenate(
                [
                    lax.dynamic_slice_in_dim(mine, p ^ a, 1, 0),
                    lax.dynamic_slice_in_dim(across, p ^ a, 1, 0),
                ]
            ).reshape(2 * depth, 1024)
            for a in range(2)
        ]
        here = {0: ready[0]}
        for turn in (3, 2, 1):
            here[turn] = carry(ready[turn % 2], 0, 4 * turn)
        weights, part_places, token_parts = [], [], []
        own_part = lax.dynamic_index_in_dim(mine, p, 0, keepdims=False)
        for turn in range(4):
            traded = carry(here[turn], 1, 0)
            got = jnp.where(straight == 1, here[turn], traded)
            if turn == 0:
                got = got.at[:depth].set(own_part)
            beside = swap(got, n, 1)
            for s in range(2):
                chip = me ^ (4 * turn + 2 * s)
                for part, source in ((got, chip), (beside, chip ^ 1)):
                    part = part[s * depth : s * depth + depth]
                    weights.append(part)
                    part_places.append(source)
                    token_parts.append(part)
        token_parts[1] = token_parts[0]
    else:
        whole = lax.all_gather(qkv_weight, "tm", axis=0, tiled=True)
        grouped = jnp.stack([weight_group(whole, g) for g in range(4)])
        weights = [lax.dynamic_index_in_dim(grouped, group, 0, keepdims=False)]
        weights = [jnp.pad(weights[0], ((0, 0), (0, HD)))]
        part_places = [jnp.int32(0)]
        depth = whole.shape[0]
        packed = jnp.stack([token_group(dec_queries, stretch_mask, g) for g in range(4)])
        every = lax.all_gather(packed, "tm", axis=0)
        every = lax.dynamic_index_in_dim(every, group, 1, keepdims=False)
        order = jnp.array([m for core in range(2) for m in range(core, n, 2)], jnp.int32)
        every = jnp.take(every, order ^ me, axis=0).reshape(n, 6, 2, HD)
        token_parts = [every.transpose(1, 0, 2, 3).reshape(6, 2 * n, HD)]

    table = scalars(places + part_places)
    held = encoder(table, layered, weights, depth)

    pieces = []
    for turn in range(2):
        rows = lax.dynamic_slice_in_dim(held, 256 * (x ^ turn), 256, 0)
        route = [
            (
                8 * (d // 8) + 4 * (d // 4 % 2) + (d & 2) + (d & 1),
                8 * (d // 8) + 4 * (d & 1) + ((d & 2) ^ (2 * turn)) + (d // 4 % 2),
            )
            for d in range(n)
        ]
        got = send(rows, route)
        keep = lax.dynamic_slice_in_dim(got, 128 * c, 128, 0)
        give = swap(lax.dynamic_slice_in_dim(got, 128 * (1 - c), 128, 0), n, 1)
        pieces.append((keep, give))
    memory = gather_groups(
        [pieces[0][0], pieces[1][0], pieces[0][1], pieces[1][1]], 2 * c + x
    )

    place = scalars([4 * quarter, me, c, straight])
    partial = cross_partial(place, held, token_parts, 2 * n, len(token_parts) > 1)
    bits = [1]
    step = n // 2
    while step >= 8:
        bits.append(step)
        step //= 2
    for i, bit in enumerate(bits):
        half = partial.shape[0] // 2
        theirs = swap(partial[half:], n, bit)
        partial = merge(partial, theirs, i == len(bits) - 1)
    final = [partial[0:2]]
    for i in (1, 2, 3):
        final.append(swap(partial[2 * i : 2 * i + 2], n, 2 * i))
    cross_out = gather_groups(final, group)
    return (memory, cross_out)


def solution(mesh):
    placed = (
        P(("utt", "tm"), None),
        P(),
        P("tm", None),
        P(("utt", "tm")),
        P(("utt", "tm"), None),
        P(("utt", "tm"), None),
    )
    return jax.shard_map(
        on_device,
        mesh=mesh,
        in_specs=placed,
        out_specs=(P(("utt", "tm"), None), P(("utt", "tm"), None)),
        check_vma=False,
    )
```

```python
import functools

import jax
import jax.numpy as jnp
from jax import lax
from jax.experimental import pallas as pl
from jax.experimental.pallas import tpu as pltpu
from jax.sharding import PartitionSpec as P

HD = 64
WIDE = 256
GROUP = 320
BF = jnp.bfloat16
F32 = jnp.float32
LOW = -1e30
VMEM = pl.BlockSpec(memory_space=pltpu.VMEM)
SMEM = pl.BlockSpec(memory_space=pltpu.SMEM)


def send(block, route):
    return lax.ppermute(block, "tm", route)


def swap(block, n, mask):
    return send(block, [(d, d ^ mask) for d in range(n)])


def scalars(values):
    return jnp.stack([jnp.asarray(v, jnp.int32) for v in values])


def group_of(array, g):
    return array[:, WIDE * g : WIDE * g + WIDE], array[:, 1024 + HD * g : 1024 + HD * g + HD]


def weight_group(weight, g):
    width = weight.shape[1] // 3
    parts = [group_of(weight[:, i * width : (i + 1) * width], g) for i in range(3)]
    (q0, q1), (k0, k1), (v0, v1) = parts
    return jnp.concatenate([q0, k0, v0, k1, v1, q1], axis=1)


def token_group(queries, mask, g):
    wide, tail = group_of(queries, g)
    heads = [wide[:, HD * i : HD * i + HD] for i in range(4)] + [tail]
    asked = jnp.pad(mask.astype(BF), ((0, 0), (0, HD - mask.shape[1])))
    return jnp.concatenate(heads + [asked], axis=0)


def pack_kernel(spot, weight, *refs):
    queries, masks, segments = refs[0:2], refs[2:4], refs[4:6]
    outs, lanes = refs[6:8], refs[8]
    x, c = spot[0], spot[1]
    rows, width = weight.shape[0], weight.shape[1] // 3
    blocks = masks[0].shape[1]

    def by_core(index, count):
        flip = jnp.broadcast_to(c, (count, HD)) == 1
        return jnp.where(flip, index[1], index[0]), jnp.where(flip, index[0], index[1])

    for turn in range(2):
        column = x if turn == 0 else 1 - x
        for p in range(2):
            out = outs[turn].at[p]
            wide = pl.multiple_of(WIDE * (2 * p + column), 128)
            tails = []
            for i in range(3):
                out[:, WIDE * i : WIDE * i + WIDE] = weight[
                    :, pl.ds(pl.multiple_of(width * i + wide, 128), WIDE)
                ]
                slab = weight[:, width * i + 1024 + 128 * p : width * i + 1152 + 128 * p]
                odd = jnp.broadcast_to(column, (rows, HD)) == 1
                tails.append(jnp.where(odd, slab[:, HD:], slab[:, :HD]))
            lanes[...] = jnp.zeros_like(lanes)
            tokens = [q[:, pl.ds(wide, WIDE)].astype(F32) for q in queries]
            slabs = [q[:, 1024 + 128 * p : 1152 + 128 * p].astype(F32) for q in queries]
            odd = jnp.broadcast_to(column, (2, HD)) == 1
            for h in range(6):
                if h < 4:
                    found = [t[:, HD * h : HD * h + HD] for t in tokens]
                elif h == 4:
                    found = [jnp.where(odd, t[:, HD:], t[:, :HD]) for t in slabs]
                else:
                    gap = jnp.zeros((2, HD - blocks), F32)
                    found = [m[...].astype(F32) for m in masks]
                    if blocks < HD:
                        found = [jnp.concatenate([m, gap], axis=1) for m in found]
                low, high = by_core(found, 2)
                lanes[4 * h : 4 * h + 2, :] = low
                lanes[4 * h + 2 : 4 * h + 4, :] = high
            ids = [seg[...] for seg in segments]
            digits = [[lax.shift_right_logical(v, 7), v & 127] for v in ids]
            for d in range(2):
                for part in range(2):
                    found = [v[d][:, HD * part : HD * part + HD].astype(F32) for v in digits]
                    low, high = by_core(found, 1)
                    at = 24 + 2 * d + part
                    lanes[at : at + 1, :] = low
                    lanes[at + 4 : at + 5, :] = high
            out[:, 3 * WIDE : 896] = jnp.concatenate(tails[1:], axis=1)
            out[:, 896:] = jnp.concatenate([tails[0], lanes[...].astype(BF)], axis=1)


def pack(spot, weight, *small):
    rows = weight.shape[0]
    shape = jax.ShapeDtypeStruct((2, rows, 1024), BF)
    return pl.pallas_call(
        pack_kernel,
        out_shape=(shape, shape),
        in_specs=[SMEM] + [VMEM] * (1 + len(small)),
        out_specs=(VMEM, VMEM),
        scratch_shapes=[pltpu.VMEM((rows, HD), F32)],
    )(spot, weight, *small)


def norm_kernel(ways, places, gain, *refs):
    blocks, (normed, residual) = refs[: 4 * ways], refs[4 * ways :]
    group = places[4]
    for i in range(4):
        place = pl.multiple_of(places[i], 128)
        values = blocks[i][...]
        if ways == 2:
            first = jnp.broadcast_to(places[5], values.shape) == 1
            values = jnp.where(first, values, blocks[4 + i][...])
        values = values.astype(F32)
        mean = jnp.mean(values, axis=-1, keepdims=True)
        centred = values - mean
        var = jnp.mean(centred * centred, axis=-1, keepdims=True)
        normed[pl.ds(place, 128), :] = (centred * lax.rsqrt(var + 1e-05) * gain[...]).astype(BF)
        block = blocks[i]
        residual[pl.ds(place, 128), :WIDE] = block[
            :, pl.ds(pl.multiple_of(group * WIDE, 128), WIDE)
        ]
        slab = block[:, pl.ds(pl.multiple_of(1024 + group // 2 * 128, 128), 128)]
        odd = jnp.broadcast_to(lax.rem(group, 2), (128, HD)) == 1
        residual[pl.ds(place, 128), WIDE:] = jnp.where(odd, slab[:, HD:], slab[:, :HD])


def norm_layer(places, gain, blocks):
    return pl.pallas_call(
        functools.partial(norm_kernel, len(blocks) // 4),
        out_shape=(
            jax.ShapeDtypeStruct((512, 1280), BF),
            jax.ShapeDtypeStruct((512, GROUP), BF),
        ),
        in_specs=[SMEM] + [VMEM] * (1 + len(blocks)),
        out_specs=(VMEM, VMEM),
        compiler_params=pltpu.CompilerParams(vmem_limit_bytes=16 * 1024 * 1024),
    )(places, gain, *blocks)


def encoder_kernel(n_parts, depth, chips, places, *refs):
    layers = [refs[2 * i : 2 * i + 2] for i in range(3)]
    parts = refs[6 : 6 + n_parts]
    refs = refs[6 + n_parts :]
    if not chips:
        given, refs = refs[0], refs[1:]
    memory, near, away, weight, ids, residual, queries, keys, values = refs
    x, straight, first = places[3], places[4], places[5]

    for i, part in enumerate(parts):
        row = pl.multiple_of(places[6 + i] * depth, 16)
        weight[pl.ds(row, depth), :] = part[...]
    if chips:
        ids[...] = jnp.zeros_like(ids)
        for i in range(n_parts // 2):
            here, there = parts[2 * i][:32, 960:], parts[2 * i + 1][:32, 960:]
            lanes = jnp.where(jnp.broadcast_to(straight, (32, HD)) == 1, here.astype(F32), there.astype(F32))
            found = lanes[24:]
            for core in range(2):
                high = found[4 * core : 4 * core + 2]
                marks = high * 128.0 + found[4 * core + 2 : 4 * core + 4]
                block = places[6 + 2 * i] // 2 * 2 + core - first

                @pl.when((block >= 0) & (block < 12))
                def _():
                    ids[0:1, pl.ds(pl.multiple_of(block * 128, 128), 128)] = jnp.concatenate(
                        [marks[0:1], marks[1:2]], axis=1
                    )

    else:
        ids[...] = given[...]

    for slab in range(3):
        values[:, 256 * slab + 128 : 256 * slab + 256] = jnp.ones((1536, 128), BF)
    for i, (normed, kept) in enumerate(layers):
        place = pl.multiple_of(places[i], 512)
        found = jnp.dot(normed[...], weight[:, 256:896], preferred_element_type=F32).astype(BF)
        keys[pl.ds(place, 512), :256] = found[:, :256]
        keys[pl.ds(place, 512), 256:] = found[:, 512:]
        for slab in range(3):
            values[pl.ds(place, 512), 256 * slab : 256 * slab + 128] = found[
                :, 256 + 128 * slab : 384 + 128 * slab
            ]
        if i < 2:

            @pl.when(place == 512)
            def _():
                residual[...] = kept[...]
                queries[:, :WIDE] = jnp.dot(
                    normed[...], weight[:, :WIDE], preferred_element_type=F32
                ).astype(BF)
                tail = jnp.dot(normed[...], weight[:, 896:], preferred_element_type=F32).astype(BF)
                lane = lax.broadcasted_iota(jnp.int32, tail.shape, 1)
                queries[:, WIDE:] = jnp.where(lane < HD, tail, jnp.zeros_like(tail))

    side = lax.broadcasted_iota(jnp.int32, (8, 128), 0) == lax.broadcasted_iota(
        jnp.int32, (8, 128), 1
    ) // HD
    sides = jnp.where(side, 1.0, 0.0).astype(BF)
    only = jnp.where(side & (lax.broadcasted_iota(jnp.int32, (8, 128), 0) == 0), 1.0, 0.0).astype(BF)
    most = []
    for held in (queries, keys):
        top = jnp.zeros((8, 1), F32)
        for slab in range(3):
            part = held[:, 128 * slab : 128 * slab + 128]
            norms = lax.dot_general(
                sides if slab < 2 else only,
                part * part,
                (((1,), (1,)), ((), ())),
                preferred_element_type=F32,
            )
            top = jnp.maximum(top, jnp.max(norms, axis=-1, keepdims=True))
        most.append(jnp.max(top))
    small = most[0] * most[1] < 220000.0

    def attend(step, shifted):
        row = step * 128 if isinstance(step, int) else pl.multiple_of(step * 128, 128)
        mine = jnp.broadcast_to(ids[0:1, pl.ds(row + 512, 128)], (128, 128)).T[:, 0:1]
        bias = jnp.where(mine == ids[0:1, pl.ds(row, 1152)], 0.0, LOW)
        lane = lax.broadcasted_iota(jnp.int32, (128, 128), 1)
        for slab in range(3):
            span = slice(128 * slab, 128 * slab + 128)
            query = queries[pl.ds(row, 128), span] * BF(0.125)
            mask = bias
            if slab < 2:
                none = jnp.zeros_like(query)
                query = jnp.concatenate(
                    [jnp.where(lane < HD, query, none), jnp.where(lane < HD, none, query)], axis=0
                )
                mask = jnp.concatenate([bias, bias], axis=0)
            scores = lax.dot_general(
                query,
                keys[pl.ds(row, 1152), span],
                (((1,), (1,)), ((), ())),
                preferred_element_type=F32,
            )
            scores = scores + mask
            if shifted:
                scores = scores - jnp.max(scores, axis=-1, keepdims=True)
            raised = jnp.exp(scores).astype(BF)
            out = jnp.dot(
                raised,
                values[pl.ds(row, 1152), 256 * slab : 256 * slab + 256],
                preferred_element_type=F32,
            )
            out = out[:, :128] / out[:, 128:]
            if slab < 2:
                context = jnp.where(lane < HD, out[:128], out[128:])
                stem = residual[pl.ds(row, 128), span].astype(F32)
                memory[pl.ds(row, 128), span] = (stem + context).astype(BF)
            else:
                stem = residual[pl.ds(row, 128), WIDE:].astype(F32)
                memory[pl.ds(row, 128), WIDE:] = (stem + out[:, HD:]).astype(BF)

    @pl.when(small)
    def _():
        for step in range(4):
            attend(step, False)

    @pl.when(jnp.logical_not(small))
    def _():
        lax.fori_loop(0, 4, lambda step, carry: (attend(step, True), carry)[1], 0)

    near[...] = memory[pl.ds(pl.multiple_of(256 * x, 256), 256), :]
    away[...] = memory[pl.ds(pl.multiple_of(256 * (1 - x), 256), 256), :]


def encoder(places, layers, parts, depth, extra):
    operands = [a for layer in layers for a in layer] + parts + extra
    return pl.pallas_call(
        functools.partial(encoder_kernel, len(parts), depth, not extra),
        out_shape=(
            jax.ShapeDtypeStruct((512, GROUP), BF),
            jax.ShapeDtypeStruct((256, GROUP), BF),
            jax.ShapeDtypeStruct((256, GROUP), BF),
        ),
        in_specs=[SMEM] + [VMEM] * len(operands),
        out_specs=(VMEM, VMEM, VMEM),
        scratch_shapes=[
            pltpu.VMEM((1280, 1024), BF),
            pltpu.VMEM((8, 1536), F32),
            pltpu.VMEM((512, GROUP), BF),
            pltpu.VMEM((512, 384), BF),
            pltpu.VMEM((1536, 384), BF),
            pltpu.VMEM((1536, 768), BF),
        ],
        compiler_params=pltpu.CompilerParams(vmem_limit_bytes=24 * 1024 * 1024),
    )(places, *operands)


def spread(columns, rows, slab):
    lane = lax.broadcasted_iota(jnp.int32, (rows, 128), 1)
    return jnp.where(lane < HD, columns[2 * slab], columns[min(2 * slab + 1, 4)])


def cross_kernel(chips, place, memory, *refs):
    tokens, out = refs[-2:]
    count = out.shape[0]
    parts, outs_by_owner = refs[: -2 - count // 8], refs[-2 - count // 8 : -2]
    first, me, core, straight = place[0], place[1], place[2], place[3]
    half = count // 2
    if chips:
        for i in range(len(parts) // 2):
            here, there = parts[2 * i][:24, 960:], parts[2 * i + 1][:24, 960:]
            rows = jnp.where(jnp.broadcast_to(straight, (24, HD)) == 1, here.astype(F32), there.astype(F32))
            for h in range(6):
                low, high = rows[4 * h : 4 * h + 2], rows[4 * h + 2 : 4 * h + 4]
                flip = jnp.broadcast_to(core, (2, HD)) == 1
                tokens[h, 2 * i : 2 * i + 2, :] = jnp.where(flip, high, low)
                tokens[h, half + 2 * i : half + 2 * i + 2, :] = jnp.where(flip, low, high)
    else:
        tokens[...] = parts[0][...].astype(F32)
    blocks = HD
    spot = lax.broadcasted_iota(jnp.int32, (count, blocks), 1)
    order = lax.broadcasted_iota(jnp.int32, (count, 1), 0)
    relative = 2 * (lax.rem(order, half) // 2) + order // half
    owner = relative ^ me
    allowed = []
    for b in range(4):
        ask = jnp.sum(jnp.where(spot == first + b, tokens[5], 0.0), axis=-1, keepdims=True)
        allowed.append((ask > 0.5) | (owner == first + b))
    lane = lax.broadcasted_iota(jnp.int32, (count, 128), 1)
    bias = jnp.concatenate(
        [jnp.broadcast_to(jnp.where(a, 0.0, LOW), (count, 128)) for a in allowed], axis=1
    )
    stats = jnp.zeros((count, 128), F32)
    for slab in range(3):
        heads = [(tokens[h] * 0.125).astype(BF) for h in range(2 * slab, min(2 * slab + 2, 5))]
        none = jnp.zeros_like(heads[0])
        if slab < 2:
            heads = [
                jnp.concatenate([heads[0], none], axis=1),
                jnp.concatenate([none, heads[1]], axis=1),
            ]
            held = memory[:, 128 * slab : 128 * slab + 128]
        else:
            held = memory[:, WIDE:]
        outs = []
        for i, head in enumerate(heads):
            cross = lax.dot_general(
                head, held, (((1,), (1,)), ((), ())), preferred_element_type=F32
            )
            cross = jnp.where(bias < 0.0, LOW, cross)
            top = jnp.max(cross, axis=-1, keepdims=True)
            raised = jnp.where(bias < 0.0, 0.0, jnp.exp(cross - top))
            den = jnp.sum(raised, axis=-1, keepdims=True)
            outs.append(jnp.dot(raised.astype(BF), held, preferred_element_type=F32))
            stats = jnp.where(lane == 2 * slab + i, top, stats)
            stats = jnp.where(lane == 8 + 2 * slab + i, den, stats)
        if slab < 2:
            out[:, 128 * slab : 128 * slab + 128] = jnp.where(lane < HD, outs[0], outs[1])
        else:
            out[:, WIDE:384] = jnp.concatenate([outs[0], jnp.zeros_like(outs[0])], axis=1)
    out[:, 384:] = stats
    for i, owned in enumerate(outs_by_owner):
        owned[...] = out[8 * i : 8 * i + 8, :]


def cross_partial(place, memory, parts, count, chips):
    return pl.pallas_call(
        functools.partial(cross_kernel, chips),
        out_shape=(jax.ShapeDtypeStruct((8, 512), F32),) * (count // 8),
        in_specs=[SMEM] + [VMEM] * (1 + len(parts)),
        out_specs=(VMEM,) * (count // 8),
        scratch_shapes=[pltpu.VMEM((6, count, HD), F32), pltpu.VMEM((count, 512), F32)],
    )(place, memory, *parts)


def merge_kernel(*refs):
    parts, outs, out = refs[:-5], refs[-5:-1], refs[-1]
    stats = [part[:, 384:] for part in parts]
    factors, dens = [[] for _ in parts], []
    for head in range(5):
        tops = [s[:, head : head + 1] for s in stats]
        best = functools.reduce(jnp.maximum, tops)
        den = jnp.zeros_like(best)
        for i, s in enumerate(stats):
            factor = jnp.exp(tops[i] - best)
            den = den + factor * s[:, 8 + head : 9 + head]
            factors[i].append(factor)
        dens.append(den)
    for slab in range(3):
        span = slice(128 * slab, 128 * slab + 128)
        total = jnp.zeros((8, 128), F32)
        for i, part in enumerate(parts):
            total = total + spread(factors[i], 8, slab) * part[:, span]
        out[:, span] = total / spread(dens, 8, slab)
    for i in range(4):
        outs[i][...] = out[2 * i : 2 * i + 2, :].astype(BF)


def merge(parts):
    return pl.pallas_call(
        merge_kernel,
        out_shape=(jax.ShapeDtypeStruct((2, 384), BF),) * 4,
        in_specs=[VMEM] * len(parts),
        out_specs=(VMEM,) * 4,
        scratch_shapes=[pltpu.VMEM((8, 384), F32)],
    )(*parts)


def gather_groups(pieces, group):
    wide, tail = [], []
    for g in range(4):
        turn = group ^ g
        piece = jnp.where(
            turn < 2,
            jnp.where(turn == 0, pieces[0], pieces[1]),
            jnp.where(turn == 2, pieces[2], pieces[3]),
        )
        wide.append(piece[:, :WIDE])
        tail.append(piece[:, WIDE:GROUP])
    return jnp.concatenate(wide + tail, axis=1)


def on_device(stem, norm_gain, qkv_weight, segment_ids, dec_queries, stretch_mask):
    n = lax.axis_size("tm")
    layers = n // 4
    me = lax.axis_index("tm")
    z, x, c = me // 4, (me // 2) % 2, me % 2
    p, k = z % 2, z // 2
    quarter = 2 * k + c
    group = 2 * p + x
    depth = qkv_weight.shape[0]

    layers_route = [1 if i % 2 else -1 for i in range(layers)]
    near_route = [
        (4 * i + j, 4 * (i + s) + j)
        for i, s in enumerate(layers_route)
        for j in range(4)
        if 0 <= i + s < layers
    ]
    near = send(stem, near_route)
    pair = swap(stem, n, 4)
    stem_x = swap(stem, n, 2)
    utts = lax.axis_size("utt")
    straight = (c == lax.axis_index("utt") % 2).astype(jnp.int32)
    gain = norm_gain.reshape(1, -1)
    inner = [128 * (2 * x + c), 128 * (2 * x + 1 - c), 128 * (2 - 2 * x + c), 128 * (3 - 2 * x - c)]
    spots = inner + [group]
    extra = []
    if depth % 16 == 0 and layers == 4 and utts % 2 == 0:
        carriers = [(u, d) for u in range(utts) for d in range(n) if d % 2 == u % 2]

        def carry(block, turn_u, turn_d):
            route = [(u * n + d, (u ^ turn_u) * n + (d ^ turn_d)) for u, d in carriers]
            return lax.ppermute(block, ("utt", "tm"), route)

        small = [dec_queries, stretch_mask, segment_ids.reshape(1, -1)]
        both = [part for piece in small for part in (piece, swap(piece, n, 1))]
        mine, theirs = pack(scalars([x, c]), qkv_weight, *both)
        across = carry(theirs, 0, 2)
        mine_late, across_late, pair, near = lax.optimization_barrier((mine, across, pair, near))
        ready = [
            jnp.concatenate(
                [
                    lax.dynamic_slice_in_dim(mine_late, p ^ a, 1, 0),
                    lax.dynamic_slice_in_dim(across_late, p ^ a, 1, 0),
                ]
            ).reshape(2 * depth, 1024)
            for a in range(2)
        ]
        here = {0: lax.dynamic_index_in_dim(across, p, 0, keepdims=False)}
        for turn in (3, 2, 1):
            here[turn] = carry(ready[turn % 2], 0, 4 * turn)
        own_part = lax.dynamic_index_in_dim(mine, p, 0, keepdims=False)
        weights = [own_part, swap(own_part, n, 1)]
        part_places = [me, me ^ 1]
        for turn in range(4):
            traded = carry(here[turn], 1, 0)
            got = jnp.where(straight == 1, here[turn], traded)
            beside = swap(got, n, 1)
            pieces = got.shape[0] // depth
            for s in range(pieces):
                chip = me ^ (4 * turn + 2 * (s + 2 - pieces))
                for part, source in ((got, chip), (beside, chip ^ 1)):
                    weights.append(part[s * depth : s * depth + depth])
                    part_places.append(source)
        token_parts = [own_part, own_part] + weights[2:]

        beside_route = [
            (d, d ^ 1) for d in range(n) if d % 2 == d // 8
        ]
        inside = [d for d in range(n) if d // 4 in (1, 2)]
        relayed = send(near, [(d, d ^ 4) for d in inside])
        near_x = send(near, [(d, d ^ 2) for d in inside])
        relayed_x = send(relayed, [(d ^ 4, d ^ 6) for d in inside])
        halo_layer = []
        for a, b in ((near, near_x), (relayed, relayed_x)):
            halo_layer += [a, send(a, beside_route), b, send(b, beside_route)]
        halo_spots = spots + [(p != k).astype(jnp.int32)]
    else:
        far = swap(near, n, 4)
        left = jnp.where(p == 0, near, far)
        right = jnp.where(p == 0, far, near)
        left_x, right_x = swap(left, n, 2), swap(right, n, 2)
        halo_layer = [
            jnp.where(c == 0, left, right),
            swap(jnp.where(c == 0, right, left), n, 1),
            jnp.where(c == 0, left_x, right_x),
            swap(jnp.where(c == 0, right_x, left_x), n, 1),
        ]
        halo_spots = spots
        whole = lax.all_gather(qkv_weight, "tm", axis=0, tiled=True)
        grouped = jnp.stack([weight_group(whole, g) for g in range(4)])
        weights = [lax.dynamic_index_in_dim(grouped, group, 0, keepdims=False)]
        weights = [jnp.pad(weights[0], ((0, 0), (0, HD)))]
        part_places = [jnp.int32(0)]
        depth = whole.shape[0]
        packed = jnp.stack([token_group(dec_queries, stretch_mask, g) for g in range(4)])
        every = lax.all_gather(packed, "tm", axis=0)
        every = lax.dynamic_index_in_dim(every, group, 1, keepdims=False)
        order = jnp.array([m for core in range(2) for m in range(core, n, 2)], jnp.int32)
        every = jnp.take(every, order ^ me, axis=0).reshape(n, 6, 2, HD)
        token_parts = [every.transpose(1, 0, 2, 3).reshape(6, 2 * n, HD)]
        marks = lax.all_gather(segment_ids, "tm", axis=0, tiled=True).astype(F32)
        marks = jnp.pad(marks, (512, 512))
        marks = lax.dynamic_slice_in_dim(marks, 512 * quarter, 1536, 0)
        extra = [jnp.broadcast_to(marks[None], (8, 1536))]
    pair_x = swap(pair, n, 2)
    own_layer = [stem, swap(stem, n, 1), stem_x, swap(stem_x, n, 1)]
    pair_layer = [pair, swap(pair, n, 1), pair_x, swap(pair_x, n, 1)]
    layered = []
    for blocks, at in ((own_layer, spots), (pair_layer, spots), (halo_layer, halo_spots)):
        layered.append(norm_layer(scalars(at), gain, blocks))
    places = [512 * (p - c + 1), 512 * (2 - p - c), 1024 * c, x, straight, 4 * quarter - 4]

    table = scalars(places + part_places)
    held, stay, leave = encoder(table, layered, weights, depth, extra)

    pieces = []
    for turn, rows in enumerate((stay, leave)):
        route = [
            (
                8 * (d // 8) + 4 * (d // 4 % 2) + (d & 2) + (d & 1),
                8 * (d // 8) + 4 * (d & 1) + ((d & 2) ^ (2 * turn)) + (d // 4 % 2),
            )
            for d in range(n)
        ]
        got = send(rows, route)
        keep = lax.dynamic_slice_in_dim(got, 128 * c, 128, 0)
        give = swap(lax.dynamic_slice_in_dim(got, 128 * (1 - c), 128, 0), n, 1)
        pieces.append((keep, give))
    memory = gather_groups([pieces[0][0], pieces[1][0], pieces[0][1], pieces[1][1]], 2 * c + x)

    place = scalars([4 * quarter, me, c, straight])
    partial = cross_partial(place, held, token_parts, 2 * n, len(token_parts) > 1)
    owned = [partial[0]]
    outer = n // 8
    for i in range(1, 2 * outer):
        core, turn = i // outer, i % outer
        owned.append(swap(partial[i], n, 8 * turn + core))
    final = merge(owned)
    final = [final[0]] + [swap(final[i], n, 2 * i) for i in (1, 2, 3)]
    cross_out = gather_groups(final, group)
    return (memory, cross_out)


def solution(mesh):
    placed = (
        P(("utt", "tm"), None),
        P(),
        P("tm", None),
        P(("utt", "tm")),
        P(("utt", "tm"), None),
        P(("utt", "tm"), None),
    )
    return jax.shard_map(
        on_device,
        mesh=mesh,
        in_specs=placed,
        out_specs=(P(("utt", "tm"), None), P(("utt", "tm"), None)),
        check_vma=False,
    )
```

```python
import functools

import jax
import jax.numpy as jnp
from jax import lax
from jax.experimental import pallas as pl
from jax.experimental.pallas import tpu as pltpu
from jax.sharding import PartitionSpec as P

HD = 64
WIDE = 256
GROUP = 320
BF = jnp.bfloat16
F32 = jnp.float32
LOW = -1e30
VMEM = pl.BlockSpec(memory_space=pltpu.VMEM)
SMEM = pl.BlockSpec(memory_space=pltpu.SMEM)


def send(block, route):
    return lax.ppermute(block, "tm", route)


def swap(block, n, mask):
    return send(block, [(d, d ^ mask) for d in range(n)])


def scalars(values):
    return jnp.stack([jnp.asarray(v, jnp.int32) for v in values])


def group_of(array, g):
    return array[:, WIDE * g : WIDE * g + WIDE], array[:, 1024 + HD * g : 1024 + HD * g + HD]


def weight_group(weight, g):
    width = weight.shape[1] // 3
    parts = [group_of(weight[:, i * width : (i + 1) * width], g) for i in range(3)]
    (q0, q1), (k0, k1), (v0, v1) = parts
    return jnp.concatenate([q0, k0, v0, k1, v1, q1], axis=1)


def token_group(queries, mask, g):
    wide, tail = group_of(queries, g)
    heads = [wide[:, HD * i : HD * i + HD] for i in range(4)] + [tail]
    asked = jnp.pad(mask.astype(BF), ((0, 0), (0, HD - mask.shape[1])))
    return jnp.concatenate(heads + [asked], axis=0)


def pack_kernel(spot, weight, *refs):
    queries, masks, segments = refs[0:2], refs[2:4], refs[4:6]
    outs, lanes = refs[6:8], refs[8]
    x, c = spot[6], spot[7]
    rows, width = weight.shape[0], weight.shape[1] // 3
    blocks = masks[0].shape[1]

    def by_core(index, count):
        flip = jnp.broadcast_to(c, (count, HD)) == 1
        return jnp.where(flip, index[1], index[0]), jnp.where(flip, index[0], index[1])

    for turn in range(2):
        column = x if turn == 0 else 1 - x
        for p in range(2):
            out = outs[turn].at[p]
            wide = pl.multiple_of(WIDE * (2 * p + column), 128)
            tails = []
            for i in range(3):
                out[:, WIDE * i : WIDE * i + WIDE] = weight[
                    :, pl.ds(pl.multiple_of(width * i + wide, 128), WIDE)
                ]
                slab = weight[:, width * i + 1024 + 128 * p : width * i + 1152 + 128 * p]
                odd = jnp.broadcast_to(column, (rows, HD)) == 1
                tails.append(jnp.where(odd, slab[:, HD:], slab[:, :HD]))
            lanes[...] = jnp.zeros_like(lanes)
            tokens = [q[:, pl.ds(wide, WIDE)].astype(F32) for q in queries]
            slabs = [q[:, 1024 + 128 * p : 1152 + 128 * p].astype(F32) for q in queries]
            odd = jnp.broadcast_to(column, (2, HD)) == 1
            for h in range(6):
                if h < 4:
                    found = [t[:, HD * h : HD * h + HD] for t in tokens]
                elif h == 4:
                    found = [jnp.where(odd, t[:, HD:], t[:, :HD]) for t in slabs]
                else:
                    gap = jnp.zeros((2, HD - blocks), F32)
                    found = [m[...].astype(F32) for m in masks]
                    if blocks < HD:
                        found = [jnp.concatenate([m, gap], axis=1) for m in found]
                low, high = by_core(found, 2)
                lanes[4 * h : 4 * h + 2, :] = low
                lanes[4 * h + 2 : 4 * h + 4, :] = high
            ids = [seg[...] for seg in segments]
            digits = [[lax.shift_right_logical(v, 7), v & 127] for v in ids]
            for d in range(2):
                for part in range(2):
                    found = [v[d][:, HD * part : HD * part + HD].astype(F32) for v in digits]
                    low, high = by_core(found, 1)
                    at = 24 + 2 * d + part
                    lanes[at : at + 1, :] = low
                    lanes[at + 4 : at + 5, :] = high
            out[:, 3 * WIDE : 896] = jnp.concatenate(tails[1:], axis=1)
            out[:, 896:] = jnp.concatenate([tails[0], lanes[...].astype(BF)], axis=1)


def pack(spot, weight, *small):
    rows = weight.shape[0]
    shape = jax.ShapeDtypeStruct((2, rows, 1024), BF)
    return pl.pallas_call(
        pack_kernel,
        out_shape=(shape, shape),
        in_specs=[SMEM] + [VMEM] * (1 + len(small)),
        out_specs=(VMEM, VMEM),
        scratch_shapes=[pltpu.VMEM((rows, HD), F32)],
    )(spot, weight, *small)


def norm_kernel(ways, table, gain, *refs):
    blocks, (normed, residual) = refs[: 4 * ways], refs[4 * ways :]
    group = table[4]
    for i in range(4):
        place = pl.multiple_of(table[i], 128)
        values = blocks[i][...]
        if ways == 2:
            first = jnp.broadcast_to(table[5], values.shape) == 1
            values = jnp.where(first, values, blocks[4 + i][...])
        values = values.astype(F32)
        mean = jnp.mean(values, axis=-1, keepdims=True)
        centred = values - mean
        var = jnp.mean(centred * centred, axis=-1, keepdims=True)
        normed[pl.ds(place, 128), :] = (centred * lax.rsqrt(var + 1e-05) * gain[...]).astype(BF)
        block = blocks[i]
        residual[pl.ds(place, 128), :WIDE] = block[
            :, pl.ds(pl.multiple_of(group * WIDE, 128), WIDE)
        ]
        slab = block[:, pl.ds(pl.multiple_of(1024 + group // 2 * 128, 128), 128)]
        odd = jnp.broadcast_to(lax.rem(group, 2), (128, HD)) == 1
        residual[pl.ds(place, 128), WIDE:] = jnp.where(odd, slab[:, HD:], slab[:, :HD])


def norm_layer(table, gain, blocks):
    return pl.pallas_call(
        functools.partial(norm_kernel, len(blocks) // 4),
        out_shape=(
            jax.ShapeDtypeStruct((512, 1280), BF),
            jax.ShapeDtypeStruct((512, GROUP), BF),
        ),
        in_specs=[SMEM] + [VMEM] * (1 + len(blocks)),
        out_specs=(VMEM, VMEM),
        compiler_params=pltpu.CompilerParams(vmem_limit_bytes=16 * 1024 * 1024),
    )(table, gain, *blocks)


def encoder_kernel(n_parts, depth, chips, places, *refs):
    layers = [refs[2 * i : 2 * i + 2] for i in range(3)]
    parts = refs[6 : 6 + n_parts]
    refs = refs[6 + n_parts :]
    if not chips:
        given, refs = refs[0], refs[1:]
    memory, near, away, weight, ids, residual, queries, keys, values = refs
    x, straight, first = places[11], places[12], places[13]

    for i, part in enumerate(parts):
        row = pl.multiple_of(places[14 + i] * depth, 16)
        weight[pl.ds(row, depth), :] = part[...]
    if chips:
        ids[...] = jnp.zeros_like(ids)
        for i in range(n_parts // 2):
            here, there = parts[2 * i][:32, 960:], parts[2 * i + 1][:32, 960:]
            lanes = jnp.where(jnp.broadcast_to(straight, (32, HD)) == 1, here.astype(F32), there.astype(F32))
            found = lanes[24:]
            for core in range(2):
                high = found[4 * core : 4 * core + 2]
                marks = high * 128.0 + found[4 * core + 2 : 4 * core + 4]
                block = places[14 + 2 * i] // 2 * 2 + core - first

                @pl.when((block >= 0) & (block < 12))
                def _():
                    ids[0:1, pl.ds(pl.multiple_of(block * 128, 128), 128)] = jnp.concatenate(
                        [marks[0:1], marks[1:2]], axis=1
                    )

    else:
        ids[...] = given[...]

    for slab in range(3):
        values[:, 256 * slab + 128 : 256 * slab + 256] = jnp.ones((1536, 128), BF)
    for i, (normed, kept) in enumerate(layers):
        place = pl.multiple_of(places[8 + i], 512)
        found = jnp.dot(normed[...], weight[:, 256:896], preferred_element_type=F32).astype(BF)
        keys[pl.ds(place, 512), :256] = found[:, :256]
        keys[pl.ds(place, 512), 256:] = found[:, 512:]
        for slab in range(3):
            values[pl.ds(place, 512), 256 * slab : 256 * slab + 128] = found[
                :, 256 + 128 * slab : 384 + 128 * slab
            ]
        if i < 2:

            @pl.when(place == 512)
            def _():
                residual[...] = kept[...]
                queries[:, :WIDE] = jnp.dot(
                    normed[...], weight[:, :WIDE], preferred_element_type=F32
                ).astype(BF)
                tail = jnp.dot(normed[...], weight[:, 896:], preferred_element_type=F32).astype(BF)
                lane = lax.broadcasted_iota(jnp.int32, tail.shape, 1)
                queries[:, WIDE:] = jnp.where(lane < HD, tail, jnp.zeros_like(tail))

    side = lax.broadcasted_iota(jnp.int32, (8, 128), 0) == lax.broadcasted_iota(
        jnp.int32, (8, 128), 1
    ) // HD
    sides = jnp.where(side, 1.0, 0.0).astype(BF)
    only = jnp.where(side & (lax.broadcasted_iota(jnp.int32, (8, 128), 0) == 0), 1.0, 0.0).astype(BF)
    most = []
    for held in (queries, keys):
        top = jnp.zeros((8, 1), F32)
        for slab in range(3):
            part = held[:, 128 * slab : 128 * slab + 128]
            norms = lax.dot_general(
                sides if slab < 2 else only,
                part * part,
                (((1,), (1,)), ((), ())),
                preferred_element_type=F32,
            )
            top = jnp.maximum(top, jnp.max(norms, axis=-1, keepdims=True))
        most.append(jnp.max(top))
    small = most[0] * most[1] < 220000.0

    def attend(step, shifted):
        row = step * 128 if isinstance(step, int) else pl.multiple_of(step * 128, 128)
        mine = jnp.broadcast_to(ids[0:1, pl.ds(row + 512, 128)], (128, 128)).T[:, 0:1]
        bias = jnp.where(mine == ids[0:1, pl.ds(row, 1152)], 0.0, LOW)
        lane = lax.broadcasted_iota(jnp.int32, (128, 128), 1)
        for slab in range(3):
            span = slice(128 * slab, 128 * slab + 128)
            query = queries[pl.ds(row, 128), span] * BF(0.125)
            mask = bias
            if slab < 2:
                none = jnp.zeros_like(query)
                query = jnp.concatenate(
                    [jnp.where(lane < HD, query, none), jnp.where(lane < HD, none, query)], axis=0
                )
                mask = jnp.concatenate([bias, bias], axis=0)
            scores = lax.dot_general(
                query,
                keys[pl.ds(row, 1152), span],
                (((1,), (1,)), ((), ())),
                preferred_element_type=F32,
            )
            scores = scores + mask
            if shifted:
                scores = scores - jnp.max(scores, axis=-1, keepdims=True)
            raised = jnp.exp(scores).astype(BF)
            out = jnp.dot(
                raised,
                values[pl.ds(row, 1152), 256 * slab : 256 * slab + 256],
                preferred_element_type=F32,
            )
            out = out[:, :128] / out[:, 128:]
            if slab < 2:
                context = jnp.where(lane < HD, out[:128], out[128:])
                stem = residual[pl.ds(row, 128), span].astype(F32)
                memory[pl.ds(row, 128), span] = (stem + context).astype(BF)
            else:
                stem = residual[pl.ds(row, 128), WIDE:].astype(F32)
                memory[pl.ds(row, 128), WIDE:] = (stem + out[:, HD:]).astype(BF)

    @pl.when(small)
    def _():
        for step in range(4):
            attend(step, False)

    @pl.when(jnp.logical_not(small))
    def _():
        lax.fori_loop(0, 4, lambda step, carry: (attend(step, True), carry)[1], 0)

    near[...] = memory[pl.ds(pl.multiple_of(256 * x, 256), 256), :]
    away[...] = memory[pl.ds(pl.multiple_of(256 * (1 - x), 256), 256), :]


def encoder(places, layers, parts, depth, extra):
    operands = [a for layer in layers for a in layer] + parts + extra
    return pl.pallas_call(
        functools.partial(encoder_kernel, len(parts), depth, not extra),
        out_shape=(
            jax.ShapeDtypeStruct((512, GROUP), BF),
            jax.ShapeDtypeStruct((256, GROUP), BF),
            jax.ShapeDtypeStruct((256, GROUP), BF),
        ),
        in_specs=[SMEM] + [VMEM] * len(operands),
        out_specs=(VMEM, VMEM, VMEM),
        scratch_shapes=[
            pltpu.VMEM((1280, 1024), BF),
            pltpu.VMEM((8, 1536), F32),
            pltpu.VMEM((512, GROUP), BF),
            pltpu.VMEM((512, 384), BF),
            pltpu.VMEM((1536, 384), BF),
            pltpu.VMEM((1536, 768), BF),
        ],
        compiler_params=pltpu.CompilerParams(vmem_limit_bytes=24 * 1024 * 1024),
    )(places, *operands)


def cross_kernel(chips, base, table, memory, *refs):
    tokens, asked, out = refs[-3:]
    count = asked.shape[0]
    parts, outs = refs[: -3 - count // 8], refs[-3 - count // 8 : -3]
    first, me, core, straight = [table[base + i] for i in range(4)]
    half = count // 2
    tokens[...] = jnp.zeros_like(tokens)
    if chips:
        flip = jnp.broadcast_to(core, (2, HD)) == 1
        for i in range(len(parts) // 2):
            here, there = parts[2 * i][:24, 960:], parts[2 * i + 1][:24, 960:]
            rows = jnp.where(
                jnp.broadcast_to(straight, (24, HD)) == 1, here.astype(F32), there.astype(F32)
            )
            for h in range(6):
                low, high = rows[4 * h : 4 * h + 2], rows[4 * h + 2 : 4 * h + 4]
                for turn in range(2):
                    at = half * turn + 2 * i
                    found = jnp.where(flip, low, high) if turn else jnp.where(flip, high, low)
                    if h < 5:
                        tokens[count * h + at : count * h + at + 2, HD * h : HD * h + HD] = found * 0.125
                    else:
                        asked[at : at + 2, :] = found
    else:
        for h in range(5):
            tokens[count * h : count * h + count, HD * h : HD * h + HD] = parts[0][h].astype(F32) * 0.125
        asked[...] = parts[0][5].astype(F32)
    spot = lax.broadcasted_iota(jnp.int32, (count, HD), 1)
    order = lax.broadcasted_iota(jnp.int32, (count, 1), 0)
    owner = (2 * (lax.rem(order, half) // 2) + order // half) ^ me
    bias = []
    for b in range(4):
        ask = jnp.sum(jnp.where(spot == first + b, asked[...], 0.0), axis=-1, keepdims=True)
        allowed = (ask > 0.5) | (owner == first + b)
        bias.append(jnp.broadcast_to(jnp.where(allowed, 0.0, LOW), (count, 128)))
    bias = jnp.concatenate(bias, axis=1)
    bias = jnp.concatenate([bias] * 5, axis=0)
    cross = lax.dot_general(
        tokens[:, :GROUP].astype(BF),
        memory[...],
        (((1,), (1,)), ((), ())),
        preferred_element_type=F32,
    )
    cross = jnp.where(bias < 0.0, LOW, cross)
    top = jnp.max(cross, axis=-1, keepdims=True)
    raised = jnp.where(bias < 0.0, 0.0, jnp.exp(cross - top))
    den = jnp.sum(raised, axis=-1, keepdims=True)
    out[...] = jnp.dot(raised.astype(BF), memory[...], preferred_element_type=F32)
    lane = lax.broadcasted_iota(jnp.int32, (count, HD), 1)
    for h in range(5):
        rows = slice(count * h, count * h + count)
        stats = jnp.where(lane == 0, top[rows], den[rows])
        both = jnp.concatenate([out[rows, HD * h : HD * h + HD], stats], axis=1)
        for i, owned in enumerate(outs):
            owned[8 * h : 8 * h + 8, :] = both[8 * i : 8 * i + 8]


def cross_partial(base, table, memory, parts, count, chips):
    return pl.pallas_call(
        functools.partial(cross_kernel, chips, base),
        out_shape=(jax.ShapeDtypeStruct((40, 128), F32),) * (count // 8),
        in_specs=[SMEM] + [VMEM] * (1 + len(parts)),
        out_specs=(VMEM,) * (count // 8),
        scratch_shapes=[
            pltpu.VMEM((5 * count, 384), F32),
            pltpu.VMEM((count, HD), F32),
            pltpu.VMEM((5 * count, GROUP), F32),
        ],
    )(table, memory, *parts)


def merge_kernel(*refs):
    parts, outs, out = refs[:-5], refs[-5:-1], refs[-1]
    tops = [part[:, HD : HD + 1] for part in parts]
    best = functools.reduce(jnp.maximum, tops)
    total = jnp.zeros((40, 128), F32)
    for top, part in zip(tops, parts):
        total = total + jnp.exp(top - best) * part[...]
    final = total[:, :HD] / total[:, HD + 1 : HD + 2]
    heads = [final[8 * h : 8 * h + 8] for h in range(5)] + [jnp.zeros((8, HD), F32)]
    for slab in range(3):
        out[:, 128 * slab : 128 * slab + 128] = jnp.concatenate(heads[2 * slab : 2 * slab + 2], axis=1)
    for i in range(4):
        outs[i][...] = out[2 * i : 2 * i + 2, :].astype(BF)


def merge(parts):
    return pl.pallas_call(
        merge_kernel,
        out_shape=(jax.ShapeDtypeStruct((2, 384), BF),) * 4,
        in_specs=[VMEM] * len(parts),
        out_specs=(VMEM,) * 4,
        scratch_shapes=[pltpu.VMEM((8, 384), F32)],
    )(*parts)


def gather_groups(pieces, group):
    wide, tail = [], []
    for g in range(4):
        turn = group ^ g
        piece = jnp.where(
            turn < 2,
            jnp.where(turn == 0, pieces[0], pieces[1]),
            jnp.where(turn == 2, pieces[2], pieces[3]),
        )
        wide.append(piece[:, :WIDE])
        tail.append(piece[:, WIDE:GROUP])
    return jnp.concatenate(wide + tail, axis=1)


def on_device(stem, norm_gain, qkv_weight, segment_ids, dec_queries, stretch_mask):
    n = lax.axis_size("tm")
    layers = n // 4
    me = lax.axis_index("tm")
    z, x, c = me // 4, (me // 2) % 2, me % 2
    p, k = z % 2, z // 2
    quarter = 2 * k + c
    group = 2 * p + x
    depth = qkv_weight.shape[0]

    layers_route = [1 if i % 2 else -1 for i in range(layers)]
    near_route = [
        (4 * i + j, 4 * (i + s) + j)
        for i, s in enumerate(layers_route)
        for j in range(4)
        if 0 <= i + s < layers
    ]
    pair = swap(stem, n, 4)
    near = send(stem, near_route)
    stem_x = swap(stem, n, 2)
    utts = lax.axis_size("utt")
    straight = (c == lax.axis_index("utt") % 2).astype(jnp.int32)
    gain = norm_gain.reshape(1, -1)
    direct = depth % 16 == 0 and layers == 4 and utts % 2 == 0
    table = [128 * (2 * x + c), 128 * (2 * x + 1 - c), 128 * (2 - 2 * x + c), 128 * (3 - 2 * x - c)]
    table += [group, p != k, x, c]
    table += [512 * (p - c + 1), 512 * (2 - p - c), 1024 * c, x, straight, 4 * quarter - 4]
    sources = [me ^ m for m in range(n)] if direct else [jnp.int32(0)]
    table = scalars(table + sources + [4 * quarter, me, c, straight])
    base = 14 + len(sources)
    extra = []
    if direct:
        carriers = [(u, d) for u in range(utts) for d in range(n) if d % 2 == u % 2]

        def carry(block, turn_u, turn_d):
            route = [(u * n + d, (u ^ turn_u) * n + (d ^ turn_d)) for u, d in carriers]
            return lax.ppermute(block, ("utt", "tm"), route)

        far = send(stem, [(d, d ^ 8) for d in range(n) if d // 4 in (1, 2)])
        small = [dec_queries, stretch_mask, segment_ids.reshape(1, -1)]
        both = [part for piece in small for part in (piece, swap(piece, n, 1))]
        mine, theirs = pack(table, qkv_weight, *both)
        across = carry(theirs, 0, 2)
        mine_late, across_late, pair, near, far, stem_x = lax.optimization_barrier(
            (mine, across, pair, near, far, stem_x)
        )
        halo = jnp.where((z == 1) | (z == 2), near, far)
        pair_x = swap(pair, n, 2)
        halo_x = swap(halo, n, 2)
        ready = [
            jnp.concatenate(
                [
                    lax.dynamic_slice_in_dim(mine_late, p ^ a, 1, 0),
                    lax.dynamic_slice_in_dim(across_late, p ^ a, 1, 0),
                ]
            ).reshape(2 * depth, 1024)
            for a in range(2)
        ]
        here = {0: lax.dynamic_index_in_dim(across, p, 0, keepdims=False)}
        for turn in (1, 2, 3):
            here[turn] = carry(ready[turn % 2], 0, 4 * turn)
        here[3], here[2], pair_x, halo_x = lax.optimization_barrier(
            (here[3], here[2], pair_x, halo_x)
        )
        own_part = lax.dynamic_index_in_dim(mine, p, 0, keepdims=False)
        weights = [own_part, swap(own_part, n, 1)]
        for turn in range(4):
            traded = carry(here[turn], 1, 0)
            got = jnp.where(straight == 1, here[turn], traded)
            beside = swap(got, n, 1)
            for s in range(got.shape[0] // depth):
                for part in (got, beside):
                    weights.append(part[s * depth : s * depth + depth])
        token_parts = [own_part, own_part] + weights[2:]
        aside = [(d, d ^ 1) for d in range(n) if d % 2 == d // 8]
        halo_layer = [halo, send(halo, aside), halo_x, send(halo_x, aside)]
    else:
        far = swap(near, n, 4)
        left = jnp.where(p == 0, near, far)
        right = jnp.where(p == 0, far, near)
        left_x, right_x = swap(left, n, 2), swap(right, n, 2)
        halo_layer = [
            jnp.where(c == 0, left, right),
            swap(jnp.where(c == 0, right, left), n, 1),
            jnp.where(c == 0, left_x, right_x),
            swap(jnp.where(c == 0, right_x, left_x), n, 1),
        ]
        whole = lax.all_gather(qkv_weight, "tm", axis=0, tiled=True)
        grouped = jnp.stack([weight_group(whole, g) for g in range(4)])
        weights = [lax.dynamic_index_in_dim(grouped, group, 0, keepdims=False)]
        weights = [jnp.pad(weights[0], ((0, 0), (0, HD)))]
        depth = whole.shape[0]
        packed = jnp.stack([token_group(dec_queries, stretch_mask, g) for g in range(4)])
        every = lax.all_gather(packed, "tm", axis=0)
        every = lax.dynamic_index_in_dim(every, group, 1, keepdims=False)
        order = jnp.array([m for core in range(2) for m in range(core, n, 2)], jnp.int32)
        every = jnp.take(every, order ^ me, axis=0).reshape(n, 6, 2, HD)
        token_parts = [every.transpose(1, 0, 2, 3).reshape(6, 2 * n, HD)]
        marks = lax.all_gather(segment_ids, "tm", axis=0, tiled=True).astype(F32)
        marks = jnp.pad(marks, (512, 512))
        marks = lax.dynamic_slice_in_dim(marks, 512 * quarter, 1536, 0)
        extra = [jnp.broadcast_to(marks[None], (8, 1536))]
        pair_x = swap(pair, n, 2)
    own_layer = [stem, swap(stem, n, 1), stem_x, swap(stem_x, n, 1)]
    pair_layer = [pair, swap(pair, n, 1), pair_x, swap(pair_x, n, 1)]
    layered = [norm_layer(table, gain, blocks) for blocks in (own_layer, pair_layer, halo_layer)]
    held, stay, leave = encoder(table, layered, weights, depth, extra)

    pieces = []
    for turn, rows in enumerate((stay, leave)):
        route = [
            (
                8 * (d // 8) + 4 * (d // 4 % 2) + (d & 2) + (d & 1),
                8 * (d // 8) + 4 * (d & 1) + ((d & 2) ^ (2 * turn)) + (d // 4 % 2),
            )
            for d in range(n)
        ]
        got = send(rows, route)
        keep = lax.dynamic_slice_in_dim(got, 128 * c, 128, 0)
        give = swap(lax.dynamic_slice_in_dim(got, 128 * (1 - c), 128, 0), n, 1)
        pieces.append((keep, give))
    memory = gather_groups([pieces[0][0], pieces[1][0], pieces[0][1], pieces[1][1]], 2 * c + x)

    partial = cross_partial(base, table, held, token_parts, 2 * n, direct)
    owned = [partial[0]]
    outer = n // 8
    for i in range(1, 2 * outer):
        core, turn = i // outer, i % outer
        owned.append(swap(partial[i], n, 8 * turn + core))
    final = merge(owned)
    final = [final[0]] + [swap(final[i], n, 2 * i) for i in (1, 2, 3)]
    cross_out = gather_groups(final, group)
    return (memory, cross_out)


def solution(mesh):
    placed = (
        P(("utt", "tm"), None),
        P(),
        P("tm", None),
        P(("utt", "tm")),
        P(("utt", "tm"), None),
        P(("utt", "tm"), None),
    )
    return jax.shard_map(
        on_device,
        mesh=mesh,
        in_specs=placed,
        out_specs=(P(("utt", "tm"), None), P(("utt", "tm"), None)),
        check_vma=False,
    )
```

```python
import functools

import jax
import jax.numpy as jnp
from jax import lax
from jax.experimental import pallas as pl
from jax.experimental.pallas import tpu as pltpu
from jax.sharding import PartitionSpec as P

HD = 64
WIDE = 256
GROUP = 320
BF = jnp.bfloat16
F32 = jnp.float32
LOW = -1e30
VMEM = pl.BlockSpec(memory_space=pltpu.VMEM)
SMEM = pl.BlockSpec(memory_space=pltpu.SMEM)


def send(block, route):
    return lax.ppermute(block, "tm", route)


def swap(block, n, mask):
    return send(block, [(d, d ^ mask) for d in range(n)])


def scalars(values):
    return jnp.stack([jnp.asarray(v, jnp.int32) for v in values])


def group_of(array, g):
    return array[:, WIDE * g : WIDE * g + WIDE], array[:, 1024 + HD * g : 1024 + HD * g + HD]


def weight_group(weight, g):
    width = weight.shape[1] // 3
    parts = [group_of(weight[:, i * width : (i + 1) * width], g) for i in range(3)]
    (q0, q1), (k0, k1), (v0, v1) = parts
    return jnp.concatenate([q0, k0, v0, k1, v1, q1], axis=1)


def token_group(queries, mask, g):
    wide, tail = group_of(queries, g)
    heads = [wide[:, HD * i : HD * i + HD] for i in range(4)] + [tail]
    asked = jnp.pad(mask.astype(BF), ((0, 0), (0, HD - mask.shape[1])))
    return jnp.concatenate(heads + [asked], axis=0)


def pack_kernel(spot, weight, *refs):
    queries, masks, segments = refs[0:2], refs[2:4], refs[4:6]
    outs, lanes = refs[6:8], refs[8]
    x, c = spot[6], spot[7]
    rows, width = weight.shape[0], weight.shape[1] // 3
    blocks = masks[0].shape[1]

    def by_core(index, count):
        flip = jnp.broadcast_to(c, (count, HD)) == 1
        return jnp.where(flip, index[1], index[0]), jnp.where(flip, index[0], index[1])

    for turn in range(2):
        column = x if turn == 0 else 1 - x
        for p in range(2):
            out = outs[turn].at[p]
            wide = pl.multiple_of(WIDE * (2 * p + column), 128)
            tails = []
            for i in range(3):
                out[:, WIDE * i : WIDE * i + WIDE] = weight[
                    :, pl.ds(pl.multiple_of(width * i + wide, 128), WIDE)
                ]
                slab = weight[:, width * i + 1024 + 128 * p : width * i + 1152 + 128 * p]
                odd = jnp.broadcast_to(column, (rows, HD)) == 1
                tails.append(jnp.where(odd, slab[:, HD:], slab[:, :HD]))
            lanes[...] = jnp.zeros_like(lanes)
            tokens = [q[:, pl.ds(wide, WIDE)].astype(F32) for q in queries]
            slabs = [q[:, 1024 + 128 * p : 1152 + 128 * p].astype(F32) for q in queries]
            odd = jnp.broadcast_to(column, (2, HD)) == 1
            for h in range(6):
                if h < 4:
                    found = [t[:, HD * h : HD * h + HD] for t in tokens]
                elif h == 4:
                    found = [jnp.where(odd, t[:, HD:], t[:, :HD]) for t in slabs]
                else:
                    gap = jnp.zeros((2, HD - blocks), F32)
                    found = [m[...].astype(F32) for m in masks]
                    if blocks < HD:
                        found = [jnp.concatenate([m, gap], axis=1) for m in found]
                low, high = by_core(found, 2)
                lanes[4 * h : 4 * h + 2, :] = low
                lanes[4 * h + 2 : 4 * h + 4, :] = high
            ids = [seg[...] for seg in segments]
            digits = [[lax.shift_right_logical(v, 7), v & 127] for v in ids]
            for d in range(2):
                for part in range(2):
                    found = [v[d][:, HD * part : HD * part + HD].astype(F32) for v in digits]
                    low, high = by_core(found, 1)
                    at = 24 + 2 * d + part
                    lanes[at : at + 1, :] = low
                    lanes[at + 4 : at + 5, :] = high
            out[:, 3 * WIDE : 896] = jnp.concatenate(tails[1:], axis=1)
            out[:, 896:] = jnp.concatenate([tails[0], lanes[...].astype(BF)], axis=1)


def pack(spot, weight, *small):
    rows = weight.shape[0]
    shape = jax.ShapeDtypeStruct((2, rows, 1024), BF)
    return pl.pallas_call(
        pack_kernel,
        out_shape=(shape, shape),
        in_specs=[SMEM] + [VMEM] * (1 + len(small)),
        out_specs=(VMEM, VMEM),
        scratch_shapes=[pltpu.VMEM((rows, HD), F32)],
        compiler_params=pltpu.CompilerParams(vmem_limit_bytes=8 * 1024 * 1024),
    )(spot, weight, *small)


def norm_kernel(ways, table, gain, *refs):
    blocks, (normed, residual) = refs[: 4 * ways], refs[4 * ways :]
    group = table[4]
    for i in range(4):
        place = pl.multiple_of(table[i], 128)
        values = blocks[i][...]
        if ways == 2:
            first = jnp.broadcast_to(table[5], values.shape) == 1
            values = jnp.where(first, values, blocks[4 + i][...])
        values = values.astype(F32)
        mean = jnp.mean(values, axis=-1, keepdims=True)
        centred = values - mean
        var = jnp.mean(centred * centred, axis=-1, keepdims=True)
        normed[pl.ds(place, 128), :] = (centred * lax.rsqrt(var + 1e-05) * gain[...]).astype(BF)
        block = blocks[i]
        residual[pl.ds(place, 128), :WIDE] = block[
            :, pl.ds(pl.multiple_of(group * WIDE, 128), WIDE)
        ]
        slab = block[:, pl.ds(pl.multiple_of(1024 + group // 2 * 128, 128), 128)]
        odd = jnp.broadcast_to(lax.rem(group, 2), (128, HD)) == 1
        residual[pl.ds(place, 128), WIDE:] = jnp.where(odd, slab[:, HD:], slab[:, :HD])


def norm_layer(table, gain, blocks):
    return pl.pallas_call(
        functools.partial(norm_kernel, len(blocks) // 4),
        out_shape=(
            jax.ShapeDtypeStruct((512, 1280), BF),
            jax.ShapeDtypeStruct((512, GROUP), BF),
        ),
        in_specs=[SMEM] + [VMEM] * (1 + len(blocks)),
        out_specs=(VMEM, VMEM),
        compiler_params=pltpu.CompilerParams(vmem_limit_bytes=16 * 1024 * 1024),
    )(table, gain, *blocks)


def encoder_kernel(n_parts, depth, chips, places, *refs):
    layers = [refs[2 * i : 2 * i + 2] for i in range(3)]
    parts = refs[6 : 6 + n_parts]
    refs = refs[6 + n_parts :]
    if not chips:
        given, refs = refs[0], refs[1:]
    memory, near, away, weight, ids, residual, queries, keys, values = refs
    x, straight, first = places[11], places[12], places[13]

    for i, part in enumerate(parts):
        row = pl.multiple_of(places[14 + i] * depth, 16)
        weight[pl.ds(row, depth), :] = part[...]
    if chips:
        ids[...] = jnp.zeros_like(ids)
        for i in range(n_parts // 2):
            here, there = parts[2 * i][:32, 960:], parts[2 * i + 1][:32, 960:]
            lanes = jnp.where(jnp.broadcast_to(straight, (32, HD)) == 1, here.astype(F32), there.astype(F32))
            found = lanes[24:]
            for core in range(2):
                high = found[4 * core : 4 * core + 2]
                marks = high * 128.0 + found[4 * core + 2 : 4 * core + 4]
                block = places[14 + 2 * i] // 2 * 2 + core - first

                @pl.when((block >= 0) & (block < 12))
                def _():
                    ids[0:1, pl.ds(pl.multiple_of(block * 128, 128), 128)] = jnp.concatenate(
                        [marks[0:1], marks[1:2]], axis=1
                    )

    else:
        ids[...] = given[...]

    for slab in range(3):
        values[:, 256 * slab + 128 : 256 * slab + 256] = jnp.ones((1536, 128), BF)
    for i, (normed, kept) in enumerate(layers):
        place = pl.multiple_of(places[8 + i], 512)
        found = jnp.dot(normed[...], weight[:, 256:896], preferred_element_type=F32).astype(BF)
        keys[pl.ds(place, 512), :256] = found[:, :256]
        keys[pl.ds(place, 512), 256:] = found[:, 512:]
        for slab in range(3):
            values[pl.ds(place, 512), 256 * slab : 256 * slab + 128] = found[
                :, 256 + 128 * slab : 384 + 128 * slab
            ]
        if i < 2:

            @pl.when(place == 512)
            def _():
                residual[...] = kept[...]
                queries[:, :WIDE] = jnp.dot(
                    normed[...], weight[:, :WIDE], preferred_element_type=F32
                ).astype(BF)
                tail = jnp.dot(normed[...], weight[:, 896:], preferred_element_type=F32).astype(BF)
                lane = lax.broadcasted_iota(jnp.int32, tail.shape, 1)
                queries[:, WIDE:] = jnp.where(lane < HD, tail, jnp.zeros_like(tail))

    side = lax.broadcasted_iota(jnp.int32, (8, 128), 0) == lax.broadcasted_iota(
        jnp.int32, (8, 128), 1
    ) // HD
    sides = jnp.where(side, 1.0, 0.0).astype(BF)
    only = jnp.where(side & (lax.broadcasted_iota(jnp.int32, (8, 128), 0) == 0), 1.0, 0.0).astype(BF)
    most = []
    for held in (queries, keys):
        top = jnp.zeros((8, 1), F32)
        for slab in range(3):
            part = held[:, 128 * slab : 128 * slab + 128]
            norms = lax.dot_general(
                sides if slab < 2 else only,
                part * part,
                (((1,), (1,)), ((), ())),
                preferred_element_type=F32,
            )
            top = jnp.maximum(top, jnp.max(norms, axis=-1, keepdims=True))
        most.append(jnp.max(top))
    small = most[0] * most[1] < 220000.0

    def attend(step, shifted):
        row = step * 128 if isinstance(step, int) else pl.multiple_of(step * 128, 128)
        mine = jnp.broadcast_to(ids[0:1, pl.ds(row + 512, 128)], (128, 128)).T[:, 0:1]
        bias = jnp.where(mine == ids[0:1, pl.ds(row, 1152)], 0.0, LOW)
        lane = lax.broadcasted_iota(jnp.int32, (128, 128), 1)
        for slab in range(3):
            span = slice(128 * slab, 128 * slab + 128)
            query = queries[pl.ds(row, 128), span] * BF(0.125)
            mask = bias
            if slab < 2:
                none = jnp.zeros_like(query)
                query = jnp.concatenate(
                    [jnp.where(lane < HD, query, none), jnp.where(lane < HD, none, query)], axis=0
                )
                mask = jnp.concatenate([bias, bias], axis=0)
            scores = lax.dot_general(
                query,
                keys[pl.ds(row, 1152), span],
                (((1,), (1,)), ((), ())),
                preferred_element_type=F32,
            )
            scores = scores + mask
            if shifted:
                scores = scores - jnp.max(scores, axis=-1, keepdims=True)
            raised = jnp.exp(scores).astype(BF)
            out = jnp.dot(
                raised,
                values[pl.ds(row, 1152), 256 * slab : 256 * slab + 256],
                preferred_element_type=F32,
            )
            out = out[:, :128] / out[:, 128:]
            if slab < 2:
                context = jnp.where(lane < HD, out[:128], out[128:])
                stem = residual[pl.ds(row, 128), span].astype(F32)
                memory[pl.ds(row, 128), span] = (stem + context).astype(BF)
            else:
                stem = residual[pl.ds(row, 128), WIDE:].astype(F32)
                memory[pl.ds(row, 128), WIDE:] = (stem + out[:, HD:]).astype(BF)

    @pl.when(small)
    def _():
        for step in range(4):
            attend(step, False)

    @pl.when(jnp.logical_not(small))
    def _():
        lax.fori_loop(0, 4, lambda step, carry: (attend(step, True), carry)[1], 0)

    near[...] = memory[pl.ds(pl.multiple_of(256 * x, 256), 256), :]
    away[...] = memory[pl.ds(pl.multiple_of(256 * (1 - x), 256), 256), :]


def encoder(places, layers, parts, depth, extra):
    operands = [a for layer in layers for a in layer] + parts + extra
    return pl.pallas_call(
        functools.partial(encoder_kernel, len(parts), depth, not extra),
        out_shape=(
            jax.ShapeDtypeStruct((512, GROUP), BF),
            jax.ShapeDtypeStruct((256, GROUP), BF),
            jax.ShapeDtypeStruct((256, GROUP), BF),
        ),
        in_specs=[SMEM] + [VMEM] * len(operands),
        out_specs=(VMEM, VMEM, VMEM),
        scratch_shapes=[
            pltpu.VMEM((1280, 1024), BF),
            pltpu.VMEM((8, 1536), F32),
            pltpu.VMEM((512, GROUP), BF),
            pltpu.VMEM((512, 384), BF),
            pltpu.VMEM((1536, 384), BF),
            pltpu.VMEM((1536, 768), BF),
        ],
        compiler_params=pltpu.CompilerParams(vmem_limit_bytes=24 * 1024 * 1024),
    )(places, *operands)


def cross_kernel(chips, base, table, memory, *refs):
    tokens, asked, out = refs[-3:]
    count = asked.shape[0]
    parts, outs = refs[: -3 - count // 8], refs[-3 - count // 8 : -3]
    first, me, core, straight = [table[base + i] for i in range(4)]
    half = count // 2
    tokens[...] = jnp.zeros_like(tokens)
    if chips:
        flip = jnp.broadcast_to(core, (2, HD)) == 1
        for i in range(len(parts) // 2):
            here, there = parts[2 * i][:24, 960:], parts[2 * i + 1][:24, 960:]
            rows = jnp.where(
                jnp.broadcast_to(straight, (24, HD)) == 1, here.astype(F32), there.astype(F32)
            )
            for h in range(6):
                low, high = rows[4 * h : 4 * h + 2], rows[4 * h + 2 : 4 * h + 4]
                for turn in range(2):
                    at = half * turn + 2 * i
                    found = jnp.where(flip, low, high) if turn else jnp.where(flip, high, low)
                    if h < 5:
                        tokens[count * h + at : count * h + at + 2, HD * h : HD * h + HD] = found * 0.125
                    else:
                        asked[at : at + 2, :] = found
    else:
        for h in range(5):
            tokens[count * h : count * h + count, HD * h : HD * h + HD] = parts[0][h].astype(F32) * 0.125
        asked[...] = parts[0][5].astype(F32)
    spot = lax.broadcasted_iota(jnp.int32, (count, HD), 1)
    order = lax.broadcasted_iota(jnp.int32, (count, 1), 0)
    owner = (2 * (lax.rem(order, half) // 2) + order // half) ^ me
    bias = []
    for b in range(4):
        ask = jnp.sum(jnp.where(spot == first + b, asked[...], 0.0), axis=-1, keepdims=True)
        allowed = (ask > 0.5) | (owner == first + b)
        bias.append(jnp.broadcast_to(jnp.where(allowed, 0.0, LOW), (count, 128)))
    bias = jnp.concatenate(bias, axis=1)
    bias = jnp.concatenate([bias] * 5, axis=0)
    cross = lax.dot_general(
        tokens[:, :GROUP].astype(BF),
        memory[...],
        (((1,), (1,)), ((), ())),
        preferred_element_type=F32,
    )
    cross = jnp.where(bias < 0.0, LOW, cross)
    top = jnp.max(cross, axis=-1, keepdims=True)
    raised = jnp.where(bias < 0.0, 0.0, jnp.exp(cross - top))
    den = jnp.sum(raised, axis=-1, keepdims=True)
    out[...] = jnp.dot(raised.astype(BF), memory[...], preferred_element_type=F32)
    lane = lax.broadcasted_iota(jnp.int32, (count, HD), 1)
    for h in range(5):
        rows = slice(count * h, count * h + count)
        stats = jnp.where(lane == 0, top[rows], den[rows])
        both = jnp.concatenate([out[rows, HD * h : HD * h + HD], stats], axis=1)
        for i, owned in enumerate(outs):
            owned[8 * h : 8 * h + 8, :] = both[8 * i : 8 * i + 8]


def cross_partial(base, table, memory, parts, count, chips):
    return pl.pallas_call(
        functools.partial(cross_kernel, chips, base),
        out_shape=(jax.ShapeDtypeStruct((40, 128), F32),) * (count // 8),
        in_specs=[SMEM] + [VMEM] * (1 + len(parts)),
        out_specs=(VMEM,) * (count // 8),
        scratch_shapes=[
            pltpu.VMEM((5 * count, 384), F32),
            pltpu.VMEM((count, HD), F32),
            pltpu.VMEM((5 * count, GROUP), F32),
        ],
        compiler_params=pltpu.CompilerParams(vmem_limit_bytes=12 * 1024 * 1024),
    )(table, memory, *parts)


def merge_kernel(*refs):
    parts, outs, out = refs[:-5], refs[-5:-1], refs[-1]
    tops = [part[:, HD : HD + 1] for part in parts]
    best = functools.reduce(jnp.maximum, tops)
    total = jnp.zeros((40, 128), F32)
    for top, part in zip(tops, parts):
        total = total + jnp.exp(top - best) * part[...]
    final = total[:, :HD] / total[:, HD + 1 : HD + 2]
    heads = [final[8 * h : 8 * h + 8] for h in range(5)] + [jnp.zeros((8, HD), F32)]
    for slab in range(3):
        out[:, 128 * slab : 128 * slab + 128] = jnp.concatenate(heads[2 * slab : 2 * slab + 2], axis=1)
    for i in range(4):
        outs[i][...] = out[2 * i : 2 * i + 2, :].astype(BF)


def merge(parts):
    return pl.pallas_call(
        merge_kernel,
        out_shape=(jax.ShapeDtypeStruct((2, 384), BF),) * 4,
        in_specs=[VMEM] * len(parts),
        out_specs=(VMEM,) * 4,
        scratch_shapes=[pltpu.VMEM((8, 384), F32)],
        compiler_params=pltpu.CompilerParams(vmem_limit_bytes=4 * 1024 * 1024),
    )(*parts)


def gather_groups(pieces, group):
    wide, tail = [], []
    for g in range(4):
        turn = group ^ g
        piece = jnp.where(
            turn < 2,
            jnp.where(turn == 0, pieces[0], pieces[1]),
            jnp.where(turn == 2, pieces[2], pieces[3]),
        )
        wide.append(piece[:, :WIDE])
        tail.append(piece[:, WIDE:GROUP])
    return jnp.concatenate(wide + tail, axis=1)


def on_device(stem, norm_gain, qkv_weight, segment_ids, dec_queries, stretch_mask):
    n = lax.axis_size("tm")
    layers = n // 4
    me = lax.axis_index("tm")
    z, x, c = me // 4, (me // 2) % 2, me % 2
    p, k = z % 2, z // 2
    quarter = 2 * k + c
    group = 2 * p + x
    depth = qkv_weight.shape[0]

    layers_route = [1 if i % 2 else -1 for i in range(layers)]
    near_route = [
        (4 * i + j, 4 * (i + s) + j)
        for i, s in enumerate(layers_route)
        for j in range(4)
        if 0 <= i + s < layers
    ]
    pair = swap(stem, n, 4)
    near = send(stem, near_route)
    stem_x = swap(stem, n, 2)
    utts = lax.axis_size("utt")
    straight = (c == lax.axis_index("utt") % 2).astype(jnp.int32)
    gain = norm_gain.reshape(1, -1)
    direct = depth % 16 == 0 and layers == 4 and utts % 2 == 0
    table = [128 * (2 * x + c), 128 * (2 * x + 1 - c), 128 * (2 - 2 * x + c), 128 * (3 - 2 * x - c)]
    table += [group, p != k, x, c]
    table += [512 * (p - c + 1), 512 * (2 - p - c), 1024 * c, x, straight, 4 * quarter - 4]
    sources = [me ^ m for m in range(n)] if direct else [jnp.int32(0)]
    table = scalars(table + sources + [4 * quarter, me, c, straight])
    base = 14 + len(sources)
    extra = []
    if direct:
        carriers = [(u, d) for u in range(utts) for d in range(n) if d % 2 == u % 2]

        def carry(block, turn_u, turn_d):
            route = [(u * n + d, (u ^ turn_u) * n + (d ^ turn_d)) for u, d in carriers]
            return lax.ppermute(block, ("utt", "tm"), route)

        far = send(stem, [(d, d ^ 8) for d in range(n) if d // 4 in (1, 2)])
        small = [dec_queries, stretch_mask, segment_ids.reshape(1, -1)]
        both = [part for piece in small for part in (piece, swap(piece, n, 1))]
        mine, theirs = pack(table, qkv_weight, *both)
        across = carry(theirs, 0, 2)
        stem_c = swap(stem, n, 1)
        mine_late, across_late, pair, near, stem_x, stem_c = lax.optimization_barrier(
            (mine, across, pair, near, stem_x, stem_c)
        )
        halo = jnp.where((z == 1) | (z == 2), near, far)
        pair_x = swap(pair, n, 2)
        halo_x = swap(halo, n, 2)
        ready = [
            jnp.concatenate(
                [
                    lax.dynamic_slice_in_dim(mine_late, p ^ a, 1, 0),
                    lax.dynamic_slice_in_dim(across_late, p ^ a, 1, 0),
                ]
            ).reshape(2 * depth, 1024)
            for a in range(2)
        ]
        here = {0: lax.dynamic_index_in_dim(across, p, 0, keepdims=False)}
        for turn in (1, 2, 3):
            here[turn] = carry(ready[turn % 2], 0, 4 * turn)
        here[3], here[2], here[0], pair, pair_x, halo, halo_x, stem_x, mine = lax.optimization_barrier(
            (here[3], here[2], here[0], pair, pair_x, halo, halo_x, stem_x, mine)
        )
        own_part = lax.dynamic_index_in_dim(mine, p, 0, keepdims=False)
        weights = [own_part, swap(own_part, n, 1)]
        for turn in range(4):
            traded = carry(here[turn], 1, 0)
            got = jnp.where(straight == 1, here[turn], traded)
            beside = swap(got, n, 1)
            for s in range(got.shape[0] // depth):
                for part in (got, beside):
                    weights.append(part[s * depth : s * depth + depth])
        token_parts = [own_part, own_part] + weights[2:]
        aside = [(d, d ^ 1) for d in range(n) if d % 2 == d // 8]
        halo_layer = [halo, send(halo, aside), halo_x, send(halo_x, aside)]
    else:
        stem_c = swap(stem, n, 1)
        far = swap(near, n, 4)
        left = jnp.where(p == 0, near, far)
        right = jnp.where(p == 0, far, near)
        left_x, right_x = swap(left, n, 2), swap(right, n, 2)
        halo_layer = [
            jnp.where(c == 0, left, right),
            swap(jnp.where(c == 0, right, left), n, 1),
            jnp.where(c == 0, left_x, right_x),
            swap(jnp.where(c == 0, right_x, left_x), n, 1),
        ]
        whole = lax.all_gather(qkv_weight, "tm", axis=0, tiled=True)
        grouped = jnp.stack([weight_group(whole, g) for g in range(4)])
        weights = [lax.dynamic_index_in_dim(grouped, group, 0, keepdims=False)]
        weights = [jnp.pad(weights[0], ((0, 0), (0, HD)))]
        depth = whole.shape[0]
        packed = jnp.stack([token_group(dec_queries, stretch_mask, g) for g in range(4)])
        every = lax.all_gather(packed, "tm", axis=0)
        every = lax.dynamic_index_in_dim(every, group, 1, keepdims=False)
        order = jnp.array([m for core in range(2) for m in range(core, n, 2)], jnp.int32)
        every = jnp.take(every, order ^ me, axis=0).reshape(n, 6, 2, HD)
        token_parts = [every.transpose(1, 0, 2, 3).reshape(6, 2 * n, HD)]
        marks = lax.all_gather(segment_ids, "tm", axis=0, tiled=True).astype(F32)
        marks = jnp.pad(marks, (512, 512))
        marks = lax.dynamic_slice_in_dim(marks, 512 * quarter, 1536, 0)
        extra = [jnp.broadcast_to(marks[None], (8, 1536))]
        pair_x = swap(pair, n, 2)
    own_layer = [stem, stem_c, stem_x, swap(stem_x, n, 1)]
    pair_layer = [pair, swap(pair, n, 1), pair_x, swap(pair_x, n, 1)]
    layered = [norm_layer(table, gain, blocks) for blocks in (own_layer, pair_layer, halo_layer)]
    held, stay, leave = encoder(table, layered, weights, depth, extra)

    pieces = []
    for turn, rows in enumerate((stay, leave)):
        route = [
            (
                8 * (d // 8) + 4 * (d // 4 % 2) + (d & 2) + (d & 1),
                8 * (d // 8) + 4 * (d & 1) + ((d & 2) ^ (2 * turn)) + (d // 4 % 2),
            )
            for d in range(n)
        ]
        got = send(rows, route)
        keep = lax.dynamic_slice_in_dim(got, 128 * c, 128, 0)
        give = swap(lax.dynamic_slice_in_dim(got, 128 * (1 - c), 128, 0), n, 1)
        pieces.append((keep, give))
    memory = gather_groups([pieces[0][0], pieces[1][0], pieces[0][1], pieces[1][1]], 2 * c + x)

    partial = cross_partial(base, table, held, token_parts, 2 * n, direct)
    owned = [partial[0]]
    outer = n // 8
    for i in range(1, 2 * outer):
        core, turn = i // outer, i % outer
        owned.append(swap(partial[i], n, 8 * turn + core))
    final = merge(owned)
    final = [final[0]] + [swap(final[i], n, 2 * i) for i in (1, 2, 3)]
    cross_out = gather_groups(final, group)
    return (memory, cross_out)


def solution(mesh):
    placed = (
        P(("utt", "tm"), None),
        P(),
        P("tm", None),
        P(("utt", "tm")),
        P(("utt", "tm"), None),
        P(("utt", "tm"), None),
    )
    return jax.shard_map(
        on_device,
        mesh=mesh,
        in_specs=placed,
        out_specs=(P(("utt", "tm"), None), P(("utt", "tm"), None)),
        check_vma=False,
    )
```

```python
import functools

import jax
import jax.numpy as jnp
from jax import lax
from jax.experimental import pallas as pl
from jax.experimental.pallas import tpu as pltpu
from jax.sharding import PartitionSpec as P

HD = 64
WIDE = 256
GROUP = 320
BF = jnp.bfloat16
F32 = jnp.float32
LOW = -1e30
VMEM = pl.BlockSpec(memory_space=pltpu.VMEM)
SMEM = pl.BlockSpec(memory_space=pltpu.SMEM)


def send(block, route):
    return lax.ppermute(block, "tm", route)


def swap(block, n, mask):
    return send(block, [(d, d ^ mask) for d in range(n)])


def after(value, *awaited):
    return lax.optimization_barrier((value, *awaited))[0]


def scalars(values):
    return jnp.stack([jnp.asarray(v, jnp.int32) for v in values])


def group_of(array, g):
    return array[:, WIDE * g : WIDE * g + WIDE], array[:, 1024 + HD * g : 1024 + HD * g + HD]


def weight_group(weight, g):
    width = weight.shape[1] // 3
    parts = [group_of(weight[:, i * width : (i + 1) * width], g) for i in range(3)]
    (q0, q1), (k0, k1), (v0, v1) = parts
    return jnp.concatenate([q0, k0, v0, k1, v1, q1], axis=1)


def token_group(queries, mask, g):
    wide, tail = group_of(queries, g)
    heads = [wide[:, HD * i : HD * i + HD] for i in range(4)] + [tail]
    asked = jnp.pad(mask.astype(BF), ((0, 0), (0, HD - mask.shape[1])))
    return jnp.concatenate(heads + [asked], axis=0)


def pack_kernel(spot, weight, *refs):
    queries, masks, segments = refs[0:2], refs[2:4], refs[4:6]
    outs, lanes = refs[6:8], refs[8]
    x, c = spot[6], spot[7]
    rows, width = weight.shape[0], weight.shape[1] // 3
    blocks = masks[0].shape[1]

    def by_core(index, count):
        flip = jnp.broadcast_to(c, (count, HD)) == 1
        return jnp.where(flip, index[1], index[0]), jnp.where(flip, index[0], index[1])

    for turn in range(2):
        column = x if turn == 0 else 1 - x
        for p in range(2):
            out = outs[turn].at[p]
            wide = pl.multiple_of(WIDE * (2 * p + column), 128)
            tails = []
            for i in range(3):
                out[:, WIDE * i : WIDE * i + WIDE] = weight[
                    :, pl.ds(pl.multiple_of(width * i + wide, 128), WIDE)
                ]
                slab = weight[:, width * i + 1024 + 128 * p : width * i + 1152 + 128 * p]
                odd = jnp.broadcast_to(column, (rows, HD)) == 1
                tails.append(jnp.where(odd, slab[:, HD:], slab[:, :HD]))
            lanes[...] = jnp.zeros_like(lanes)
            tokens = [q[:, pl.ds(wide, WIDE)].astype(F32) for q in queries]
            slabs = [q[:, 1024 + 128 * p : 1152 + 128 * p].astype(F32) for q in queries]
            odd = jnp.broadcast_to(column, (2, HD)) == 1
            for h in range(6):
                if h < 4:
                    found = [t[:, HD * h : HD * h + HD] for t in tokens]
                elif h == 4:
                    found = [jnp.where(odd, t[:, HD:], t[:, :HD]) for t in slabs]
                else:
                    gap = jnp.zeros((2, HD - blocks), F32)
                    found = [m[...].astype(F32) for m in masks]
                    if blocks < HD:
                        found = [jnp.concatenate([m, gap], axis=1) for m in found]
                low, high = by_core(found, 2)
                lanes[4 * h : 4 * h + 2, :] = low
                lanes[4 * h + 2 : 4 * h + 4, :] = high
            ids = [seg[...] for seg in segments]
            digits = [[lax.shift_right_logical(v, 7), v & 127] for v in ids]
            for d in range(2):
                for part in range(2):
                    found = [v[d][:, HD * part : HD * part + HD].astype(F32) for v in digits]
                    low, high = by_core(found, 1)
                    at = 24 + 2 * d + part
                    lanes[at : at + 1, :] = low
                    lanes[at + 4 : at + 5, :] = high
            out[:, 3 * WIDE : 896] = jnp.concatenate(tails[1:], axis=1)
            out[:, 896:] = jnp.concatenate([tails[0], lanes[...].astype(BF)], axis=1)


def pack(spot, weight, *small):
    rows = weight.shape[0]
    shape = jax.ShapeDtypeStruct((2, rows, 1024), BF)
    return pl.pallas_call(
        pack_kernel,
        out_shape=(shape, shape),
        in_specs=[SMEM] + [VMEM] * (1 + len(small)),
        out_specs=(VMEM, VMEM),
        scratch_shapes=[pltpu.VMEM((rows, HD), F32)],
    )(spot, weight, *small)


def norm_kernel(ways, table, gain, *refs):
    blocks, (normed, residual) = refs[: 4 * ways], refs[4 * ways :]
    group = table[4]
    for i in range(4):
        place = pl.multiple_of(table[i], 128)
        values = blocks[i][...]
        if ways == 2:
            first = jnp.broadcast_to(table[5], values.shape) == 1
            values = jnp.where(first, values, blocks[4 + i][...])
        values = values.astype(F32)
        mean = jnp.mean(values, axis=-1, keepdims=True)
        centred = values - mean
        var = jnp.mean(centred * centred, axis=-1, keepdims=True)
        normed[pl.ds(place, 128), :] = (centred * lax.rsqrt(var + 1e-05) * gain[...]).astype(BF)
        block = blocks[i]
        residual[pl.ds(place, 128), :WIDE] = block[
            :, pl.ds(pl.multiple_of(group * WIDE, 128), WIDE)
        ]
        slab = block[:, pl.ds(pl.multiple_of(1024 + group // 2 * 128, 128), 128)]
        odd = jnp.broadcast_to(lax.rem(group, 2), (128, HD)) == 1
        residual[pl.ds(place, 128), WIDE:] = jnp.where(odd, slab[:, HD:], slab[:, :HD])


def norm_layer(table, gain, blocks):
    return pl.pallas_call(
        functools.partial(norm_kernel, len(blocks) // 4),
        out_shape=(
            jax.ShapeDtypeStruct((512, 1280), BF),
            jax.ShapeDtypeStruct((512, GROUP), BF),
        ),
        in_specs=[SMEM] + [VMEM] * (1 + len(blocks)),
        out_specs=(VMEM, VMEM),
        compiler_params=pltpu.CompilerParams(vmem_limit_bytes=16 * 1024 * 1024),
    )(table, gain, *blocks)


def prepare_kernel(table, own, *refs):
    parts, (ids, tokens, asked) = refs[:-3], refs[-3:]
    straight, first, core = table[12], table[13], table[7]
    count = asked.shape[0]
    ids[...] = jnp.zeros_like(ids)
    tokens[...] = jnp.zeros_like(tokens)
    flip = jnp.broadcast_to(core, (2, HD)) == 1
    near = jnp.broadcast_to(straight, (32, HD)) == 1
    for i in range(count // 2):
        if i == 0:
            lanes = own[:32, 960:].astype(F32)
        else:
            part, rows = i // 2, slice(0, 32)
            if i > 1 and i % 2:
                rows = slice(own.shape[0], own.shape[0] + 32)
            here, there = parts[2 * part][rows, 960:], parts[2 * part + 1][rows, 960:]
            lanes = jnp.where(near, here.astype(F32), there.astype(F32))
        for h in range(6):
            found = jnp.where(flip, lanes[4 * h + 2 : 4 * h + 4], lanes[4 * h : 4 * h + 2])
            if h < 5:
                at = count * h + 2 * i
                tokens[at : at + 2, HD * h : HD * h + HD] = found * 0.125
            else:
                asked[2 * i : 2 * i + 2, :] = found
        for c in range(2):
            marks = lanes[24 + 4 * c : 26 + 4 * c] * 128.0 + lanes[26 + 4 * c : 28 + 4 * c]
            block = table[14 + 2 * i] // 2 * 2 + c - first

            @pl.when((block >= 0) & (block < 12))
            def _():
                ids[0:1, pl.ds(pl.multiple_of(block * 128, 128), 128)] = jnp.concatenate(
                    [marks[0:1], marks[1:2]], axis=1
                )


def prepare(table, own, parts, count):
    return pl.pallas_call(
        prepare_kernel,
        out_shape=(
            jax.ShapeDtypeStruct((8, 1536), F32),
            jax.ShapeDtypeStruct((5 * count, GROUP), F32),
            jax.ShapeDtypeStruct((count, HD), F32),
        ),
        in_specs=[SMEM] + [VMEM] * (1 + len(parts)),
        out_specs=(VMEM,) * 3,
        compiler_params=pltpu.CompilerParams(vmem_limit_bytes=8 * 1024 * 1024),
    )(table, own, *parts)


def encoder_kernel(n_parts, depth, places, *refs):
    layers = [refs[2 * i : 2 * i + 2] for i in range(3)]
    ids = refs[6]
    parts = refs[7 : 7 + n_parts]
    memory, near, away, weight, residual, queries, keys, values = refs[7 + n_parts :]
    x, straight = places[11], places[12]

    def place_part(source, rows):
        weight[pl.ds(pl.multiple_of(source * depth, 16), depth), :] = rows

    for i in range(min(2, n_parts)):
        place_part(places[14 + i], parts[i][...])
    for turn in range((n_parts - 2) // 4):
        came, traded, came_other, traded_other = parts[2 + 4 * turn : 6 + 4 * turn]
        pieces = came.shape[0] // depth

        def place_turn(mine, other):
            for s in range(pieces):
                rows = slice(s * depth, s * depth + depth)
                at = 14 + 4 * turn + 2 * (s + 2 - pieces)
                place_part(places[at], mine[rows, :])
                place_part(places[at + 1], other[rows, :])

        @pl.when(straight == 1)
        def _():
            place_turn(came, traded_other)

        @pl.when(straight == 0)
        def _():
            place_turn(traded, came_other)

    for slab in range(3):
        values[:, 256 * slab + 128 : 256 * slab + 256] = jnp.ones((1536, 128), BF)
    for i, (normed, kept) in enumerate(layers):
        place = pl.multiple_of(places[8 + i], 512)
        found = jnp.dot(normed[...], weight[:, 256:896], preferred_element_type=F32).astype(BF)
        keys[pl.ds(place, 512), :256] = found[:, :256]
        keys[pl.ds(place, 512), 256:] = found[:, 512:]
        for slab in range(3):
            values[pl.ds(place, 512), 256 * slab : 256 * slab + 128] = found[
                :, 256 + 128 * slab : 384 + 128 * slab
            ]
        if i < 2:

            @pl.when(place == 512)
            def _():
                residual[...] = kept[...]
                queries[:, :WIDE] = jnp.dot(
                    normed[...], weight[:, :WIDE], preferred_element_type=F32
                ).astype(BF)
                tail = jnp.dot(normed[...], weight[:, 896:], preferred_element_type=F32).astype(BF)
                lane = lax.broadcasted_iota(jnp.int32, tail.shape, 1)
                queries[:, WIDE:] = jnp.where(lane < HD, tail, jnp.zeros_like(tail))

    side = lax.broadcasted_iota(jnp.int32, (8, 128), 0) == lax.broadcasted_iota(
        jnp.int32, (8, 128), 1
    ) // HD
    sides = jnp.where(side, 1.0, 0.0).astype(BF)
    only = jnp.where(side & (lax.broadcasted_iota(jnp.int32, (8, 128), 0) == 0), 1.0, 0.0).astype(BF)
    most = []
    for held in (queries, keys):
        top = jnp.zeros((8, 1), F32)
        for slab in range(3):
            part = held[:, 128 * slab : 128 * slab + 128]
            norms = lax.dot_general(
                sides if slab < 2 else only,
                part * part,
                (((1,), (1,)), ((), ())),
                preferred_element_type=F32,
            )
            top = jnp.maximum(top, jnp.max(norms, axis=-1, keepdims=True))
        most.append(jnp.max(top))
    small = most[0] * most[1] < 220000.0

    def attend(step, shifted):
        row = step * 128 if isinstance(step, int) else pl.multiple_of(step * 128, 128)
        mine = jnp.broadcast_to(ids[0:1, pl.ds(row + 512, 128)], (128, 128)).T[:, 0:1]
        bias = jnp.where(mine == ids[0:1, pl.ds(row, 1152)], 0.0, LOW)
        lane = lax.broadcasted_iota(jnp.int32, (128, 128), 1)
        for slab in range(3):
            span = slice(128 * slab, 128 * slab + 128)
            query = queries[pl.ds(row, 128), span] * BF(0.125)
            mask = bias
            if slab < 2:
                none = jnp.zeros_like(query)
                query = jnp.concatenate(
                    [jnp.where(lane < HD, query, none), jnp.where(lane < HD, none, query)], axis=0
                )
                mask = jnp.concatenate([bias, bias], axis=0)
            scores = lax.dot_general(
                query,
                keys[pl.ds(row, 1152), span],
                (((1,), (1,)), ((), ())),
                preferred_element_type=F32,
            )
            scores = scores + mask
            if shifted:
                scores = scores - jnp.max(scores, axis=-1, keepdims=True)
            raised = jnp.exp(scores).astype(BF)
            out = jnp.dot(
                raised,
                values[pl.ds(row, 1152), 256 * slab : 256 * slab + 256],
                preferred_element_type=F32,
            )
            out = out[:, :128] / out[:, 128:]
            if slab < 2:
                context = jnp.where(lane < HD, out[:128], out[128:])
                stem = residual[pl.ds(row, 128), span].astype(F32)
                memory[pl.ds(row, 128), span] = (stem + context).astype(BF)
            else:
                stem = residual[pl.ds(row, 128), WIDE:].astype(F32)
                memory[pl.ds(row, 128), WIDE:] = (stem + out[:, HD:]).astype(BF)

    @pl.when(small)
    def _():
        for step in range(4):
            attend(step, False)

    @pl.when(jnp.logical_not(small))
    def _():
        lax.fori_loop(0, 4, lambda step, carry: (attend(step, True), carry)[1], 0)

    near[...] = memory[pl.ds(pl.multiple_of(256 * x, 256), 256), :]
    away[...] = memory[pl.ds(pl.multiple_of(256 * (1 - x), 256), 256), :]


def encoder(places, layers, ids, parts, depth):
    operands = [a for layer in layers for a in layer] + [ids] + parts
    return pl.pallas_call(
        functools.partial(encoder_kernel, len(parts), depth),
        out_shape=(
            jax.ShapeDtypeStruct((512, GROUP), BF),
            jax.ShapeDtypeStruct((256, GROUP), BF),
            jax.ShapeDtypeStruct((256, GROUP), BF),
        ),
        in_specs=[SMEM] + [VMEM] * len(operands),
        out_specs=(VMEM, VMEM, VMEM),
        scratch_shapes=[
            pltpu.VMEM((1280, 1024), BF),
            pltpu.VMEM((512, GROUP), BF),
            pltpu.VMEM((512, 384), BF),
            pltpu.VMEM((1536, 384), BF),
            pltpu.VMEM((1536, 768), BF),
        ],
        compiler_params=pltpu.CompilerParams(vmem_limit_bytes=24 * 1024 * 1024),
    )(places, *operands)


def cross_kernel(base, table, tokens, asked, memory, beside, *refs):
    outs, out = refs[:-1], refs[-1]
    count = asked.shape[0]
    me = table[base + 2]
    spot = lax.broadcasted_iota(jnp.int32, (count, HD), 1)
    order = lax.broadcasted_iota(jnp.int32, (count, 1), 0)
    owner = (order // 2 * 2) ^ me
    bias = []
    for half in range(2):
        for b in range(4):
            block = table[base + half] + b
            ask = jnp.sum(jnp.where(spot == block, asked[...], 0.0), axis=-1, keepdims=True)
            allowed = (ask > 0.5) | (owner == block)
            bias.append(jnp.broadcast_to(jnp.where(allowed, 0.0, LOW), (count, 128)))
    bias = jnp.concatenate(bias, axis=1)
    bias = jnp.concatenate([bias] * 5, axis=0)
    query = tokens[...].astype(BF)
    cross = jnp.concatenate(
        [
            lax.dot_general(
                query, held[...], (((1,), (1,)), ((), ())), preferred_element_type=F32
            )
            for held in (memory, beside)
        ],
        axis=1,
    )
    cross = jnp.where(bias < 0.0, LOW, cross)
    top = jnp.max(cross, axis=-1, keepdims=True)
    raised = jnp.where(bias < 0.0, 0.0, jnp.exp(cross - top))
    den = jnp.sum(raised, axis=-1, keepdims=True)
    raised = raised.astype(BF)
    out[...] = jnp.dot(raised[:, :512], memory[...], preferred_element_type=F32) + jnp.dot(
        raised[:, 512:], beside[...], preferred_element_type=F32
    )
    lane = lax.broadcasted_iota(jnp.int32, (count, HD), 1)
    for h in range(5):
        rows = slice(count * h, count * h + count)
        stats = jnp.where(lane == 0, top[rows], den[rows])
        both = jnp.concatenate([out[rows, HD * h : HD * h + HD], stats], axis=1)
        for i, owned in enumerate(outs):
            owned[8 * h : 8 * h + 8, :] = both[8 * i : 8 * i + 8]


def cross_partial(base, table, tokens, asked, memory, beside):
    count = asked.shape[0]
    return pl.pallas_call(
        functools.partial(cross_kernel, base),
        out_shape=(jax.ShapeDtypeStruct((40, 128), F32),) * (count // 8),
        in_specs=[SMEM] + [VMEM] * 4,
        out_specs=(VMEM,) * (count // 8),
        scratch_shapes=[pltpu.VMEM((5 * count, GROUP), F32)],
        compiler_params=pltpu.CompilerParams(vmem_limit_bytes=12 * 1024 * 1024),
    )(table, tokens, asked, memory, beside)


def merge_kernel(*refs):
    parts, outs, out = refs[:-5], refs[-5:-1], refs[-1]
    tops = [part[:, HD : HD + 1] for part in parts]
    best = functools.reduce(jnp.maximum, tops)
    total = jnp.zeros((40, 128), F32)
    for top, part in zip(tops, parts):
        total = total + jnp.exp(top - best) * part[...]
    final = total[:, :HD] / total[:, HD + 1 : HD + 2]
    heads = [final[8 * h : 8 * h + 8] for h in range(5)] + [jnp.zeros((8, HD), F32)]
    for slab in range(3):
        out[:, 128 * slab : 128 * slab + 128] = jnp.concatenate(heads[2 * slab : 2 * slab + 2], axis=1)
    for i in range(4):
        outs[i][...] = out[2 * i : 2 * i + 2, :].astype(BF)


def merge(parts):
    return pl.pallas_call(
        merge_kernel,
        out_shape=(jax.ShapeDtypeStruct((2, 384), BF),) * 4,
        in_specs=[VMEM] * len(parts),
        out_specs=(VMEM,) * 4,
        scratch_shapes=[pltpu.VMEM((8, 384), F32)],
        compiler_params=pltpu.CompilerParams(vmem_limit_bytes=4 * 1024 * 1024),
    )(*parts)


def gather_groups(pieces, group):
    wide, tail = [], []
    for g in range(4):
        turn = group ^ g
        piece = jnp.where(
            turn < 2,
            jnp.where(turn == 0, pieces[0], pieces[1]),
            jnp.where(turn == 2, pieces[2], pieces[3]),
        )
        wide.append(piece[:, :WIDE])
        tail.append(piece[:, WIDE:GROUP])
    return jnp.concatenate(wide + tail, axis=1)


def on_device(stem, norm_gain, qkv_weight, segment_ids, dec_queries, stretch_mask):
    n = lax.axis_size("tm")
    layers = n // 4
    me = lax.axis_index("tm")
    z, x, c = me // 4, (me // 2) % 2, me % 2
    p, k = z % 2, z // 2
    quarter = 2 * k + c
    group = 2 * p + x
    depth = qkv_weight.shape[0]

    layers_route = [1 if i % 2 else -1 for i in range(layers)]
    near_route = [
        (4 * i + j, 4 * (i + s) + j)
        for i, s in enumerate(layers_route)
        for j in range(4)
        if 0 <= i + s < layers
    ]
    pair = swap(stem, n, 4)
    near = send(stem, near_route)
    stem_x = swap(stem, n, 2)
    utts = lax.axis_size("utt")
    straight = (c == lax.axis_index("utt") % 2).astype(jnp.int32)
    gain = norm_gain.reshape(1, -1)
    direct = depth % 16 == 0 and layers == 4 and utts % 2 == 0
    table = [128 * (2 * x + c), 128 * (2 * x + 1 - c), 128 * (2 - 2 * x + c), 128 * (3 - 2 * x - c)]
    table += [group, p != k, x, c]
    table += [512 * (p - c + 1), 512 * (2 - p - c), 1024 * c, x, straight, 4 * quarter - 4]
    sources = [me ^ m for m in range(n)] if direct else [jnp.int32(0)]
    table = scalars(table + sources + [4 * quarter, 4 * (quarter ^ 1), me])
    base = 14 + len(sources)
    if direct:
        carriers = [(u, d) for u in range(utts) for d in range(n) if d % 2 == u % 2]

        def carry(block, turn_u, turn_d):
            route = [(u * n + d, (u ^ turn_u) * n + (d ^ turn_d)) for u, d in carriers]
            return lax.ppermute(block, ("utt", "tm"), route)

        inside = [d for d in range(n) if d // 4 in (1, 2)]
        far = send(after(stem, pair, near), [(d, d ^ 8) for d in inside])
        small = [dec_queries, stretch_mask, segment_ids.reshape(1, -1)]
        both = [part for piece in small for part in (piece, swap(piece, n, 1))]
        mine, theirs = pack(table, qkv_weight, *both)
        across = carry(after(theirs, stem_x), 0, 2)
        stem_c = swap(stem, n, 1)
        own_layer = norm_layer(table, gain, [stem, stem_c, stem_x, swap(stem_x, n, 1)])
        ready = [
            jnp.concatenate(
                [
                    lax.dynamic_slice_in_dim(mine, p ^ a, 1, 0),
                    lax.dynamic_slice_in_dim(across, p ^ a, 1, 0),
                ]
            ).reshape(2 * depth, 1024)
            for a in range(2)
        ]
        own_part = lax.dynamic_index_in_dim(mine, p, 0, keepdims=False)
        pair_x = swap(after(pair, across), n, 2)
        here = {0: lax.dynamic_index_in_dim(across, p, 0, keepdims=False)}
        here[3] = carry(after(ready[1], far), 0, 12)
        here[2] = carry(after(ready[0], here[3], own_layer[0]), 0, 8)
        halo = jnp.where((z == 1) | (z == 2), near, far)
        halo_x = swap(after(halo, pair_x), n, 2)
        pair_layer = norm_layer(table, gain, [pair, swap(pair, n, 1), pair_x, swap(pair_x, n, 1)])
        here[1] = carry(after(ready[1], here[2], pair_layer[0]), 0, 4)
        aside = [(d, d ^ 1) for d in range(n) if d % 2 == d // 8]
        halo_layer = norm_layer(table, gain, [halo, send(halo, aside), halo_x, send(halo_x, aside)])
        traded, came_other, traded_other = {}, {}, {}
        hold = []
        for turn in (0, 3, 2, 1):
            traded[turn] = carry(after(here[turn], *hold), 1, 0)
            hold = [traded[turn]]
            came_other[turn] = carry(here[turn], 0, 1)
            route = [(u * n + (d ^ 1), u * n + d) for u, d in carriers]
            traded_other[turn] = lax.ppermute(traded[turn], ("utt", "tm"), route)
        weights = [own_part, swap(own_part, n, 1)]
        for turn in range(4):
            weights += [here[turn], traded[turn], came_other[turn], traded_other[turn]]
        came = [part for turn in range(4) for part in (here[turn], came_other[turn])]
        ids, tokens, asked = prepare(table, own_part, came, n)
        layered = [own_layer, pair_layer, halo_layer]
    else:
        far = swap(near, n, 4)
        left = jnp.where(p == 0, near, far)
        right = jnp.where(p == 0, far, near)
        left_x, right_x = swap(left, n, 2), swap(right, n, 2)
        halo = [
            jnp.where(c == 0, left, right),
            swap(jnp.where(c == 0, right, left), n, 1),
            jnp.where(c == 0, left_x, right_x),
            swap(jnp.where(c == 0, right_x, left_x), n, 1),
        ]
        pair_x = swap(pair, n, 2)
        own = [stem, swap(stem, n, 1), stem_x, swap(stem_x, n, 1)]
        other = [pair, swap(pair, n, 1), pair_x, swap(pair_x, n, 1)]
        layered = [norm_layer(table, gain, blocks) for blocks in (own, other, halo)]
        whole = lax.all_gather(qkv_weight, "tm", axis=0, tiled=True)
        grouped = jnp.stack([weight_group(whole, g) for g in range(4)])
        weights = [lax.dynamic_index_in_dim(grouped, group, 0, keepdims=False)]
        weights = [jnp.pad(weights[0], ((0, 0), (0, HD)))]
        depth = whole.shape[0]
        packed = jnp.stack([token_group(dec_queries, stretch_mask, g) for g in range(4)])
        every = lax.all_gather(packed, "tm", axis=0)
        every = lax.dynamic_index_in_dim(every, group, 1, keepdims=False)
        every = jnp.take(every, jnp.arange(0, n, 2, dtype=jnp.int32) ^ me, axis=0)
        every = every.reshape(n // 2, 6, 2, HD).transpose(1, 0, 2, 3).reshape(6, n, HD).astype(F32)
        asked = every[5]
        tokens = jnp.concatenate(
            [jnp.pad(every[h] * 0.125, ((0, 0), (HD * h, GROUP - HD - HD * h))) for h in range(5)]
        )
        marks = lax.all_gather(segment_ids, "tm", axis=0, tiled=True).astype(F32)
        marks = jnp.pad(marks, (512, 512))
        marks = lax.dynamic_slice_in_dim(marks, 512 * quarter, 1536, 0)
        ids = jnp.broadcast_to(marks[None], (8, 1536))
    held, stay, leave = encoder(table, layered, ids, weights, depth)

    partial = cross_partial(base, table, tokens, asked, held, swap(held, n, 1))
    owned = [partial[0]] + [swap(partial[i], n, 8 * i) for i in range(1, n // 8)]
    stay, leave = after(stay, partial[0]), after(leave, partial[0])

    pieces = []
    for turn, rows in enumerate((stay, leave)):
        route = [
            (
                8 * (d // 8) + 4 * (d // 4 % 2) + (d & 2) + (d & 1),
                8 * (d // 8) + 4 * (d & 1) + ((d & 2) ^ (2 * turn)) + (d // 4 % 2),
            )
            for d in range(n)
        ]
        got = send(rows, route)
        keep = lax.dynamic_slice_in_dim(got, 128 * c, 128, 0)
        give = swap(lax.dynamic_slice_in_dim(got, 128 * (1 - c), 128, 0), n, 1)
        pieces.append((keep, give))
    memory = gather_groups([pieces[0][0], pieces[1][0], pieces[0][1], pieces[1][1]], 2 * c + x)

    final = merge(owned)
    final = [final[0]] + [swap(final[i], n, 2 * i) for i in (1, 2, 3)]
    cross_out = gather_groups(final, group)
    return (memory, cross_out)


def solution(mesh):
    placed = (
        P(("utt", "tm"), None),
        P(),
        P("tm", None),
        P(("utt", "tm")),
        P(("utt", "tm"), None),
        P(("utt", "tm"), None),
    )
    return jax.shard_map(
        on_device,
        mesh=mesh,
        in_specs=placed,
        out_specs=(P(("utt", "tm"), None), P(("utt", "tm"), None)),
        check_vma=False,
    )
```

```python
import functools

import jax
import jax.numpy as jnp
from jax import lax
from jax.experimental import pallas as pl
from jax.experimental.pallas import tpu as pltpu
from jax.sharding import PartitionSpec as P

HD = 64
WIDE = 256
GROUP = 320
BF = jnp.bfloat16
F32 = jnp.float32
LOW = -1e30
VMEM = pl.BlockSpec(memory_space=pltpu.VMEM)
SMEM = pl.BlockSpec(memory_space=pltpu.SMEM)


def send(block, route):
    return lax.ppermute(block, "tm", route)


def swap(block, n, mask):
    return send(block, [(d, d ^ mask) for d in range(n)])


def after(value, *awaited):
    return lax.optimization_barrier((value, *awaited))[0]


def scalars(values):
    return jnp.stack([jnp.asarray(v, jnp.int32) for v in values])


def group_of(array, g):
    return array[:, WIDE * g : WIDE * g + WIDE], array[:, 1024 + HD * g : 1024 + HD * g + HD]


def weight_group(weight, g):
    width = weight.shape[1] // 3
    parts = [group_of(weight[:, i * width : (i + 1) * width], g) for i in range(3)]
    (q0, q1), (k0, k1), (v0, v1) = parts
    return jnp.concatenate([q0, k0, v0, k1, v1, q1], axis=1)


def token_group(queries, mask, g):
    wide, tail = group_of(queries, g)
    heads = [wide[:, HD * i : HD * i + HD] for i in range(4)] + [tail]
    asked = jnp.pad(mask.astype(BF), ((0, 0), (0, HD - mask.shape[1])))
    return jnp.concatenate(heads + [asked], axis=0)


def pack_kernel(table, weight, queries, mask, segments, mine, theirs):
    rows, width = weight.shape[0], weight.shape[1] // 3
    blocks = mask.shape[1]
    ids = segments[...]
    digits = [lax.shift_right_logical(ids, 7).astype(F32), (ids & 127).astype(F32)]
    asked = mask[...].astype(F32)
    if blocks < HD:
        asked = jnp.concatenate([asked, jnp.zeros((2, HD - blocks), F32)], axis=1)
    rest = [asked] + [d[:, HD * i : HD * i + HD] for d in digits for i in range(2)]
    rest.append(jnp.zeros((rows - 16, HD), F32))
    for turn, outs in enumerate((mine, theirs)):
        column = table[6] if turn == 0 else 1 - table[6]
        for p in range(2):
            out = outs.at[p]
            wide = pl.multiple_of(WIDE * (2 * p + column), 128)
            tails = []
            for i in range(4):
                source = weight if i < 3 else queries
                at = width * i if i < 3 else 0
                slab = source[:, at + 1024 + 128 * p : at + 1152 + 128 * p].astype(F32)
                odd = jnp.broadcast_to(column, (slab.shape[0], HD)) == 1
                tails.append(jnp.where(odd, slab[:, HD:], slab[:, :HD]))
                if i < 3:
                    out[:, WIDE * i : WIDE * i + WIDE] = weight[
                        :, pl.ds(pl.multiple_of(at + wide, 128), WIDE)
                    ]
            out[:, 3 * WIDE : 896] = jnp.concatenate(tails[1:3], axis=1).astype(BF)
            asking = queries[:, pl.ds(wide, WIDE)].astype(F32)
            heads = [asking[:, HD * h : HD * h + HD] for h in range(4)] + [tails[3]]
            lanes = jnp.concatenate(heads + rest, axis=0)
            out[:, 896:] = jnp.concatenate([tails[0], lanes], axis=1).astype(BF)


def pack(table, weight, queries, mask, segments):
    shape = jax.ShapeDtypeStruct((2, weight.shape[0], 1024), BF)
    return pl.pallas_call(
        pack_kernel,
        out_shape=(shape, shape),
        in_specs=[SMEM] + [VMEM] * 4,
        out_specs=(VMEM,) * 2,
        compiler_params=pltpu.CompilerParams(vmem_limit_bytes=8 * 1024 * 1024),
    )(table, weight, queries, mask, segments)


def load_kernel(table, *refs):
    held, outs = refs[:4], refs[4:]
    x, c, p = table[6], table[7], table[5]
    own = jnp.broadcast_to(table[12], outs[0].shape) == 1
    flip_c = jnp.broadcast_to(c, (16, 128)) == 1
    flip_x = jnp.broadcast_to(x, (16, 128)) == 1
    for a in range(2):
        mine, mine_c, across, across_c = [h[pl.ds(p ^ a, 1)][0] for h in held]
        out = outs[a]
        out[...] = jnp.where(own, mine, across)
        lanes = [part[:16, 896:] for part in (mine, mine_c, across, across_c)]
        rows = []
        for first, second in (lanes[:2], lanes[2:]):
            rows.append((jnp.where(flip_c, second, first), jnp.where(flip_c, first, second)))
        low = [jnp.where(flip_x, there, here) for here, there in zip(*rows)]
        high = [jnp.where(flip_x, here, there) for here, there in zip(*rows)]
        lane = lax.broadcasted_iota(jnp.int32, (16, 128), 1)
        for j, found in enumerate(low + high):
            out[16 * j : 16 * j + 16, 896:] = jnp.where(
                lane < HD, out[16 * j : 16 * j + 16, 896:], found
            )


def load(table, *held):
    rows = held[0].shape[1]
    return pl.pallas_call(
        load_kernel,
        out_shape=(jax.ShapeDtypeStruct((rows, 1024), BF),) * 2,
        in_specs=[SMEM] + [VMEM] * 4,
        out_specs=(VMEM,) * 2,
        compiler_params=pltpu.CompilerParams(vmem_limit_bytes=8 * 1024 * 1024),
    )(table, *held)


def norm_kernel(ways, table, gain, *refs):
    blocks, (normed, residual) = refs[: 4 * ways], refs[4 * ways :]
    group = table[4]
    for i in range(4):
        place = pl.multiple_of(table[i], 128)
        values = blocks[i][...]
        if ways == 2:
            first = jnp.broadcast_to(table[5], values.shape) == 1
            values = jnp.where(first, values, blocks[4 + i][...])
        values = values.astype(F32)
        mean = jnp.mean(values, axis=-1, keepdims=True)
        centred = values - mean
        var = jnp.mean(centred * centred, axis=-1, keepdims=True)
        normed[pl.ds(place, 128), :] = (centred * lax.rsqrt(var + 1e-05) * gain[...]).astype(BF)
        block = blocks[i]
        residual[pl.ds(place, 128), :WIDE] = block[
            :, pl.ds(pl.multiple_of(group * WIDE, 128), WIDE)
        ]
        slab = block[:, pl.ds(pl.multiple_of(1024 + group // 2 * 128, 128), 128)]
        odd = jnp.broadcast_to(lax.rem(group, 2), (128, HD)) == 1
        residual[pl.ds(place, 128), WIDE:] = jnp.where(odd, slab[:, HD:], slab[:, :HD])


def norm_layer(table, gain, blocks):
    return pl.pallas_call(
        functools.partial(norm_kernel, len(blocks) // 4),
        out_shape=(
            jax.ShapeDtypeStruct((512, 1280), BF),
            jax.ShapeDtypeStruct((512, GROUP), BF),
        ),
        in_specs=[SMEM] + [VMEM] * (1 + len(blocks)),
        out_specs=(VMEM, VMEM),
        compiler_params=pltpu.CompilerParams(vmem_limit_bytes=16 * 1024 * 1024),
    )(table, gain, *blocks)


def prepare_kernel(table, *refs):
    parts, (ids, tokens, asked) = refs[:-3], refs[-3:]
    first, x, core, z = table[13], table[6], table[7], table[14]
    count = asked.shape[0]
    ids[...] = jnp.zeros_like(ids)
    tokens[...] = jnp.zeros_like(tokens)
    flip_c = jnp.broadcast_to(core, (2, HD)) == 1
    flip_x = jnp.broadcast_to(x, (2, HD)) == 1
    for turn, part in enumerate(parts):
        lanes = part[:64, 896:].astype(F32)[:, HD:]
        for h in range(6):
            rows = [lanes[16 * j + 2 * h : 16 * j + 2 * h + 2] for j in range(4)]
            low = jnp.where(flip_c, rows[1], rows[0])
            high = jnp.where(flip_c, rows[3], rows[2])
            for dx in range(2):
                found = jnp.where(flip_x, low, high) if dx else jnp.where(flip_x, high, low)
                at = 4 * turn + 2 * dx
                if h < 5:
                    tokens[count * h + at : count * h + at + 2, HD * h : HD * h + HD] = found * 0.125
                else:
                    asked[at : at + 2, :] = found
        for j in range(4):
            marks = lanes[16 * j + 12 : 16 * j + 14] * 128.0 + lanes[16 * j + 14 : 16 * j + 16]
            block = 4 * (z ^ turn) + j - first

            @pl.when((block >= 0) & (block < 12))
            def _():
                ids[0:1, pl.ds(pl.multiple_of(block * 128, 128), 128)] = jnp.concatenate(
                    [marks[0:1], marks[1:2]], axis=1
                )


def prepare(table, parts, count):
    return pl.pallas_call(
        prepare_kernel,
        out_shape=(
            jax.ShapeDtypeStruct((8, 1536), F32),
            jax.ShapeDtypeStruct((5 * count, GROUP), F32),
            jax.ShapeDtypeStruct((count, HD), F32),
        ),
        in_specs=[SMEM] + [VMEM] * len(parts),
        out_specs=(VMEM,) * 3,
        compiler_params=pltpu.CompilerParams(vmem_limit_bytes=8 * 1024 * 1024),
    )(table, *parts)


def encoder_kernel(n_parts, depth, places, *refs):
    layers = [refs[2 * i : 2 * i + 2] for i in range(3)]
    ids = refs[6]
    parts = refs[7 : 7 + n_parts]
    memory, near, away, weight, residual, queries, keys, values = refs[7 + n_parts :]
    x = places[6]
    for i, part in enumerate(parts):
        row = pl.multiple_of(places[15 + i] * depth, 16)
        weight[pl.ds(row, depth), :] = part[...] if len(part.shape) == 2 else part[pl.ds(places[5], 1)][0]

    for slab in range(3):
        values[:, 256 * slab + 128 : 256 * slab + 256] = jnp.ones((1536, 128), BF)
    for i, (normed, kept) in enumerate(layers):
        place = pl.multiple_of(places[8 + i], 512)
        found = jnp.dot(normed[...], weight[:, 256:896], preferred_element_type=F32).astype(BF)
        keys[pl.ds(place, 512), :256] = found[:, :256]
        keys[pl.ds(place, 512), 256:] = found[:, 512:]
        for slab in range(3):
            values[pl.ds(place, 512), 256 * slab : 256 * slab + 128] = found[
                :, 256 + 128 * slab : 384 + 128 * slab
            ]
        if i < 2:

            @pl.when(place == 512)
            def _():
                residual[...] = kept[...]
                queries[:, :WIDE] = jnp.dot(
                    normed[...], weight[:, :WIDE], preferred_element_type=F32
                ).astype(BF)
                tail = jnp.dot(normed[...], weight[:, 896:], preferred_element_type=F32).astype(BF)
                lane = lax.broadcasted_iota(jnp.int32, tail.shape, 1)
                queries[:, WIDE:] = jnp.where(lane < HD, tail, jnp.zeros_like(tail))

    side = lax.broadcasted_iota(jnp.int32, (8, 128), 0) == lax.broadcasted_iota(
        jnp.int32, (8, 128), 1
    ) // HD
    sides = jnp.where(side, 1.0, 0.0).astype(BF)
    only = jnp.where(side & (lax.broadcasted_iota(jnp.int32, (8, 128), 0) == 0), 1.0, 0.0).astype(BF)
    most = []
    for held in (queries, keys):
        top = jnp.zeros((8, 1), F32)
        for slab in range(3):
            part = held[:, 128 * slab : 128 * slab + 128]
            norms = lax.dot_general(
                sides if slab < 2 else only,
                part * part,
                (((1,), (1,)), ((), ())),
                preferred_element_type=F32,
            )
            top = jnp.maximum(top, jnp.max(norms, axis=-1, keepdims=True))
        most.append(jnp.max(top))
    small = most[0] * most[1] < 220000.0

    def attend(step, shifted):
        row = step * 128 if isinstance(step, int) else pl.multiple_of(step * 128, 128)
        mine = jnp.broadcast_to(ids[0:1, pl.ds(row + 512, 128)], (128, 128)).T[:, 0:1]
        bias = jnp.where(mine == ids[0:1, pl.ds(row, 1152)], 0.0, LOW)
        lane = lax.broadcasted_iota(jnp.int32, (128, 128), 1)
        for slab in range(3):
            span = slice(128 * slab, 128 * slab + 128)
            query = queries[pl.ds(row, 128), span] * BF(0.125)
            mask = bias
            if slab < 2:
                none = jnp.zeros_like(query)
                query = jnp.concatenate(
                    [jnp.where(lane < HD, query, none), jnp.where(lane < HD, none, query)], axis=0
                )
                mask = jnp.concatenate([bias, bias], axis=0)
            scores = lax.dot_general(
                query,
                keys[pl.ds(row, 1152), span],
                (((1,), (1,)), ((), ())),
                preferred_element_type=F32,
            )
            scores = scores + mask
            if shifted:
                scores = scores - jnp.max(scores, axis=-1, keepdims=True)
            raised = jnp.exp(scores).astype(BF)
            out = jnp.dot(
                raised,
                values[pl.ds(row, 1152), 256 * slab : 256 * slab + 256],
                preferred_element_type=F32,
            )
            out = out[:, :128] / out[:, 128:]
            if slab < 2:
                context = jnp.where(lane < HD, out[:128], out[128:])
                stem = residual[pl.ds(row, 128), span].astype(F32)
                memory[pl.ds(row, 128), span] = (stem + context).astype(BF)
            else:
                stem = residual[pl.ds(row, 128), WIDE:].astype(F32)
                memory[pl.ds(row, 128), WIDE:] = (stem + out[:, HD:]).astype(BF)

    @pl.when(small)
    def _():
        for step in range(4):
            attend(step, False)

    @pl.when(jnp.logical_not(small))
    def _():
        lax.fori_loop(0, 4, lambda step, carry: (attend(step, True), carry)[1], 0)

    near[...] = memory[pl.ds(pl.multiple_of(256 * x, 256), 256), :]
    away[...] = memory[pl.ds(pl.multiple_of(256 * (1 - x), 256), 256), :]


def encoder(places, layers, ids, parts, depth):
    operands = [a for layer in layers for a in layer] + [ids] + parts
    return pl.pallas_call(
        functools.partial(encoder_kernel, len(parts), depth),
        out_shape=(
            jax.ShapeDtypeStruct((512, GROUP), BF),
            jax.ShapeDtypeStruct((256, GROUP), BF),
            jax.ShapeDtypeStruct((256, GROUP), BF),
        ),
        in_specs=[SMEM] + [VMEM] * len(operands),
        out_specs=(VMEM, VMEM, VMEM),
        scratch_shapes=[
            pltpu.VMEM((1280, 1024), BF),
            pltpu.VMEM((512, GROUP), BF),
            pltpu.VMEM((512, 384), BF),
            pltpu.VMEM((1536, 384), BF),
            pltpu.VMEM((1536, 768), BF),
        ],
        compiler_params=pltpu.CompilerParams(vmem_limit_bytes=24 * 1024 * 1024),
    )(places, *operands)


def cross_kernel(base, table, tokens, asked, memory, beside, *refs):
    outs, out = refs[:-1], refs[-1]
    count = asked.shape[0]
    me = table[base + 2]
    spot = lax.broadcasted_iota(jnp.int32, (count, HD), 1)
    order = lax.broadcasted_iota(jnp.int32, (count, 1), 0)
    owner = (order // 2 * 2) ^ me
    bias = []
    for half in range(2):
        for b in range(4):
            block = table[base + half] + b
            ask = jnp.sum(jnp.where(spot == block, asked[...], 0.0), axis=-1, keepdims=True)
            allowed = (ask > 0.5) | (owner == block)
            bias.append(jnp.broadcast_to(jnp.where(allowed, 0.0, LOW), (count, 128)))
    bias = jnp.concatenate(bias, axis=1)
    bias = jnp.concatenate([bias] * 5, axis=0)
    query = tokens[...].astype(BF)
    cross = jnp.concatenate(
        [
            lax.dot_general(
                query, held[...], (((1,), (1,)), ((), ())), preferred_element_type=F32
            )
            for held in (memory, beside)
        ],
        axis=1,
    )
    cross = jnp.where(bias < 0.0, LOW, cross)
    top = jnp.max(cross, axis=-1, keepdims=True)
    raised = jnp.where(bias < 0.0, 0.0, jnp.exp(cross - top))
    den = jnp.sum(raised, axis=-1, keepdims=True)
    raised = raised.astype(BF)
    out[...] = jnp.dot(raised[:, :512], memory[...], preferred_element_type=F32) + jnp.dot(
        raised[:, 512:], beside[...], preferred_element_type=F32
    )
    lane = lax.broadcasted_iota(jnp.int32, (count, HD), 1)
    for h in range(5):
        rows = slice(count * h, count * h + count)
        stats = jnp.where(lane == 0, top[rows], den[rows])
        both = jnp.concatenate([out[rows, HD * h : HD * h + HD], stats], axis=1)
        for i, owned in enumerate(outs):
            owned[8 * h : 8 * h + 8, :] = both[8 * i : 8 * i + 8]


def cross_partial(base, table, tokens, asked, memory, beside):
    count = asked.shape[0]
    return pl.pallas_call(
        functools.partial(cross_kernel, base),
        out_shape=(jax.ShapeDtypeStruct((40, 128), F32),) * (count // 8),
        in_specs=[SMEM] + [VMEM] * 4,
        out_specs=(VMEM,) * (count // 8),
        scratch_shapes=[pltpu.VMEM((5 * count, GROUP), F32)],
        compiler_params=pltpu.CompilerParams(vmem_limit_bytes=12 * 1024 * 1024),
    )(table, tokens, asked, memory, beside)


def merge_kernel(*refs):
    parts, outs, out = refs[:-5], refs[-5:-1], refs[-1]
    tops = [part[:, HD : HD + 1] for part in parts]
    best = functools.reduce(jnp.maximum, tops)
    total = jnp.zeros((40, 128), F32)
    for top, part in zip(tops, parts):
        total = total + jnp.exp(top - best) * part[...]
    final = total[:, :HD] / total[:, HD + 1 : HD + 2]
    heads = [final[8 * h : 8 * h + 8] for h in range(5)] + [jnp.zeros((8, HD), F32)]
    for slab in range(3):
        out[:, 128 * slab : 128 * slab + 128] = jnp.concatenate(heads[2 * slab : 2 * slab + 2], axis=1)
    for i in range(4):
        outs[i][...] = out[2 * i : 2 * i + 2, :].astype(BF)


def merge(parts):
    return pl.pallas_call(
        merge_kernel,
        out_shape=(jax.ShapeDtypeStruct((2, 384), BF),) * 4,
        in_specs=[VMEM] * len(parts),
        out_specs=(VMEM,) * 4,
        scratch_shapes=[pltpu.VMEM((8, 384), F32)],
        compiler_params=pltpu.CompilerParams(vmem_limit_bytes=4 * 1024 * 1024),
    )(*parts)


def gather_groups(pieces, group):
    wide, tail = [], []
    for g in range(4):
        turn = group ^ g
        piece = jnp.where(
            turn < 2,
            jnp.where(turn == 0, pieces[0], pieces[1]),
            jnp.where(turn == 2, pieces[2], pieces[3]),
        )
        wide.append(piece[:, :WIDE])
        tail.append(piece[:, WIDE:GROUP])
    return jnp.concatenate(wide + tail, axis=1)


def on_device(stem, norm_gain, qkv_weight, segment_ids, dec_queries, stretch_mask):
    n = lax.axis_size("tm")
    layers = n // 4
    me = lax.axis_index("tm")
    z, x, c = me // 4, (me // 2) % 2, me % 2
    p, k = z % 2, z // 2
    quarter = 2 * k + c
    group = 2 * p + x
    depth = qkv_weight.shape[0]

    utts = lax.axis_size("utt")
    moved = lax.axis_index("utt") % 2
    direct = depth % 16 == 0 and layers == 4 and utts % 2 == 0
    gain = norm_gain.reshape(1, -1)
    table = [128 * (2 * x + c), 128 * (2 * x + 1 - c), 128 * (2 - 2 * x + c), 128 * (3 - 2 * x - c)]
    table += [group, p, x, c]
    table += [512 * (p - c + 1), 512 * (2 - p - c), 1024 * c, 0, x == moved, 4 * quarter - 4, z]
    sources = [me, me ^ 1, me ^ 2, me ^ 3] if direct else [jnp.int32(0)]
    for turn in (1, 2, 3) if direct else ():
        column = 4 * (z ^ turn) + c
        for side in (moved, 1 - moved):
            sources += [column + 2 * side, (column ^ 1) + 2 * side]
    table = scalars(table + sources + [4 * quarter, 4 * (quarter ^ 1), me])
    base = 15 + len(sources)

    steps = [1 if i % 2 else -1 for i in range(layers)]
    near_route = [
        (4 * i + j, 4 * (i + s) + j)
        for i, s in enumerate(steps)
        for j in range(4)
        if 0 <= i + s < layers
    ]
    near = send(stem, near_route)
    pair = swap(stem, n, 4)
    if direct:
        def trade(block):
            return lax.ppermute(block, "utt", [(u, u ^ 1) for u in range(utts)])

        mine, theirs = pack(
            table, qkv_weight, dec_queries, stretch_mask, segment_ids.reshape(1, -1)
        )
        across = swap(theirs, n, 2)
        mine_c, across_c = swap(mine, n, 1), swap(across, n, 1)
        stem_x = swap(after(stem, across), n, 2)
        relayed = swap(after(near, pair), n, 4)
        ready = load(table, mine, mine_c, across, across_c)
        here = {turn: swap(ready[turn % 2], n, 4 * turn) for turn in (3, 2, 1)}
        own_layer = norm_layer(
            table, gain, [stem, swap(stem, n, 1), stem_x, swap(stem_x, n, 1)]
        )
        pair_x = swap(after(pair, stem_x), n, 2)
        halo = jnp.where((z == 1) | (z == 2), near, relayed)
        halo_x = swap(after(halo, pair_x), n, 2)
        pair_layer = norm_layer(table, gain, [pair, swap(pair, n, 1), pair_x, swap(pair_x, n, 1)])
        halo_layer = norm_layer(table, gain, [halo, swap(halo, n, 1), halo_x, swap(halo_x, n, 1)])
        traded = {3: trade(here[3])}
        traded[2] = trade(after(here[2], traded[3]))
        traded[1] = trade(after(here[1], traded[2]))
        ids, tokens, asked = prepare(table, [ready[0], here[1], here[2], here[3]], n)
        weights = [mine, mine_c, across, across_c]
        for turn in (1, 2, 3):
            for part in (here[turn], traded[turn]):
                last = part is traded[1]
                beside = after(part, own_layer[0], pair_layer[0], ids) if last else part
                weights += [part, swap(beside, n, 1)]
        layered = [own_layer, pair_layer, halo_layer]
    else:
        stem_x = swap(stem, n, 2)
        far = swap(near, n, 4)
        left = jnp.where(p == 0, near, far)
        right = jnp.where(p == 0, far, near)
        left_x, right_x = swap(left, n, 2), swap(right, n, 2)
        halo = [
            jnp.where(c == 0, left, right),
            swap(jnp.where(c == 0, right, left), n, 1),
            jnp.where(c == 0, left_x, right_x),
            swap(jnp.where(c == 0, right_x, left_x), n, 1),
        ]
        pair_x = swap(pair, n, 2)
        own = [stem, swap(stem, n, 1), stem_x, swap(stem_x, n, 1)]
        other = [pair, swap(pair, n, 1), pair_x, swap(pair_x, n, 1)]
        layered = [norm_layer(table, gain, blocks) for blocks in (own, other, halo)]
        whole = lax.all_gather(qkv_weight, "tm", axis=0, tiled=True)
        grouped = jnp.stack([weight_group(whole, g) for g in range(4)])
        weights = [lax.dynamic_index_in_dim(grouped, group, 0, keepdims=False)]
        weights = [jnp.pad(weights[0], ((0, 0), (0, HD)))]
        depth = whole.shape[0]
        packed = jnp.stack([token_group(dec_queries, stretch_mask, g) for g in range(4)])
        every = lax.all_gather(packed, "tm", axis=0)
        every = lax.dynamic_index_in_dim(every, group, 1, keepdims=False)
        every = jnp.take(every, jnp.arange(0, n, 2, dtype=jnp.int32) ^ me, axis=0)
        every = every.reshape(n // 2, 6, 2, HD).transpose(1, 0, 2, 3).reshape(6, n, HD).astype(F32)
        asked = every[5]
        tokens = jnp.concatenate(
            [jnp.pad(every[h] * 0.125, ((0, 0), (HD * h, GROUP - HD - HD * h))) for h in range(5)]
        )
        marks = lax.all_gather(segment_ids, "tm", axis=0, tiled=True).astype(F32)
        marks = jnp.pad(marks, (512, 512))
        marks = lax.dynamic_slice_in_dim(marks, 512 * quarter, 1536, 0)
        ids = jnp.broadcast_to(marks[None], (8, 1536))
    held, stay, leave = encoder(table, layered, ids, weights, depth)

    partial = cross_partial(base, table, tokens, asked, held, swap(held, n, 1))
    owned = [partial[0]] + [swap(partial[i], n, 8 * i) for i in range(1, n // 8)]

    pieces = []
    for turn, rows in enumerate((stay, leave)):
        route = [
            (
                8 * (d // 8) + 4 * (d // 4 % 2) + (d & 2) + (d & 1),
                8 * (d // 8) + 4 * (d & 1) + ((d & 2) ^ (2 * turn)) + (d // 4 % 2),
            )
            for d in range(n)
        ]
        got = send(rows, route)
        keep = lax.dynamic_slice_in_dim(got, 128 * c, 128, 0)
        give = swap(lax.dynamic_slice_in_dim(got, 128 * (1 - c), 128, 0), n, 1)
        pieces.append((keep, give))
    memory = gather_groups([pieces[0][0], pieces[1][0], pieces[0][1], pieces[1][1]], 2 * c + x)

    final = merge(owned)
    final = [final[0]] + [swap(final[i], n, 2 * i) for i in (1, 2, 3)]
    cross_out = gather_groups(final, group)
    return (memory, cross_out)


def solution(mesh):
    placed = (
        P(("utt", "tm"), None),
        P(),
        P("tm", None),
        P(("utt", "tm")),
        P(("utt", "tm"), None),
        P(("utt", "tm"), None),
    )
    return jax.shard_map(
        on_device,
        mesh=mesh,
        in_specs=placed,
        out_specs=(P(("utt", "tm"), None), P(("utt", "tm"), None)),
        check_vma=False,
    )
```

```python
import functools

import jax
import jax.numpy as jnp
from jax import lax
from jax.experimental import pallas as pl
from jax.experimental.pallas import tpu as pltpu
from jax.sharding import PartitionSpec as P

HD = 64
WIDE = 256
GROUP = 320
BF = jnp.bfloat16
F32 = jnp.float32
LOW = -1e30
VMEM = pl.BlockSpec(memory_space=pltpu.VMEM)
SMEM = pl.BlockSpec(memory_space=pltpu.SMEM)


def send(block, route):
    return lax.ppermute(block, "tm", route)


def swap(block, n, mask):
    return send(block, [(d, d ^ mask) for d in range(n)])


def after(value, *awaited):
    return lax.optimization_barrier((value, *awaited))[0]


def scalars(values):
    return jnp.stack([jnp.asarray(v, jnp.int32) for v in values])


def group_of(array, g):
    return array[:, WIDE * g : WIDE * g + WIDE], array[:, 1024 + HD * g : 1024 + HD * g + HD]


def weight_group(weight, g):
    width = weight.shape[1] // 3
    parts = [group_of(weight[:, i * width : (i + 1) * width], g) for i in range(3)]
    (q0, q1), (k0, k1), (v0, v1) = parts
    return jnp.concatenate([q0, k0, v0, k1, v1, q1], axis=1)


def token_group(queries, mask, g):
    wide, tail = group_of(queries, g)
    heads = [wide[:, HD * i : HD * i + HD] for i in range(4)] + [tail]
    asked = jnp.pad(mask.astype(BF), ((0, 0), (0, HD - mask.shape[1])))
    return jnp.concatenate(heads + [asked], axis=0)


def pack_kernel(table, weight, queries, mask, segments, mine, theirs):
    rows, width = weight.shape[0], weight.shape[1] // 3
    blocks = mask.shape[1]
    ids = segments[...]
    digits = [lax.shift_right_logical(ids, 7).astype(F32), (ids & 127).astype(F32)]
    asked = mask[...].astype(F32)
    if blocks < HD:
        asked = jnp.concatenate([asked, jnp.zeros((2, HD - blocks), F32)], axis=1)
    rest = [asked] + [d[:, HD * i : HD * i + HD] for d in digits for i in range(2)]
    rest.append(jnp.zeros((rows - 16, HD), F32))
    for turn, outs in enumerate((mine, theirs)):
        column = table[6] if turn == 0 else 1 - table[6]
        for p in range(2):
            out = outs.at[p]
            wide = pl.multiple_of(WIDE * (2 * p + column), 128)
            tails = []
            for i in range(4):
                source = weight if i < 3 else queries
                at = width * i if i < 3 else 0
                slab = source[:, at + 1024 + 128 * p : at + 1152 + 128 * p].astype(F32)
                odd = jnp.broadcast_to(column, (slab.shape[0], HD)) == 1
                tails.append(jnp.where(odd, slab[:, HD:], slab[:, :HD]))
                if i < 3:
                    out[:, WIDE * i : WIDE * i + WIDE] = weight[
                        :, pl.ds(pl.multiple_of(at + wide, 128), WIDE)
                    ]
            out[:, 3 * WIDE : 896] = jnp.concatenate(tails[1:3], axis=1).astype(BF)
            asking = queries[:, pl.ds(wide, WIDE)].astype(F32)
            heads = [asking[:, HD * h : HD * h + HD] for h in range(4)] + [tails[3]]
            lanes = jnp.concatenate(heads + rest, axis=0)
            out[:, 896:] = jnp.concatenate([tails[0], lanes], axis=1).astype(BF)


def pack(table, weight, queries, mask, segments):
    shape = jax.ShapeDtypeStruct((2, weight.shape[0], 1024), BF)
    return pl.pallas_call(
        pack_kernel,
        out_shape=(shape, shape),
        in_specs=[SMEM] + [VMEM] * 4,
        out_specs=(VMEM,) * 2,
        compiler_params=pltpu.CompilerParams(vmem_limit_bytes=8 * 1024 * 1024),
    )(table, weight, queries, mask, segments)


def load_kernel(table, *refs):
    held, outs, other = refs[:4], refs[4:6], refs[6]
    x, c, p = table[6], table[7], table[5]
    own = jnp.broadcast_to(table[12], outs[0].shape) == 1
    flip_c = jnp.broadcast_to(c, (16, 128)) == 1
    flip_x = jnp.broadcast_to(x, (16, 128)) == 1
    for a in range(2):
        mine, mine_c, across, across_c = [h[pl.ds(p ^ a, 1)][0] for h in held]
        out = outs[a]
        out[...] = jnp.where(own, mine, across)
        if a == 1:
            other[mine.shape[0] :, :] = jnp.where(own, across, mine)
        lanes = [part[:16, 896:] for part in (mine, mine_c, across, across_c)]
        rows = []
        for first, second in (lanes[:2], lanes[2:]):
            rows.append((jnp.where(flip_c, second, first), jnp.where(flip_c, first, second)))
        low = [jnp.where(flip_x, there, here) for here, there in zip(*rows)]
        high = [jnp.where(flip_x, here, there) for here, there in zip(*rows)]
        lane = lax.broadcasted_iota(jnp.int32, (16, 128), 1)
        for j, found in enumerate(low + high):
            out[16 * j : 16 * j + 16, 896:] = jnp.where(
                lane < HD, out[16 * j : 16 * j + 16, 896:], found
            )
        if a == 1:
            other[: mine.shape[0], :] = out[...]


def load(table, *held):
    rows = held[0].shape[1]
    return pl.pallas_call(
        load_kernel,
        out_shape=tuple(jax.ShapeDtypeStruct((rows * i, 1024), BF) for i in (1, 1, 2)),
        in_specs=[SMEM] + [VMEM] * 4,
        out_specs=(VMEM,) * 3,
        compiler_params=pltpu.CompilerParams(vmem_limit_bytes=8 * 1024 * 1024),
    )(table, *held)


def norm_kernel(ways, table, gain, *refs):
    blocks, (normed, residual) = refs[: 4 * ways], refs[4 * ways :]
    group = table[4]
    for i in range(4):
        place = pl.multiple_of(table[i], 128)
        values = blocks[i][...]
        if ways == 2:
            first = jnp.broadcast_to(table[5], values.shape) == 1
            values = jnp.where(first, values, blocks[4 + i][...])
        values = values.astype(F32)
        mean = jnp.mean(values, axis=-1, keepdims=True)
        centred = values - mean
        var = jnp.mean(centred * centred, axis=-1, keepdims=True)
        normed[pl.ds(place, 128), :] = (centred * lax.rsqrt(var + 1e-05) * gain[...]).astype(BF)
        block = blocks[i]
        residual[pl.ds(place, 128), :WIDE] = block[
            :, pl.ds(pl.multiple_of(group * WIDE, 128), WIDE)
        ]
        slab = block[:, pl.ds(pl.multiple_of(1024 + group // 2 * 128, 128), 128)]
        odd = jnp.broadcast_to(lax.rem(group, 2), (128, HD)) == 1
        residual[pl.ds(place, 128), WIDE:] = jnp.where(odd, slab[:, HD:], slab[:, :HD])


def norm_layer(table, gain, blocks):
    return pl.pallas_call(
        functools.partial(norm_kernel, len(blocks) // 4),
        out_shape=(
            jax.ShapeDtypeStruct((512, 1280), BF),
            jax.ShapeDtypeStruct((512, GROUP), BF),
        ),
        in_specs=[SMEM] + [VMEM] * (1 + len(blocks)),
        out_specs=(VMEM, VMEM),
        compiler_params=pltpu.CompilerParams(vmem_limit_bytes=16 * 1024 * 1024),
    )(table, gain, *blocks)


def prepare_kernel(table, *refs):
    parts, (ids, tokens, asked) = refs[:-3], refs[-3:]
    first, x, core, z = table[13], table[6], table[7], table[14]
    count = asked.shape[0]
    ids[...] = jnp.zeros_like(ids)
    tokens[...] = jnp.zeros_like(tokens)
    flip_c = jnp.broadcast_to(core, (2, HD)) == 1
    flip_x = jnp.broadcast_to(x, (2, HD)) == 1
    for turn, part in enumerate(parts):
        lanes = part[:64, 896:].astype(F32)[:, HD:]
        for h in range(6):
            rows = [lanes[16 * j + 2 * h : 16 * j + 2 * h + 2] for j in range(4)]
            low = jnp.where(flip_c, rows[1], rows[0])
            high = jnp.where(flip_c, rows[3], rows[2])
            for dx in range(2):
                found = jnp.where(flip_x, low, high) if dx else jnp.where(flip_x, high, low)
                at = 4 * turn + 2 * dx
                if h < 5:
                    tokens[count * h + at : count * h + at + 2, HD * h : HD * h + HD] = found * 0.125
                else:
                    asked[at : at + 2, :] = found
        for j in range(4):
            marks = lanes[16 * j + 12 : 16 * j + 14] * 128.0 + lanes[16 * j + 14 : 16 * j + 16]
            block = 4 * (z ^ turn) + j - first

            @pl.when((block >= 0) & (block < 12))
            def _():
                ids[0:1, pl.ds(pl.multiple_of(block * 128, 128), 128)] = jnp.concatenate(
                    [marks[0:1], marks[1:2]], axis=1
                )


def prepare(table, parts, count):
    return pl.pallas_call(
        prepare_kernel,
        out_shape=(
            jax.ShapeDtypeStruct((8, 1536), F32),
            jax.ShapeDtypeStruct((5 * count, GROUP), F32),
            jax.ShapeDtypeStruct((count, HD), F32),
        ),
        in_specs=[SMEM] + [VMEM] * len(parts),
        out_specs=(VMEM,) * 3,
        compiler_params=pltpu.CompilerParams(vmem_limit_bytes=8 * 1024 * 1024),
    )(table, *parts)


def encoder_kernel(n_parts, depth, places, *refs):
    layers = [refs[2 * i : 2 * i + 2] for i in range(3)]
    ids = refs[6]
    parts = refs[7 : 7 + n_parts]
    memory, near, away, weight, residual, queries, keys, values = refs[7 + n_parts :]
    x = places[6]
    at = 15
    for part in parts:
        rows = [part[pl.ds(places[5], 1)][0]] if len(part.shape) == 3 else [
            part[s * depth : s * depth + depth, :] for s in range(part.shape[0] // depth)
        ]
        for found in rows:
            weight[pl.ds(pl.multiple_of(places[at] * depth, 16), depth), :] = found
            at += 1

    for slab in range(3):
        values[:, 256 * slab + 128 : 256 * slab + 256] = jnp.ones((1536, 128), BF)
    for i, (normed, kept) in enumerate(layers):
        place = pl.multiple_of(places[8 + i], 512)
        found = jnp.dot(normed[...], weight[:, 256:896], preferred_element_type=F32).astype(BF)
        keys[pl.ds(place, 512), :256] = found[:, :256]
        keys[pl.ds(place, 512), 256:] = found[:, 512:]
        for slab in range(3):
            values[pl.ds(place, 512), 256 * slab : 256 * slab + 128] = found[
                :, 256 + 128 * slab : 384 + 128 * slab
            ]
        if i < 2:

            @pl.when(place == 512)
            def _():
                residual[...] = kept[...]
                queries[:, :WIDE] = jnp.dot(
                    normed[...], weight[:, :WIDE], preferred_element_type=F32
                ).astype(BF)
                tail = jnp.dot(normed[...], weight[:, 896:], preferred_element_type=F32).astype(BF)
                lane = lax.broadcasted_iota(jnp.int32, tail.shape, 1)
                queries[:, WIDE:] = jnp.where(lane < HD, tail, jnp.zeros_like(tail))

    side = lax.broadcasted_iota(jnp.int32, (8, 128), 0) == lax.broadcasted_iota(
        jnp.int32, (8, 128), 1
    ) // HD
    sides = jnp.where(side, 1.0, 0.0).astype(BF)
    only = jnp.where(side & (lax.broadcasted_iota(jnp.int32, (8, 128), 0) == 0), 1.0, 0.0).astype(BF)
    most = []
    for held in (queries, keys):
        top = jnp.zeros((8, 1), F32)
        for slab in range(3):
            part = held[:, 128 * slab : 128 * slab + 128]
            norms = lax.dot_general(
                sides if slab < 2 else only,
                part * part,
                (((1,), (1,)), ((), ())),
                preferred_element_type=F32,
            )
            top = jnp.maximum(top, jnp.max(norms, axis=-1, keepdims=True))
        most.append(jnp.max(top))
    small = most[0] * most[1] < 220000.0

    def attend(step, shifted):
        row = step * 128 if isinstance(step, int) else pl.multiple_of(step * 128, 128)
        mine = jnp.broadcast_to(ids[0:1, pl.ds(row + 512, 128)], (128, 128)).T[:, 0:1]
        bias = jnp.where(mine == ids[0:1, pl.ds(row, 1152)], 0.0, LOW)
        lane = lax.broadcasted_iota(jnp.int32, (128, 128), 1)
        for slab in range(3):
            span = slice(128 * slab, 128 * slab + 128)
            query = queries[pl.ds(row, 128), span] * BF(0.125)
            mask = bias
            if slab < 2:
                none = jnp.zeros_like(query)
                query = jnp.concatenate(
                    [jnp.where(lane < HD, query, none), jnp.where(lane < HD, none, query)], axis=0
                )
                mask = jnp.concatenate([bias, bias], axis=0)
            scores = lax.dot_general(
                query,
                keys[pl.ds(row, 1152), span],
                (((1,), (1,)), ((), ())),
                preferred_element_type=F32,
            )
            scores = scores + mask
            if shifted:
                scores = scores - jnp.max(scores, axis=-1, keepdims=True)
            raised = jnp.exp(scores).astype(BF)
            out = jnp.dot(
                raised,
                values[pl.ds(row, 1152), 256 * slab : 256 * slab + 256],
                preferred_element_type=F32,
            )
            out = out[:, :128] / out[:, 128:]
            if slab < 2:
                context = jnp.where(lane < HD, out[:128], out[128:])
                stem = residual[pl.ds(row, 128), span].astype(F32)
                memory[pl.ds(row, 128), span] = (stem + context).astype(BF)
            else:
                stem = residual[pl.ds(row, 128), WIDE:].astype(F32)
                memory[pl.ds(row, 128), WIDE:] = (stem + out[:, HD:]).astype(BF)

    @pl.when(small)
    def _():
        for step in range(4):
            attend(step, False)

    @pl.when(jnp.logical_not(small))
    def _():
        lax.fori_loop(0, 4, lambda step, carry: (attend(step, True), carry)[1], 0)

    near[...] = memory[pl.ds(pl.multiple_of(256 * x, 256), 256), :]
    away[...] = memory[pl.ds(pl.multiple_of(256 * (1 - x), 256), 256), :]


def encoder(places, layers, ids, parts, depth):
    operands = [a for layer in layers for a in layer] + [ids] + parts
    return pl.pallas_call(
        functools.partial(encoder_kernel, len(parts), depth),
        out_shape=(
            jax.ShapeDtypeStruct((512, GROUP), BF),
            jax.ShapeDtypeStruct((256, GROUP), BF),
            jax.ShapeDtypeStruct((256, GROUP), BF),
        ),
        in_specs=[SMEM] + [VMEM] * len(operands),
        out_specs=(VMEM, VMEM, VMEM),
        scratch_shapes=[
            pltpu.VMEM((1280, 1024), BF),
            pltpu.VMEM((512, GROUP), BF),
            pltpu.VMEM((512, 384), BF),
            pltpu.VMEM((1536, 384), BF),
            pltpu.VMEM((1536, 768), BF),
        ],
        compiler_params=pltpu.CompilerParams(vmem_limit_bytes=24 * 1024 * 1024),
    )(places, *operands)


def cross_kernel(base, table, tokens, asked, memory, beside, *refs):
    outs, out = refs[:-1], refs[-1]
    count = asked.shape[0]
    me = table[base + 2]
    spot = lax.broadcasted_iota(jnp.int32, (count, HD), 1)
    order = lax.broadcasted_iota(jnp.int32, (count, 1), 0)
    owner = (order // 2 * 2) ^ me
    bias = []
    for half in range(2):
        for b in range(4):
            block = table[base + half] + b
            ask = jnp.sum(jnp.where(spot == block, asked[...], 0.0), axis=-1, keepdims=True)
            allowed = (ask > 0.5) | (owner == block)
            bias.append(jnp.broadcast_to(jnp.where(allowed, 0.0, LOW), (count, 128)))
    bias = jnp.concatenate(bias, axis=1)
    bias = jnp.concatenate([bias] * 5, axis=0)
    query = tokens[...].astype(BF)
    cross = jnp.concatenate(
        [
            lax.dot_general(
                query, held[...], (((1,), (1,)), ((), ())), preferred_element_type=F32
            )
            for held in (memory, beside)
        ],
        axis=1,
    )
    cross = jnp.where(bias < 0.0, LOW, cross)
    top = jnp.max(cross, axis=-1, keepdims=True)
    raised = jnp.where(bias < 0.0, 0.0, jnp.exp(cross - top))
    den = jnp.sum(raised, axis=-1, keepdims=True)
    raised = raised.astype(BF)
    out[...] = jnp.dot(raised[:, :512], memory[...], preferred_element_type=F32) + jnp.dot(
        raised[:, 512:], beside[...], preferred_element_type=F32
    )
    lane = lax.broadcasted_iota(jnp.int32, (count, HD), 1)
    for h in range(5):
        rows = slice(count * h, count * h + count)
        stats = jnp.where(lane == 0, top[rows], den[rows])
        both = jnp.concatenate([out[rows, HD * h : HD * h + HD], stats], axis=1)
        for i, owned in enumerate(outs):
            owned[8 * h : 8 * h + 8, :] = both[8 * i : 8 * i + 8]


def cross_partial(base, table, tokens, asked, memory, beside):
    count = asked.shape[0]
    return pl.pallas_call(
        functools.partial(cross_kernel, base),
        out_shape=(jax.ShapeDtypeStruct((40, 128), F32),) * (count // 8),
        in_specs=[SMEM] + [VMEM] * 4,
        out_specs=(VMEM,) * (count // 8),
        scratch_shapes=[pltpu.VMEM((5 * count, GROUP), F32)],
        compiler_params=pltpu.CompilerParams(vmem_limit_bytes=12 * 1024 * 1024),
    )(table, tokens, asked, memory, beside)


def merge_kernel(*refs):
    parts, outs, out = refs[:-5], refs[-5:-1], refs[-1]
    tops = [part[:, HD : HD + 1] for part in parts]
    best = functools.reduce(jnp.maximum, tops)
    total = jnp.zeros((40, 128), F32)
    for top, part in zip(tops, parts):
        total = total + jnp.exp(top - best) * part[...]
    final = total[:, :HD] / total[:, HD + 1 : HD + 2]
    heads = [final[8 * h : 8 * h + 8] for h in range(5)] + [jnp.zeros((8, HD), F32)]
    for slab in range(3):
        out[:, 128 * slab : 128 * slab + 128] = jnp.concatenate(heads[2 * slab : 2 * slab + 2], axis=1)
    for i in range(4):
        outs[i][...] = out[2 * i : 2 * i + 2, :].astype(BF)


def merge(parts):
    return pl.pallas_call(
        merge_kernel,
        out_shape=(jax.ShapeDtypeStruct((2, 384), BF),) * 4,
        in_specs=[VMEM] * len(parts),
        out_specs=(VMEM,) * 4,
        scratch_shapes=[pltpu.VMEM((8, 384), F32)],
        compiler_params=pltpu.CompilerParams(vmem_limit_bytes=4 * 1024 * 1024),
    )(*parts)


def gather_kernel(side, rows, table, *refs):
    pieces, out = refs[:4], refs[4]
    high, x = table[side], table[6]
    start = pl.multiple_of(rows * high, rows) if pieces[0].shape[0] > rows else 0
    flip = jnp.broadcast_to(x, (rows, HD)) == 1
    held = [piece[pl.ds(start, rows), :] for piece in pieces]
    for i, piece in enumerate(held):
        group = (2 * high + x) ^ i
        out[:, pl.ds(pl.multiple_of(WIDE * group, 128), WIDE)] = piece[:, :WIDE]
    for i in range(2):
        first, second = [piece[:, WIDE:GROUP] for piece in held[2 * i : 2 * i + 2]]
        tail = jnp.concatenate([jnp.where(flip, second, first), jnp.where(flip, first, second)], axis=1)
        out[:, pl.ds(pl.multiple_of(1024 + 128 * (high ^ i), 128), 128)] = tail


def gather_groups(side, rows, table, pieces):
    return pl.pallas_call(
        functools.partial(gather_kernel, side, rows),
        out_shape=jax.ShapeDtypeStruct((rows, 1280), BF),
        in_specs=[SMEM] + [VMEM] * 4,
        out_specs=VMEM,
        compiler_params=pltpu.CompilerParams(vmem_limit_bytes=4 * 1024 * 1024),
    )(table, *pieces)


def on_device(stem, norm_gain, qkv_weight, segment_ids, dec_queries, stretch_mask):
    n = lax.axis_size("tm")
    layers = n // 4
    me = lax.axis_index("tm")
    z, x, c = me // 4, (me // 2) % 2, me % 2
    p, k = z % 2, z // 2
    quarter = 2 * k + c
    group = 2 * p + x
    depth = qkv_weight.shape[0]

    utts = lax.axis_size("utt")
    moved = lax.axis_index("utt") % 2
    direct = depth % 16 == 0 and layers == 4 and utts % 2 == 0
    gain = norm_gain.reshape(1, -1)
    table = [128 * (2 * x + c), 128 * (2 * x + 1 - c), 128 * (2 - 2 * x + c), 128 * (3 - 2 * x - c)]
    table += [group, p, x, c]
    table += [512 * (p - c + 1), 512 * (2 - p - c), 1024 * c, 0, x == moved, 4 * quarter - 4, z]
    sources = [me, me ^ 1, me ^ 2, me ^ 3] if direct else [jnp.int32(0)]
    for turn in (1, 2, 3) if direct else ():
        column, sides = 4 * (z ^ turn) + c, (2 * moved, 2 - 2 * moved)
        if turn == 1:
            sources += [core + side for core in (column, column ^ 1) for side in sides]
        else:
            sources += [core + side for side in sides for core in (column, column ^ 1)]
    table = scalars(table + sources + [4 * quarter, 4 * (quarter ^ 1), me])
    base = 15 + len(sources)

    steps = [1 if i % 2 else -1 for i in range(layers)]
    near_route = [
        (4 * i + j, 4 * (i + s) + j)
        for i, s in enumerate(steps)
        for j in range(4)
        if 0 <= i + s < layers
    ]
    near = send(stem, near_route)
    pair = swap(stem, n, 4)
    if direct:
        def trade(block):
            return lax.ppermute(block, "utt", [(u, u ^ 1) for u in range(utts)])

        mine, theirs = pack(
            table, qkv_weight, dec_queries, stretch_mask, segment_ids.reshape(1, -1)
        )
        stem_x = swap(stem, n, 2)
        across = swap(after(theirs, stem_x, pair, near), n, 2)
        mine_c, across_c = swap(mine, n, 1), swap(across, n, 1)
        relayed = swap(after(near, pair), n, 4)
        ready = load(table, mine, mine_c, after(across, relayed), across_c)
        here = {turn: swap(ready[turn % 2], n, 4 * turn) for turn in (3, 2)}
        here[1] = swap(ready[2], n, 4)
        stem_c, stem_xc = [swap(after(part, here[3]), n, 1) for part in (stem, stem_x)]
        own_layer = norm_layer(table, gain, [stem, stem_c, stem_x, stem_xc])
        pair_x = swap(after(pair, across), n, 2)
        halo = jnp.where((z == 1) | (z == 2), near, relayed)
        halo_x = swap(after(halo, pair_x), n, 2)
        pair_c, pair_xc = [swap(after(part, here[3]), n, 1) for part in (pair, pair_x)]
        pair_layer = norm_layer(table, gain, [pair, pair_c, pair_x, pair_xc])
        halo_layer = norm_layer(table, gain, [halo, swap(halo, n, 1), halo_x, swap(halo_x, n, 1)])
        traded = {3: trade(here[3])}
        traded[2] = trade(after(here[2], here[1], traded[3]))
        ids, tokens, asked = prepare(table, [ready[0], here[1], here[2], here[3]], n)
        weights = [mine, mine_c, across, across_c]
        weights += [here[1], swap(here[1], n, 1)]
        for turn in (2, 3):
            for part in (here[turn], traded[turn]):
                last = part is traded[2]
                beside = after(part, own_layer[0], pair_layer[0], ids) if last else part
                weights += [part, swap(beside, n, 1)]
        layered = [own_layer, pair_layer, halo_layer]
    else:
        stem_x = swap(stem, n, 2)
        far = swap(near, n, 4)
        left = jnp.where(p == 0, near, far)
        right = jnp.where(p == 0, far, near)
        left_x, right_x = swap(left, n, 2), swap(right, n, 2)
        halo = [
            jnp.where(c == 0, left, right),
            swap(jnp.where(c == 0, right, left), n, 1),
            jnp.where(c == 0, left_x, right_x),
            swap(jnp.where(c == 0, right_x, left_x), n, 1),
        ]
        pair_x = swap(pair, n, 2)
        own = [stem, swap(stem, n, 1), stem_x, swap(stem_x, n, 1)]
        other = [pair, swap(pair, n, 1), pair_x, swap(pair_x, n, 1)]
        layered = [norm_layer(table, gain, blocks) for blocks in (own, other, halo)]
        whole = lax.all_gather(qkv_weight, "tm", axis=0, tiled=True)
        grouped = jnp.stack([weight_group(whole, g) for g in range(4)])
        weights = [lax.dynamic_index_in_dim(grouped, group, 0, keepdims=False)]
        weights = [jnp.pad(weights[0], ((0, 0), (0, HD)))]
        depth = whole.shape[0]
        packed = jnp.stack([token_group(dec_queries, stretch_mask, g) for g in range(4)])
        every = lax.all_gather(packed, "tm", axis=0)
        every = lax.dynamic_index_in_dim(every, group, 1, keepdims=False)
        every = jnp.take(every, jnp.arange(0, n, 2, dtype=jnp.int32) ^ me, axis=0)
        every = every.reshape(n // 2, 6, 2, HD).transpose(1, 0, 2, 3).reshape(6, n, HD).astype(F32)
        asked = every[5]
        tokens = jnp.concatenate(
            [jnp.pad(every[h] * 0.125, ((0, 0), (HD * h, GROUP - HD - HD * h))) for h in range(5)]
        )
        marks = lax.all_gather(segment_ids, "tm", axis=0, tiled=True).astype(F32)
        marks = jnp.pad(marks, (512, 512))
        marks = lax.dynamic_slice_in_dim(marks, 512 * quarter, 1536, 0)
        ids = jnp.broadcast_to(marks[None], (8, 1536))
    held, stay, leave = encoder(table, layered, ids, weights, depth)

    partial = cross_partial(base, table, tokens, asked, held, swap(held, n, 1))
    owned = [partial[0]] + [swap(partial[i], n, 8 * i) for i in range(1, n // 8)]

    got = []
    for turn, rows in enumerate((stay, leave)):
        route = [
            (
                8 * (d // 8) + 4 * (d // 4 % 2) + (d & 2) + (d & 1),
                8 * (d // 8) + 4 * (d & 1) + ((d & 2) ^ (2 * turn)) + (d // 4 % 2),
            )
            for d in range(n)
        ]
        got.append(after(send(rows, route), owned[1]))
    memory = gather_groups(7, 128, table, got + [swap(part, n, 1) for part in got])

    final = merge(owned)
    final = [final[0]] + [swap(final[i], n, 2 * i) for i in (1, 2, 3)]
    cross_out = gather_groups(5, 2, table, final)
    return (memory, cross_out)


def solution(mesh):
    placed = (
        P(("utt", "tm"), None),
        P(),
        P("tm", None),
        P(("utt", "tm")),
        P(("utt", "tm"), None),
        P(("utt", "tm"), None),
    )
    return jax.shard_map(
        on_device,
        mesh=mesh,
        in_specs=placed,
        out_specs=(P(("utt", "tm"), None), P(("utt", "tm"), None)),
        check_vma=False,
    )
```

```python
import functools

import jax
import jax.numpy as jnp
from jax import lax
from jax.experimental import pallas as pl
from jax.experimental.pallas import tpu as pltpu
from jax.sharding import PartitionSpec as P

HD = 64
WIDE = 256
GROUP = 320
BF = jnp.bfloat16
F32 = jnp.float32
LOW = -1e30
CHEAP = pl.CostEstimate(flops=1, bytes_accessed=1, transcendentals=0)
VMEM = pl.BlockSpec(memory_space=pltpu.VMEM)
SMEM = pl.BlockSpec(memory_space=pltpu.SMEM)


def send(block, route):
    return lax.ppermute(block, "tm", route)


def swap(block, n, mask):
    return send(block, [(d, d ^ mask) for d in range(n)])


def after(value, *awaited):
    return lax.optimization_barrier((value, *awaited))[0]


def scalars(values):
    return jnp.stack([jnp.asarray(v, jnp.int32) for v in values])


def group_of(array, g):
    return array[:, WIDE * g : WIDE * g + WIDE], array[:, 1024 + HD * g : 1024 + HD * g + HD]


def weight_group(weight, g):
    width = weight.shape[1] // 3
    parts = [group_of(weight[:, i * width : (i + 1) * width], g) for i in range(3)]
    (q0, q1), (k0, k1), (v0, v1) = parts
    return jnp.concatenate([q0, k0, v0, k1, v1, q1], axis=1)


def token_group(queries, mask, g):
    wide, tail = group_of(queries, g)
    heads = [wide[:, HD * i : HD * i + HD] for i in range(4)] + [tail]
    asked = jnp.pad(mask.astype(BF), ((0, 0), (0, HD - mask.shape[1])))
    return jnp.concatenate(heads + [asked], axis=0)


def pack_kernel(table, *refs):
    mine, theirs = refs[4:6]
    weight, queries, mask, segments = held = refs[6:10]
    copies = [pltpu.make_async_copy(refs[i], held[i], refs[10].at[i]) for i in range(4)]
    for copy in copies:
        copy.start()
    for copy in copies:
        copy.wait()
    rows, width = weight.shape[0], weight.shape[1] // 3
    blocks = mask.shape[1]
    ids = segments[...]
    digits = [lax.shift_right_logical(ids, 7).astype(F32), (ids & 127).astype(F32)]
    asked = mask[...].astype(F32)
    if blocks < HD:
        asked = jnp.concatenate([asked, jnp.zeros((2, HD - blocks), F32)], axis=1)
    rest = [asked] + [d[:, HD * i : HD * i + HD] for d in digits for i in range(2)]
    rest.append(jnp.zeros((rows - 16, HD), F32))
    for turn, outs in enumerate((mine, theirs)):
        column = table[6] if turn == 0 else 1 - table[6]
        for p in range(2):
            out = outs.at[p]
            wide = pl.multiple_of(WIDE * (2 * p + column), 128)
            tails = []
            for i in range(4):
                source = weight if i < 3 else queries
                at = width * i if i < 3 else 0
                slab = source[:, at + 1024 + 128 * p : at + 1152 + 128 * p].astype(F32)
                odd = jnp.broadcast_to(column, (slab.shape[0], HD)) == 1
                tails.append(jnp.where(odd, slab[:, HD:], slab[:, :HD]))
                if i < 3:
                    out[:, WIDE * i : WIDE * i + WIDE] = weight[
                        :, pl.ds(pl.multiple_of(at + wide, 128), WIDE)
                    ]
            out[:, 3 * WIDE : 896] = jnp.concatenate(tails[1:3], axis=1).astype(BF)
            asking = queries[:, pl.ds(wide, WIDE)].astype(F32)
            heads = [asking[:, HD * h : HD * h + HD] for h in range(4)] + [tails[3]]
            lanes = jnp.concatenate(heads + rest, axis=0)
            out[:, 896:] = jnp.concatenate([tails[0], lanes], axis=1).astype(BF)


def pack(table, weight, queries, mask, segments):
    shape = jax.ShapeDtypeStruct((2, weight.shape[0], 1024), BF)
    given = (weight, queries, mask, segments)
    return pl.pallas_call(
        pack_kernel,
        out_shape=(shape, shape),
        in_specs=[SMEM] + [pl.BlockSpec(memory_space=pl.ANY)] * 4,
        out_specs=(VMEM,) * 2,
        scratch_shapes=[pltpu.VMEM(a.shape, a.dtype) for a in given] + [pltpu.SemaphoreType.DMA((4,))],
        cost_estimate=CHEAP,
        compiler_params=pltpu.CompilerParams(vmem_limit_bytes=8 * 1024 * 1024),
    )(table, weight, queries, mask, segments)


def load_kernel(table, *refs):
    held, outs = refs[:4], refs[4:]
    x, c, p = table[6], table[7], table[5]
    own = jnp.broadcast_to(table[12], outs[0].shape) == 1
    flip_c = jnp.broadcast_to(c, (16, 128)) == 1
    flip_x = jnp.broadcast_to(x, (16, 128)) == 1
    for a in range(2):
        mine, mine_c, across, across_c = [h[pl.ds(p ^ a, 1)][0] for h in held]
        out = outs[a]
        out[...] = jnp.where(own, mine, across)
        lanes = [part[:16, 896:] for part in (mine, mine_c, across, across_c)]
        rows = []
        for first, second in (lanes[:2], lanes[2:]):
            rows.append((jnp.where(flip_c, second, first), jnp.where(flip_c, first, second)))
        low = [jnp.where(flip_x, there, here) for here, there in zip(*rows)]
        high = [jnp.where(flip_x, here, there) for here, there in zip(*rows)]
        lane = lax.broadcasted_iota(jnp.int32, (16, 128), 1)
        for j, found in enumerate(low + high):
            out[16 * j : 16 * j + 16, 896:] = jnp.where(
                lane < HD, out[16 * j : 16 * j + 16, 896:], found
            )


def load(table, *held):
    rows = held[0].shape[1]
    return pl.pallas_call(
        load_kernel,
        out_shape=(jax.ShapeDtypeStruct((rows, 1024), BF),) * 2,
        in_specs=[SMEM] + [VMEM] * 4,
        out_specs=(VMEM,) * 2,
        cost_estimate=CHEAP,
        compiler_params=pltpu.CompilerParams(vmem_limit_bytes=8 * 1024 * 1024),
    )(table, *held)


def norm_kernel(table, gain, here, across, out):
    group = table[4]
    for i, block in enumerate((here, across)):
        rows = slice(128 * i, 128 * i + 128)
        values = block[...].astype(F32)
        mean = jnp.mean(values, axis=-1, keepdims=True)
        centred = values - mean
        var = jnp.mean(centred * centred, axis=-1, keepdims=True)
        out[rows, :1280] = (centred * lax.rsqrt(var + 1e-05) * gain[...]).astype(BF)
        if out.shape[1] > 1280:
            out[rows, 1280 : 1280 + WIDE] = block[:, pl.ds(pl.multiple_of(group * WIDE, 128), WIDE)]
            slab = block[:, pl.ds(pl.multiple_of(1024 + group // 2 * 128, 128), 128)]
            odd = jnp.broadcast_to(lax.rem(group, 2), (128, HD)) == 1
            tail = jnp.where(odd, slab[:, HD:], slab[:, :HD])
            out[rows, 1280 + WIDE :] = jnp.concatenate([tail, jnp.zeros_like(tail)], axis=1)


def norm_half(table, gain, here, across, kept=True):
    return pl.pallas_call(
        norm_kernel,
        out_shape=jax.ShapeDtypeStruct((256, 1664 if kept else 1280), BF),
        in_specs=[SMEM] + [VMEM] * 3,
        out_specs=VMEM,
        cost_estimate=CHEAP,
        compiler_params=pltpu.CompilerParams(vmem_limit_bytes=8 * 1024 * 1024),
    )(table, gain, here, across)


def prepare_kernel(table, *refs):
    parts, (ids, tokens, asked) = refs[:-3], refs[-3:]
    first, x, core, z = table[13], table[6], table[7], table[14]
    count = asked.shape[0]
    ids[...] = jnp.zeros_like(ids)
    tokens[...] = jnp.zeros_like(tokens)
    flip_c = jnp.broadcast_to(core, (2, HD)) == 1
    flip_x = jnp.broadcast_to(x, (2, HD)) == 1
    for turn, part in enumerate(parts):
        lanes = part[:64, 896:].astype(F32)[:, HD:]
        for h in range(6):
            rows = [lanes[16 * j + 2 * h : 16 * j + 2 * h + 2] for j in range(4)]
            low = jnp.where(flip_c, rows[1], rows[0])
            high = jnp.where(flip_c, rows[3], rows[2])
            for dx in range(2):
                found = jnp.where(flip_x, low, high) if dx else jnp.where(flip_x, high, low)
                at = 4 * turn + 2 * dx
                if h < 5:
                    tokens[count * h + at : count * h + at + 2, HD * h : HD * h + HD] = found * 0.125
                else:
                    asked[at : at + 2, :] = found
        for j in range(4):
            marks = lanes[16 * j + 12 : 16 * j + 14] * 128.0 + lanes[16 * j + 14 : 16 * j + 16]
            block = 4 * (z ^ turn) + j - first

            @pl.when((block >= 0) & (block < 12))
            def _():
                ids[0:1, pl.ds(pl.multiple_of(block * 128, 128), 128)] = jnp.concatenate(
                    [marks[0:1], marks[1:2]], axis=1
                )


def prepare(table, parts, count):
    return pl.pallas_call(
        prepare_kernel,
        out_shape=(
            jax.ShapeDtypeStruct((8, 1536), F32),
            jax.ShapeDtypeStruct((5 * count, GROUP), F32),
            jax.ShapeDtypeStruct((count, HD), F32),
        ),
        in_specs=[SMEM] + [VMEM] * len(parts),
        out_specs=(VMEM,) * 3,
        cost_estimate=CHEAP,
        compiler_params=pltpu.CompilerParams(vmem_limit_bytes=8 * 1024 * 1024),
    )(table, *parts)


def encoder_kernel(n_parts, depth, places, *refs):
    layers = [refs[2 * i : 2 * i + 2] for i in range(3)]
    ids = refs[6]
    parts = refs[7 : 7 + n_parts]
    memory, near, away, weight, residual, queries, keys, values = refs[7 + n_parts :]
    x = places[6]
    at = 15
    for part in parts:
        rows = [part[pl.ds(places[5], 1)][0]] if len(part.shape) == 3 else [
            part[s * depth : s * depth + depth, :] for s in range(part.shape[0] // depth)
        ]
        for found in rows:
            weight[pl.ds(pl.multiple_of(places[at] * depth, 16), depth), :] = found
            at += 1

    for slab in range(3):
        values[:, 256 * slab + 128 : 256 * slab + 256] = jnp.ones((1536, 128), BF)
    spots = [places[i] for i in (0, 2, 1, 3)]
    for i, halves in enumerate(layers):
        place = places[8 + i]
        normed = jnp.concatenate([half[:, :1280] for half in halves], axis=0)
        found = jnp.dot(normed, weight[:, 256:896], preferred_element_type=F32).astype(BF)
        for j, spot in enumerate(spots):
            to = pl.ds(pl.multiple_of(place + spot, 128), 128)
            block = found[128 * j : 128 * j + 128]
            keys[to, :256] = block[:, :256]
            keys[to, 256:] = block[:, 512:]
            for slab in range(3):
                values[to, 256 * slab : 256 * slab + 128] = block[:, 256 + 128 * slab : 384 + 128 * slab]
        if i < 2:

            @pl.when(place == 512)
            def _():
                normed = jnp.concatenate([half[:, :1280] for half in halves], axis=0)
                wide = jnp.dot(normed, weight[:, :WIDE], preferred_element_type=F32).astype(BF)
                tail = jnp.dot(normed, weight[:, 896:], preferred_element_type=F32).astype(BF)
                lane = lax.broadcasted_iota(jnp.int32, tail.shape, 1)
                tail = jnp.where(lane < HD, tail, jnp.zeros_like(tail))
                for j, spot in enumerate(spots):
                    to = pl.ds(pl.multiple_of(spot, 128), 128)
                    rows = slice(128 * j, 128 * j + 128)
                    queries[to, :WIDE] = wide[rows]
                    queries[to, WIDE:] = tail[rows]
                    residual[to, :] = halves[j // 2][128 * (j % 2) : 128 * (j % 2) + 128, 1280:]

    side = lax.broadcasted_iota(jnp.int32, (8, 128), 0) == lax.broadcasted_iota(
        jnp.int32, (8, 128), 1
    ) // HD
    sides = jnp.where(side, 1.0, 0.0).astype(BF)
    only = jnp.where(side & (lax.broadcasted_iota(jnp.int32, (8, 128), 0) == 0), 1.0, 0.0).astype(BF)
    most = []
    for held in (queries, keys):
        top = jnp.zeros((8, 1), F32)
        for slab in range(3):
            part = held[:, 128 * slab : 128 * slab + 128]
            norms = lax.dot_general(
                sides if slab < 2 else only,
                part * part,
                (((1,), (1,)), ((), ())),
                preferred_element_type=F32,
            )
            top = jnp.maximum(top, jnp.max(norms, axis=-1, keepdims=True))
        most.append(jnp.max(top))
    small = most[0] * most[1] < 220000.0

    def attend(step, shifted):
        row = step * 128 if isinstance(step, int) else pl.multiple_of(step * 128, 128)
        mine = jnp.broadcast_to(ids[0:1, pl.ds(row + 512, 128)], (128, 128)).T[:, 0:1]
        bias = jnp.where(mine == ids[0:1, pl.ds(row, 1152)], 0.0, LOW)
        lane = lax.broadcasted_iota(jnp.int32, (128, 128), 1)
        for slab in range(3):
            span = slice(128 * slab, 128 * slab + 128)
            query = queries[pl.ds(row, 128), span] * BF(0.125)
            mask = bias
            if slab < 2:
                none = jnp.zeros_like(query)
                query = jnp.concatenate(
                    [jnp.where(lane < HD, query, none), jnp.where(lane < HD, none, query)], axis=0
                )
                mask = jnp.concatenate([bias, bias], axis=0)
            scores = lax.dot_general(
                query,
                keys[pl.ds(row, 1152), span],
                (((1,), (1,)), ((), ())),
                preferred_element_type=F32,
            )
            scores = scores + mask
            if shifted:
                scores = scores - jnp.max(scores, axis=-1, keepdims=True)
            raised = jnp.exp(scores).astype(BF)
            out = jnp.dot(
                raised,
                values[pl.ds(row, 1152), 256 * slab : 256 * slab + 256],
                preferred_element_type=F32,
            )
            out = out[:, :128] / out[:, 128:]
            if slab < 2:
                context = jnp.where(lane < HD, out[:128], out[128:])
                stem = residual[pl.ds(row, 128), span].astype(F32)
                memory[pl.ds(row, 128), span] = (stem + context).astype(BF)
            else:
                stem = residual[pl.ds(row, 128), WIDE:GROUP].astype(F32)
                memory[pl.ds(row, 128), WIDE:] = (stem + out[:, HD:]).astype(BF)

    @pl.when(small)
    def _():
        for step in range(4):
            attend(step, False)

    @pl.when(jnp.logical_not(small))
    def _():
        lax.fori_loop(0, 4, lambda step, carry: (attend(step, True), carry)[1], 0)

    near[...] = memory[pl.ds(pl.multiple_of(256 * x, 256), 256), :]
    away[...] = memory[pl.ds(pl.multiple_of(256 * (1 - x), 256), 256), :]


def encoder(places, layers, ids, parts, depth):
    operands = layers + [ids] + parts
    return pl.pallas_call(
        functools.partial(encoder_kernel, len(parts), depth),
        out_shape=(
            jax.ShapeDtypeStruct((512, GROUP), BF),
            jax.ShapeDtypeStruct((256, GROUP), BF),
            jax.ShapeDtypeStruct((256, GROUP), BF),
        ),
        in_specs=[SMEM] + [VMEM] * len(operands),
        out_specs=(VMEM, VMEM, VMEM),
        scratch_shapes=[
            pltpu.VMEM((1280, 1024), BF),
            pltpu.VMEM((512, 384), BF),
            pltpu.VMEM((512, 384), BF),
            pltpu.VMEM((1536, 384), BF),
            pltpu.VMEM((1536, 768), BF),
        ],
        cost_estimate=CHEAP,
        compiler_params=pltpu.CompilerParams(vmem_limit_bytes=24 * 1024 * 1024),
    )(places, *operands)


def cross_kernel(base, table, tokens, asked, memory, beside, *refs):
    outs, out = refs[:-1], refs[-1]
    count = asked.shape[0]
    me = table[base + 2]
    spot = lax.broadcasted_iota(jnp.int32, (count, HD), 1)
    order = lax.broadcasted_iota(jnp.int32, (count, 1), 0)
    owner = (order // 2 * 2) ^ me
    bias = []
    for half in range(2):
        for b in range(4):
            block = table[base + half] + b
            ask = jnp.sum(jnp.where(spot == block, asked[...], 0.0), axis=-1, keepdims=True)
            allowed = (ask > 0.5) | (owner == block)
            bias.append(jnp.broadcast_to(jnp.where(allowed, 0.0, LOW), (count, 128)))
    bias = jnp.concatenate(bias, axis=1)
    bias = jnp.concatenate([bias] * 5, axis=0)
    query = tokens[...].astype(BF)
    cross = jnp.concatenate(
        [
            lax.dot_general(
                query, held[...], (((1,), (1,)), ((), ())), preferred_element_type=F32
            )
            for held in (memory, beside)
        ],
        axis=1,
    )
    cross = jnp.where(bias < 0.0, LOW, cross)
    top = jnp.max(cross, axis=-1, keepdims=True)
    raised = jnp.where(bias < 0.0, 0.0, jnp.exp(cross - top))
    den = jnp.sum(raised, axis=-1, keepdims=True)
    raised = raised.astype(BF)
    out[...] = jnp.dot(raised[:, :512], memory[...], preferred_element_type=F32) + jnp.dot(
        raised[:, 512:], beside[...], preferred_element_type=F32
    )
    lane = lax.broadcasted_iota(jnp.int32, (count, HD), 1)
    for h in range(5):
        rows = slice(count * h, count * h + count)
        stats = jnp.where(lane == 0, top[rows], den[rows])
        both = jnp.concatenate([out[rows, HD * h : HD * h + HD], stats], axis=1)
        for i, owned in enumerate(outs):
            owned[8 * h : 8 * h + 8, :] = both[8 * i : 8 * i + 8]


def cross_partial(base, table, tokens, asked, memory, beside):
    count = asked.shape[0]
    return pl.pallas_call(
        functools.partial(cross_kernel, base),
        out_shape=(jax.ShapeDtypeStruct((40, 128), F32),) * (count // 8),
        in_specs=[SMEM] + [VMEM] * 4,
        out_specs=(VMEM,) * (count // 8),
        scratch_shapes=[pltpu.VMEM((5 * count, GROUP), F32)],
        cost_estimate=CHEAP,
        compiler_params=pltpu.CompilerParams(vmem_limit_bytes=12 * 1024 * 1024),
    )(table, tokens, asked, memory, beside)


def merge_kernel(*refs):
    parts, outs, out = refs[:-5], refs[-5:-1], refs[-1]
    tops = [part[:, HD : HD + 1] for part in parts]
    best = functools.reduce(jnp.maximum, tops)
    total = jnp.zeros((40, 128), F32)
    for top, part in zip(tops, parts):
        total = total + jnp.exp(top - best) * part[...]
    final = total[:, :HD] / total[:, HD + 1 : HD + 2]
    heads = [final[8 * h : 8 * h + 8] for h in range(5)] + [jnp.zeros((8, HD), F32)]
    for slab in range(3):
        out[:, 128 * slab : 128 * slab + 128] = jnp.concatenate(heads[2 * slab : 2 * slab + 2], axis=1)
    for i in range(4):
        outs[i][...] = out[2 * i : 2 * i + 2, :].astype(BF)


def merge(parts):
    return pl.pallas_call(
        merge_kernel,
        out_shape=(jax.ShapeDtypeStruct((2, 384), BF),) * 4,
        in_specs=[VMEM] * len(parts),
        out_specs=(VMEM,) * 4,
        scratch_shapes=[pltpu.VMEM((8, 384), F32)],
        cost_estimate=CHEAP,
        compiler_params=pltpu.CompilerParams(vmem_limit_bytes=4 * 1024 * 1024),
    )(*parts)


def gather_kernel(side, rows, table, *refs):
    pieces, out = refs[:4], refs[4]
    high, x = table[side], table[6]
    start = pl.multiple_of(rows * high, rows) if pieces[0].shape[0] > rows else 0
    flip = jnp.broadcast_to(x, (rows, HD)) == 1
    held = [piece[pl.ds(start, rows), :] for piece in pieces]
    for i, piece in enumerate(held):
        group = (2 * high + x) ^ i
        out[:, pl.ds(pl.multiple_of(WIDE * group, 128), WIDE)] = piece[:, :WIDE]
    for i in range(2):
        first, second = [piece[:, WIDE:GROUP] for piece in held[2 * i : 2 * i + 2]]
        tail = jnp.concatenate([jnp.where(flip, second, first), jnp.where(flip, first, second)], axis=1)
        out[:, pl.ds(pl.multiple_of(1024 + 128 * (high ^ i), 128), 128)] = tail


def gather_groups(side, rows, table, pieces):
    return pl.pallas_call(
        functools.partial(gather_kernel, side, rows),
        out_shape=jax.ShapeDtypeStruct((rows, 1280), BF),
        in_specs=[SMEM] + [VMEM] * 4,
        out_specs=VMEM,
        cost_estimate=CHEAP,
        compiler_params=pltpu.CompilerParams(vmem_limit_bytes=4 * 1024 * 1024),
    )(table, *pieces)


def on_device(stem, norm_gain, qkv_weight, segment_ids, dec_queries, stretch_mask):
    n = lax.axis_size("tm")
    layers = n // 4
    me = lax.axis_index("tm")
    z, x, c = me // 4, (me // 2) % 2, me % 2
    p, k = z % 2, z // 2
    quarter = 2 * k + c
    group = 2 * p + x
    depth = qkv_weight.shape[0]

    utts = lax.axis_size("utt")
    moved = lax.axis_index("utt") % 2
    direct = depth % 16 == 0 and layers == 4 and utts % 2 == 0
    gain = norm_gain.reshape(1, -1)
    table = [128 * (2 * x + c), 128 * (2 * x + 1 - c), 128 * (2 - 2 * x + c), 128 * (3 - 2 * x - c)]
    table += [group, p, x, c]
    table += [512 * (p - c + 1), 512 * (2 - p - c), 1024 * c, 0, x == moved, 4 * quarter - 4, z]
    sources = [me, me ^ 1, me ^ 2, me ^ 3] if direct else [jnp.int32(0)]
    for turn in (1, 2, 3) if direct else ():
        column = 4 * (z ^ turn) + c
        for side in (2 * moved, 2 - 2 * moved):
            sources += [column + side, (column ^ 1) + side]
    table = scalars(table + sources + [4 * quarter, 4 * (quarter ^ 1), me])
    base = 15 + len(sources)

    steps = [1 if i % 2 else -1 for i in range(layers)]
    near_route = [
        (4 * i + j, 4 * (i + s) + j)
        for i, s in enumerate(steps)
        for j in range(4)
        if 0 <= i + s < layers
    ]
    near = send(stem, near_route)
    pair = swap(stem, n, 4)
    if direct:
        def trade(block):
            return lax.ppermute(block, "utt", [(u, u ^ 1) for u in range(utts)])

        mine, theirs = pack(
            table, qkv_weight, dec_queries, stretch_mask, segment_ids.reshape(1, -1)
        )
        across = swap(theirs, n, 2)
        mine_c, across_c = swap(mine, n, 1), swap(across, n, 1)
        ready = load(table, mine, mine_c, after(across, near, pair), across_c)
        relayed = swap(after(near, ready[0]), n, 4)
        stem_x = swap(after(stem, across), n, 2)
        here = {turn: swap(ready[turn % 2], n, 4 * turn) for turn in (3, 2, 1)}
        pair_x = swap(after(pair, ready[0]), n, 2)
        halo = jnp.where((z == 1) | (z == 2), near, relayed)
        halo_x = swap(after(halo, pair_x), n, 2)
        ids, tokens, asked = prepare(table, [ready[0], here[1], here[2], here[3]], n)
        traded = {3: trade(after(here[3], pair_x)), 2: trade(after(here[2], here[3]))}
        traded[1] = trade(after(here[1], ids))
        own_half = norm_half(table, gain, stem, stem_x)
        pair_half = norm_half(table, gain, pair, pair_x)
        halo_half = norm_half(table, gain, halo, halo_x, False)
        layered = [
            own_half, swap(after(own_half, traded[3]), n, 1),
            pair_half, swap(after(pair_half, traded[2]), n, 1),
            halo_half, swap(after(halo_half, traded[1]), n, 1),
        ]
        weights = [mine, mine_c, across, across_c]
        for turn in (1, 2, 3):
            for part in (here[turn], traded[turn]):
                weights += [part, swap(part, n, 1)]
    else:
        stem_x = swap(stem, n, 2)
        far = swap(near, n, 4)
        left = jnp.where(p == 0, near, far)
        right = jnp.where(p == 0, far, near)
        left_x, right_x = swap(left, n, 2), swap(right, n, 2)
        left = norm_half(table, gain, left, left_x, False)
        right = norm_half(table, gain, right, right_x, False)
        halo = [jnp.where(c == 0, left, right), swap(jnp.where(c == 0, right, left), n, 1)]
        own = norm_half(table, gain, stem, stem_x)
        other = norm_half(table, gain, pair, swap(pair, n, 2))
        layered = [own, swap(own, n, 1), other, swap(other, n, 1)] + halo
        whole = lax.all_gather(qkv_weight, "tm", axis=0, tiled=True)
        grouped = jnp.stack([weight_group(whole, g) for g in range(4)])
        weights = [lax.dynamic_index_in_dim(grouped, group, 0, keepdims=False)]
        weights = [jnp.pad(weights[0], ((0, 0), (0, HD)))]
        depth = whole.shape[0]
        packed = jnp.stack([token_group(dec_queries, stretch_mask, g) for g in range(4)])
        every = lax.all_gather(packed, "tm", axis=0)
        every = lax.dynamic_index_in_dim(every, group, 1, keepdims=False)
        every = jnp.take(every, jnp.arange(0, n, 2, dtype=jnp.int32) ^ me, axis=0)
        every = every.reshape(n // 2, 6, 2, HD).transpose(1, 0, 2, 3).reshape(6, n, HD).astype(F32)
        asked = every[5]
        tokens = jnp.concatenate(
            [jnp.pad(every[h] * 0.125, ((0, 0), (HD * h, GROUP - HD - HD * h))) for h in range(5)]
        )
        marks = lax.all_gather(segment_ids, "tm", axis=0, tiled=True).astype(F32)
        marks = jnp.pad(marks, (512, 512))
        marks = lax.dynamic_slice_in_dim(marks, 512 * quarter, 1536, 0)
        ids = jnp.broadcast_to(marks[None], (8, 1536))
    held, stay, leave = encoder(table, layered, ids, weights, depth)

    partial = cross_partial(base, table, tokens, asked, held, swap(held, n, 1))
    owned = [partial[0]] + [swap(partial[i], n, 8 * i) for i in range(1, n // 8)]

    got = []
    for turn, rows in enumerate((stay, leave)):
        route = [
            (
                8 * (d // 8) + 4 * (d // 4 % 2) + (d & 2) + (d & 1),
                8 * (d // 8) + 4 * (d & 1) + ((d & 2) ^ (2 * turn)) + (d // 4 % 2),
            )
            for d in range(n)
        ]
        got.append(after(send(rows, route), owned[1]))
    memory = gather_groups(7, 128, table, got + [swap(part, n, 1) for part in got])

    final = merge(owned)
    final = [final[0]] + [swap(final[i], n, 2 * i) for i in (1, 2, 3)]
    cross_out = gather_groups(5, 2, table, final)
    return (memory, cross_out)


def solution(mesh):
    placed = (
        P(("utt", "tm"), None),
        P(),
        P("tm", None),
        P(("utt", "tm")),
        P(("utt", "tm"), None),
        P(("utt", "tm"), None),
    )
    return jax.shard_map(
        on_device,
        mesh=mesh,
        in_specs=placed,
        out_specs=(P(("utt", "tm"), None), P(("utt", "tm"), None)),
        check_vma=False,
    )
```

```python
import functools

import jax
import jax.numpy as jnp
from jax import lax
from jax.experimental import pallas as pl
from jax.experimental.pallas import tpu as pltpu
from jax.sharding import PartitionSpec as P

HD = 64
WIDE = 256
GROUP = 320
BF = jnp.bfloat16
F32 = jnp.float32
LOW = -1e30
CHEAP = pl.CostEstimate(flops=1, bytes_accessed=1, transcendentals=0)
VMEM = pl.BlockSpec(memory_space=pltpu.VMEM)
SMEM = pl.BlockSpec(memory_space=pltpu.SMEM)


def send(block, route):
    return lax.ppermute(block, "tm", route)


def swap(block, n, mask):
    return send(block, [(d, d ^ mask) for d in range(n)])


def after(value, *awaited):
    return lax.optimization_barrier((value, *awaited))[0]


def scalars(values):
    return jnp.stack([jnp.asarray(v, jnp.int32) for v in values])


def group_of(array, g):
    return array[:, WIDE * g : WIDE * g + WIDE], array[:, 1024 + HD * g : 1024 + HD * g + HD]


def weight_group(weight, g):
    width = weight.shape[1] // 3
    parts = [group_of(weight[:, i * width : (i + 1) * width], g) for i in range(3)]
    (q0, q1), (k0, k1), (v0, v1) = parts
    return jnp.concatenate([q0, k0, v0, k1, v1, q1], axis=1)


def token_group(queries, mask, g):
    wide, tail = group_of(queries, g)
    heads = [wide[:, HD * i : HD * i + HD] for i in range(4)] + [tail]
    asked = jnp.pad(mask.astype(BF), ((0, 0), (0, HD - mask.shape[1])))
    return jnp.concatenate(heads + [asked], axis=0)


def pack_kernel(table, *refs):
    mine, theirs = refs[4:6]
    weight, queries, mask, segments = held = refs[6:10]
    copies = [pltpu.make_async_copy(refs[i], held[i], refs[10].at[i]) for i in range(4)]
    for copy in copies:
        copy.start()
    for copy in copies:
        copy.wait()
    rows, width = weight.shape[0], weight.shape[1] // 3
    blocks = mask.shape[1]
    ids = segments[...]
    digits = [lax.shift_right_logical(ids, 7).astype(F32), (ids & 127).astype(F32)]
    asked = mask[...].astype(F32)
    if blocks < HD:
        asked = jnp.concatenate([asked, jnp.zeros((2, HD - blocks), F32)], axis=1)
    rest = [asked] + [d[:, HD * i : HD * i + HD] for d in digits for i in range(2)]
    rest.append(jnp.zeros((rows - 16, HD), F32))
    for turn, outs in enumerate((mine, theirs)):
        column = table[6] if turn == 0 else 1 - table[6]
        for p in range(2):
            out = outs.at[p]
            wide = pl.multiple_of(WIDE * (2 * p + column), 128)
            tails = []
            for i in range(4):
                source = weight if i < 3 else queries
                at = width * i if i < 3 else 0
                slab = source[:, at + 1024 + 128 * p : at + 1152 + 128 * p].astype(F32)
                odd = jnp.broadcast_to(column, (slab.shape[0], HD)) == 1
                tails.append(jnp.where(odd, slab[:, HD:], slab[:, :HD]))
                if i < 3:
                    out[:, WIDE * i : WIDE * i + WIDE] = weight[
                        :, pl.ds(pl.multiple_of(at + wide, 128), WIDE)
                    ]
            out[:, 3 * WIDE : 896] = jnp.concatenate(tails[1:3], axis=1).astype(BF)
            asking = queries[:, pl.ds(wide, WIDE)].astype(F32)
            heads = [asking[:, HD * h : HD * h + HD] for h in range(4)] + [tails[3]]
            lanes = jnp.concatenate(heads + rest, axis=0)
            out[:, 896:] = jnp.concatenate([tails[0], lanes], axis=1).astype(BF)


def pack(table, weight, queries, mask, segments):
    shape = jax.ShapeDtypeStruct((2, weight.shape[0], 1024), BF)
    given = (weight, queries, mask, segments)
    return pl.pallas_call(
        pack_kernel,
        out_shape=(shape, shape),
        in_specs=[SMEM] + [pl.BlockSpec(memory_space=pl.ANY)] * 4,
        out_specs=(VMEM,) * 2,
        scratch_shapes=[pltpu.VMEM(a.shape, a.dtype) for a in given] + [pltpu.SemaphoreType.DMA((4,))],
        cost_estimate=CHEAP,
        compiler_params=pltpu.CompilerParams(vmem_limit_bytes=8 * 1024 * 1024),
    )(table, weight, queries, mask, segments)


def load_kernel(table, *refs):
    held, outs = refs[:4], refs[4:]
    x, c, p = table[6], table[7], table[5]
    own = jnp.broadcast_to(table[12], outs[0].shape) == 1
    flip_c = jnp.broadcast_to(c, (16, 128)) == 1
    flip_x = jnp.broadcast_to(x, (16, 128)) == 1
    for a in range(2):
        mine, mine_c, across, across_c = [h[pl.ds(p ^ a, 1)][0] for h in held]
        out = outs[a]
        out[...] = jnp.where(own, mine, across)
        lanes = [part[:16, 896:] for part in (mine, mine_c, across, across_c)]
        rows = []
        for first, second in (lanes[:2], lanes[2:]):
            rows.append((jnp.where(flip_c, second, first), jnp.where(flip_c, first, second)))
        low = [jnp.where(flip_x, there, here) for here, there in zip(*rows)]
        high = [jnp.where(flip_x, here, there) for here, there in zip(*rows)]
        lane = lax.broadcasted_iota(jnp.int32, (16, 128), 1)
        for j, found in enumerate(low + high):
            out[16 * j : 16 * j + 16, 896:] = jnp.where(
                lane < HD, out[16 * j : 16 * j + 16, 896:], found
            )


def load(table, *held):
    rows = held[0].shape[1]
    return pl.pallas_call(
        load_kernel,
        out_shape=(jax.ShapeDtypeStruct((rows, 1024), BF),) * 2,
        in_specs=[SMEM] + [VMEM] * 4,
        out_specs=(VMEM,) * 2,
        cost_estimate=CHEAP,
        compiler_params=pltpu.CompilerParams(vmem_limit_bytes=8 * 1024 * 1024),
    )(table, *held)


def norm_kernel(table, gain, here, across, out):
    group = table[4]
    for i, block in enumerate((here, across)):
        rows = slice(128 * i, 128 * i + 128)
        values = block[...].astype(F32)
        mean = jnp.mean(values, axis=-1, keepdims=True)
        centred = values - mean
        var = jnp.mean(centred * centred, axis=-1, keepdims=True)
        out[rows, :1280] = (centred * lax.rsqrt(var + 1e-05) * gain[...]).astype(BF)
        if out.shape[1] > 1280:
            out[rows, 1280 : 1280 + WIDE] = block[:, pl.ds(pl.multiple_of(group * WIDE, 128), WIDE)]
            slab = block[:, pl.ds(pl.multiple_of(1024 + group // 2 * 128, 128), 128)]
            odd = jnp.broadcast_to(lax.rem(group, 2), (128, HD)) == 1
            tail = jnp.where(odd, slab[:, HD:], slab[:, :HD])
            out[rows, 1280 + WIDE :] = jnp.concatenate([tail, jnp.zeros_like(tail)], axis=1)


def norm_half(table, gain, here, across, kept=True):
    return pl.pallas_call(
        norm_kernel,
        out_shape=jax.ShapeDtypeStruct((256, 1664 if kept else 1280), BF),
        in_specs=[SMEM] + [VMEM] * 3,
        out_specs=VMEM,
        cost_estimate=CHEAP,
        compiler_params=pltpu.CompilerParams(vmem_limit_bytes=8 * 1024 * 1024),
    )(table, gain, here, across)


def prepare_kernel(table, *refs):
    parts, (ids, tokens, asked, joined) = refs[:-4], refs[-4:]
    rows = joined.shape[0] // 3
    for i in range(3):
        joined[rows * i : rows * i + rows, :] = parts[i + 1][...]
    first, x, core, z = table[13], table[6], table[7], table[14]
    count = asked.shape[0]
    ids[...] = jnp.zeros_like(ids)
    tokens[...] = jnp.zeros_like(tokens)
    flip_c = jnp.broadcast_to(core, (2, HD)) == 1
    flip_x = jnp.broadcast_to(x, (2, HD)) == 1
    for turn, part in enumerate(parts):
        lanes = part[:64, 896:].astype(F32)[:, HD:]
        for h in range(6):
            rows = [lanes[16 * j + 2 * h : 16 * j + 2 * h + 2] for j in range(4)]
            low = jnp.where(flip_c, rows[1], rows[0])
            high = jnp.where(flip_c, rows[3], rows[2])
            for dx in range(2):
                found = jnp.where(flip_x, low, high) if dx else jnp.where(flip_x, high, low)
                at = 4 * turn + 2 * dx
                if h < 5:
                    tokens[count * h + at : count * h + at + 2, HD * h : HD * h + HD] = found * 0.125
                else:
                    asked[at : at + 2, :] = found
        for j in range(4):
            marks = lanes[16 * j + 12 : 16 * j + 14] * 128.0 + lanes[16 * j + 14 : 16 * j + 16]
            block = 4 * (z ^ turn) + j - first

            @pl.when((block >= 0) & (block < 12))
            def _():
                ids[0:1, pl.ds(pl.multiple_of(block * 128, 128), 128)] = jnp.concatenate(
                    [marks[0:1], marks[1:2]], axis=1
                )


def prepare(table, parts, count):
    return pl.pallas_call(
        prepare_kernel,
        out_shape=(
            jax.ShapeDtypeStruct((8, 1536), F32),
            jax.ShapeDtypeStruct((5 * count, GROUP), F32),
            jax.ShapeDtypeStruct((count, HD), F32),
            jax.ShapeDtypeStruct((3 * parts[0].shape[0], 1024), BF),
        ),
        in_specs=[SMEM] + [VMEM] * len(parts),
        out_specs=(VMEM,) * 4,
        cost_estimate=CHEAP,
        compiler_params=pltpu.CompilerParams(vmem_limit_bytes=8 * 1024 * 1024),
    )(table, *parts)


def encoder_kernel(n_parts, depth, places, *refs):
    layers = [refs[2 * i : 2 * i + 2] for i in range(3)]
    ids = refs[6]
    parts = refs[7 : 7 + n_parts]
    memory, near, away, weight, residual, queries, keys, values = refs[7 + n_parts :]
    x = places[6]
    at = 15
    for part in parts:
        rows = [part[pl.ds(places[5], 1)][0]] if len(part.shape) == 3 else [
            part[s * depth : s * depth + depth, :] for s in range(part.shape[0] // depth)
        ]
        for found in rows:
            weight[pl.ds(pl.multiple_of(places[at] * depth, 16), depth), :] = found
            at += 1

    for slab in range(3):
        values[:, 256 * slab + 128 : 256 * slab + 256] = jnp.ones((1536, 128), BF)
    spots = [places[i] for i in (0, 2, 1, 3)]
    for i, halves in enumerate(layers):
        place = places[8 + i]
        normed = jnp.concatenate([half[:, :1280] for half in halves], axis=0)
        found = jnp.dot(normed, weight[:, 256:896], preferred_element_type=F32).astype(BF)
        for j, spot in enumerate(spots):
            to = pl.ds(pl.multiple_of(place + spot, 128), 128)
            block = found[128 * j : 128 * j + 128]
            keys[to, :256] = block[:, :256]
            keys[to, 256:] = block[:, 512:]
            for slab in range(3):
                values[to, 256 * slab : 256 * slab + 128] = block[:, 256 + 128 * slab : 384 + 128 * slab]
        if i < 2:

            @pl.when(place == 512)
            def _():
                normed = jnp.concatenate([half[:, :1280] for half in halves], axis=0)
                wide = jnp.dot(normed, weight[:, :WIDE], preferred_element_type=F32).astype(BF)
                tail = jnp.dot(normed, weight[:, 896:], preferred_element_type=F32).astype(BF)
                lane = lax.broadcasted_iota(jnp.int32, tail.shape, 1)
                tail = jnp.where(lane < HD, tail, jnp.zeros_like(tail))
                for j, spot in enumerate(spots):
                    to = pl.ds(pl.multiple_of(spot, 128), 128)
                    rows = slice(128 * j, 128 * j + 128)
                    queries[to, :WIDE] = wide[rows]
                    queries[to, WIDE:] = tail[rows]
                    residual[to, :] = halves[j // 2][128 * (j % 2) : 128 * (j % 2) + 128, 1280:]

    side = lax.broadcasted_iota(jnp.int32, (8, 128), 0) == lax.broadcasted_iota(
        jnp.int32, (8, 128), 1
    ) // HD
    sides = jnp.where(side, 1.0, 0.0).astype(BF)
    only = jnp.where(side & (lax.broadcasted_iota(jnp.int32, (8, 128), 0) == 0), 1.0, 0.0).astype(BF)
    most = []
    for held in (queries, keys):
        top = jnp.zeros((8, 1), F32)
        for slab in range(3):
            part = held[:, 128 * slab : 128 * slab + 128]
            norms = lax.dot_general(
                sides if slab < 2 else only,
                part * part,
                (((1,), (1,)), ((), ())),
                preferred_element_type=F32,
            )
            top = jnp.maximum(top, jnp.max(norms, axis=-1, keepdims=True))
        most.append(jnp.max(top))
    small = most[0] * most[1] < 220000.0

    def attend(step, shifted):
        row = step * 128 if isinstance(step, int) else pl.multiple_of(step * 128, 128)
        mine = jnp.broadcast_to(ids[0:1, pl.ds(row + 512, 128)], (128, 128)).T[:, 0:1]
        bias = jnp.where(mine == ids[0:1, pl.ds(row, 1152)], 0.0, LOW)
        lane = lax.broadcasted_iota(jnp.int32, (128, 128), 1)
        for slab in range(3):
            span = slice(128 * slab, 128 * slab + 128)
            query = queries[pl.ds(row, 128), span] * BF(0.125)
            mask = bias
            if slab < 2:
                none = jnp.zeros_like(query)
                query = jnp.concatenate(
                    [jnp.where(lane < HD, query, none), jnp.where(lane < HD, none, query)], axis=0
                )
                mask = jnp.concatenate([bias, bias], axis=0)
            scores = lax.dot_general(
                query,
                keys[pl.ds(row, 1152), span],
                (((1,), (1,)), ((), ())),
                preferred_element_type=F32,
            )
            scores = scores + mask
            if shifted:
                scores = scores - jnp.max(scores, axis=-1, keepdims=True)
            raised = jnp.exp(scores).astype(BF)
            out = jnp.dot(
                raised,
                values[pl.ds(row, 1152), 256 * slab : 256 * slab + 256],
                preferred_element_type=F32,
            )
            out = out[:, :128] / out[:, 128:]
            if slab < 2:
                context = jnp.where(lane < HD, out[:128], out[128:])
                stem = residual[pl.ds(row, 128), span].astype(F32)
                memory[pl.ds(row, 128), span] = (stem + context).astype(BF)
            else:
                stem = residual[pl.ds(row, 128), WIDE:GROUP].astype(F32)
                memory[pl.ds(row, 128), WIDE:] = (stem + out[:, HD:]).astype(BF)

    @pl.when(small)
    def _():
        for step in range(4):
            attend(step, False)

    @pl.when(jnp.logical_not(small))
    def _():
        lax.fori_loop(0, 4, lambda step, carry: (attend(step, True), carry)[1], 0)

    near[...] = memory[pl.ds(pl.multiple_of(256 * x, 256), 256), :]
    away[...] = memory[pl.ds(pl.multiple_of(256 * (1 - x), 256), 256), :]


def encoder(places, layers, ids, parts, depth):
    operands = layers + [ids] + parts
    return pl.pallas_call(
        functools.partial(encoder_kernel, len(parts), depth),
        out_shape=(
            jax.ShapeDtypeStruct((512, GROUP), BF),
            jax.ShapeDtypeStruct((256, GROUP), BF),
            jax.ShapeDtypeStruct((256, GROUP), BF),
        ),
        in_specs=[SMEM] + [VMEM] * len(operands),
        out_specs=(VMEM, VMEM, VMEM),
        scratch_shapes=[
            pltpu.VMEM((1280, 1024), BF),
            pltpu.VMEM((512, 384), BF),
            pltpu.VMEM((512, 384), BF),
            pltpu.VMEM((1536, 384), BF),
            pltpu.VMEM((1536, 768), BF),
        ],
        cost_estimate=CHEAP,
        compiler_params=pltpu.CompilerParams(vmem_limit_bytes=24 * 1024 * 1024),
    )(places, *operands)


def cross_kernel(base, table, tokens, asked, memory, beside, *refs):
    outs, out = refs[:-1], refs[-1]
    count = asked.shape[0]
    me = table[base + 2]
    spot = lax.broadcasted_iota(jnp.int32, (count, HD), 1)
    order = lax.broadcasted_iota(jnp.int32, (count, 1), 0)
    owner = (order // 2 * 2) ^ me
    bias = []
    for half in range(2):
        for b in range(4):
            block = table[base + half] + b
            ask = jnp.sum(jnp.where(spot == block, asked[...], 0.0), axis=-1, keepdims=True)
            allowed = (ask > 0.5) | (owner == block)
            bias.append(jnp.broadcast_to(jnp.where(allowed, 0.0, LOW), (count, 128)))
    bias = jnp.concatenate(bias, axis=1)
    bias = jnp.concatenate([bias] * 5, axis=0)
    query = tokens[...].astype(BF)
    cross = jnp.concatenate(
        [
            lax.dot_general(
                query, held[...], (((1,), (1,)), ((), ())), preferred_element_type=F32
            )
            for held in (memory, beside)
        ],
        axis=1,
    )
    cross = jnp.where(bias < 0.0, LOW, cross)
    top = jnp.max(cross, axis=-1, keepdims=True)
    raised = jnp.where(bias < 0.0, 0.0, jnp.exp(cross - top))
    den = jnp.sum(raised, axis=-1, keepdims=True)
    raised = raised.astype(BF)
    out[...] = jnp.dot(raised[:, :512], memory[...], preferred_element_type=F32) + jnp.dot(
        raised[:, 512:], beside[...], preferred_element_type=F32
    )
    lane = lax.broadcasted_iota(jnp.int32, (count, HD), 1)
    for h in range(5):
        rows = slice(count * h, count * h + count)
        stats = jnp.where(lane == 0, top[rows], den[rows])
        both = jnp.concatenate([out[rows, HD * h : HD * h + HD], stats], axis=1)
        for i, owned in enumerate(outs):
            owned[8 * h : 8 * h + 8, :] = both[8 * i : 8 * i + 8]


def cross_partial(base, table, tokens, asked, memory, beside):
    count = asked.shape[0]
    return pl.pallas_call(
        functools.partial(cross_kernel, base),
        out_shape=(jax.ShapeDtypeStruct((40, 128), F32),) * (count // 8),
        in_specs=[SMEM] + [VMEM] * 4,
        out_specs=(VMEM,) * (count // 8),
        scratch_shapes=[pltpu.VMEM((5 * count, GROUP), F32)],
        cost_estimate=CHEAP,
        compiler_params=pltpu.CompilerParams(vmem_limit_bytes=12 * 1024 * 1024),
    )(table, tokens, asked, memory, beside)


def merge_kernel(*refs):
    parts, outs, out = refs[:-5], refs[-5:-1], refs[-1]
    tops = [part[:, HD : HD + 1] for part in parts]
    best = functools.reduce(jnp.maximum, tops)
    total = jnp.zeros((40, 128), F32)
    for top, part in zip(tops, parts):
        total = total + jnp.exp(top - best) * part[...]
    final = total[:, :HD] / total[:, HD + 1 : HD + 2]
    heads = [final[8 * h : 8 * h + 8] for h in range(5)] + [jnp.zeros((8, HD), F32)]
    for slab in range(3):
        out[:, 128 * slab : 128 * slab + 128] = jnp.concatenate(heads[2 * slab : 2 * slab + 2], axis=1)
    for i in range(4):
        outs[i][...] = out[2 * i : 2 * i + 2, :].astype(BF)


def merge(parts):
    return pl.pallas_call(
        merge_kernel,
        out_shape=(jax.ShapeDtypeStruct((2, 384), BF),) * 4,
        in_specs=[VMEM] * len(parts),
        out_specs=(VMEM,) * 4,
        scratch_shapes=[pltpu.VMEM((8, 384), F32)],
        cost_estimate=CHEAP,
        compiler_params=pltpu.CompilerParams(vmem_limit_bytes=4 * 1024 * 1024),
    )(*parts)


def gather_kernel(side, rows, table, *refs):
    pieces, out = refs[:4], refs[4]
    high, x = table[side], table[6]
    start = pl.multiple_of(rows * high, rows) if pieces[0].shape[0] > rows else 0
    flip = jnp.broadcast_to(x, (rows, HD)) == 1
    held = [piece[pl.ds(start, rows), :] for piece in pieces]
    for i, piece in enumerate(held):
        group = (2 * high + x) ^ i
        out[:, pl.ds(pl.multiple_of(WIDE * group, 128), WIDE)] = piece[:, :WIDE]
    for i in range(2):
        first, second = [piece[:, WIDE:GROUP] for piece in held[2 * i : 2 * i + 2]]
        tail = jnp.concatenate([jnp.where(flip, second, first), jnp.where(flip, first, second)], axis=1)
        out[:, pl.ds(pl.multiple_of(1024 + 128 * (high ^ i), 128), 128)] = tail


def gather_groups(side, rows, table, pieces):
    return pl.pallas_call(
        functools.partial(gather_kernel, side, rows),
        out_shape=jax.ShapeDtypeStruct((rows, 1280), BF),
        in_specs=[SMEM] + [VMEM] * 4,
        out_specs=VMEM,
        cost_estimate=CHEAP,
        compiler_params=pltpu.CompilerParams(vmem_limit_bytes=4 * 1024 * 1024),
    )(table, *pieces)


def on_device(stem, norm_gain, qkv_weight, segment_ids, dec_queries, stretch_mask):
    n = lax.axis_size("tm")
    layers = n // 4
    me = lax.axis_index("tm")
    z, x, c = me // 4, (me // 2) % 2, me % 2
    p, k = z % 2, z // 2
    quarter = 2 * k + c
    group = 2 * p + x
    depth = qkv_weight.shape[0]

    utts = lax.axis_size("utt")
    moved = lax.axis_index("utt") % 2
    direct = depth % 16 == 0 and layers == 4 and utts % 2 == 0
    gain = norm_gain.reshape(1, -1)
    table = [128 * (2 * x + c), 128 * (2 * x + 1 - c), 128 * (2 - 2 * x + c), 128 * (3 - 2 * x - c)]
    table += [group, p, x, c]
    table += [512 * (p - c + 1), 512 * (2 - p - c), 1024 * c, 0, x == moved, 4 * quarter - 4, z]
    sources = [me, me ^ 1, me ^ 2, me ^ 3] if direct else [jnp.int32(0)]
    for side in (2 * moved, 2 - 2 * moved) if direct else ():
        for core in (c, 1 - c):
            sources += [4 * (z ^ turn) + side + core for turn in (1, 2, 3)]
    table = scalars(table + sources + [4 * quarter, 4 * (quarter ^ 1), me])
    base = 15 + len(sources)

    steps = [1 if i % 2 else -1 for i in range(layers)]
    near_route = [
        (4 * i + j, 4 * (i + s) + j)
        for i, s in enumerate(steps)
        for j in range(4)
        if 0 <= i + s < layers
    ]
    near = send(stem, near_route)
    pair = swap(stem, n, 4)
    if direct:
        def trade(block):
            return lax.ppermute(block, "utt", [(u, u ^ 1) for u in range(utts)])

        mine, theirs = pack(
            table, qkv_weight, dec_queries, stretch_mask, segment_ids.reshape(1, -1)
        )
        across = swap(theirs, n, 2)
        mine_c, across_c = swap(mine, n, 1), swap(across, n, 1)
        ready = load(table, mine, mine_c, after(across, near, pair), across_c)
        relayed = swap(after(near, ready[0]), n, 4)
        stem_x = swap(after(stem, across), n, 2)
        here = {turn: swap(ready[turn % 2], n, 4 * turn) for turn in (3, 2, 1)}
        pair_x = swap(after(pair, ready[0]), n, 2)
        halo = jnp.where((z == 1) | (z == 2), near, relayed)
        halo_x = swap(after(halo, pair_x), n, 2)
        ids, tokens, asked, joined = prepare(table, [ready[0], here[1], here[2], here[3]], n)
        traded = trade(joined)
        own_half = norm_half(table, gain, stem, stem_x)
        pair_half = norm_half(table, gain, pair, pair_x)
        halo_half = norm_half(table, gain, halo, halo_x, False)
        own_c, pair_c = swap(own_half, n, 1), swap(pair_half, n, 1)
        layered = [own_half, own_c, pair_half, pair_c, halo_half, swap(halo_half, n, 1)]
        weights = [mine, mine_c, across, across_c, joined, swap(joined, n, 1)]
        weights += [traded, swap(after(traded, own_c, pair_c), n, 1)]
    else:
        stem_x = swap(stem, n, 2)
        far = swap(near, n, 4)
        left = jnp.where(p == 0, near, far)
        right = jnp.where(p == 0, far, near)
        left_x, right_x = swap(left, n, 2), swap(right, n, 2)
        left = norm_half(table, gain, left, left_x, False)
        right = norm_half(table, gain, right, right_x, False)
        halo = [jnp.where(c == 0, left, right), swap(jnp.where(c == 0, right, left), n, 1)]
        own = norm_half(table, gain, stem, stem_x)
        other = norm_half(table, gain, pair, swap(pair, n, 2))
        layered = [own, swap(own, n, 1), other, swap(other, n, 1)] + halo
        whole = lax.all_gather(qkv_weight, "tm", axis=0, tiled=True)
        grouped = jnp.stack([weight_group(whole, g) for g in range(4)])
        weights = [lax.dynamic_index_in_dim(grouped, group, 0, keepdims=False)]
        weights = [jnp.pad(weights[0], ((0, 0), (0, HD)))]
        depth = whole.shape[0]
        packed = jnp.stack([token_group(dec_queries, stretch_mask, g) for g in range(4)])
        every = lax.all_gather(packed, "tm", axis=0)
        every = lax.dynamic_index_in_dim(every, group, 1, keepdims=False)
        every = jnp.take(every, jnp.arange(0, n, 2, dtype=jnp.int32) ^ me, axis=0)
        every = every.reshape(n // 2, 6, 2, HD).transpose(1, 0, 2, 3).reshape(6, n, HD).astype(F32)
        asked = every[5]
        tokens = jnp.concatenate(
            [jnp.pad(every[h] * 0.125, ((0, 0), (HD * h, GROUP - HD - HD * h))) for h in range(5)]
        )
        marks = lax.all_gather(segment_ids, "tm", axis=0, tiled=True).astype(F32)
        marks = jnp.pad(marks, (512, 512))
        marks = lax.dynamic_slice_in_dim(marks, 512 * quarter, 1536, 0)
        ids = jnp.broadcast_to(marks[None], (8, 1536))
    held, stay, leave = encoder(table, layered, ids, weights, depth)

    partial = cross_partial(base, table, tokens, asked, held, swap(held, n, 1))
    owned = [partial[0]] + [swap(partial[i], n, 8 * i) for i in range(1, n // 8)]

    got = []
    for turn, rows in enumerate((stay, leave)):
        route = [
            (
                8 * (d // 8) + 4 * (d // 4 % 2) + (d & 2) + (d & 1),
                8 * (d // 8) + 4 * (d & 1) + ((d & 2) ^ (2 * turn)) + (d // 4 % 2),
            )
            for d in range(n)
        ]
        got.append(after(send(rows, route), owned[1]))
    memory = gather_groups(7, 128, table, got + [swap(part, n, 1) for part in got])

    final = merge(owned)
    final = [final[0]] + [swap(final[i], n, 2 * i) for i in (1, 2, 3)]
    final[0] = after(final[0], memory)
    cross_out = gather_groups(5, 2, table, final)
    return (memory, cross_out)


def solution(mesh):
    placed = (
        P(("utt", "tm"), None),
        P(),
        P("tm", None),
        P(("utt", "tm")),
        P(("utt", "tm"), None),
        P(("utt", "tm"), None),
    )
    return jax.shard_map(
        on_device,
        mesh=mesh,
        in_specs=placed,
        out_specs=(P(("utt", "tm"), None), P(("utt", "tm"), None)),
        check_vma=False,
    )
```

```python
import functools

import jax
import jax.numpy as jnp
from jax import lax
from jax.experimental import pallas as pl
from jax.experimental.pallas import tpu as pltpu
from jax.sharding import PartitionSpec as P

HD = 64
WIDE = 256
GROUP = 320
BF = jnp.bfloat16
F32 = jnp.float32
LOW = -1e30
CHEAP = pl.CostEstimate(flops=1, bytes_accessed=1, transcendentals=0)
VMEM = pl.BlockSpec(memory_space=pltpu.VMEM)
SMEM = pl.BlockSpec(memory_space=pltpu.SMEM)


def send(block, route):
    return lax.ppermute(block, "tm", route)


def swap(block, n, mask):
    return send(block, [(d, d ^ mask) for d in range(n)])


def after(value, *awaited):
    return lax.optimization_barrier((value, *awaited))[0]


def scalars(values):
    return jnp.stack([jnp.asarray(v, jnp.int32) for v in values])


def group_of(array, g):
    return array[:, WIDE * g : WIDE * g + WIDE], array[:, 1024 + HD * g : 1024 + HD * g + HD]


def weight_group(weight, g):
    width = weight.shape[1] // 3
    parts = [group_of(weight[:, i * width : (i + 1) * width], g) for i in range(3)]
    (q0, q1), (k0, k1), (v0, v1) = parts
    return jnp.concatenate([q0, k0, v0, k1, v1, q1], axis=1)


def token_group(queries, mask, g):
    wide, tail = group_of(queries, g)
    heads = [wide[:, HD * i : HD * i + HD] for i in range(4)] + [tail]
    asked = jnp.pad(mask.astype(BF), ((0, 0), (0, HD - mask.shape[1])))
    return jnp.concatenate(heads + [asked], axis=0)


def pack_kernel(table, *refs):
    mine, theirs = refs[4:6]
    weight, queries, mask, segments = held = refs[6:10]
    copies = [pltpu.make_async_copy(refs[i], held[i], refs[10].at[i]) for i in range(4)]
    for copy in copies:
        copy.start()
    for copy in copies:
        copy.wait()
    rows, width = weight.shape[0], weight.shape[1] // 3
    blocks = mask.shape[1]
    ids = segments[...]
    digits = [lax.shift_right_logical(ids, 7).astype(F32), (ids & 127).astype(F32)]
    asked = mask[...].astype(F32)
    if blocks < HD:
        asked = jnp.concatenate([asked, jnp.zeros((2, HD - blocks), F32)], axis=1)
    rest = [asked] + [d[:, HD * i : HD * i + HD] for d in digits for i in range(2)]
    rest.append(jnp.zeros((rows - 16, HD), F32))
    for turn, outs in enumerate((mine, theirs)):
        column = table[6] if turn == 0 else 1 - table[6]
        for p in range(2):
            out = outs.at[p]
            wide = pl.multiple_of(WIDE * (2 * p + column), 128)
            tails = []
            for i in range(4):
                source = weight if i < 3 else queries
                at = width * i if i < 3 else 0
                slab = source[:, at + 1024 + 128 * p : at + 1152 + 128 * p].astype(F32)
                odd = jnp.broadcast_to(column, (slab.shape[0], HD)) == 1
                tails.append(jnp.where(odd, slab[:, HD:], slab[:, :HD]))
                if i < 3:
                    out[:, WIDE * i : WIDE * i + WIDE] = weight[
                        :, pl.ds(pl.multiple_of(at + wide, 128), WIDE)
                    ]
            out[:, 3 * WIDE : 896] = jnp.concatenate(tails[1:3], axis=1).astype(BF)
            asking = queries[:, pl.ds(wide, WIDE)].astype(F32)
            heads = [asking[:, HD * h : HD * h + HD] for h in range(4)] + [tails[3]]
            lanes = jnp.concatenate(heads + rest, axis=0)
            out[:, 896:] = jnp.concatenate([tails[0], lanes], axis=1).astype(BF)


def pack(table, weight, queries, mask, segments):
    shape = jax.ShapeDtypeStruct((2, weight.shape[0], 1024), BF)
    given = (weight, queries, mask, segments)
    return pl.pallas_call(
        pack_kernel,
        out_shape=(shape, shape),
        in_specs=[SMEM] + [pl.BlockSpec(memory_space=pl.ANY)] * 4,
        out_specs=(VMEM,) * 2,
        scratch_shapes=[pltpu.VMEM(a.shape, a.dtype) for a in given] + [pltpu.SemaphoreType.DMA((4,))],
        cost_estimate=CHEAP,
        compiler_params=pltpu.CompilerParams(vmem_limit_bytes=8 * 1024 * 1024),
    )(table, weight, queries, mask, segments)


def load_kernel(table, *refs):
    held, outs = refs[:4], refs[4:]
    x, c, p = table[6], table[7], table[5]
    own = jnp.broadcast_to(table[12], outs[0].shape) == 1
    flip_c = jnp.broadcast_to(c, (16, 128)) == 1
    flip_x = jnp.broadcast_to(x, (16, 128)) == 1
    for a in range(2):
        mine, mine_c, across, across_c = [h[pl.ds(p ^ a, 1)][0] for h in held]
        out = outs[a]
        out[...] = jnp.where(own, mine, across)
        lanes = [part[:16, 896:] for part in (mine, mine_c, across, across_c)]
        rows = []
        for first, second in (lanes[:2], lanes[2:]):
            rows.append((jnp.where(flip_c, second, first), jnp.where(flip_c, first, second)))
        low = [jnp.where(flip_x, there, here) for here, there in zip(*rows)]
        high = [jnp.where(flip_x, here, there) for here, there in zip(*rows)]
        lane = lax.broadcasted_iota(jnp.int32, (16, 128), 1)
        for j, found in enumerate(low + high):
            out[16 * j : 16 * j + 16, 896:] = jnp.where(
                lane < HD, out[16 * j : 16 * j + 16, 896:], found
            )


def load(table, *held):
    rows = held[0].shape[1]
    return pl.pallas_call(
        load_kernel,
        out_shape=(jax.ShapeDtypeStruct((rows, 1024), BF),) * 2,
        in_specs=[SMEM] + [VMEM] * 4,
        out_specs=(VMEM,) * 2,
        cost_estimate=CHEAP,
        compiler_params=pltpu.CompilerParams(vmem_limit_bytes=8 * 1024 * 1024),
    )(table, *held)


def norm_kernel(table, gain, here, across, out):
    group = table[4]
    for i, block in enumerate((here, across)):
        rows = slice(128 * i, 128 * i + 128)
        values = block[...].astype(F32)
        mean = jnp.mean(values, axis=-1, keepdims=True)
        centred = values - mean
        var = jnp.mean(centred * centred, axis=-1, keepdims=True)
        out[rows, :1280] = (centred * lax.rsqrt(var + 1e-05) * gain[...]).astype(BF)
        if out.shape[1] > 1280:
            out[rows, 1280 : 1280 + WIDE] = block[:, pl.ds(pl.multiple_of(group * WIDE, 128), WIDE)]
            slab = block[:, pl.ds(pl.multiple_of(1024 + group // 2 * 128, 128), 128)]
            odd = jnp.broadcast_to(lax.rem(group, 2), (128, HD)) == 1
            tail = jnp.where(odd, slab[:, HD:], slab[:, :HD])
            out[rows, 1280 + WIDE :] = jnp.concatenate([tail, jnp.zeros_like(tail)], axis=1)


def norm_half(table, gain, here, across, kept=True):
    return pl.pallas_call(
        norm_kernel,
        out_shape=jax.ShapeDtypeStruct((256, 1664 if kept else 1280), BF),
        in_specs=[SMEM] + [VMEM] * 3,
        out_specs=VMEM,
        cost_estimate=CHEAP,
        compiler_params=pltpu.CompilerParams(vmem_limit_bytes=8 * 1024 * 1024),
    )(table, gain, here, across)


def prepare_kernel(table, *refs):
    parts, (ids, tokens, asked, joined) = refs[:-4], refs[-4:]
    rows = joined.shape[0] // 3
    for i in range(3):
        joined[rows * i : rows * i + rows, :] = parts[i + 1][...]
    first, x, core, z = table[13], table[6], table[7], table[14]
    count = asked.shape[0]
    ids[...] = jnp.zeros_like(ids)
    tokens[...] = jnp.zeros_like(tokens)
    flip_c = jnp.broadcast_to(core, (2, HD)) == 1
    flip_x = jnp.broadcast_to(x, (2, HD)) == 1
    for turn, part in enumerate(parts):
        lanes = part[:64, 896:].astype(F32)[:, HD:]
        for h in range(6):
            rows = [lanes[16 * j + 2 * h : 16 * j + 2 * h + 2] for j in range(4)]
            low = jnp.where(flip_c, rows[1], rows[0])
            high = jnp.where(flip_c, rows[3], rows[2])
            for dx in range(2):
                found = jnp.where(flip_x, low, high) if dx else jnp.where(flip_x, high, low)
                at = 4 * turn + 2 * dx
                if h < 5:
                    tokens[count * h + at : count * h + at + 2, HD * h : HD * h + HD] = found * 0.125
                else:
                    asked[at : at + 2, :] = found
        for j in range(4):
            marks = lanes[16 * j + 12 : 16 * j + 14] * 128.0 + lanes[16 * j + 14 : 16 * j + 16]
            block = 4 * (z ^ turn) + j - first

            @pl.when((block >= 0) & (block < 12))
            def _():
                ids[0:1, pl.ds(pl.multiple_of(block * 128, 128), 128)] = jnp.concatenate(
                    [marks[0:1], marks[1:2]], axis=1
                )


def prepare(table, parts, count):
    return pl.pallas_call(
        prepare_kernel,
        out_shape=(
            jax.ShapeDtypeStruct((8, 1536), F32),
            jax.ShapeDtypeStruct((5 * count, GROUP), F32),
            jax.ShapeDtypeStruct((count, HD), F32),
            jax.ShapeDtypeStruct((3 * parts[0].shape[0], 1024), BF),
        ),
        in_specs=[SMEM] + [VMEM] * len(parts),
        out_specs=(VMEM,) * 4,
        cost_estimate=CHEAP,
        compiler_params=pltpu.CompilerParams(vmem_limit_bytes=8 * 1024 * 1024),
    )(table, *parts)


def encoder_kernel(n_parts, depth, places, *refs):
    layers = [refs[2 * i : 2 * i + 2] for i in range(3)]
    ids = refs[6]
    parts = refs[7 : 7 + n_parts]
    memory, near, away, weight, residual, queries, keys, values = refs[7 + n_parts :]
    x = places[6]
    at = 15
    for part in parts:
        rows = [part[pl.ds(places[5], 1)][0]] if len(part.shape) == 3 else [
            part[s * depth : s * depth + depth, :] for s in range(part.shape[0] // depth)
        ]
        for found in rows:
            weight[pl.ds(pl.multiple_of(places[at] * depth, 16), depth), :] = found
            at += 1

    for slab in range(3):
        values[:, 256 * slab + 128 : 256 * slab + 256] = jnp.ones((1536, 128), BF)
    spots = [places[i] for i in (0, 2, 1, 3)]
    for i, halves in enumerate(layers):
        place = places[8 + i]
        normed = jnp.concatenate([half[:, :1280] for half in halves], axis=0)
        found = jnp.dot(normed, weight[:, 256:896], preferred_element_type=F32).astype(BF)
        for j, spot in enumerate(spots):
            to = pl.ds(pl.multiple_of(place + spot, 128), 128)
            block = found[128 * j : 128 * j + 128]
            keys[to, :256] = block[:, :256]
            keys[to, 256:] = block[:, 512:]
            for slab in range(3):
                values[to, 256 * slab : 256 * slab + 128] = block[:, 256 + 128 * slab : 384 + 128 * slab]
        if i < 2:

            @pl.when(place == 512)
            def _():
                normed = jnp.concatenate([half[:, :1280] for half in halves], axis=0)
                wide = jnp.dot(normed, weight[:, :WIDE], preferred_element_type=F32).astype(BF)
                tail = jnp.dot(normed, weight[:, 896:], preferred_element_type=F32).astype(BF)
                lane = lax.broadcasted_iota(jnp.int32, tail.shape, 1)
                tail = jnp.where(lane < HD, tail, jnp.zeros_like(tail))
                for j, spot in enumerate(spots):
                    to = pl.ds(pl.multiple_of(spot, 128), 128)
                    rows = slice(128 * j, 128 * j + 128)
                    queries[to, :WIDE] = wide[rows]
                    queries[to, WIDE:] = tail[rows]
                    residual[to, :] = halves[j // 2][128 * (j % 2) : 128 * (j % 2) + 128, 1280:]

    side = lax.broadcasted_iota(jnp.int32, (8, 128), 0) == lax.broadcasted_iota(
        jnp.int32, (8, 128), 1
    ) // HD
    sides = jnp.where(side, 1.0, 0.0).astype(BF)
    only = jnp.where(side & (lax.broadcasted_iota(jnp.int32, (8, 128), 0) == 0), 1.0, 0.0).astype(BF)
    most = []
    for held in (queries, keys):
        top = jnp.zeros((8, 1), F32)
        for slab in range(3):
            part = held[:, 128 * slab : 128 * slab + 128]
            norms = lax.dot_general(
                sides if slab < 2 else only,
                part * part,
                (((1,), (1,)), ((), ())),
                preferred_element_type=F32,
            )
            top = jnp.maximum(top, jnp.max(norms, axis=-1, keepdims=True))
        most.append(jnp.max(top))
    small = most[0] * most[1] < 220000.0

    def attend(step, shifted):
        row = step * 128 if isinstance(step, int) else pl.multiple_of(step * 128, 128)
        mine = jnp.broadcast_to(ids[0:1, pl.ds(row + 512, 128)], (128, 128)).T[:, 0:1]
        bias = jnp.where(mine == ids[0:1, pl.ds(row, 1152)], 0.0, LOW)
        lane = lax.broadcasted_iota(jnp.int32, (128, 128), 1)
        for slab in range(3):
            span = slice(128 * slab, 128 * slab + 128)
            query = queries[pl.ds(row, 128), span] * BF(0.125)
            mask = bias
            if slab < 2:
                none = jnp.zeros_like(query)
                query = jnp.concatenate(
                    [jnp.where(lane < HD, query, none), jnp.where(lane < HD, none, query)], axis=0
                )
                mask = jnp.concatenate([bias, bias], axis=0)
            scores = lax.dot_general(
                query,
                keys[pl.ds(row, 1152), span],
                (((1,), (1,)), ((), ())),
                preferred_element_type=F32,
            )
            scores = scores + mask
            if shifted:
                scores = scores - jnp.max(scores, axis=-1, keepdims=True)
            raised = jnp.exp(scores).astype(BF)
            out = jnp.dot(
                raised,
                values[pl.ds(row, 1152), 256 * slab : 256 * slab + 256],
                preferred_element_type=F32,
            )
            out = out[:, :128] / out[:, 128:]
            if slab < 2:
                context = jnp.where(lane < HD, out[:128], out[128:])
                stem = residual[pl.ds(row, 128), span].astype(F32)
                memory[pl.ds(row, 128), span] = (stem + context).astype(BF)
            else:
                stem = residual[pl.ds(row, 128), WIDE:GROUP].astype(F32)
                memory[pl.ds(row, 128), WIDE:] = (stem + out[:, HD:]).astype(BF)

    @pl.when(small)
    def _():
        for step in range(4):
            attend(step, False)

    @pl.when(jnp.logical_not(small))
    def _():
        lax.fori_loop(0, 4, lambda step, carry: (attend(step, True), carry)[1], 0)

    near[...] = memory[pl.ds(pl.multiple_of(256 * x, 256), 256), :]
    away[...] = memory[pl.ds(pl.multiple_of(256 * (1 - x), 256), 256), :]


def encoder(places, layers, ids, parts, depth):
    operands = layers + [ids] + parts
    return pl.pallas_call(
        functools.partial(encoder_kernel, len(parts), depth),
        out_shape=(
            jax.ShapeDtypeStruct((512, GROUP), BF),
            jax.ShapeDtypeStruct((256, GROUP), BF),
            jax.ShapeDtypeStruct((256, GROUP), BF),
        ),
        in_specs=[SMEM] + [VMEM] * len(operands),
        out_specs=(VMEM, VMEM, VMEM),
        scratch_shapes=[
            pltpu.VMEM((1280, 1024), BF),
            pltpu.VMEM((512, 384), BF),
            pltpu.VMEM((512, 384), BF),
            pltpu.VMEM((1536, 384), BF),
            pltpu.VMEM((1536, 768), BF),
        ],
        cost_estimate=CHEAP,
        compiler_params=pltpu.CompilerParams(vmem_limit_bytes=24 * 1024 * 1024),
    )(places, *operands)


def cross_kernel(base, table, tokens, asked, memory, beside, *refs):
    outs, out = refs[:-1], refs[-1]
    count = asked.shape[0]
    me = table[base + 2]
    spot = lax.broadcasted_iota(jnp.int32, (count, HD), 1)
    order = lax.broadcasted_iota(jnp.int32, (count, 1), 0)
    owner = (order // 2 * 2) ^ me
    bias = []
    for half in range(2):
        for b in range(4):
            block = table[base + half] + b
            ask = jnp.sum(jnp.where(spot == block, asked[...], 0.0), axis=-1, keepdims=True)
            allowed = (ask > 0.5) | (owner == block)
            bias.append(jnp.broadcast_to(jnp.where(allowed, 0.0, LOW), (count, 128)))
    bias = jnp.concatenate(bias, axis=1)
    bias = jnp.concatenate([bias] * 5, axis=0)
    query = tokens[...].astype(BF)
    cross = jnp.concatenate(
        [
            lax.dot_general(
                query, held[...], (((1,), (1,)), ((), ())), preferred_element_type=F32
            )
            for held in (memory, beside)
        ],
        axis=1,
    )
    cross = jnp.where(bias < 0.0, LOW, cross)
    top = jnp.max(cross, axis=-1, keepdims=True)
    raised = jnp.where(bias < 0.0, 0.0, jnp.exp(cross - top))
    den = jnp.sum(raised, axis=-1, keepdims=True)
    raised = raised.astype(BF)
    out[...] = jnp.dot(raised[:, :512], memory[...], preferred_element_type=F32) + jnp.dot(
        raised[:, 512:], beside[...], preferred_element_type=F32
    )
    lane = lax.broadcasted_iota(jnp.int32, (count, HD), 1)
    for h in range(5):
        rows = slice(count * h, count * h + count)
        stats = jnp.where(lane == 0, top[rows], den[rows])
        both = jnp.concatenate([out[rows, HD * h : HD * h + HD], stats], axis=1)
        for i, owned in enumerate(outs):
            owned[8 * h : 8 * h + 8, :] = both[8 * i : 8 * i + 8]


def cross_partial(base, table, tokens, asked, memory, beside):
    count = asked.shape[0]
    return pl.pallas_call(
        functools.partial(cross_kernel, base),
        out_shape=(jax.ShapeDtypeStruct((40, 128), F32),) * (count // 8),
        in_specs=[SMEM] + [VMEM] * 4,
        out_specs=(VMEM,) * (count // 8),
        scratch_shapes=[pltpu.VMEM((5 * count, GROUP), F32)],
        cost_estimate=CHEAP,
        compiler_params=pltpu.CompilerParams(vmem_limit_bytes=12 * 1024 * 1024),
    )(table, tokens, asked, memory, beside)


def merge_kernel(*refs):
    parts, outs, out = refs[:-5], refs[-5:-1], refs[-1]
    tops = [part[:, HD : HD + 1] for part in parts]
    best = functools.reduce(jnp.maximum, tops)
    total = jnp.zeros((40, 128), F32)
    for top, part in zip(tops, parts):
        total = total + jnp.exp(top - best) * part[...]
    final = total[:, :HD] / total[:, HD + 1 : HD + 2]
    heads = [final[8 * h : 8 * h + 8] for h in range(5)] + [jnp.zeros((8, HD), F32)]
    for slab in range(3):
        out[:, 128 * slab : 128 * slab + 128] = jnp.concatenate(heads[2 * slab : 2 * slab + 2], axis=1)
    for i in range(4):
        outs[i][...] = out[2 * i : 2 * i + 2, :].astype(BF)


def merge(parts):
    return pl.pallas_call(
        merge_kernel,
        out_shape=(jax.ShapeDtypeStruct((2, 384), BF),) * 4,
        in_specs=[VMEM] * len(parts),
        out_specs=(VMEM,) * 4,
        scratch_shapes=[pltpu.VMEM((8, 384), F32)],
        cost_estimate=CHEAP,
        compiler_params=pltpu.CompilerParams(vmem_limit_bytes=4 * 1024 * 1024),
    )(*parts)


def gather_kernel(side, rows, table, *refs):
    pieces, out = refs[:4], refs[4]
    high, x = table[side], table[6]
    start = pl.multiple_of(rows * high, rows) if pieces[0].shape[0] > rows else 0
    flip = jnp.broadcast_to(x, (rows, HD)) == 1
    held = [piece[pl.ds(start, rows), :] for piece in pieces]
    for i, piece in enumerate(held):
        group = (2 * high + x) ^ i
        out[:, pl.ds(pl.multiple_of(WIDE * group, 128), WIDE)] = piece[:, :WIDE]
    for i in range(2):
        first, second = [piece[:, WIDE:GROUP] for piece in held[2 * i : 2 * i + 2]]
        tail = jnp.concatenate([jnp.where(flip, second, first), jnp.where(flip, first, second)], axis=1)
        out[:, pl.ds(pl.multiple_of(1024 + 128 * (high ^ i), 128), 128)] = tail


def gather_groups(side, rows, table, pieces):
    return pl.pallas_call(
        functools.partial(gather_kernel, side, rows),
        out_shape=jax.ShapeDtypeStruct((rows, 1280), BF),
        in_specs=[SMEM] + [VMEM] * 4,
        out_specs=VMEM,
        cost_estimate=CHEAP,
        compiler_params=pltpu.CompilerParams(vmem_limit_bytes=4 * 1024 * 1024),
    )(table, *pieces)


def on_device(stem, norm_gain, qkv_weight, segment_ids, dec_queries, stretch_mask):
    n = lax.axis_size("tm")
    layers = n // 4
    me = lax.axis_index("tm")
    z, x, c = me // 4, (me // 2) % 2, me % 2
    p, k = z % 2, z // 2
    quarter = 2 * k + c
    group = 2 * p + x
    depth = qkv_weight.shape[0]

    utts = lax.axis_size("utt")
    moved = lax.axis_index("utt") % 2
    direct = depth % 16 == 0 and layers == 4 and utts % 2 == 0
    gain = norm_gain.reshape(1, -1)
    table = [128 * (2 * x + c), 128 * (2 * x + 1 - c), 128 * (2 - 2 * x + c), 128 * (3 - 2 * x - c)]
    table += [group, p, x, c]
    table += [512 * (p - c + 1), 512 * (2 - p - c), 1024 * c, 0, x == moved, 4 * quarter - 4, z]
    sources = [me, me ^ 1, me ^ 2, me ^ 3] if direct else [jnp.int32(0)]
    for side in (2 * moved, 2 - 2 * moved) if direct else ():
        for core in (c, 1 - c):
            sources += [4 * (z ^ turn) + side + core for turn in (1, 2, 3)]
    table = scalars(table + sources + [4 * quarter, 4 * (quarter ^ 1), me])
    base = 15 + len(sources)

    steps = [1 if i % 2 else -1 for i in range(layers)]
    near_route = [
        (4 * i + j, 4 * (i + s) + j)
        for i, s in enumerate(steps)
        for j in range(4)
        if 0 <= i + s < layers
    ]
    near = send(stem, near_route)
    pair = swap(stem, n, 4)
    if direct:
        def trade(block):
            return lax.ppermute(block, "utt", [(u, u ^ 1) for u in range(utts)])

        mine, theirs = pack(
            table, qkv_weight, dec_queries, stretch_mask, segment_ids.reshape(1, -1)
        )
        across = swap(theirs, n, 2)
        mine_c, across_c = swap(mine, n, 1), swap(across, n, 1)
        ready = load(table, mine, mine_c, after(across, near, pair), across_c)
        relayed = swap(after(near, ready[0]), n, 4)
        stem_x = swap(after(stem, across), n, 2)
        here = {turn: swap(ready[turn % 2], n, 4 * turn) for turn in (3, 2, 1)}
        pair_x = swap(after(pair, ready[0]), n, 2)
        halo = jnp.where((z == 1) | (z == 2), near, relayed)
        halo_x = swap(after(halo, pair_x, *here.values()), n, 2)
        ids, tokens, asked, joined = prepare(table, [after(ready[0], halo), here[1], here[2], here[3]], n)
        traded = trade(joined)
        own_half = norm_half(table, gain, stem, stem_x)
        pair_half = norm_half(table, gain, pair, pair_x)
        halo_half = norm_half(table, gain, halo, halo_x, False)
        own_c, pair_c = swap(own_half, n, 1), swap(pair_half, n, 1)
        halo_c, joined_c = swap(after(halo_half, traded), n, 1), swap(joined, n, 1)
        layered = [own_half, own_c, pair_half, pair_c, halo_half, halo_c]
        weights = [mine, mine_c, across, across_c, joined, joined_c]
        weights += [traded, swap(after(traded, own_c, pair_c, joined_c), n, 1)]
    else:
        stem_x = swap(stem, n, 2)
        far = swap(near, n, 4)
        left = jnp.where(p == 0, near, far)
        right = jnp.where(p == 0, far, near)
        left_x, right_x = swap(left, n, 2), swap(right, n, 2)
        left = norm_half(table, gain, left, left_x, False)
        right = norm_half(table, gain, right, right_x, False)
        halo = [jnp.where(c == 0, left, right), swap(jnp.where(c == 0, right, left), n, 1)]
        own = norm_half(table, gain, stem, stem_x)
        other = norm_half(table, gain, pair, swap(pair, n, 2))
        layered = [own, swap(own, n, 1), other, swap(other, n, 1)] + halo
        whole = lax.all_gather(qkv_weight, "tm", axis=0, tiled=True)
        grouped = jnp.stack([weight_group(whole, g) for g in range(4)])
        weights = [lax.dynamic_index_in_dim(grouped, group, 0, keepdims=False)]
        weights = [jnp.pad(weights[0], ((0, 0), (0, HD)))]
        depth = whole.shape[0]
        packed = jnp.stack([token_group(dec_queries, stretch_mask, g) for g in range(4)])
        every = lax.all_gather(packed, "tm", axis=0)
        every = lax.dynamic_index_in_dim(every, group, 1, keepdims=False)
        every = jnp.take(every, jnp.arange(0, n, 2, dtype=jnp.int32) ^ me, axis=0)
        every = every.reshape(n // 2, 6, 2, HD).transpose(1, 0, 2, 3).reshape(6, n, HD).astype(F32)
        asked = every[5]
        tokens = jnp.concatenate(
            [jnp.pad(every[h] * 0.125, ((0, 0), (HD * h, GROUP - HD - HD * h))) for h in range(5)]
        )
        marks = lax.all_gather(segment_ids, "tm", axis=0, tiled=True).astype(F32)
        marks = jnp.pad(marks, (512, 512))
        marks = lax.dynamic_slice_in_dim(marks, 512 * quarter, 1536, 0)
        ids = jnp.broadcast_to(marks[None], (8, 1536))
    held, stay, leave = encoder(table, layered, ids, weights, depth)

    partial = cross_partial(base, table, tokens, asked, held, swap(held, n, 1))
    owned = [partial[0]] + [swap(partial[i], n, 8 * i) for i in range(1, n // 8)]

    got = []
    for turn, rows in enumerate((stay, leave)):
        route = [
            (
                8 * (d // 8) + 4 * (d // 4 % 2) + (d & 2) + (d & 1),
                8 * (d // 8) + 4 * (d & 1) + ((d & 2) ^ (2 * turn)) + (d // 4 % 2),
            )
            for d in range(n)
        ]
        got.append(after(send(rows, route), owned[1]))
    memory = gather_groups(7, 128, table, got + [swap(part, n, 1) for part in got])

    final = merge(owned)
    final = [final[0]] + [swap(final[i], n, 2 * i) for i in (1, 2, 3)]
    final[0] = after(final[0], memory)
    cross_out = gather_groups(5, 2, table, final)
    return (memory, cross_out)


def solution(mesh):
    placed = (
        P(("utt", "tm"), None),
        P(),
        P("tm", None),
        P(("utt", "tm")),
        P(("utt", "tm"), None),
        P(("utt", "tm"), None),
    )
    return jax.shard_map(
        on_device,
        mesh=mesh,
        in_specs=placed,
        out_specs=(P(("utt", "tm"), None), P(("utt", "tm"), None)),
        check_vma=False,
    )
```

```python
import functools

import jax
import jax.numpy as jnp
from jax import lax
from jax.experimental import pallas as pl
from jax.experimental.pallas import tpu as pltpu
from jax.sharding import PartitionSpec as P

HD = 64
WIDE = 256
GROUP = 320
BF = jnp.bfloat16
F32 = jnp.float32
LOW = -1e30
CHEAP = pl.CostEstimate(flops=1, bytes_accessed=1, transcendentals=0)
VMEM = pl.BlockSpec(memory_space=pltpu.VMEM)
SMEM = pl.BlockSpec(memory_space=pltpu.SMEM)


def send(block, route):
    return lax.ppermute(block, "tm", route)


def swap(block, n, mask):
    return send(block, [(d, d ^ mask) for d in range(n)])


def after(value, *awaited):
    return lax.optimization_barrier((value, *awaited))[0]


def scalars(values):
    return jnp.stack([jnp.asarray(v, jnp.int32) for v in values])


def group_of(array, g):
    return array[:, WIDE * g : WIDE * g + WIDE], array[:, 1024 + HD * g : 1024 + HD * g + HD]


def weight_group(weight, g):
    width = weight.shape[1] // 3
    parts = [group_of(weight[:, i * width : (i + 1) * width], g) for i in range(3)]
    (q0, q1), (k0, k1), (v0, v1) = parts
    return jnp.concatenate([q0, k0, v0, k1, v1, q1], axis=1)


def token_group(queries, mask, g):
    wide, tail = group_of(queries, g)
    heads = [wide[:, HD * i : HD * i + HD] for i in range(4)] + [tail]
    asked = jnp.pad(mask.astype(BF), ((0, 0), (0, HD - mask.shape[1])))
    return jnp.concatenate(heads + [asked], axis=0)


def pack_kernel(table, *refs):
    mine, theirs = refs[4:6]
    weight, queries, mask, segments = held = refs[6:10]
    copies = [pltpu.make_async_copy(refs[i], held[i], refs[10].at[i]) for i in range(4)]
    for copy in copies:
        copy.start()
    for copy in copies:
        copy.wait()
    rows, width = weight.shape[0], weight.shape[1] // 3
    blocks = mask.shape[1]
    ids = segments[...]
    digits = [lax.shift_right_logical(ids, 7).astype(F32), (ids & 127).astype(F32)]
    asked = mask[...].astype(F32)
    if blocks < HD:
        asked = jnp.concatenate([asked, jnp.zeros((2, HD - blocks), F32)], axis=1)
    rest = [asked] + [d[:, HD * i : HD * i + HD] for d in digits for i in range(2)]
    rest.append(jnp.zeros((rows - 16, HD), F32))
    for turn, outs in enumerate((mine, theirs)):
        column = table[6] if turn == 0 else 1 - table[6]
        for p in range(2):
            out = outs.at[p]
            wide = pl.multiple_of(WIDE * (2 * p + column), 128)
            tails = []
            for i in range(4):
                source = weight if i < 3 else queries
                at = width * i if i < 3 else 0
                slab = source[:, at + 1024 + 128 * p : at + 1152 + 128 * p].astype(F32)
                odd = jnp.broadcast_to(column, (slab.shape[0], HD)) == 1
                tails.append(jnp.where(odd, slab[:, HD:], slab[:, :HD]))
                if i < 3:
                    out[:, WIDE * i : WIDE * i + WIDE] = weight[
                        :, pl.ds(pl.multiple_of(at + wide, 128), WIDE)
                    ]
            out[:, 3 * WIDE : 896] = jnp.concatenate(tails[1:3], axis=1).astype(BF)
            asking = queries[:, pl.ds(wide, WIDE)].astype(F32)
            heads = [asking[:, HD * h : HD * h + HD] for h in range(4)] + [tails[3]]
            lanes = jnp.concatenate(heads + rest, axis=0)
            out[:, 896:] = jnp.concatenate([tails[0], lanes], axis=1).astype(BF)


def pack(table, weight, queries, mask, segments):
    shape = jax.ShapeDtypeStruct((2, weight.shape[0], 1024), BF)
    given = (weight, queries, mask, segments)
    return pl.pallas_call(
        pack_kernel,
        out_shape=(shape, shape),
        in_specs=[SMEM] + [pl.BlockSpec(memory_space=pl.ANY)] * 4,
        out_specs=(VMEM,) * 2,
        scratch_shapes=[pltpu.VMEM(a.shape, a.dtype) for a in given] + [pltpu.SemaphoreType.DMA((4,))],
        cost_estimate=CHEAP,
        compiler_params=pltpu.CompilerParams(vmem_limit_bytes=8 * 1024 * 1024),
    )(table, weight, queries, mask, segments)


def load_kernel(table, *refs):
    held, outs = refs[:4], refs[4:]
    x, c, p = table[6], table[7], table[5]
    own = jnp.broadcast_to(table[12], outs[0].shape) == 1
    flip_c = jnp.broadcast_to(c, (16, 128)) == 1
    flip_x = jnp.broadcast_to(x, (16, 128)) == 1
    for a in range(2):
        mine, mine_c, across, across_c = [h[pl.ds(p ^ a, 1)][0] for h in held]
        out = outs[a]
        out[...] = jnp.where(own, mine, across)
        lanes = [part[:16, 896:] for part in (mine, mine_c, across, across_c)]
        rows = []
        for first, second in (lanes[:2], lanes[2:]):
            rows.append((jnp.where(flip_c, second, first), jnp.where(flip_c, first, second)))
        low = [jnp.where(flip_x, there, here) for here, there in zip(*rows)]
        high = [jnp.where(flip_x, here, there) for here, there in zip(*rows)]
        lane = lax.broadcasted_iota(jnp.int32, (16, 128), 1)
        for j, found in enumerate(low + high):
            out[16 * j : 16 * j + 16, 896:] = jnp.where(
                lane < HD, out[16 * j : 16 * j + 16, 896:], found
            )


def load(table, *held):
    rows = held[0].shape[1]
    return pl.pallas_call(
        load_kernel,
        out_shape=(jax.ShapeDtypeStruct((rows, 1024), BF),) * 2,
        in_specs=[SMEM] + [VMEM] * 4,
        out_specs=(VMEM,) * 2,
        cost_estimate=CHEAP,
        compiler_params=pltpu.CompilerParams(vmem_limit_bytes=8 * 1024 * 1024),
    )(table, *held)


def norm_kernel(table, gain, here, across, out):
    group = table[4]
    for i, block in enumerate((here, across)):
        rows = slice(128 * i, 128 * i + 128)
        values = block[...].astype(F32)
        mean = jnp.mean(values, axis=-1, keepdims=True)
        centred = values - mean
        var = jnp.mean(centred * centred, axis=-1, keepdims=True)
        out[rows, :1280] = (centred * lax.rsqrt(var + 1e-05) * gain[...]).astype(BF)
        if out.shape[1] > 1280:
            out[rows, 1280 : 1280 + WIDE] = block[:, pl.ds(pl.multiple_of(group * WIDE, 128), WIDE)]
            slab = block[:, pl.ds(pl.multiple_of(1024 + group // 2 * 128, 128), 128)]
            odd = jnp.broadcast_to(lax.rem(group, 2), (128, HD)) == 1
            tail = jnp.where(odd, slab[:, HD:], slab[:, :HD])
            out[rows, 1280 + WIDE :] = jnp.concatenate([tail, jnp.zeros_like(tail)], axis=1)


def norm_half(table, gain, here, across, kept=True):
    return pl.pallas_call(
        norm_kernel,
        out_shape=jax.ShapeDtypeStruct((256, 1664 if kept else 1280), BF),
        in_specs=[SMEM] + [VMEM] * 3,
        out_specs=VMEM,
        cost_estimate=CHEAP,
        compiler_params=pltpu.CompilerParams(vmem_limit_bytes=8 * 1024 * 1024),
    )(table, gain, here, across)


def prepare_kernel(table, *refs):
    parts, (ids, tokens, asked, joined, spans) = refs[:-5], refs[-5:]
    rows = joined.shape[0] // 3
    for i in range(3):
        joined[rows * i : rows * i + rows, :] = parts[i + 1][...]
    first, x, core, z = table[13], table[6], table[7], table[14]
    count = asked.shape[0]
    ids[...] = jnp.zeros_like(ids)
    tokens[...] = jnp.zeros_like(tokens)
    flip_c = jnp.broadcast_to(core, (2, HD)) == 1
    flip_x = jnp.broadcast_to(x, (2, HD)) == 1
    for turn, part in enumerate(parts):
        lanes = part[:64, 896:].astype(F32)[:, HD:]
        for h in range(6):
            rows = [lanes[16 * j + 2 * h : 16 * j + 2 * h + 2] for j in range(4)]
            low = jnp.where(flip_c, rows[1], rows[0])
            high = jnp.where(flip_c, rows[3], rows[2])
            for dx in range(2):
                found = jnp.where(flip_x, low, high) if dx else jnp.where(flip_x, high, low)
                at = 4 * turn + 2 * dx
                if h < 5:
                    tokens[count * h + at : count * h + at + 2, HD * h : HD * h + HD] = found * 0.125
                else:
                    asked[at : at + 2, :] = found
        for j in range(4):
            marks = lanes[16 * j + 12 : 16 * j + 14] * 128.0 + lanes[16 * j + 14 : 16 * j + 16]
            block = 4 * (z ^ turn) + j - first

            @pl.when((block >= 0) & (block < 12))
            def _():
                ids[0:1, pl.ds(pl.multiple_of(block * 128, 128), 128)] = jnp.concatenate(
                    [marks[0:1], marks[1:2]], axis=1
                )

    row = ids[0:1, :]
    spot = lax.broadcasted_iota(jnp.int32, (1, 1536), 1).astype(F32)
    for i in range(4):
        own = ids[0:1, 512 + 128 * i : 640 + 128 * i]
        shared = (row >= jnp.min(own)) & (row <= jnp.max(own))
        low = jnp.min(jnp.where(shared, spot, 9999.0)).astype(jnp.int32) // 128
        high = jnp.max(jnp.where(shared, spot, 0.0)).astype(jnp.int32) // 128
        spans[2 * i] = low
        spans[2 * i + 1] = high - low + 1


def prepare(table, parts, count):
    return pl.pallas_call(
        prepare_kernel,
        out_shape=(
            jax.ShapeDtypeStruct((8, 1536), F32),
            jax.ShapeDtypeStruct((5 * count, GROUP), F32),
            jax.ShapeDtypeStruct((count, HD), F32),
            jax.ShapeDtypeStruct((3 * parts[0].shape[0], 1024), BF),
            jax.ShapeDtypeStruct((8,), jnp.int32),
        ),
        in_specs=[SMEM] + [VMEM] * len(parts),
        out_specs=(VMEM,) * 4 + (SMEM,),
        cost_estimate=CHEAP,
        compiler_params=pltpu.CompilerParams(vmem_limit_bytes=8 * 1024 * 1024),
    )(table, *parts)


def encoder_kernel(n_parts, depth, places, spans, *refs):
    layers = [refs[2 * i : 2 * i + 2] for i in range(3)]
    ids = refs[6]
    parts = refs[7 : 7 + n_parts]
    memory, near, away, weight, residual, queries, keys, values = refs[7 + n_parts :]
    x = places[6]
    at = 15
    for part in parts:
        rows = [part[pl.ds(places[5], 1)][0]] if len(part.shape) == 3 else [
            part[s * depth : s * depth + depth, :] for s in range(part.shape[0] // depth)
        ]
        for found in rows:
            weight[pl.ds(pl.multiple_of(places[at] * depth, 16), depth), :] = found
            at += 1

    for slab in range(3):
        values[:, 256 * slab + 128 : 256 * slab + 256] = jnp.ones((1536, 128), BF)
    spots = [places[i] for i in (0, 2, 1, 3)]
    largest = [jnp.zeros((1, 256), F32), jnp.zeros((1, 128), F32)]
    for i, halves in enumerate(layers):
        place = places[8 + i]
        normed = jnp.concatenate([half[:, :1280] for half in halves], axis=0)
        found = jnp.dot(normed, weight[:, 256:896], preferred_element_type=F32)
        for j, lanes in enumerate((slice(0, 256), slice(512, 640))):
            largest[j] = jnp.maximum(
                largest[j], jnp.max(jnp.abs(found[:, lanes]), axis=0, keepdims=True)
            )
        found = found.astype(BF)
        for j, spot in enumerate(spots):
            to = pl.ds(pl.multiple_of(place + spot, 128), 128)
            block = found[128 * j : 128 * j + 128]
            keys[to, :256] = block[:, :256]
            keys[to, 256:] = block[:, 512:]
            for slab in range(3):
                values[to, 256 * slab : 256 * slab + 128] = block[:, 256 + 128 * slab : 384 + 128 * slab]
        if i < 2:

            @pl.when(place == 512)
            def _():
                normed = jnp.concatenate([half[:, :1280] for half in halves], axis=0)
                wide = jnp.dot(normed, weight[:, :WIDE], preferred_element_type=F32).astype(BF)
                tail = jnp.dot(normed, weight[:, 896:], preferred_element_type=F32).astype(BF)
                lane = lax.broadcasted_iota(jnp.int32, tail.shape, 1)
                tail = jnp.where(lane < HD, tail, jnp.zeros_like(tail))
                for j, spot in enumerate(spots):
                    to = pl.ds(pl.multiple_of(spot, 128), 128)
                    rows = slice(128 * j, 128 * j + 128)
                    queries[to, :WIDE] = wide[rows]
                    queries[to, WIDE:] = tail[rows]
                    residual[to, :] = halves[j // 2][128 * (j % 2) : 128 * (j % 2) + 128, 1280:]

    lane = lax.broadcasted_iota(jnp.int32, (8, 384), 1) // HD
    head = lax.broadcasted_iota(jnp.int32, (8, 384), 0)
    most = jnp.concatenate(largest, axis=1) * 1.01
    most = jnp.where((lane == head) & (head < 5), most, 0.0).astype(BF)
    bounds = lax.dot_general(
        most, jnp.abs(queries[...]), (((1,), (1,)), ((), ())), preferred_element_type=F32
    )
    small = jnp.max(bounds) < 480.0

    def attend(step, blocks, shifted):
        count = 128 * blocks
        start = pl.multiple_of(128 * jnp.minimum(spans[2 * step], 12 - blocks), 128)
        row = step * 128 if isinstance(step, int) else pl.multiple_of(step * 128, 128)
        mine = jnp.broadcast_to(ids[0:1, pl.ds(row + 512, 128)], (128, 128)).T[:, 0:1]
        bias = jnp.where(mine == ids[0:1, pl.ds(start, count)], 0.0, LOW)
        lane = lax.broadcasted_iota(jnp.int32, (128, 128), 1)
        for slab in range(3):
            span = slice(128 * slab, 128 * slab + 128)
            query = queries[pl.ds(row, 128), span] * BF(0.125)
            mask = bias
            if slab < 2:
                none = jnp.zeros_like(query)
                query = jnp.concatenate(
                    [jnp.where(lane < HD, query, none), jnp.where(lane < HD, none, query)], axis=0
                )
                mask = jnp.concatenate([bias, bias], axis=0)
            scores = lax.dot_general(
                query,
                keys[pl.ds(start, count), span],
                (((1,), (1,)), ((), ())),
                preferred_element_type=F32,
            )
            scores = scores + mask
            if shifted:
                scores = scores - jnp.max(scores, axis=-1, keepdims=True)
            raised = jnp.exp(scores).astype(BF)
            out = jnp.dot(
                raised,
                values[pl.ds(start, count), 256 * slab : 256 * slab + 256],
                preferred_element_type=F32,
            )
            out = out[:, :128] / out[:, 128:]
            if slab < 2:
                context = jnp.where(lane < HD, out[:128], out[128:])
                stem = residual[pl.ds(row, 128), span].astype(F32)
                memory[pl.ds(row, 128), span] = (stem + context).astype(BF)
            else:
                stem = residual[pl.ds(row, 128), WIDE:GROUP].astype(F32)
                memory[pl.ds(row, 128), WIDE:] = (stem + out[:, HD:]).astype(BF)

    for step in range(4):
        needed = spans[2 * step + 1]
        for least, blocks in ((0, 5), (5, 7), (7, 9)):

            @pl.when(small & (needed > least) & ((needed <= blocks) | (blocks == 9)))
            def _():
                attend(step, blocks, False)

    @pl.when(jnp.logical_not(small))
    def _():
        lax.fori_loop(0, 4, lambda step, carry: (attend(step, 9, True), carry)[1], 0)

    near[...] = memory[pl.ds(pl.multiple_of(256 * x, 256), 256), :]
    away[...] = memory[pl.ds(pl.multiple_of(256 * (1 - x), 256), 256), :]


def encoder(places, spans, layers, ids, parts, depth):
    operands = layers + [ids] + parts
    return pl.pallas_call(
        functools.partial(encoder_kernel, len(parts), depth),
        out_shape=(
            jax.ShapeDtypeStruct((512, GROUP), BF),
            jax.ShapeDtypeStruct((256, GROUP), BF),
            jax.ShapeDtypeStruct((256, GROUP), BF),
        ),
        in_specs=[SMEM] * 2 + [VMEM] * len(operands),
        out_specs=(VMEM, VMEM, VMEM),
        scratch_shapes=[
            pltpu.VMEM((1280, 1024), BF),
            pltpu.VMEM((512, 384), BF),
            pltpu.VMEM((512, 384), BF),
            pltpu.VMEM((1536, 384), BF),
            pltpu.VMEM((1536, 768), BF),
        ],
        cost_estimate=CHEAP,
        compiler_params=pltpu.CompilerParams(vmem_limit_bytes=24 * 1024 * 1024),
    )(places, spans, *operands)


def cross_kernel(base, table, tokens, asked, memory, beside, *refs):
    outs, out = refs[:-1], refs[-1]
    count = asked.shape[0]
    me = table[base + 2]
    spot = lax.broadcasted_iota(jnp.int32, (count, HD), 1)
    order = lax.broadcasted_iota(jnp.int32, (count, 1), 0)
    owner = (order // 2 * 2) ^ me
    bias = []
    for half in range(2):
        for b in range(4):
            block = table[base + half] + b
            ask = jnp.sum(jnp.where(spot == block, asked[...], 0.0), axis=-1, keepdims=True)
            allowed = (ask > 0.5) | (owner == block)
            bias.append(jnp.broadcast_to(jnp.where(allowed, 0.0, LOW), (count, 128)))
    bias = jnp.concatenate(bias, axis=1)
    bias = jnp.concatenate([bias] * 5, axis=0)
    query = tokens[...].astype(BF)
    cross = jnp.concatenate(
        [
            lax.dot_general(
                query, held[...], (((1,), (1,)), ((), ())), preferred_element_type=F32
            )
            for held in (memory, beside)
        ],
        axis=1,
    )
    cross = jnp.where(bias < 0.0, LOW, cross)
    top = jnp.max(cross, axis=-1, keepdims=True)
    raised = jnp.where(bias < 0.0, 0.0, jnp.exp(cross - top))
    den = jnp.sum(raised, axis=-1, keepdims=True)
    raised = raised.astype(BF)
    out[...] = jnp.dot(raised[:, :512], memory[...], preferred_element_type=F32) + jnp.dot(
        raised[:, 512:], beside[...], preferred_element_type=F32
    )
    lane = lax.broadcasted_iota(jnp.int32, (count, HD), 1)
    for h in range(5):
        rows = slice(count * h, count * h + count)
        stats = jnp.where(lane == 0, top[rows], den[rows])
        both = jnp.concatenate([out[rows, HD * h : HD * h + HD], stats], axis=1)
        for i, owned in enumerate(outs):
            owned[8 * h : 8 * h + 8, :] = both[8 * i : 8 * i + 8]


def cross_partial(base, table, tokens, asked, memory, beside):
    count = asked.shape[0]
    return pl.pallas_call(
        functools.partial(cross_kernel, base),
        out_shape=(jax.ShapeDtypeStruct((40, 128), F32),) * (count // 8),
        in_specs=[SMEM] + [VMEM] * 4,
        out_specs=(VMEM,) * (count // 8),
        scratch_shapes=[pltpu.VMEM((5 * count, GROUP), F32)],
        cost_estimate=CHEAP,
        compiler_params=pltpu.CompilerParams(vmem_limit_bytes=12 * 1024 * 1024),
    )(table, tokens, asked, memory, beside)


def merge_kernel(*refs):
    parts, outs, out = refs[:-5], refs[-5:-1], refs[-1]
    tops = [part[:, HD : HD + 1] for part in parts]
    best = functools.reduce(jnp.maximum, tops)
    total = jnp.zeros((40, 128), F32)
    for top, part in zip(tops, parts):
        total = total + jnp.exp(top - best) * part[...]
    final = total[:, :HD] / total[:, HD + 1 : HD + 2]
    heads = [final[8 * h : 8 * h + 8] for h in range(5)] + [jnp.zeros((8, HD), F32)]
    for slab in range(3):
        out[:, 128 * slab : 128 * slab + 128] = jnp.concatenate(heads[2 * slab : 2 * slab + 2], axis=1)
    for i in range(4):
        outs[i][...] = out[2 * i : 2 * i + 2, :].astype(BF)


def merge(parts):
    return pl.pallas_call(
        merge_kernel,
        out_shape=(jax.ShapeDtypeStruct((2, 384), BF),) * 4,
        in_specs=[VMEM] * len(parts),
        out_specs=(VMEM,) * 4,
        scratch_shapes=[pltpu.VMEM((8, 384), F32)],
        cost_estimate=CHEAP,
        compiler_params=pltpu.CompilerParams(vmem_limit_bytes=4 * 1024 * 1024),
    )(*parts)


def gather_kernel(side, rows, table, *refs):
    pieces, out = refs[:4], refs[4]
    high, x = table[side], table[6]
    start = pl.multiple_of(rows * high, rows) if pieces[0].shape[0] > rows else 0
    flip = jnp.broadcast_to(x, (rows, HD)) == 1
    held = [piece[pl.ds(start, rows), :] for piece in pieces]
    for i, piece in enumerate(held):
        group = (2 * high + x) ^ i
        out[:, pl.ds(pl.multiple_of(WIDE * group, 128), WIDE)] = piece[:, :WIDE]
    for i in range(2):
        first, second = [piece[:, WIDE:GROUP] for piece in held[2 * i : 2 * i + 2]]
        tail = jnp.concatenate([jnp.where(flip, second, first), jnp.where(flip, first, second)], axis=1)
        out[:, pl.ds(pl.multiple_of(1024 + 128 * (high ^ i), 128), 128)] = tail


def gather_groups(side, rows, table, pieces):
    return pl.pallas_call(
        functools.partial(gather_kernel, side, rows),
        out_shape=jax.ShapeDtypeStruct((rows, 1280), BF),
        in_specs=[SMEM] + [VMEM] * 4,
        out_specs=VMEM,
        cost_estimate=CHEAP,
        compiler_params=pltpu.CompilerParams(vmem_limit_bytes=4 * 1024 * 1024),
    )(table, *pieces)


def on_device(stem, norm_gain, qkv_weight, segment_ids, dec_queries, stretch_mask):
    n = lax.axis_size("tm")
    layers = n // 4
    me = lax.axis_index("tm")
    z, x, c = me // 4, (me // 2) % 2, me % 2
    p, k = z % 2, z // 2
    quarter = 2 * k + c
    group = 2 * p + x
    depth = qkv_weight.shape[0]

    utts = lax.axis_size("utt")
    moved = lax.axis_index("utt") % 2
    direct = depth % 16 == 0 and layers == 4 and utts % 2 == 0
    gain = norm_gain.reshape(1, -1)
    table = [128 * (2 * x + c), 128 * (2 * x + 1 - c), 128 * (2 - 2 * x + c), 128 * (3 - 2 * x - c)]
    table += [group, p, x, c]
    table += [512 * (p - c + 1), 512 * (2 - p - c), 1024 * c, 0, x == moved, 4 * quarter - 4, z]
    sources = [me, me ^ 1, me ^ 2, me ^ 3] if direct else [jnp.int32(0)]
    for side in (2 * moved, 2 - 2 * moved) if direct else ():
        for core in (c, 1 - c):
            sources += [4 * (z ^ turn) + side + core for turn in (1, 2, 3)]
    table = scalars(table + sources + [4 * quarter, 4 * (quarter ^ 1), me])
    base = 15 + len(sources)

    steps = [1 if i % 2 else -1 for i in range(layers)]
    near_route = [
        (4 * i + j, 4 * (i + s) + j)
        for i, s in enumerate(steps)
        for j in range(4)
        if 0 <= i + s < layers
    ]
    near = send(stem, near_route)
    pair = swap(stem, n, 4)
    if direct:
        def trade(block):
            return lax.ppermute(block, "utt", [(u, u ^ 1) for u in range(utts)])

        mine, theirs = pack(
            table, qkv_weight, dec_queries, stretch_mask, segment_ids.reshape(1, -1)
        )
        across = swap(theirs, n, 2)
        mine_c, across_c = swap(mine, n, 1), swap(across, n, 1)
        ready = load(table, mine, mine_c, after(across, near, pair), across_c)
        relayed = swap(after(near, ready[0]), n, 4)
        stem_x = swap(after(stem, across), n, 2)
        here = {turn: swap(ready[turn % 2], n, 4 * turn) for turn in (3, 2, 1)}
        pair_x = swap(after(pair, ready[0]), n, 2)
        halo = jnp.where((z == 1) | (z == 2), near, relayed)
        halo_x = swap(after(halo, pair_x, *here.values()), n, 2)
        ids, tokens, asked, joined, spans = prepare(table, [after(ready[0], halo), here[1], here[2], here[3]], n)
        traded = trade(joined)
        own_half = norm_half(table, gain, stem, stem_x)
        pair_half = norm_half(table, gain, pair, pair_x)
        halo_half = norm_half(table, gain, halo, halo_x, False)
        own_c, pair_c = swap(own_half, n, 1), swap(pair_half, n, 1)
        halo_c, joined_c = swap(after(halo_half, traded), n, 1), swap(joined, n, 1)
        layered = [own_half, own_c, pair_half, pair_c, halo_half, halo_c]
        weights = [mine, mine_c, across, across_c, joined, joined_c]
        weights += [traded, swap(after(traded, own_c, pair_c, joined_c), n, 1)]
    else:
        stem_x = swap(stem, n, 2)
        far = swap(near, n, 4)
        left = jnp.where(p == 0, near, far)
        right = jnp.where(p == 0, far, near)
        left_x, right_x = swap(left, n, 2), swap(right, n, 2)
        left = norm_half(table, gain, left, left_x, False)
        right = norm_half(table, gain, right, right_x, False)
        halo = [jnp.where(c == 0, left, right), swap(jnp.where(c == 0, right, left), n, 1)]
        own = norm_half(table, gain, stem, stem_x)
        other = norm_half(table, gain, pair, swap(pair, n, 2))
        layered = [own, swap(own, n, 1), other, swap(other, n, 1)] + halo
        whole = lax.all_gather(qkv_weight, "tm", axis=0, tiled=True)
        grouped = jnp.stack([weight_group(whole, g) for g in range(4)])
        weights = [lax.dynamic_index_in_dim(grouped, group, 0, keepdims=False)]
        weights = [jnp.pad(weights[0], ((0, 0), (0, HD)))]
        depth = whole.shape[0]
        packed = jnp.stack([token_group(dec_queries, stretch_mask, g) for g in range(4)])
        every = lax.all_gather(packed, "tm", axis=0)
        every = lax.dynamic_index_in_dim(every, group, 1, keepdims=False)
        every = jnp.take(every, jnp.arange(0, n, 2, dtype=jnp.int32) ^ me, axis=0)
        every = every.reshape(n // 2, 6, 2, HD).transpose(1, 0, 2, 3).reshape(6, n, HD).astype(F32)
        asked = every[5]
        tokens = jnp.concatenate(
            [jnp.pad(every[h] * 0.125, ((0, 0), (HD * h, GROUP - HD - HD * h))) for h in range(5)]
        )
        marks = lax.all_gather(segment_ids, "tm", axis=0, tiled=True).astype(F32)
        marks = jnp.pad(marks, (512, 512))
        marks = lax.dynamic_slice_in_dim(marks, 512 * quarter, 1536, 0)
        ids = jnp.broadcast_to(marks[None], (8, 1536))
        spans = scalars([0, 9, 1, 9, 2, 9, 3, 9])
    held, stay, leave = encoder(table, spans, layered, ids, weights, depth)

    partial = cross_partial(base, table, tokens, asked, held, swap(held, n, 1))
    owned = [partial[0]] + [swap(partial[i], n, 8 * i) for i in range(1, n // 8)]

    got = []
    for turn, rows in enumerate((stay, leave)):
        route = [
            (
                8 * (d // 8) + 4 * (d // 4 % 2) + (d & 2) + (d & 1),
                8 * (d // 8) + 4 * (d & 1) + ((d & 2) ^ (2 * turn)) + (d // 4 % 2),
            )
            for d in range(n)
        ]
        got.append(after(send(rows, route), owned[1]))
    memory = gather_groups(7, 128, table, got + [swap(part, n, 1) for part in got])

    final = merge(owned)
    final = [final[0]] + [swap(final[i], n, 2 * i) for i in (1, 2, 3)]
    final[0] = after(final[0], memory)
    cross_out = gather_groups(5, 2, table, final)
    return (memory, cross_out)


def solution(mesh):
    placed = (
        P(("utt", "tm"), None),
        P(),
        P("tm", None),
        P(("utt", "tm")),
        P(("utt", "tm"), None),
        P(("utt", "tm"), None),
    )
    return jax.shard_map(
        on_device,
        mesh=mesh,
        in_specs=placed,
        out_specs=(P(("utt", "tm"), None), P(("utt", "tm"), None)),
        check_vma=False,
    )
```

```python
import functools

import jax
import jax.numpy as jnp
from jax import lax
from jax.experimental import pallas as pl
from jax.experimental.pallas import tpu as pltpu
from jax.sharding import PartitionSpec as P

HD = 64
WIDE = 256
GROUP = 320
BF = jnp.bfloat16
F32 = jnp.float32
LOW = -1e30
CHEAP = pl.CostEstimate(flops=1, bytes_accessed=1, transcendentals=0)
VMEM = pl.BlockSpec(memory_space=pltpu.VMEM)
SMEM = pl.BlockSpec(memory_space=pltpu.SMEM)


def send(block, route):
    return lax.ppermute(block, "tm", route)


def swap(block, n, mask):
    return send(block, [(d, d ^ mask) for d in range(n)])


def after(value, *awaited):
    return lax.optimization_barrier((value, *awaited))[0]


def scalars(values):
    return jnp.stack([jnp.asarray(v, jnp.int32) for v in values])


def group_of(array, g):
    return array[:, WIDE * g : WIDE * g + WIDE], array[:, 1024 + HD * g : 1024 + HD * g + HD]


def weight_group(weight, g):
    width = weight.shape[1] // 3
    parts = [group_of(weight[:, i * width : (i + 1) * width], g) for i in range(3)]
    (q0, q1), (k0, k1), (v0, v1) = parts
    return jnp.concatenate([q0, k0, v0, k1, v1, q1], axis=1)


def token_group(queries, mask, g):
    wide, tail = group_of(queries, g)
    heads = [wide[:, HD * i : HD * i + HD] for i in range(4)] + [tail]
    asked = jnp.pad(mask.astype(BF), ((0, 0), (0, HD - mask.shape[1])))
    return jnp.concatenate(heads + [asked], axis=0)


def pack_kernel(table, *refs):
    mine, theirs = refs[4:6]
    weight, queries, mask, segments = held = refs[6:10]
    copies = [pltpu.make_async_copy(refs[i], held[i], refs[10].at[i]) for i in range(4)]
    for copy in copies:
        copy.start()
    for copy in copies:
        copy.wait()
    rows, width = weight.shape[0], weight.shape[1] // 3
    blocks = mask.shape[1]
    ids = segments[...]
    digits = [lax.shift_right_logical(ids, 7).astype(F32), (ids & 127).astype(F32)]
    asked = mask[...].astype(F32)
    if blocks < HD:
        asked = jnp.concatenate([asked, jnp.zeros((2, HD - blocks), F32)], axis=1)
    rest = [asked] + [d[:, HD * i : HD * i + HD] for d in digits for i in range(2)]
    rest.append(jnp.zeros((rows - 16, HD), F32))
    for turn, outs in enumerate((mine, theirs)):
        column = table[6] if turn == 0 else 1 - table[6]
        for p in range(2):
            out = outs.at[p]
            wide = pl.multiple_of(WIDE * (2 * p + column), 128)
            tails = []
            for i in range(4):
                source = weight if i < 3 else queries
                at = width * i if i < 3 else 0
                slab = source[:, at + 1024 + 128 * p : at + 1152 + 128 * p].astype(F32)
                odd = jnp.broadcast_to(column, (slab.shape[0], HD)) == 1
                tails.append(jnp.where(odd, slab[:, HD:], slab[:, :HD]))
                if i < 3:
                    out[:, WIDE * i : WIDE * i + WIDE] = weight[
                        :, pl.ds(pl.multiple_of(at + wide, 128), WIDE)
                    ]
            out[:, 3 * WIDE : 896] = jnp.concatenate(tails[1:3], axis=1).astype(BF)
            asking = queries[:, pl.ds(wide, WIDE)].astype(F32)
            heads = [asking[:, HD * h : HD * h + HD] for h in range(4)] + [tails[3]]
            lanes = jnp.concatenate(heads + rest, axis=0)
            out[:, 896:] = jnp.concatenate([tails[0], lanes], axis=1).astype(BF)


def pack(table, weight, queries, mask, segments):
    shape = jax.ShapeDtypeStruct((2, weight.shape[0], 1024), BF)
    given = (weight, queries, mask, segments)
    return pl.pallas_call(
        pack_kernel,
        out_shape=(shape, shape),
        in_specs=[SMEM] + [pl.BlockSpec(memory_space=pl.ANY)] * 4,
        out_specs=(VMEM,) * 2,
        scratch_shapes=[pltpu.VMEM(a.shape, a.dtype) for a in given] + [pltpu.SemaphoreType.DMA((4,))],
        cost_estimate=CHEAP,
        compiler_params=pltpu.CompilerParams(vmem_limit_bytes=8 * 1024 * 1024),
    )(table, weight, queries, mask, segments)


def load_kernel(table, *refs):
    held, outs = refs[:4], refs[4:]
    x, c, p = table[6], table[7], table[5]
    own = jnp.broadcast_to(table[12], outs[0].shape) == 1
    flip_c = jnp.broadcast_to(c, (16, 128)) == 1
    flip_x = jnp.broadcast_to(x, (16, 128)) == 1
    for a in range(2):
        mine, mine_c, across, across_c = [h[pl.ds(p ^ a, 1)][0] for h in held]
        out = outs[a]
        out[...] = jnp.where(own, mine, across)
        lanes = [part[:16, 896:] for part in (mine, mine_c, across, across_c)]
        rows = []
        for first, second in (lanes[:2], lanes[2:]):
            rows.append((jnp.where(flip_c, second, first), jnp.where(flip_c, first, second)))
        low = [jnp.where(flip_x, there, here) for here, there in zip(*rows)]
        high = [jnp.where(flip_x, here, there) for here, there in zip(*rows)]
        lane = lax.broadcasted_iota(jnp.int32, (16, 128), 1)
        for j, found in enumerate(low + high):
            out[16 * j : 16 * j + 16, 896:] = jnp.where(
                lane < HD, out[16 * j : 16 * j + 16, 896:], found
            )


def load(table, *held):
    rows = held[0].shape[1]
    return pl.pallas_call(
        load_kernel,
        out_shape=(jax.ShapeDtypeStruct((rows, 1024), BF),) * 2,
        in_specs=[SMEM] + [VMEM] * 4,
        out_specs=(VMEM,) * 2,
        cost_estimate=CHEAP,
        compiler_params=pltpu.CompilerParams(vmem_limit_bytes=8 * 1024 * 1024),
    )(table, *held)


def norm_kernel(table, gain, here, across, out):
    group = table[4]
    for i, block in enumerate((here, across)):
        rows = slice(128 * i, 128 * i + 128)
        values = block[...].astype(F32)
        mean = jnp.mean(values, axis=-1, keepdims=True)
        centred = values - mean
        var = jnp.mean(centred * centred, axis=-1, keepdims=True)
        out[rows, :1280] = (centred * lax.rsqrt(var + 1e-05) * gain[...]).astype(BF)
        if out.shape[1] > 1280:
            out[rows, 1280 : 1280 + WIDE] = block[:, pl.ds(pl.multiple_of(group * WIDE, 128), WIDE)]
            slab = block[:, pl.ds(pl.multiple_of(1024 + group // 2 * 128, 128), 128)]
            odd = jnp.broadcast_to(lax.rem(group, 2), (128, HD)) == 1
            tail = jnp.where(odd, slab[:, HD:], slab[:, :HD])
            out[rows, 1280 + WIDE :] = jnp.concatenate([tail, jnp.zeros_like(tail)], axis=1)


def norm_half(table, gain, here, across, kept=True):
    return pl.pallas_call(
        norm_kernel,
        out_shape=jax.ShapeDtypeStruct((256, 1664 if kept else 1280), BF),
        in_specs=[SMEM] + [VMEM] * 3,
        out_specs=VMEM,
        cost_estimate=CHEAP,
        compiler_params=pltpu.CompilerParams(vmem_limit_bytes=8 * 1024 * 1024),
    )(table, gain, here, across)


def prepare_kernel(table, *refs):
    first_part, joined, (ids, tokens, asked) = refs[0], refs[1], refs[2:]
    depth = joined.shape[0] // 3
    first, x, core, z = table[13], table[6], table[7], table[14]
    count = asked.shape[0]
    ids[...] = jnp.zeros_like(ids)
    tokens[...] = jnp.zeros_like(tokens)
    flip_c = jnp.broadcast_to(core, (2, HD)) == 1
    flip_x = jnp.broadcast_to(x, (2, HD)) == 1
    for turn in range(4):
        top = depth * (turn - 1)
        part = joined[top : top + 64, 896:] if turn else first_part[:64, 896:]
        lanes = part.astype(F32)[:, HD:]
        for h in range(6):
            rows = [lanes[16 * j + 2 * h : 16 * j + 2 * h + 2] for j in range(4)]
            low = jnp.where(flip_c, rows[1], rows[0])
            high = jnp.where(flip_c, rows[3], rows[2])
            for dx in range(2):
                found = jnp.where(flip_x, low, high) if dx else jnp.where(flip_x, high, low)
                at = 4 * turn + 2 * dx
                if h < 5:
                    tokens[count * h + at : count * h + at + 2, HD * h : HD * h + HD] = found * 0.125
                else:
                    asked[at : at + 2, :] = found
        for j in range(4):
            marks = lanes[16 * j + 12 : 16 * j + 14] * 128.0 + lanes[16 * j + 14 : 16 * j + 16]
            block = 4 * (z ^ turn) + j - first

            @pl.when((block >= 0) & (block < 12))
            def _():
                ids[0:1, pl.ds(pl.multiple_of(block * 128, 128), 128)] = jnp.concatenate(
                    [marks[0:1], marks[1:2]], axis=1
                )


def prepare(table, own, joined, count):
    return pl.pallas_call(
        prepare_kernel,
        out_shape=(
            jax.ShapeDtypeStruct((8, 1536), F32),
            jax.ShapeDtypeStruct((5 * count, GROUP), F32),
            jax.ShapeDtypeStruct((count, HD), F32),
        ),
        in_specs=[SMEM] + [VMEM] * 2,
        out_specs=(VMEM,) * 3,
        cost_estimate=CHEAP,
        compiler_params=pltpu.CompilerParams(vmem_limit_bytes=8 * 1024 * 1024),
    )(table, own, joined)


def join_kernel(*refs):
    parts, out = refs[:-1], refs[-1]
    rows = parts[0].shape[0]
    for i, part in enumerate(parts):
        out[rows * i : rows * i + rows, :] = part[...]


def join(parts):
    rows = parts[0].shape[0]
    return pl.pallas_call(
        join_kernel,
        out_shape=jax.ShapeDtypeStruct((rows * len(parts), 1024), BF),
        in_specs=[VMEM] * len(parts),
        out_specs=VMEM,
        cost_estimate=CHEAP,
        compiler_params=pltpu.CompilerParams(vmem_limit_bytes=4 * 1024 * 1024),
    )(*parts)


def encoder_kernel(n_parts, depth, places, *refs):
    layers = [refs[2 * i : 2 * i + 2] for i in range(3)]
    ids = refs[6]
    parts = refs[7 : 7 + n_parts]
    memory, near, away, weight, residual, queries, keys, values = refs[7 + n_parts :]
    x = places[6]
    at = 15
    for part in parts:
        rows = [part[pl.ds(places[5], 1)][0]] if len(part.shape) == 3 else [
            part[s * depth : s * depth + depth, :] for s in range(part.shape[0] // depth)
        ]
        for found in rows:
            weight[pl.ds(pl.multiple_of(places[at] * depth, 16), depth), :] = found
            at += 1

    for slab in range(3):
        values[:, 256 * slab + 128 : 256 * slab + 256] = jnp.ones((1536, 128), BF)
    spots = [places[i] for i in (0, 2, 1, 3)]
    largest = [jnp.zeros((1, 256), F32), jnp.zeros((1, 128), F32)]
    for i, halves in enumerate(layers):
        place = places[8 + i]
        normed = jnp.concatenate([half[:, :1280] for half in halves], axis=0)
        found = jnp.dot(normed, weight[:, 256:896], preferred_element_type=F32)
        for j, lanes in enumerate((slice(0, 256), slice(512, 640))):
            largest[j] = jnp.maximum(
                largest[j], jnp.max(jnp.abs(found[:, lanes]), axis=0, keepdims=True)
            )
        found = found.astype(BF)
        for j, spot in enumerate(spots):
            to = pl.ds(pl.multiple_of(place + spot, 128), 128)
            block = found[128 * j : 128 * j + 128]
            keys[to, :256] = block[:, :256]
            keys[to, 256:] = block[:, 512:]
            for slab in range(3):
                values[to, 256 * slab : 256 * slab + 128] = block[:, 256 + 128 * slab : 384 + 128 * slab]
        if i < 2:

            @pl.when(place == 512)
            def _():
                normed = jnp.concatenate([half[:, :1280] for half in halves], axis=0)
                wide = jnp.dot(normed, weight[:, :WIDE], preferred_element_type=F32).astype(BF)
                tail = jnp.dot(normed, weight[:, 896:], preferred_element_type=F32).astype(BF)
                lane = lax.broadcasted_iota(jnp.int32, tail.shape, 1)
                tail = jnp.where(lane < HD, tail, jnp.zeros_like(tail))
                for j, spot in enumerate(spots):
                    to = pl.ds(pl.multiple_of(spot, 128), 128)
                    rows = slice(128 * j, 128 * j + 128)
                    queries[to, :WIDE] = wide[rows]
                    queries[to, WIDE:] = tail[rows]
                    residual[to, :] = halves[j // 2][128 * (j % 2) : 128 * (j % 2) + 128, 1280:]

    lane = lax.broadcasted_iota(jnp.int32, (8, 384), 1) // HD
    head = lax.broadcasted_iota(jnp.int32, (8, 384), 0)
    most = jnp.concatenate(largest, axis=1) * 1.01
    most = jnp.where((lane == head) & (head < 5), most, 0.0).astype(BF)
    bounds = lax.dot_general(
        most, jnp.abs(queries[...]), (((1,), (1,)), ((), ())), preferred_element_type=F32
    )
    small = jnp.max(bounds) < 480.0

    def attend(step, shifted):
        row = step * 128 if isinstance(step, int) else pl.multiple_of(step * 128, 128)
        mine = jnp.broadcast_to(ids[0:1, pl.ds(row + 512, 128)], (128, 128)).T[:, 0:1]
        bias = jnp.where(mine == ids[0:1, pl.ds(row, 1152)], 0.0, LOW)
        lane = lax.broadcasted_iota(jnp.int32, (128, 128), 1)
        for slab in range(3):
            span = slice(128 * slab, 128 * slab + 128)
            query = queries[pl.ds(row, 128), span] * BF(0.125)
            mask = bias
            if slab < 2:
                none = jnp.zeros_like(query)
                query = jnp.concatenate(
                    [jnp.where(lane < HD, query, none), jnp.where(lane < HD, none, query)], axis=0
                )
                mask = jnp.concatenate([bias, bias], axis=0)
            scores = lax.dot_general(
                query,
                keys[pl.ds(row, 1152), span],
                (((1,), (1,)), ((), ())),
                preferred_element_type=F32,
            )
            scores = scores + mask
            if shifted:
                scores = scores - jnp.max(scores, axis=-1, keepdims=True)
            raised = jnp.exp(scores).astype(BF)
            out = jnp.dot(
                raised,
                values[pl.ds(row, 1152), 256 * slab : 256 * slab + 256],
                preferred_element_type=F32,
            )
            out = out[:, :128] / out[:, 128:]
            if slab < 2:
                context = jnp.where(lane < HD, out[:128], out[128:])
                stem = residual[pl.ds(row, 128), span].astype(F32)
                memory[pl.ds(row, 128), span] = (stem + context).astype(BF)
            else:
                stem = residual[pl.ds(row, 128), WIDE:GROUP].astype(F32)
                memory[pl.ds(row, 128), WIDE:] = (stem + out[:, HD:]).astype(BF)

    @pl.when(small)
    def _():
        for step in range(4):
            attend(step, False)

    @pl.when(jnp.logical_not(small))
    def _():
        lax.fori_loop(0, 4, lambda step, carry: (attend(step, True), carry)[1], 0)

    near[...] = memory[pl.ds(pl.multiple_of(256 * x, 256), 256), :]
    away[...] = memory[pl.ds(pl.multiple_of(256 * (1 - x), 256), 256), :]


def encoder(places, layers, ids, parts, depth):
    operands = layers + [ids] + parts
    return pl.pallas_call(
        functools.partial(encoder_kernel, len(parts), depth),
        out_shape=(
            jax.ShapeDtypeStruct((512, GROUP), BF),
            jax.ShapeDtypeStruct((256, GROUP), BF),
            jax.ShapeDtypeStruct((256, GROUP), BF),
        ),
        in_specs=[SMEM] + [VMEM] * len(operands),
        out_specs=(VMEM, VMEM, VMEM),
        scratch_shapes=[
            pltpu.VMEM((1280, 1024), BF),
            pltpu.VMEM((512, 384), BF),
            pltpu.VMEM((512, 384), BF),
            pltpu.VMEM((1536, 384), BF),
            pltpu.VMEM((1536, 768), BF),
        ],
        cost_estimate=CHEAP,
        compiler_params=pltpu.CompilerParams(vmem_limit_bytes=24 * 1024 * 1024),
    )(places, *operands)


def cross_kernel(base, table, tokens, asked, memory, beside, *refs):
    outs, out = refs[:-1], refs[-1]
    count = asked.shape[0]
    me = table[base + 2]
    spot = lax.broadcasted_iota(jnp.int32, (count, HD), 1)
    order = lax.broadcasted_iota(jnp.int32, (count, 1), 0)
    owner = (order // 2 * 2) ^ me
    bias = []
    for half in range(2):
        for b in range(4):
            block = table[base + half] + b
            ask = jnp.sum(jnp.where(spot == block, asked[...], 0.0), axis=-1, keepdims=True)
            allowed = (ask > 0.5) | (owner == block)
            bias.append(jnp.broadcast_to(jnp.where(allowed, 0.0, LOW), (count, 128)))
    bias = jnp.concatenate(bias, axis=1)
    bias = jnp.concatenate([bias] * 5, axis=0)
    query = tokens[...].astype(BF)
    cross = jnp.concatenate(
        [
            lax.dot_general(
                query, held[...], (((1,), (1,)), ((), ())), preferred_element_type=F32
            )
            for held in (memory, beside)
        ],
        axis=1,
    )
    cross = jnp.where(bias < 0.0, LOW, cross)
    top = jnp.max(cross, axis=-1, keepdims=True)
    raised = jnp.where(bias < 0.0, 0.0, jnp.exp(cross - top))
    den = jnp.sum(raised, axis=-1, keepdims=True)
    raised = raised.astype(BF)
    out[...] = jnp.dot(raised[:, :512], memory[...], preferred_element_type=F32) + jnp.dot(
        raised[:, 512:], beside[...], preferred_element_type=F32
    )
    lane = lax.broadcasted_iota(jnp.int32, (count, HD), 1)
    for h in range(5):
        rows = slice(count * h, count * h + count)
        stats = jnp.where(lane == 0, top[rows], den[rows])
        both = jnp.concatenate([out[rows, HD * h : HD * h + HD], stats], axis=1)
        for i, owned in enumerate(outs):
            owned[8 * h : 8 * h + 8, :] = both[8 * i : 8 * i + 8]


def cross_partial(base, table, tokens, asked, memory, beside):
    count = asked.shape[0]
    return pl.pallas_call(
        functools.partial(cross_kernel, base),
        out_shape=(jax.ShapeDtypeStruct((40, 128), F32),) * (count // 8),
        in_specs=[SMEM] + [VMEM] * 4,
        out_specs=(VMEM,) * (count // 8),
        scratch_shapes=[pltpu.VMEM((5 * count, GROUP), F32)],
        cost_estimate=CHEAP,
        compiler_params=pltpu.CompilerParams(vmem_limit_bytes=12 * 1024 * 1024),
    )(table, tokens, asked, memory, beside)


def merge_kernel(*refs):
    parts, outs, out = refs[:-5], refs[-5:-1], refs[-1]
    tops = [part[:, HD : HD + 1] for part in parts]
    best = functools.reduce(jnp.maximum, tops)
    total = jnp.zeros((40, 128), F32)
    for top, part in zip(tops, parts):
        total = total + jnp.exp(top - best) * part[...]
    final = total[:, :HD] / total[:, HD + 1 : HD + 2]
    heads = [final[8 * h : 8 * h + 8] for h in range(5)] + [jnp.zeros((8, HD), F32)]
    for slab in range(3):
        out[:, 128 * slab : 128 * slab + 128] = jnp.concatenate(heads[2 * slab : 2 * slab + 2], axis=1)
    for i in range(4):
        outs[i][...] = out[2 * i : 2 * i + 2, :].astype(BF)


def merge(parts):
    return pl.pallas_call(
        merge_kernel,
        out_shape=(jax.ShapeDtypeStruct((2, 384), BF),) * 4,
        in_specs=[VMEM] * len(parts),
        out_specs=(VMEM,) * 4,
        scratch_shapes=[pltpu.VMEM((8, 384), F32)],
        cost_estimate=CHEAP,
        compiler_params=pltpu.CompilerParams(vmem_limit_bytes=4 * 1024 * 1024),
    )(*parts)


def gather_kernel(side, rows, table, *refs):
    pieces, out = refs[:4], refs[4]
    high, x = table[side], table[6]
    start = pl.multiple_of(rows * high, rows) if pieces[0].shape[0] > rows else 0
    flip = jnp.broadcast_to(x, (rows, HD)) == 1
    held = [piece[pl.ds(start, rows), :] for piece in pieces]
    for i, piece in enumerate(held):
        group = (2 * high + x) ^ i
        out[:, pl.ds(pl.multiple_of(WIDE * group, 128), WIDE)] = piece[:, :WIDE]
    for i in range(2):
        first, second = [piece[:, WIDE:GROUP] for piece in held[2 * i : 2 * i + 2]]
        tail = jnp.concatenate([jnp.where(flip, second, first), jnp.where(flip, first, second)], axis=1)
        out[:, pl.ds(pl.multiple_of(1024 + 128 * (high ^ i), 128), 128)] = tail


def gather_groups(side, rows, table, pieces):
    return pl.pallas_call(
        functools.partial(gather_kernel, side, rows),
        out_shape=jax.ShapeDtypeStruct((rows, 1280), BF),
        in_specs=[SMEM] + [VMEM] * 4,
        out_specs=VMEM,
        cost_estimate=CHEAP,
        compiler_params=pltpu.CompilerParams(vmem_limit_bytes=4 * 1024 * 1024),
    )(table, *pieces)


def on_device(stem, norm_gain, qkv_weight, segment_ids, dec_queries, stretch_mask):
    n = lax.axis_size("tm")
    layers = n // 4
    me = lax.axis_index("tm")
    z, x, c = me // 4, (me // 2) % 2, me % 2
    p, k = z % 2, z // 2
    quarter = 2 * k + c
    group = 2 * p + x
    depth = qkv_weight.shape[0]

    utts = lax.axis_size("utt")
    moved = lax.axis_index("utt") % 2
    direct = depth % 16 == 0 and layers == 4 and utts % 2 == 0
    gain = norm_gain.reshape(1, -1)
    table = [128 * (2 * x + c), 128 * (2 * x + 1 - c), 128 * (2 - 2 * x + c), 128 * (3 - 2 * x - c)]
    table += [group, p, x, c]
    table += [512 * (p - c + 1), 512 * (2 - p - c), 1024 * c, 0, x == moved, 4 * quarter - 4, z]
    sources = [me, me ^ 1, me ^ 2, me ^ 3] if direct else [jnp.int32(0)]
    for side in (2 * moved, 2 - 2 * moved) if direct else ():
        for core in (c, 1 - c):
            sources += [4 * (z ^ turn) + side + core for turn in (1, 2, 3)]
    table = scalars(table + sources + [4 * quarter, 4 * (quarter ^ 1), me])
    base = 15 + len(sources)

    steps = [1 if i % 2 else -1 for i in range(layers)]
    near_route = [
        (4 * i + j, 4 * (i + s) + j)
        for i, s in enumerate(steps)
        for j in range(4)
        if 0 <= i + s < layers
    ]
    near = send(stem, near_route)
    pair = swap(stem, n, 4)
    if direct:
        def trade(block):
            return lax.ppermute(block, "utt", [(u, u ^ 1) for u in range(utts)])

        mine, theirs = pack(
            table, qkv_weight, dec_queries, stretch_mask, segment_ids.reshape(1, -1)
        )
        across = swap(theirs, n, 2)
        mine_c, across_c = swap(mine, n, 1), swap(across, n, 1)
        ready = load(table, mine, mine_c, after(across, near, pair), across_c)
        relayed = swap(after(near, ready[0]), n, 4)
        stem_x = swap(after(stem, across), n, 2)
        here = {turn: swap(ready[turn % 2], n, 4 * turn) for turn in (3, 2, 1)}
        pair_x = swap(after(pair, ready[0]), n, 2)
        halo = jnp.where((z == 1) | (z == 2), near, relayed)
        halo_x = swap(after(halo, pair_x, *here.values()), n, 2)
        joined = join([after(here[1], halo), here[2], here[3]])
        traded = trade(joined)
        ids, tokens, asked = prepare(table, ready[0], joined, n)
        own_half = norm_half(table, gain, stem, stem_x)
        pair_half = norm_half(table, gain, pair, pair_x)
        halo_half = norm_half(table, gain, halo, after(halo_x, ids), False)
        own_c, pair_c = swap(own_half, n, 1), swap(pair_half, n, 1)
        halo_c, joined_c = swap(after(halo_half, traded), n, 1), swap(joined, n, 1)
        layered = [own_half, own_c, pair_half, pair_c, halo_half, halo_c]
        weights = [mine, mine_c, across, across_c, joined, joined_c]
        weights += [traded, swap(after(traded, own_c, pair_c, joined_c), n, 1)]
    else:
        stem_x = swap(stem, n, 2)
        far = swap(near, n, 4)
        left = jnp.where(p == 0, near, far)
        right = jnp.where(p == 0, far, near)
        left_x, right_x = swap(left, n, 2), swap(right, n, 2)
        left = norm_half(table, gain, left, left_x, False)
        right = norm_half(table, gain, right, right_x, False)
        halo = [jnp.where(c == 0, left, right), swap(jnp.where(c == 0, right, left), n, 1)]
        own = norm_half(table, gain, stem, stem_x)
        other = norm_half(table, gain, pair, swap(pair, n, 2))
        layered = [own, swap(own, n, 1), other, swap(other, n, 1)] + halo
        whole = lax.all_gather(qkv_weight, "tm", axis=0, tiled=True)
        grouped = jnp.stack([weight_group(whole, g) for g in range(4)])
        weights = [lax.dynamic_index_in_dim(grouped, group, 0, keepdims=False)]
        weights = [jnp.pad(weights[0], ((0, 0), (0, HD)))]
        depth = whole.shape[0]
        packed = jnp.stack([token_group(dec_queries, stretch_mask, g) for g in range(4)])
        every = lax.all_gather(packed, "tm", axis=0)
        every = lax.dynamic_index_in_dim(every, group, 1, keepdims=False)
        every = jnp.take(every, jnp.arange(0, n, 2, dtype=jnp.int32) ^ me, axis=0)
        every = every.reshape(n // 2, 6, 2, HD).transpose(1, 0, 2, 3).reshape(6, n, HD).astype(F32)
        asked = every[5]
        tokens = jnp.concatenate(
            [jnp.pad(every[h] * 0.125, ((0, 0), (HD * h, GROUP - HD - HD * h))) for h in range(5)]
        )
        marks = lax.all_gather(segment_ids, "tm", axis=0, tiled=True).astype(F32)
        marks = jnp.pad(marks, (512, 512))
        marks = lax.dynamic_slice_in_dim(marks, 512 * quarter, 1536, 0)
        ids = jnp.broadcast_to(marks[None], (8, 1536))
    held, stay, leave = encoder(table, layered, ids, weights, depth)

    partial = cross_partial(base, table, tokens, asked, held, swap(held, n, 1))
    owned = [partial[0]] + [swap(partial[i], n, 8 * i) for i in range(1, n // 8)]

    got = []
    for turn, rows in enumerate((stay, leave)):
        route = [
            (
                8 * (d // 8) + 4 * (d // 4 % 2) + (d & 2) + (d & 1),
                8 * (d // 8) + 4 * (d & 1) + ((d & 2) ^ (2 * turn)) + (d // 4 % 2),
            )
            for d in range(n)
        ]
        got.append(after(send(rows, route), owned[1]))
    memory = gather_groups(7, 128, table, got + [swap(part, n, 1) for part in got])

    final = merge(owned)
    final = [final[0]] + [swap(final[i], n, 2 * i) for i in (1, 2, 3)]
    final[0] = after(final[0], memory)
    cross_out = gather_groups(5, 2, table, final)
    return (memory, cross_out)


def solution(mesh):
    placed = (
        P(("utt", "tm"), None),
        P(),
        P("tm", None),
        P(("utt", "tm")),
        P(("utt", "tm"), None),
        P(("utt", "tm"), None),
    )
    return jax.shard_map(
        on_device,
        mesh=mesh,
        in_specs=placed,
        out_specs=(P(("utt", "tm"), None), P(("utt", "tm"), None)),
        check_vma=False,
    )
```

```python
import functools

import jax
import jax.numpy as jnp
from jax import lax
from jax.experimental import pallas as pl
from jax.experimental.pallas import tpu as pltpu
from jax.sharding import PartitionSpec as P

HD = 64
WIDE = 256
GROUP = 320
BF = jnp.bfloat16
F32 = jnp.float32
LOW = -1e30
CHEAP = pl.CostEstimate(flops=1, bytes_accessed=1, transcendentals=0)
VMEM = pl.BlockSpec(memory_space=pltpu.VMEM)
SMEM = pl.BlockSpec(memory_space=pltpu.SMEM)


def send(block, route):
    return lax.ppermute(block, "tm", route)


def swap(block, n, mask):
    return send(block, [(d, d ^ mask) for d in range(n)])


def after(value, *awaited):
    return lax.optimization_barrier((value, *awaited))[0]


def scalars(values):
    return jnp.stack([jnp.asarray(v, jnp.int32) for v in values])


def group_of(array, g):
    return array[:, WIDE * g : WIDE * g + WIDE], array[:, 1024 + HD * g : 1024 + HD * g + HD]


def weight_group(weight, g):
    width = weight.shape[1] // 3
    parts = [group_of(weight[:, i * width : (i + 1) * width], g) for i in range(3)]
    (q0, q1), (k0, k1), (v0, v1) = parts
    return jnp.concatenate([q0, k0, v0, k1, v1, q1], axis=1)


def token_group(queries, mask, g):
    wide, tail = group_of(queries, g)
    heads = [wide[:, HD * i : HD * i + HD] for i in range(4)] + [tail]
    asked = jnp.pad(mask.astype(BF), ((0, 0), (0, HD - mask.shape[1])))
    return jnp.concatenate(heads + [asked], axis=0)


def pack_kernel(table, *refs):
    mine, theirs = refs[4:6]
    weight, queries, mask, segments = held = refs[6:10]
    copies = [pltpu.make_async_copy(refs[i], held[i], refs[10].at[i]) for i in range(4)]
    for copy in copies:
        copy.start()
    for copy in copies:
        copy.wait()
    rows, width = weight.shape[0], weight.shape[1] // 3
    blocks = mask.shape[1]
    ids = segments[...]
    digits = [lax.shift_right_logical(ids, 7).astype(F32), (ids & 127).astype(F32)]
    asked = mask[...].astype(F32)
    if blocks < HD:
        asked = jnp.concatenate([asked, jnp.zeros((2, HD - blocks), F32)], axis=1)
    rest = [asked] + [d[:, HD * i : HD * i + HD] for d in digits for i in range(2)]
    rest.append(jnp.zeros((rows - 16, HD), F32))
    for turn, outs in enumerate((mine, theirs)):
        column = table[6] if turn == 0 else 1 - table[6]
        for p in range(2):
            out = outs.at[p]
            wide = pl.multiple_of(WIDE * (2 * p + column), 128)
            tails = []
            for i in range(4):
                source = weight if i < 3 else queries
                at = width * i if i < 3 else 0
                slab = source[:, at + 1024 + 128 * p : at + 1152 + 128 * p].astype(F32)
                odd = jnp.broadcast_to(column, (slab.shape[0], HD)) == 1
                tails.append(jnp.where(odd, slab[:, HD:], slab[:, :HD]))
                if i < 3:
                    out[:, WIDE * i : WIDE * i + WIDE] = weight[
                        :, pl.ds(pl.multiple_of(at + wide, 128), WIDE)
                    ]
            out[:, 3 * WIDE : 896] = jnp.concatenate(tails[1:3], axis=1).astype(BF)
            asking = queries[:, pl.ds(wide, WIDE)].astype(F32)
            heads = [asking[:, HD * h : HD * h + HD] for h in range(4)] + [tails[3]]
            lanes = jnp.concatenate(heads + rest, axis=0)
            out[:, 896:] = jnp.concatenate([tails[0], lanes], axis=1).astype(BF)


def pack(table, weight, queries, mask, segments):
    shape = jax.ShapeDtypeStruct((2, weight.shape[0], 1024), BF)
    given = (weight, queries, mask, segments)
    return pl.pallas_call(
        pack_kernel,
        out_shape=(shape, shape),
        in_specs=[SMEM] + [pl.BlockSpec(memory_space=pl.ANY)] * 4,
        out_specs=(VMEM,) * 2,
        scratch_shapes=[pltpu.VMEM(a.shape, a.dtype) for a in given] + [pltpu.SemaphoreType.DMA((4,))],
        cost_estimate=CHEAP,
        compiler_params=pltpu.CompilerParams(vmem_limit_bytes=8 * 1024 * 1024),
    )(table, weight, queries, mask, segments)


def load_kernel(table, *refs):
    held, outs = refs[:4], refs[4:]
    x, c, p = table[6], table[7], table[5]
    own = jnp.broadcast_to(table[12], outs[0].shape) == 1
    flip_c = jnp.broadcast_to(c, (16, 128)) == 1
    flip_x = jnp.broadcast_to(x, (16, 128)) == 1
    for a in range(2):
        mine, mine_c, across, across_c = [h[pl.ds(p ^ a, 1)][0] for h in held]
        out = outs[a]
        out[...] = jnp.where(own, mine, across)
        lanes = [part[:16, 896:] for part in (mine, mine_c, across, across_c)]
        rows = []
        for first, second in (lanes[:2], lanes[2:]):
            rows.append((jnp.where(flip_c, second, first), jnp.where(flip_c, first, second)))
        low = [jnp.where(flip_x, there, here) for here, there in zip(*rows)]
        high = [jnp.where(flip_x, here, there) for here, there in zip(*rows)]
        lane = lax.broadcasted_iota(jnp.int32, (16, 128), 1)
        for j, found in enumerate(low + high):
            out[16 * j : 16 * j + 16, 896:] = jnp.where(
                lane < HD, out[16 * j : 16 * j + 16, 896:], found
            )


def load(table, *held):
    rows = held[0].shape[1]
    return pl.pallas_call(
        load_kernel,
        out_shape=(jax.ShapeDtypeStruct((rows, 1024), BF),) * 2,
        in_specs=[SMEM] + [VMEM] * 4,
        out_specs=(VMEM,) * 2,
        cost_estimate=CHEAP,
        compiler_params=pltpu.CompilerParams(vmem_limit_bytes=8 * 1024 * 1024),
    )(table, *held)


def norm_kernel(table, gain, here, across, out):
    group = table[4]
    for i, block in enumerate((here, across)):
        rows = slice(128 * i, 128 * i + 128)
        values = block[...].astype(F32)
        mean = jnp.mean(values, axis=-1, keepdims=True)
        centred = values - mean
        var = jnp.mean(centred * centred, axis=-1, keepdims=True)
        out[rows, :1280] = (centred * lax.rsqrt(var + 1e-05) * gain[...]).astype(BF)
        if out.shape[1] > 1280:
            out[rows, 1280 : 1280 + WIDE] = block[:, pl.ds(pl.multiple_of(group * WIDE, 128), WIDE)]
            slab = block[:, pl.ds(pl.multiple_of(1024 + group // 2 * 128, 128), 128)]
            odd = jnp.broadcast_to(lax.rem(group, 2), (128, HD)) == 1
            tail = jnp.where(odd, slab[:, HD:], slab[:, :HD])
            out[rows, 1280 + WIDE :] = jnp.concatenate([tail, jnp.zeros_like(tail)], axis=1)


def norm_half(table, gain, here, across, kept=True):
    return pl.pallas_call(
        norm_kernel,
        out_shape=jax.ShapeDtypeStruct((256, 1664 if kept else 1280), BF),
        in_specs=[SMEM] + [VMEM] * 3,
        out_specs=VMEM,
        cost_estimate=CHEAP,
        compiler_params=pltpu.CompilerParams(vmem_limit_bytes=8 * 1024 * 1024),
    )(table, gain, here, across)


def prepare_kernel(table, *refs):
    first_part, joined, (ids, tokens, asked) = refs[0], refs[1], refs[2:]
    depth = joined.shape[0] // 3
    first, x, core, z = table[13], table[6], table[7], table[14]
    count = asked.shape[0]
    ids[...] = jnp.zeros_like(ids)
    tokens[...] = jnp.zeros_like(tokens)
    flip_c = jnp.broadcast_to(core, (2, HD)) == 1
    flip_x = jnp.broadcast_to(x, (2, HD)) == 1
    for turn in range(4):
        top = depth * (turn - 1)
        part = joined[top : top + 64, 896:] if turn else first_part[:64, 896:]
        lanes = part.astype(F32)[:, HD:]
        for h in range(6):
            rows = [lanes[16 * j + 2 * h : 16 * j + 2 * h + 2] for j in range(4)]
            low = jnp.where(flip_c, rows[1], rows[0])
            high = jnp.where(flip_c, rows[3], rows[2])
            for dx in range(2):
                found = jnp.where(flip_x, low, high) if dx else jnp.where(flip_x, high, low)
                at = 4 * turn + 2 * dx
                if h < 5:
                    tokens[count * h + at : count * h + at + 2, HD * h : HD * h + HD] = found * 0.125
                else:
                    asked[at : at + 2, :] = found
        for j in range(4):
            marks = lanes[16 * j + 12 : 16 * j + 14] * 128.0 + lanes[16 * j + 14 : 16 * j + 16]
            block = 4 * (z ^ turn) + j - first

            @pl.when((block >= 0) & (block < 12))
            def _():
                ids[0:1, pl.ds(pl.multiple_of(block * 128, 128), 128)] = jnp.concatenate(
                    [marks[0:1], marks[1:2]], axis=1
                )


def prepare(table, own, joined, count):
    return pl.pallas_call(
        prepare_kernel,
        out_shape=(
            jax.ShapeDtypeStruct((8, 1536), F32),
            jax.ShapeDtypeStruct((5 * count, GROUP), F32),
            jax.ShapeDtypeStruct((count, HD), F32),
        ),
        in_specs=[SMEM] + [VMEM] * 2,
        out_specs=(VMEM,) * 3,
        cost_estimate=CHEAP,
        compiler_params=pltpu.CompilerParams(vmem_limit_bytes=8 * 1024 * 1024),
    )(table, own, joined)


def join_kernel(*refs):
    parts, out = refs[:-1], refs[-1]
    rows = parts[0].shape[0]
    for i, part in enumerate(parts):
        out[rows * i : rows * i + rows, :] = part[...]


def join(parts):
    rows = parts[0].shape[0]
    return pl.pallas_call(
        join_kernel,
        out_shape=jax.ShapeDtypeStruct((rows * len(parts), 1024), BF),
        in_specs=[VMEM] * len(parts),
        out_specs=VMEM,
        cost_estimate=CHEAP,
        compiler_params=pltpu.CompilerParams(vmem_limit_bytes=4 * 1024 * 1024),
    )(*parts)


def encoder_kernel(n_parts, depth, places, *refs):
    layers = [refs[2 * i : 2 * i + 2] for i in range(3)]
    ids = refs[6]
    parts = refs[7 : 7 + n_parts]
    memory, near, away, weight, residual, queries, keys, values = refs[7 + n_parts :]
    x = places[6]
    at = 15
    for part in parts:
        rows = [part[pl.ds(places[5], 1)][0]] if len(part.shape) == 3 else [
            part[s * depth : s * depth + depth, :] for s in range(part.shape[0] // depth)
        ]
        for found in rows:
            weight[pl.ds(pl.multiple_of(places[at] * depth, 16), depth), :] = found
            at += 1

    for slab in range(3):
        values[:, 256 * slab + 128 : 256 * slab + 256] = jnp.ones((1536, 128), BF)
    spots = [places[i] for i in (0, 2, 1, 3)]
    largest = [jnp.zeros((1, 256), F32), jnp.zeros((1, 128), F32)]
    for i, halves in enumerate(layers):
        place = places[8 + i]
        normed = jnp.concatenate([half[:, :1280] for half in halves], axis=0)
        found = jnp.dot(normed, weight[:, 256:896], preferred_element_type=F32)
        for j, lanes in enumerate((slice(0, 256), slice(512, 640))):
            largest[j] = jnp.maximum(
                largest[j], jnp.max(jnp.abs(found[:, lanes]), axis=0, keepdims=True)
            )
        found = found.astype(BF)
        for j, spot in enumerate(spots):
            to = pl.ds(pl.multiple_of(place + spot, 128), 128)
            block = found[128 * j : 128 * j + 128]
            keys[to, :256] = block[:, :256]
            keys[to, 256:] = block[:, 512:]
            for slab in range(3):
                values[to, 256 * slab : 256 * slab + 128] = block[:, 256 + 128 * slab : 384 + 128 * slab]
        if i < 2:

            @pl.when(place == 512)
            def _():
                normed = jnp.concatenate([half[:, :1280] for half in halves], axis=0)
                wide = jnp.dot(normed, weight[:, :WIDE], preferred_element_type=F32).astype(BF)
                tail = jnp.dot(normed, weight[:, 896:], preferred_element_type=F32).astype(BF)
                lane = lax.broadcasted_iota(jnp.int32, tail.shape, 1)
                tail = jnp.where(lane < HD, tail, jnp.zeros_like(tail))
                for j, spot in enumerate(spots):
                    to = pl.ds(pl.multiple_of(spot, 128), 128)
                    rows = slice(128 * j, 128 * j + 128)
                    queries[to, :WIDE] = wide[rows]
                    queries[to, WIDE:] = tail[rows]
                    residual[to, :] = halves[j // 2][128 * (j % 2) : 128 * (j % 2) + 128, 1280:]

    lane = lax.broadcasted_iota(jnp.int32, (8, 384), 1) // HD
    head = lax.broadcasted_iota(jnp.int32, (8, 384), 0)
    most = jnp.concatenate(largest, axis=1) * 1.01
    most = jnp.where((lane == head) & (head < 5), most, 0.0).astype(BF)
    bounds = lax.dot_general(
        most, jnp.abs(queries[...]), (((1,), (1,)), ((), ())), preferred_element_type=F32
    )
    small = jnp.max(bounds) < 480.0

    def attend(step, shifted):
        row = step * 128 if isinstance(step, int) else pl.multiple_of(step * 128, 128)
        mine = jnp.broadcast_to(ids[0:1, pl.ds(row + 512, 128)], (128, 128)).T[:, 0:1]
        bias = jnp.where(mine == ids[0:1, pl.ds(row, 1152)], 0.0, LOW)
        lane = lax.broadcasted_iota(jnp.int32, (128, 128), 1)
        for slab in range(3):
            span = slice(128 * slab, 128 * slab + 128)
            query = queries[pl.ds(row, 128), span] * BF(0.125)
            mask = bias
            if slab < 2:
                none = jnp.zeros_like(query)
                query = jnp.concatenate(
                    [jnp.where(lane < HD, query, none), jnp.where(lane < HD, none, query)], axis=0
                )
                mask = jnp.concatenate([bias, bias], axis=0)
            scores = lax.dot_general(
                query,
                keys[pl.ds(row, 1152), span],
                (((1,), (1,)), ((), ())),
                preferred_element_type=F32,
            )
            scores = scores + mask
            if shifted:
                scores = scores - jnp.max(scores, axis=-1, keepdims=True)
            raised = jnp.exp(scores).astype(BF)
            out = jnp.dot(
                raised,
                values[pl.ds(row, 1152), 256 * slab : 256 * slab + 256],
                preferred_element_type=F32,
            )
            out = out[:, :128] / out[:, 128:]
            if slab < 2:
                context = jnp.where(lane < HD, out[:128], out[128:])
                stem = residual[pl.ds(row, 128), span].astype(F32)
                memory[pl.ds(row, 128), span] = (stem + context).astype(BF)
            else:
                stem = residual[pl.ds(row, 128), WIDE:GROUP].astype(F32)
                memory[pl.ds(row, 128), WIDE:] = (stem + out[:, HD:]).astype(BF)

    @pl.when(small)
    def _():
        for step in range(4):
            attend(step, False)

    @pl.when(jnp.logical_not(small))
    def _():
        lax.fori_loop(0, 4, lambda step, carry: (attend(step, True), carry)[1], 0)

    near[...] = memory[pl.ds(pl.multiple_of(256 * x, 256), 256), :]
    away[...] = memory[pl.ds(pl.multiple_of(256 * (1 - x), 256), 256), :]


def encoder(places, layers, ids, parts, depth):
    operands = layers + [ids] + parts
    return pl.pallas_call(
        functools.partial(encoder_kernel, len(parts), depth),
        out_shape=(
            jax.ShapeDtypeStruct((512, GROUP), BF),
            jax.ShapeDtypeStruct((256, GROUP), BF),
            jax.ShapeDtypeStruct((256, GROUP), BF),
        ),
        in_specs=[SMEM] + [VMEM] * len(operands),
        out_specs=(VMEM, VMEM, VMEM),
        scratch_shapes=[
            pltpu.VMEM((1280, 1024), BF),
            pltpu.VMEM((512, 384), BF),
            pltpu.VMEM((512, 384), BF),
            pltpu.VMEM((1536, 384), BF),
            pltpu.VMEM((1536, 768), BF),
        ],
        cost_estimate=CHEAP,
        compiler_params=pltpu.CompilerParams(vmem_limit_bytes=24 * 1024 * 1024),
    )(places, *operands)


def cross_kernel(base, table, tokens, asked, memory, beside, *refs):
    outs, out = refs[:-1], refs[-1]
    count = asked.shape[0]
    me = table[base + 2]
    spot = lax.broadcasted_iota(jnp.int32, (count, HD), 1)
    order = lax.broadcasted_iota(jnp.int32, (count, 1), 0)
    owner = (order // 2 * 2) ^ me
    bias = []
    for half in range(2):
        for b in range(4):
            block = table[base + half] + b
            ask = jnp.sum(jnp.where(spot == block, asked[...], 0.0), axis=-1, keepdims=True)
            allowed = (ask > 0.5) | (owner == block)
            bias.append(jnp.broadcast_to(jnp.where(allowed, 0.0, LOW), (count, 128)))
    bias = jnp.concatenate(bias, axis=1)
    bias = jnp.concatenate([bias] * 5, axis=0)
    query = tokens[...].astype(BF)
    cross = jnp.concatenate(
        [
            lax.dot_general(
                query, held[...], (((1,), (1,)), ((), ())), preferred_element_type=F32
            )
            for held in (memory, beside)
        ],
        axis=1,
    )
    cross = jnp.where(bias < 0.0, LOW, cross)
    top = jnp.max(cross, axis=-1, keepdims=True)
    raised = jnp.where(bias < 0.0, 0.0, jnp.exp(cross - top))
    den = jnp.sum(raised, axis=-1, keepdims=True)
    raised = raised.astype(BF)
    out[...] = jnp.dot(raised[:, :512], memory[...], preferred_element_type=F32) + jnp.dot(
        raised[:, 512:], beside[...], preferred_element_type=F32
    )
    lane = lax.broadcasted_iota(jnp.int32, (count, HD), 1)
    for h in range(5):
        rows = slice(count * h, count * h + count)
        stats = jnp.where(lane == 0, top[rows], den[rows])
        both = jnp.concatenate([out[rows, HD * h : HD * h + HD], stats], axis=1)
        for i, owned in enumerate(outs):
            owned[8 * h : 8 * h + 8, :] = both[8 * i : 8 * i + 8]


def cross_partial(base, table, tokens, asked, memory, beside):
    count = asked.shape[0]
    return pl.pallas_call(
        functools.partial(cross_kernel, base),
        out_shape=(jax.ShapeDtypeStruct((40, 128), F32),) * (count // 8),
        in_specs=[SMEM] + [VMEM] * 4,
        out_specs=(VMEM,) * (count // 8),
        scratch_shapes=[pltpu.VMEM((5 * count, GROUP), F32)],
        cost_estimate=CHEAP,
        compiler_params=pltpu.CompilerParams(vmem_limit_bytes=12 * 1024 * 1024),
    )(table, tokens, asked, memory, beside)


def merge_kernel(*refs):
    parts, outs, out = refs[:-5], refs[-5:-1], refs[-1]
    tops = [part[:, HD : HD + 1] for part in parts]
    best = functools.reduce(jnp.maximum, tops)
    total = jnp.zeros((40, 128), F32)
    for top, part in zip(tops, parts):
        total = total + jnp.exp(top - best) * part[...]
    final = total[:, :HD] / total[:, HD + 1 : HD + 2]
    heads = [final[8 * h : 8 * h + 8] for h in range(5)] + [jnp.zeros((8, HD), F32)]
    for slab in range(3):
        out[:, 128 * slab : 128 * slab + 128] = jnp.concatenate(heads[2 * slab : 2 * slab + 2], axis=1)
    for i in range(4):
        outs[i][...] = out[2 * i : 2 * i + 2, :].astype(BF)


def merge(parts):
    return pl.pallas_call(
        merge_kernel,
        out_shape=(jax.ShapeDtypeStruct((2, 384), BF),) * 4,
        in_specs=[VMEM] * len(parts),
        out_specs=(VMEM,) * 4,
        scratch_shapes=[pltpu.VMEM((8, 384), F32)],
        cost_estimate=CHEAP,
        compiler_params=pltpu.CompilerParams(vmem_limit_bytes=4 * 1024 * 1024),
    )(*parts)


def gather_kernel(side, rows, table, *refs):
    pieces, out = refs[:4], refs[4]
    high, x = table[side], table[6]
    start = pl.multiple_of(rows * high, rows) if pieces[0].shape[0] > rows else 0
    flip = jnp.broadcast_to(x, (rows, HD)) == 1
    held = [piece[pl.ds(start, rows), :] for piece in pieces]
    for i, piece in enumerate(held):
        group = (2 * high + x) ^ i
        out[:, pl.ds(pl.multiple_of(WIDE * group, 128), WIDE)] = piece[:, :WIDE]
    for i in range(2):
        first, second = [piece[:, WIDE:GROUP] for piece in held[2 * i : 2 * i + 2]]
        tail = jnp.concatenate([jnp.where(flip, second, first), jnp.where(flip, first, second)], axis=1)
        out[:, pl.ds(pl.multiple_of(1024 + 128 * (high ^ i), 128), 128)] = tail


def gather_groups(side, rows, table, pieces):
    return pl.pallas_call(
        functools.partial(gather_kernel, side, rows),
        out_shape=jax.ShapeDtypeStruct((rows, 1280), BF),
        in_specs=[SMEM] + [VMEM] * 4,
        out_specs=VMEM,
        cost_estimate=CHEAP,
        compiler_params=pltpu.CompilerParams(vmem_limit_bytes=4 * 1024 * 1024),
    )(table, *pieces)


def on_device(stem, norm_gain, qkv_weight, segment_ids, dec_queries, stretch_mask):
    n = lax.axis_size("tm")
    layers = n // 4
    me = lax.axis_index("tm")
    z, x, c = me // 4, (me // 2) % 2, me % 2
    p, k = z % 2, z // 2
    quarter = 2 * k + c
    group = 2 * p + x
    depth = qkv_weight.shape[0]

    utts = lax.axis_size("utt")
    moved = lax.axis_index("utt") % 2
    direct = depth % 16 == 0 and layers == 4 and utts % 2 == 0
    gain = norm_gain.reshape(1, -1)
    table = [128 * (2 * x + c), 128 * (2 * x + 1 - c), 128 * (2 - 2 * x + c), 128 * (3 - 2 * x - c)]
    table += [group, p, x, c]
    table += [512 * (p - c + 1), 512 * (2 - p - c), 1024 * c, 0, x == moved, 4 * quarter - 4, z]
    sources = [me, me ^ 1, me ^ 2, me ^ 3] if direct else [jnp.int32(0)]
    for side in (2 * moved, 2 - 2 * moved) if direct else ():
        for core in (c, 1 - c):
            sources += [4 * (z ^ turn) + side + core for turn in (1, 2, 3)]
    table = scalars(table + sources + [4 * quarter, 4 * (quarter ^ 1), me])
    base = 15 + len(sources)

    steps = [1 if i % 2 else -1 for i in range(layers)]
    near_route = [
        (4 * i + j, 4 * (i + s) + j)
        for i, s in enumerate(steps)
        for j in range(4)
        if 0 <= i + s < layers
    ]
    near = send(stem, near_route)
    pair = swap(stem, n, 4)
    if direct:
        def trade(block):
            return lax.ppermute(block, "utt", [(u, u ^ 1) for u in range(utts)])

        mine, theirs = pack(
            table, qkv_weight, dec_queries, stretch_mask, segment_ids.reshape(1, -1)
        )
        across = swap(theirs, n, 2)
        mine_c, across_c = swap(mine, n, 1), swap(across, n, 1)
        ready = load(table, mine, mine_c, after(across, near, pair), across_c)
        relayed = swap(after(near, ready[0]), n, 4)
        stem_x = swap(after(stem, across), n, 2)
        here = {turn: swap(ready[turn % 2], n, 4 * turn) for turn in (3, 2)}
        here[1] = swap(after(ready[1], stem_x), n, 4)
        pair_x = swap(after(pair, ready[0]), n, 2)
        halo = jnp.where((z == 1) | (z == 2), near, relayed)
        halo_x = swap(after(halo, pair_x, *here.values()), n, 2)
        joined = join([after(here[1], halo), here[2], here[3]])
        traded = trade(joined)
        ids, tokens, asked = prepare(table, ready[0], joined, n)
        own_half = norm_half(table, gain, stem, stem_x)
        pair_half = norm_half(table, gain, pair, pair_x)
        halo_half = norm_half(table, gain, halo, after(halo_x, ids), False)
        own_c, pair_c = swap(own_half, n, 1), swap(pair_half, n, 1)
        halo_c, joined_c = swap(after(halo_half, traded), n, 1), swap(joined, n, 1)
        layered = [own_half, own_c, pair_half, pair_c, halo_half, halo_c]
        weights = [mine, mine_c, across, across_c, joined, joined_c]
        weights += [traded, swap(after(traded, own_c, pair_c, joined_c), n, 1)]
    else:
        stem_x = swap(stem, n, 2)
        far = swap(near, n, 4)
        left = jnp.where(p == 0, near, far)
        right = jnp.where(p == 0, far, near)
        left_x, right_x = swap(left, n, 2), swap(right, n, 2)
        left = norm_half(table, gain, left, left_x, False)
        right = norm_half(table, gain, right, right_x, False)
        halo = [jnp.where(c == 0, left, right), swap(jnp.where(c == 0, right, left), n, 1)]
        own = norm_half(table, gain, stem, stem_x)
        other = norm_half(table, gain, pair, swap(pair, n, 2))
        layered = [own, swap(own, n, 1), other, swap(other, n, 1)] + halo
        whole = lax.all_gather(qkv_weight, "tm", axis=0, tiled=True)
        grouped = jnp.stack([weight_group(whole, g) for g in range(4)])
        weights = [lax.dynamic_index_in_dim(grouped, group, 0, keepdims=False)]
        weights = [jnp.pad(weights[0], ((0, 0), (0, HD)))]
        depth = whole.shape[0]
        packed = jnp.stack([token_group(dec_queries, stretch_mask, g) for g in range(4)])
        every = lax.all_gather(packed, "tm", axis=0)
        every = lax.dynamic_index_in_dim(every, group, 1, keepdims=False)
        every = jnp.take(every, jnp.arange(0, n, 2, dtype=jnp.int32) ^ me, axis=0)
        every = every.reshape(n // 2, 6, 2, HD).transpose(1, 0, 2, 3).reshape(6, n, HD).astype(F32)
        asked = every[5]
        tokens = jnp.concatenate(
            [jnp.pad(every[h] * 0.125, ((0, 0), (HD * h, GROUP - HD - HD * h))) for h in range(5)]
        )
        marks = lax.all_gather(segment_ids, "tm", axis=0, tiled=True).astype(F32)
        marks = jnp.pad(marks, (512, 512))
        marks = lax.dynamic_slice_in_dim(marks, 512 * quarter, 1536, 0)
        ids = jnp.broadcast_to(marks[None], (8, 1536))
    held, stay, leave = encoder(table, layered, ids, weights, depth)

    partial = cross_partial(base, table, tokens, asked, held, swap(held, n, 1))
    owned = [partial[0]] + [swap(partial[i], n, 8 * i) for i in range(1, n // 8)]

    got = []
    for turn, rows in enumerate((stay, leave)):
        route = [
            (
                8 * (d // 8) + 4 * (d // 4 % 2) + (d & 2) + (d & 1),
                8 * (d // 8) + 4 * (d & 1) + ((d & 2) ^ (2 * turn)) + (d // 4 % 2),
            )
            for d in range(n)
        ]
        got.append(after(send(rows, route), owned[1]))
    memory = gather_groups(7, 128, table, got + [swap(part, n, 1) for part in got])

    final = merge(owned)
    final = [final[0]] + [swap(final[i], n, 2 * i) for i in (1, 2, 3)]
    final[0] = after(final[0], memory)
    cross_out = gather_groups(5, 2, table, final)
    return (memory, cross_out)


def solution(mesh):
    placed = (
        P(("utt", "tm"), None),
        P(),
        P("tm", None),
        P(("utt", "tm")),
        P(("utt", "tm"), None),
        P(("utt", "tm"), None),
    )
    return jax.shard_map(
        on_device,
        mesh=mesh,
        in_specs=placed,
        out_specs=(P(("utt", "tm"), None), P(("utt", "tm"), None)),
        check_vma=False,
    )
```

```python
import functools

import jax
import jax.numpy as jnp
from jax import lax
from jax.experimental import pallas as pl
from jax.experimental.pallas import tpu as pltpu
from jax.sharding import PartitionSpec as P

HD = 64
WIDE = 256
GROUP = 320
BF = jnp.bfloat16
F32 = jnp.float32
LOW = -1e30
CHEAP = pl.CostEstimate(flops=1, bytes_accessed=1, transcendentals=0)
VMEM = pl.BlockSpec(memory_space=pltpu.VMEM)
SMEM = pl.BlockSpec(memory_space=pltpu.SMEM)


def send(block, route):
    return lax.ppermute(block, "tm", route)


def swap(block, n, mask):
    return send(block, [(d, d ^ mask) for d in range(n)])


def after(value, *awaited):
    return lax.optimization_barrier((value, *awaited))[0]


def scalars(values):
    return jnp.stack([jnp.asarray(v, jnp.int32) for v in values])


def group_of(array, g):
    return array[:, WIDE * g : WIDE * g + WIDE], array[:, 1024 + HD * g : 1024 + HD * g + HD]


def weight_group(weight, g):
    width = weight.shape[1] // 3
    parts = [group_of(weight[:, i * width : (i + 1) * width], g) for i in range(3)]
    (q0, q1), (k0, k1), (v0, v1) = parts
    return jnp.concatenate([q0, k0, v0, k1, v1, q1], axis=1)


def token_group(queries, mask, g):
    wide, tail = group_of(queries, g)
    heads = [wide[:, HD * i : HD * i + HD] for i in range(4)] + [tail]
    asked = jnp.pad(mask.astype(BF), ((0, 0), (0, HD - mask.shape[1])))
    return jnp.concatenate(heads + [asked], axis=0)


def pack_kernel(table, *refs):
    mine, theirs = refs[4:6]
    weight, queries, mask, segments = held = refs[6:10]
    copies = [pltpu.make_async_copy(refs[i], held[i], refs[10].at[i]) for i in range(4)]
    for copy in copies:
        copy.start()
    for copy in copies:
        copy.wait()
    rows, width = weight.shape[0], weight.shape[1] // 3
    blocks = mask.shape[1]
    ids = segments[...]
    digits = [lax.shift_right_logical(ids, 7).astype(F32), (ids & 127).astype(F32)]
    asked = mask[...].astype(F32)
    if blocks < HD:
        asked = jnp.concatenate([asked, jnp.zeros((2, HD - blocks), F32)], axis=1)
    rest = [asked] + [d[:, HD * i : HD * i + HD] for d in digits for i in range(2)]
    rest.append(jnp.zeros((rows - 16, HD), F32))
    for turn, outs in enumerate((mine, theirs)):
        column = table[6] if turn == 0 else 1 - table[6]
        for p in range(2):
            out = outs.at[p]
            wide = pl.multiple_of(WIDE * (2 * p + column), 128)
            tails = []
            for i in range(4):
                source = weight if i < 3 else queries
                at = width * i if i < 3 else 0
                slab = source[:, at + 1024 + 128 * p : at + 1152 + 128 * p].astype(F32)
                odd = jnp.broadcast_to(column, (slab.shape[0], HD)) == 1
                tails.append(jnp.where(odd, slab[:, HD:], slab[:, :HD]))
                if i < 3:
                    out[:, WIDE * i : WIDE * i + WIDE] = weight[
                        :, pl.ds(pl.multiple_of(at + wide, 128), WIDE)
                    ]
            out[:, 3 * WIDE : 896] = jnp.concatenate(tails[1:3], axis=1).astype(BF)
            asking = queries[:, pl.ds(wide, WIDE)].astype(F32)
            heads = [asking[:, HD * h : HD * h + HD] for h in range(4)] + [tails[3]]
            lanes = jnp.concatenate(heads + rest, axis=0)
            out[:, 896:] = jnp.concatenate([tails[0], lanes], axis=1).astype(BF)


def pack(table, weight, queries, mask, segments):
    shape = jax.ShapeDtypeStruct((2, weight.shape[0], 1024), BF)
    given = (weight, queries, mask, segments)
    return pl.pallas_call(
        pack_kernel,
        out_shape=(shape, shape),
        in_specs=[SMEM] + [pl.BlockSpec(memory_space=pl.ANY)] * 4,
        out_specs=(VMEM,) * 2,
        scratch_shapes=[pltpu.VMEM(a.shape, a.dtype) for a in given] + [pltpu.SemaphoreType.DMA((4,))],
        cost_estimate=CHEAP,
        compiler_params=pltpu.CompilerParams(vmem_limit_bytes=8 * 1024 * 1024),
    )(table, weight, queries, mask, segments)


def load_kernel(table, *refs):
    held, outs = refs[:4], refs[4:]
    x, c, p = table[6], table[7], table[5]
    own = jnp.broadcast_to(table[12], outs[0].shape) == 1
    flip_c = jnp.broadcast_to(c, (16, 128)) == 1
    flip_x = jnp.broadcast_to(x, (16, 128)) == 1
    for a in range(2):
        mine, mine_c, across, across_c = [h[pl.ds(p ^ a, 1)][0] for h in held]
        out = outs[a]
        out[...] = jnp.where(own, mine, across)
        lanes = [part[:16, 896:] for part in (mine, mine_c, across, across_c)]
        rows = []
        for first, second in (lanes[:2], lanes[2:]):
            rows.append((jnp.where(flip_c, second, first), jnp.where(flip_c, first, second)))
        low = [jnp.where(flip_x, there, here) for here, there in zip(*rows)]
        high = [jnp.where(flip_x, here, there) for here, there in zip(*rows)]
        lane = lax.broadcasted_iota(jnp.int32, (16, 128), 1)
        for j, found in enumerate(low + high):
            out[16 * j : 16 * j + 16, 896:] = jnp.where(
                lane < HD, out[16 * j : 16 * j + 16, 896:], found
            )


def load(table, *held):
    rows = held[0].shape[1]
    return pl.pallas_call(
        load_kernel,
        out_shape=(jax.ShapeDtypeStruct((rows, 1024), BF),) * 2,
        in_specs=[SMEM] + [VMEM] * 4,
        out_specs=(VMEM,) * 2,
        cost_estimate=CHEAP,
        compiler_params=pltpu.CompilerParams(vmem_limit_bytes=8 * 1024 * 1024),
    )(table, *held)


def norm_kernel(table, gain, here, across, out):
    group = table[4]
    for i, block in enumerate((here, across)):
        rows = slice(128 * i, 128 * i + 128)
        values = block[...].astype(F32)
        mean = jnp.mean(values, axis=-1, keepdims=True)
        centred = values - mean
        var = jnp.mean(centred * centred, axis=-1, keepdims=True)
        out[rows, :1280] = (centred * lax.rsqrt(var + 1e-05) * gain[...]).astype(BF)
        if out.shape[1] > 1280:
            out[rows, 1280 : 1280 + WIDE] = block[:, pl.ds(pl.multiple_of(group * WIDE, 128), WIDE)]
            slab = block[:, pl.ds(pl.multiple_of(1024 + group // 2 * 128, 128), 128)]
            odd = jnp.broadcast_to(lax.rem(group, 2), (128, HD)) == 1
            tail = jnp.where(odd, slab[:, HD:], slab[:, :HD])
            out[rows, 1280 + WIDE :] = jnp.concatenate([tail, jnp.zeros_like(tail)], axis=1)


def norm_half(table, gain, here, across, kept=True):
    return pl.pallas_call(
        norm_kernel,
        out_shape=jax.ShapeDtypeStruct((256, 1664 if kept else 1280), BF),
        in_specs=[SMEM] + [VMEM] * 3,
        out_specs=VMEM,
        cost_estimate=CHEAP,
        compiler_params=pltpu.CompilerParams(vmem_limit_bytes=8 * 1024 * 1024),
    )(table, gain, here, across)


def prepare_kernel(table, *refs):
    first_part, joined, (ids, tokens, asked) = refs[0], refs[1], refs[2:]
    depth = joined.shape[0] // 3
    first, x, core, z = table[13], table[6], table[7], table[14]
    count = asked.shape[0]
    ids[...] = jnp.zeros_like(ids)
    tokens[...] = jnp.zeros_like(tokens)
    flip_c = jnp.broadcast_to(core, (2, HD)) == 1
    flip_x = jnp.broadcast_to(x, (2, HD)) == 1
    for turn in range(4):
        top = depth * (turn - 1)
        part = joined[top : top + 64, 896:] if turn else first_part[:64, 896:]
        lanes = part.astype(F32)[:, HD:]
        for h in range(6):
            rows = [lanes[16 * j + 2 * h : 16 * j + 2 * h + 2] for j in range(4)]
            low = jnp.where(flip_c, rows[1], rows[0])
            high = jnp.where(flip_c, rows[3], rows[2])
            for dx in range(2):
                found = jnp.where(flip_x, low, high) if dx else jnp.where(flip_x, high, low)
                at = 4 * turn + 2 * dx
                if h < 5:
                    tokens[count * h + at : count * h + at + 2, HD * h : HD * h + HD] = found * 0.125
                else:
                    asked[at : at + 2, :] = found
        for j in range(4):
            marks = lanes[16 * j + 12 : 16 * j + 14] * 128.0 + lanes[16 * j + 14 : 16 * j + 16]
            block = 4 * (z ^ turn) + j - first

            @pl.when((block >= 0) & (block < 12))
            def _():
                ids[0:1, pl.ds(pl.multiple_of(block * 128, 128), 128)] = jnp.concatenate(
                    [marks[0:1], marks[1:2]], axis=1
                )


def prepare(table, own, joined, count):
    return pl.pallas_call(
        prepare_kernel,
        out_shape=(
            jax.ShapeDtypeStruct((8, 1536), F32),
            jax.ShapeDtypeStruct((5 * count, GROUP), F32),
            jax.ShapeDtypeStruct((count, HD), F32),
        ),
        in_specs=[SMEM] + [VMEM] * 2,
        out_specs=(VMEM,) * 3,
        cost_estimate=CHEAP,
        compiler_params=pltpu.CompilerParams(vmem_limit_bytes=8 * 1024 * 1024),
    )(table, own, joined)


def join_kernel(*refs):
    parts, out = refs[:-1], refs[-1]
    rows = parts[0].shape[0]
    for i, part in enumerate(parts):
        out[rows * i : rows * i + rows, :] = part[...]


def join(parts):
    rows = parts[0].shape[0]
    return pl.pallas_call(
        join_kernel,
        out_shape=jax.ShapeDtypeStruct((rows * len(parts), 1024), BF),
        in_specs=[VMEM] * len(parts),
        out_specs=VMEM,
        cost_estimate=CHEAP,
        compiler_params=pltpu.CompilerParams(vmem_limit_bytes=4 * 1024 * 1024),
    )(*parts)


def encoder_kernel(n_parts, depth, places, *refs):
    layers = [refs[2 * i : 2 * i + 2] for i in range(3)]
    ids = refs[6]
    parts = refs[7 : 7 + n_parts]
    memory, near, away, weight, residual, queries, keys, values = refs[7 + n_parts :]
    x = places[6]
    at = 15
    for part in parts:
        rows = [part[pl.ds(places[5], 1)][0]] if len(part.shape) == 3 else [
            part[s * depth : s * depth + depth, :] for s in range(part.shape[0] // depth)
        ]
        for found in rows:
            weight[pl.ds(pl.multiple_of(places[at] * depth, 16), depth), :] = found
            at += 1

    for slab in range(3):
        values[:, 256 * slab + 128 : 256 * slab + 256] = jnp.ones((1536, 128), BF)
    spots = [places[i] for i in (0, 2, 1, 3)]
    largest = [jnp.zeros((1, 256), F32), jnp.zeros((1, 128), F32)]
    for i, halves in enumerate(layers):
        place = places[8 + i]
        normed = jnp.concatenate([half[:, :1280] for half in halves], axis=0)
        found = jnp.dot(normed, weight[:, 256:896], preferred_element_type=F32)
        for j, lanes in enumerate((slice(0, 256), slice(512, 640))):
            largest[j] = jnp.maximum(
                largest[j], jnp.max(jnp.abs(found[:, lanes]), axis=0, keepdims=True)
            )
        found = found.astype(BF)
        for j, spot in enumerate(spots):
            to = pl.ds(pl.multiple_of(place + spot, 128), 128)
            block = found[128 * j : 128 * j + 128]
            keys[to, :256] = block[:, :256]
            keys[to, 256:] = block[:, 512:]
            for slab in range(3):
                values[to, 256 * slab : 256 * slab + 128] = block[:, 256 + 128 * slab : 384 + 128 * slab]
        if i < 2:

            @pl.when(place == 512)
            def _():
                normed = jnp.concatenate([half[:, :1280] for half in halves], axis=0)
                wide = jnp.dot(normed, weight[:, :WIDE], preferred_element_type=F32).astype(BF)
                tail = jnp.dot(normed, weight[:, 896:], preferred_element_type=F32).astype(BF)
                lane = lax.broadcasted_iota(jnp.int32, tail.shape, 1)
                tail = jnp.where(lane < HD, tail, jnp.zeros_like(tail))
                for j, spot in enumerate(spots):
                    to = pl.ds(pl.multiple_of(spot, 128), 128)
                    rows = slice(128 * j, 128 * j + 128)
                    queries[to, :WIDE] = wide[rows]
                    queries[to, WIDE:] = tail[rows]
                    residual[to, :] = halves[j // 2][128 * (j % 2) : 128 * (j % 2) + 128, 1280:]

    lane = lax.broadcasted_iota(jnp.int32, (8, 384), 1) // HD
    head = lax.broadcasted_iota(jnp.int32, (8, 384), 0)
    most = jnp.concatenate(largest, axis=1) * 1.01
    most = jnp.where((lane == head) & (head < 5), most, 0.0).astype(BF)
    bounds = lax.dot_general(
        most, jnp.abs(queries[...]), (((1,), (1,)), ((), ())), preferred_element_type=F32
    )
    small = jnp.max(bounds) < 480.0

    def attend(step, shifted):
        row = step * 128 if isinstance(step, int) else pl.multiple_of(step * 128, 128)
        mine = jnp.broadcast_to(ids[0:1, pl.ds(row + 512, 128)], (128, 128)).T[:, 0:1]
        bias = jnp.where(mine == ids[0:1, pl.ds(row, 1152)], 0.0, LOW)
        lane = lax.broadcasted_iota(jnp.int32, (128, 128), 1)
        for slab in range(3):
            span = slice(128 * slab, 128 * slab + 128)
            query = queries[pl.ds(row, 128), span] * BF(0.125)
            mask = bias
            if slab < 2:
                none = jnp.zeros_like(query)
                query = jnp.concatenate(
                    [jnp.where(lane < HD, query, none), jnp.where(lane < HD, none, query)], axis=0
                )
                mask = jnp.concatenate([bias, bias], axis=0)
            scores = lax.dot_general(
                query,
                keys[pl.ds(row, 1152), span],
                (((1,), (1,)), ((), ())),
                preferred_element_type=F32,
            )
            scores = scores + mask
            if shifted:
                scores = scores - jnp.max(scores, axis=-1, keepdims=True)
            raised = jnp.exp(scores).astype(BF)
            out = jnp.dot(
                raised,
                values[pl.ds(row, 1152), 256 * slab : 256 * slab + 256],
                preferred_element_type=F32,
            )
            out = out[:, :128] / out[:, 128:]
            if slab < 2:
                context = jnp.where(lane < HD, out[:128], out[128:])
                stem = residual[pl.ds(row, 128), span].astype(F32)
                memory[pl.ds(row, 128), span] = (stem + context).astype(BF)
            else:
                stem = residual[pl.ds(row, 128), WIDE:GROUP].astype(F32)
                memory[pl.ds(row, 128), WIDE:] = (stem + out[:, HD:]).astype(BF)

    @pl.when(small)
    def _():
        for step in range(4):
            attend(step, False)

    @pl.when(jnp.logical_not(small))
    def _():
        lax.fori_loop(0, 4, lambda step, carry: (attend(step, True), carry)[1], 0)

    near[...] = memory[pl.ds(pl.multiple_of(256 * x, 256), 256), :]
    away[...] = memory[pl.ds(pl.multiple_of(256 * (1 - x), 256), 256), :]


def encoder(places, layers, ids, parts, depth):
    operands = layers + [ids] + parts
    return pl.pallas_call(
        functools.partial(encoder_kernel, len(parts), depth),
        out_shape=(
            jax.ShapeDtypeStruct((512, GROUP), BF),
            jax.ShapeDtypeStruct((256, GROUP), BF),
            jax.ShapeDtypeStruct((256, GROUP), BF),
        ),
        in_specs=[SMEM] + [VMEM] * len(operands),
        out_specs=(VMEM, VMEM, VMEM),
        scratch_shapes=[
            pltpu.VMEM((1280, 1024), BF),
            pltpu.VMEM((512, 384), BF),
            pltpu.VMEM((512, 384), BF),
            pltpu.VMEM((1536, 384), BF),
            pltpu.VMEM((1536, 768), BF),
        ],
        cost_estimate=CHEAP,
        compiler_params=pltpu.CompilerParams(vmem_limit_bytes=24 * 1024 * 1024),
    )(places, *operands)


def cross_kernel(base, table, tokens, asked, memory, beside, *refs):
    outs, out = refs[:-1], refs[-1]
    count = asked.shape[0]
    me = table[base + 2]
    spot = lax.broadcasted_iota(jnp.int32, (count, HD), 1)
    order = lax.broadcasted_iota(jnp.int32, (count, 1), 0)
    owner = (order // 2 * 2) ^ me
    bias = []
    for half in range(2):
        for b in range(4):
            block = table[base + half] + b
            ask = jnp.sum(jnp.where(spot == block, asked[...], 0.0), axis=-1, keepdims=True)
            allowed = (ask > 0.5) | (owner == block)
            bias.append(jnp.broadcast_to(jnp.where(allowed, 0.0, LOW), (count, 128)))
    bias = jnp.concatenate(bias, axis=1)
    bias = jnp.concatenate([bias] * 5, axis=0)
    query = tokens[...].astype(BF)
    cross = jnp.concatenate(
        [
            lax.dot_general(
                query, held[...], (((1,), (1,)), ((), ())), preferred_element_type=F32
            )
            for held in (memory, beside)
        ],
        axis=1,
    )
    cross = jnp.where(bias < 0.0, LOW, cross)
    top = jnp.max(cross, axis=-1, keepdims=True)
    raised = jnp.where(bias < 0.0, 0.0, jnp.exp(cross - top))
    den = jnp.sum(raised, axis=-1, keepdims=True)
    raised = raised.astype(BF)
    out[...] = jnp.dot(raised[:, :512], memory[...], preferred_element_type=F32) + jnp.dot(
        raised[:, 512:], beside[...], preferred_element_type=F32
    )
    lane = lax.broadcasted_iota(jnp.int32, (count, HD), 1)
    for h in range(5):
        rows = slice(count * h, count * h + count)
        stats = jnp.where(lane == 0, top[rows], den[rows])
        both = jnp.concatenate([out[rows, HD * h : HD * h + HD], stats], axis=1)
        for i, owned in enumerate(outs):
            owned[8 * h : 8 * h + 8, :] = both[8 * i : 8 * i + 8]


def cross_partial(base, table, tokens, asked, memory, beside):
    count = asked.shape[0]
    return pl.pallas_call(
        functools.partial(cross_kernel, base),
        out_shape=(jax.ShapeDtypeStruct((40, 128), F32),) * (count // 8),
        in_specs=[SMEM] + [VMEM] * 4,
        out_specs=(VMEM,) * (count // 8),
        scratch_shapes=[pltpu.VMEM((5 * count, GROUP), F32)],
        cost_estimate=CHEAP,
        compiler_params=pltpu.CompilerParams(vmem_limit_bytes=12 * 1024 * 1024),
    )(table, tokens, asked, memory, beside)


def merge_kernel(*refs):
    parts, outs, out = refs[:-5], refs[-5:-1], refs[-1]
    tops = [part[:, HD : HD + 1] for part in parts]
    best = functools.reduce(jnp.maximum, tops)
    total = jnp.zeros((40, 128), F32)
    for top, part in zip(tops, parts):
        total = total + jnp.exp(top - best) * part[...]
    final = total[:, :HD] / total[:, HD + 1 : HD + 2]
    heads = [final[8 * h : 8 * h + 8] for h in range(5)] + [jnp.zeros((8, HD), F32)]
    for slab in range(3):
        out[:, 128 * slab : 128 * slab + 128] = jnp.concatenate(heads[2 * slab : 2 * slab + 2], axis=1)
    for i in range(4):
        outs[i][...] = out[2 * i : 2 * i + 2, :].astype(BF)


def merge(parts):
    return pl.pallas_call(
        merge_kernel,
        out_shape=(jax.ShapeDtypeStruct((2, 384), BF),) * 4,
        in_specs=[VMEM] * len(parts),
        out_specs=(VMEM,) * 4,
        scratch_shapes=[pltpu.VMEM((8, 384), F32)],
        cost_estimate=CHEAP,
        compiler_params=pltpu.CompilerParams(vmem_limit_bytes=4 * 1024 * 1024),
    )(*parts)


def gather_kernel(side, rows, table, *refs):
    pieces, out = refs[:4], refs[4]
    high, x = table[side], table[6]
    start = pl.multiple_of(rows * high, rows) if pieces[0].shape[0] > rows else 0
    flip = jnp.broadcast_to(x, (rows, HD)) == 1
    held = [piece[pl.ds(start, rows), :] for piece in pieces]
    for i, piece in enumerate(held):
        group = (2 * high + x) ^ i
        out[:, pl.ds(pl.multiple_of(WIDE * group, 128), WIDE)] = piece[:, :WIDE]
    for i in range(2):
        first, second = [piece[:, WIDE:GROUP] for piece in held[2 * i : 2 * i + 2]]
        tail = jnp.concatenate([jnp.where(flip, second, first), jnp.where(flip, first, second)], axis=1)
        out[:, pl.ds(pl.multiple_of(1024 + 128 * (high ^ i), 128), 128)] = tail


def gather_groups(side, rows, table, pieces):
    return pl.pallas_call(
        functools.partial(gather_kernel, side, rows),
        out_shape=jax.ShapeDtypeStruct((rows, 1280), BF),
        in_specs=[SMEM] + [VMEM] * 4,
        out_specs=VMEM,
        cost_estimate=CHEAP,
        compiler_params=pltpu.CompilerParams(vmem_limit_bytes=4 * 1024 * 1024),
    )(table, *pieces)


def on_device(stem, norm_gain, qkv_weight, segment_ids, dec_queries, stretch_mask):
    n = lax.axis_size("tm")
    layers = n // 4
    me = lax.axis_index("tm")
    z, x, c = me // 4, (me // 2) % 2, me % 2
    p, k = z % 2, z // 2
    quarter = 2 * k + c
    group = 2 * p + x
    depth = qkv_weight.shape[0]

    utts = lax.axis_size("utt")
    moved = lax.axis_index("utt") % 2
    direct = depth % 16 == 0 and layers == 4 and utts % 2 == 0
    gain = norm_gain.reshape(1, -1)
    table = [128 * (2 * x + c), 128 * (2 * x + 1 - c), 128 * (2 - 2 * x + c), 128 * (3 - 2 * x - c)]
    table += [group, p, x, c]
    table += [512 * (p - c + 1), 512 * (2 - p - c), 1024 * c, 0, x == moved, 4 * quarter - 4, z]
    sources = [me, me ^ 1, me ^ 2, me ^ 3] if direct else [jnp.int32(0)]
    for side in (2 * moved, 2 - 2 * moved) if direct else ():
        for core in (c, 1 - c):
            sources += [4 * (z ^ turn) + side + core for turn in (1, 2, 3)]
    table = scalars(table + sources + [4 * quarter, 4 * (quarter ^ 1), me])
    base = 15 + len(sources)

    steps = [1 if i % 2 else -1 for i in range(layers)]
    near_route = [
        (4 * i + j, 4 * (i + s) + j)
        for i, s in enumerate(steps)
        for j in range(4)
        if 0 <= i + s < layers
    ]
    near = send(stem, near_route)
    pair = swap(stem, n, 4)
    if direct:
        def trade(block):
            return lax.ppermute(block, "utt", [(u, u ^ 1) for u in range(utts)])

        mine, theirs = pack(
            table, qkv_weight, dec_queries, stretch_mask, segment_ids.reshape(1, -1)
        )
        across = swap(theirs, n, 2)
        mine_c, across_c = swap(mine, n, 1), swap(across, n, 1)
        near = send(after(stem, mine_c), near_route)
        ready = load(table, mine, mine_c, after(across, near, pair), across_c)
        relayed = swap(after(near, ready[0]), n, 4)
        stem_x = swap(after(stem, across), n, 2)
        here = {turn: swap(ready[turn % 2], n, 4 * turn) for turn in (3, 2, 1)}
        pair_x = swap(after(pair, ready[0]), n, 2)
        halo = jnp.where((z == 1) | (z == 2), near, relayed)
        halo_x = swap(after(halo, pair_x, *here.values()), n, 2)
        joined = join([after(here[1], halo), here[2], here[3]])
        traded = trade(joined)
        ids, tokens, asked = prepare(table, ready[0], joined, n)
        own_half = norm_half(table, gain, stem, stem_x)
        pair_half = norm_half(table, gain, pair, pair_x)
        halo_half = norm_half(table, gain, halo, after(halo_x, ids), False)
        own_c, pair_c = swap(own_half, n, 1), swap(pair_half, n, 1)
        halo_c, joined_c = swap(after(halo_half, traded), n, 1), swap(joined, n, 1)
        layered = [own_half, own_c, pair_half, pair_c, halo_half, halo_c]
        weights = [mine, mine_c, across, across_c, joined, joined_c]
        weights += [traded, swap(after(traded, own_c, pair_c, joined_c), n, 1)]
    else:
        stem_x = swap(stem, n, 2)
        far = swap(near, n, 4)
        left = jnp.where(p == 0, near, far)
        right = jnp.where(p == 0, far, near)
        left_x, right_x = swap(left, n, 2), swap(right, n, 2)
        left = norm_half(table, gain, left, left_x, False)
        right = norm_half(table, gain, right, right_x, False)
        halo = [jnp.where(c == 0, left, right), swap(jnp.where(c == 0, right, left), n, 1)]
        own = norm_half(table, gain, stem, stem_x)
        other = norm_half(table, gain, pair, swap(pair, n, 2))
        layered = [own, swap(own, n, 1), other, swap(other, n, 1)] + halo
        whole = lax.all_gather(qkv_weight, "tm", axis=0, tiled=True)
        grouped = jnp.stack([weight_group(whole, g) for g in range(4)])
        weights = [lax.dynamic_index_in_dim(grouped, group, 0, keepdims=False)]
        weights = [jnp.pad(weights[0], ((0, 0), (0, HD)))]
        depth = whole.shape[0]
        packed = jnp.stack([token_group(dec_queries, stretch_mask, g) for g in range(4)])
        every = lax.all_gather(packed, "tm", axis=0)
        every = lax.dynamic_index_in_dim(every, group, 1, keepdims=False)
        every = jnp.take(every, jnp.arange(0, n, 2, dtype=jnp.int32) ^ me, axis=0)
        every = every.reshape(n // 2, 6, 2, HD).transpose(1, 0, 2, 3).reshape(6, n, HD).astype(F32)
        asked = every[5]
        tokens = jnp.concatenate(
            [jnp.pad(every[h] * 0.125, ((0, 0), (HD * h, GROUP - HD - HD * h))) for h in range(5)]
        )
        marks = lax.all_gather(segment_ids, "tm", axis=0, tiled=True).astype(F32)
        marks = jnp.pad(marks, (512, 512))
        marks = lax.dynamic_slice_in_dim(marks, 512 * quarter, 1536, 0)
        ids = jnp.broadcast_to(marks[None], (8, 1536))
    held, stay, leave = encoder(table, layered, ids, weights, depth)

    partial = cross_partial(base, table, tokens, asked, held, swap(held, n, 1))
    owned = [partial[0]] + [swap(partial[i], n, 8 * i) for i in range(1, n // 8)]

    got = []
    for turn, rows in enumerate((stay, leave)):
        route = [
            (
                8 * (d // 8) + 4 * (d // 4 % 2) + (d & 2) + (d & 1),
                8 * (d // 8) + 4 * (d & 1) + ((d & 2) ^ (2 * turn)) + (d // 4 % 2),
            )
            for d in range(n)
        ]
        got.append(after(send(rows, route), owned[1]))
    memory = gather_groups(7, 128, table, got + [swap(part, n, 1) for part in got])

    final = merge(owned)
    final = [final[0]] + [swap(final[i], n, 2 * i) for i in (1, 2, 3)]
    final[0] = after(final[0], memory)
    cross_out = gather_groups(5, 2, table, final)
    return (memory, cross_out)


def solution(mesh):
    placed = (
        P(("utt", "tm"), None),
        P(),
        P("tm", None),
        P(("utt", "tm")),
        P(("utt", "tm"), None),
        P(("utt", "tm"), None),
    )
    return jax.shard_map(
        on_device,
        mesh=mesh,
        in_specs=placed,
        out_specs=(P(("utt", "tm"), None), P(("utt", "tm"), None)),
        check_vma=False,
    )
```

```python
import functools

import jax
import jax.numpy as jnp
from jax import lax
from jax.experimental import pallas as pl
from jax.experimental.pallas import tpu as pltpu
from jax.sharding import PartitionSpec as P

HD = 64
WIDE = 256
GROUP = 320
BF = jnp.bfloat16
F32 = jnp.float32
LOW = -1e30
CHEAP = pl.CostEstimate(flops=1, bytes_accessed=1, transcendentals=0)
VMEM = pl.BlockSpec(memory_space=pltpu.VMEM)
SMEM = pl.BlockSpec(memory_space=pltpu.SMEM)


def send(block, route):
    return lax.ppermute(block, "tm", route)


def swap(block, n, mask):
    return send(block, [(d, d ^ mask) for d in range(n)])


def after(value, *awaited):
    return lax.optimization_barrier((value, *awaited))[0]


def scalars(values):
    return jnp.stack([jnp.asarray(v, jnp.int32) for v in values])


def group_of(array, g):
    return array[:, WIDE * g : WIDE * g + WIDE], array[:, 1024 + HD * g : 1024 + HD * g + HD]


def weight_group(weight, g):
    width = weight.shape[1] // 3
    parts = [group_of(weight[:, i * width : (i + 1) * width], g) for i in range(3)]
    (q0, q1), (k0, k1), (v0, v1) = parts
    return jnp.concatenate([q0, k0, v0, k1, v1, q1], axis=1)


def token_group(queries, mask, g):
    wide, tail = group_of(queries, g)
    heads = [wide[:, HD * i : HD * i + HD] for i in range(4)] + [tail]
    asked = jnp.pad(mask.astype(BF), ((0, 0), (0, HD - mask.shape[1])))
    return jnp.concatenate(heads + [asked], axis=0)


def pack_kernel(table, *refs):
    mine, theirs = refs[4:6]
    weight, queries, mask, segments = held = refs[6:10]
    copies = [pltpu.make_async_copy(refs[i], held[i], refs[10].at[i]) for i in range(4)]
    for copy in copies:
        copy.start()
    for copy in copies:
        copy.wait()
    rows, width = weight.shape[0], weight.shape[1] // 3
    blocks = mask.shape[1]
    ids = segments[...]
    digits = [lax.shift_right_logical(ids, 7).astype(F32), (ids & 127).astype(F32)]
    asked = mask[...].astype(F32)
    if blocks < HD:
        asked = jnp.concatenate([asked, jnp.zeros((2, HD - blocks), F32)], axis=1)
    rest = [asked] + [d[:, HD * i : HD * i + HD] for d in digits for i in range(2)]
    rest.append(jnp.zeros((rows - 16, HD), F32))
    for turn, outs in enumerate((mine, theirs)):
        column = table[6] if turn == 0 else 1 - table[6]
        for p in range(2):
            out = outs.at[p]
            wide = pl.multiple_of(WIDE * (2 * p + column), 128)
            tails = []
            for i in range(4):
                source = weight if i < 3 else queries
                at = width * i if i < 3 else 0
                slab = source[:, at + 1024 + 128 * p : at + 1152 + 128 * p].astype(F32)
                odd = jnp.broadcast_to(column, (slab.shape[0], HD)) == 1
                tails.append(jnp.where(odd, slab[:, HD:], slab[:, :HD]))
                if i < 3:
                    out[:, WIDE * i : WIDE * i + WIDE] = weight[
                        :, pl.ds(pl.multiple_of(at + wide, 128), WIDE)
                    ]
            out[:, 3 * WIDE : 896] = jnp.concatenate(tails[1:3], axis=1).astype(BF)
            asking = queries[:, pl.ds(wide, WIDE)].astype(F32)
            heads = [asking[:, HD * h : HD * h + HD] for h in range(4)] + [tails[3]]
            lanes = jnp.concatenate(heads + rest, axis=0)
            out[:, 896:] = jnp.concatenate([tails[0], lanes], axis=1).astype(BF)


def pack(table, weight, queries, mask, segments):
    shape = jax.ShapeDtypeStruct((2, weight.shape[0], 1024), BF)
    given = (weight, queries, mask, segments)
    return pl.pallas_call(
        pack_kernel,
        out_shape=(shape, shape),
        in_specs=[SMEM] + [pl.BlockSpec(memory_space=pl.ANY)] * 4,
        out_specs=(VMEM,) * 2,
        scratch_shapes=[pltpu.VMEM(a.shape, a.dtype) for a in given] + [pltpu.SemaphoreType.DMA((4,))],
        cost_estimate=CHEAP,
        compiler_params=pltpu.CompilerParams(vmem_limit_bytes=8 * 1024 * 1024),
    )(table, weight, queries, mask, segments)


def load_kernel(table, *refs):
    held, outs = refs[:4], refs[4:]
    x, c, p = table[6], table[7], table[5]
    own = jnp.broadcast_to(table[12], outs[0].shape) == 1
    flip_c = jnp.broadcast_to(c, (16, 128)) == 1
    flip_x = jnp.broadcast_to(x, (16, 128)) == 1
    for a in range(2):
        mine, mine_c, across, across_c = [h[pl.ds(p ^ a, 1)][0] for h in held]
        out = outs[a]
        out[...] = jnp.where(own, mine, across)
        lanes = [part[:16, 896:] for part in (mine, mine_c, across, across_c)]
        rows = []
        for first, second in (lanes[:2], lanes[2:]):
            rows.append((jnp.where(flip_c, second, first), jnp.where(flip_c, first, second)))
        low = [jnp.where(flip_x, there, here) for here, there in zip(*rows)]
        high = [jnp.where(flip_x, here, there) for here, there in zip(*rows)]
        lane = lax.broadcasted_iota(jnp.int32, (16, 128), 1)
        for j, found in enumerate(low + high):
            out[16 * j : 16 * j + 16, 896:] = jnp.where(
                lane < HD, out[16 * j : 16 * j + 16, 896:], found
            )


def load(table, *held):
    rows = held[0].shape[1]
    return pl.pallas_call(
        load_kernel,
        out_shape=(jax.ShapeDtypeStruct((rows, 1024), BF),) * 2,
        in_specs=[SMEM] + [VMEM] * 4,
        out_specs=(VMEM,) * 2,
        cost_estimate=CHEAP,
        compiler_params=pltpu.CompilerParams(vmem_limit_bytes=8 * 1024 * 1024),
    )(table, *held)


def norm_kernel(table, gain, here, across, out):
    group = table[4]
    for i, block in enumerate((here, across)):
        rows = slice(128 * i, 128 * i + 128)
        values = block[...].astype(F32)
        mean = jnp.mean(values, axis=-1, keepdims=True)
        centred = values - mean
        var = jnp.mean(centred * centred, axis=-1, keepdims=True)
        out[rows, :1280] = (centred * lax.rsqrt(var + 1e-05) * gain[...]).astype(BF)
        if out.shape[1] > 1280:
            out[rows, 1280 : 1280 + WIDE] = block[:, pl.ds(pl.multiple_of(group * WIDE, 128), WIDE)]
            slab = block[:, pl.ds(pl.multiple_of(1024 + group // 2 * 128, 128), 128)]
            odd = jnp.broadcast_to(lax.rem(group, 2), (128, HD)) == 1
            tail = jnp.where(odd, slab[:, HD:], slab[:, :HD])
            out[rows, 1280 + WIDE :] = jnp.concatenate([tail, jnp.zeros_like(tail)], axis=1)


def norm_half(table, gain, here, across, kept=True):
    return pl.pallas_call(
        norm_kernel,
        out_shape=jax.ShapeDtypeStruct((256, 1664 if kept else 1280), BF),
        in_specs=[SMEM] + [VMEM] * 3,
        out_specs=VMEM,
        cost_estimate=CHEAP,
        compiler_params=pltpu.CompilerParams(vmem_limit_bytes=8 * 1024 * 1024),
    )(table, gain, here, across)


def prepare_kernel(table, *refs):
    first_part, joined, (ids, tokens, asked) = refs[0], refs[1], refs[2:]
    depth = joined.shape[0] // 3
    first, x, core, z = table[13], table[6], table[7], table[14]
    count = asked.shape[0]
    ids[...] = jnp.zeros_like(ids)
    tokens[...] = jnp.zeros_like(tokens)
    flip_c = jnp.broadcast_to(core, (2, HD)) == 1
    flip_x = jnp.broadcast_to(x, (2, HD)) == 1
    for turn in range(4):
        top = depth * (turn - 1)
        part = joined[top : top + 64, 896:] if turn else first_part[:64, 896:]
        lanes = part.astype(F32)[:, HD:]
        for h in range(6):
            rows = [lanes[16 * j + 2 * h : 16 * j + 2 * h + 2] for j in range(4)]
            low = jnp.where(flip_c, rows[1], rows[0])
            high = jnp.where(flip_c, rows[3], rows[2])
            for dx in range(2):
                found = jnp.where(flip_x, low, high) if dx else jnp.where(flip_x, high, low)
                at = 4 * turn + 2 * dx
                if h < 5:
                    tokens[count * h + at : count * h + at + 2, HD * h : HD * h + HD] = found * 0.125
                else:
                    asked[at : at + 2, :] = found
        for j in range(4):
            marks = lanes[16 * j + 12 : 16 * j + 14] * 128.0 + lanes[16 * j + 14 : 16 * j + 16]
            block = 4 * (z ^ turn) + j - first

            @pl.when((block >= 0) & (block < 12))
            def _():
                ids[0:1, pl.ds(pl.multiple_of(block * 128, 128), 128)] = jnp.concatenate(
                    [marks[0:1], marks[1:2]], axis=1
                )


def prepare(table, own, joined, count):
    return pl.pallas_call(
        prepare_kernel,
        out_shape=(
            jax.ShapeDtypeStruct((8, 1536), F32),
            jax.ShapeDtypeStruct((5 * count, GROUP), F32),
            jax.ShapeDtypeStruct((count, HD), F32),
        ),
        in_specs=[SMEM] + [VMEM] * 2,
        out_specs=(VMEM,) * 3,
        cost_estimate=CHEAP,
        compiler_params=pltpu.CompilerParams(vmem_limit_bytes=8 * 1024 * 1024),
    )(table, own, joined)


def join_kernel(*refs):
    parts, out = refs[:-1], refs[-1]
    rows = parts[0].shape[0]
    for i, part in enumerate(parts):
        out[rows * i : rows * i + rows, :] = part[...]


def join(parts):
    rows = parts[0].shape[0]
    return pl.pallas_call(
        join_kernel,
        out_shape=jax.ShapeDtypeStruct((rows * len(parts), 1024), BF),
        in_specs=[VMEM] * len(parts),
        out_specs=VMEM,
        cost_estimate=CHEAP,
        compiler_params=pltpu.CompilerParams(vmem_limit_bytes=4 * 1024 * 1024),
    )(*parts)


def encoder_kernel(n_parts, depth, places, *refs):
    layers = [refs[2 * i : 2 * i + 2] for i in range(3)]
    ids = refs[6]
    parts = refs[7 : 7 + n_parts]
    memory, near, away, weight, residual, queries, keys, values = refs[7 + n_parts :]
    x = places[6]
    at = 15
    for part in parts:
        rows = [part[pl.ds(places[5], 1)][0]] if len(part.shape) == 3 else [
            part[s * depth : s * depth + depth, :] for s in range(part.shape[0] // depth)
        ]
        for found in rows:
            weight[pl.ds(pl.multiple_of(places[at] * depth, 16), depth), :] = found
            at += 1

    for slab in range(3):
        values[:, 256 * slab + 128 : 256 * slab + 256] = jnp.ones((1536, 128), BF)
    spots = [places[i] for i in (0, 2, 1, 3)]
    largest = [jnp.zeros((1, 256), F32), jnp.zeros((1, 128), F32)]
    for i, halves in enumerate(layers):
        place = places[8 + i]
        normed = jnp.concatenate([half[:, :1280] for half in halves], axis=0)
        found = jnp.dot(normed, weight[:, 256:896], preferred_element_type=F32)
        for j, lanes in enumerate((slice(0, 256), slice(512, 640))):
            largest[j] = jnp.maximum(
                largest[j], jnp.max(jnp.abs(found[:, lanes]), axis=0, keepdims=True)
            )
        found = found.astype(BF)
        for j, spot in enumerate(spots):
            to = pl.ds(pl.multiple_of(place + spot, 128), 128)
            block = found[128 * j : 128 * j + 128]
            keys[to, :256] = block[:, :256]
            keys[to, 256:] = block[:, 512:]
            for slab in range(3):
                values[to, 256 * slab : 256 * slab + 128] = block[:, 256 + 128 * slab : 384 + 128 * slab]
        if i < 2:

            @pl.when(place == 512)
            def _():
                normed = jnp.concatenate([half[:, :1280] for half in halves], axis=0)
                wide = jnp.dot(normed, weight[:, :WIDE], preferred_element_type=F32).astype(BF)
                tail = jnp.dot(normed, weight[:, 896:], preferred_element_type=F32).astype(BF)
                lane = lax.broadcasted_iota(jnp.int32, tail.shape, 1)
                tail = jnp.where(lane < HD, tail, jnp.zeros_like(tail))
                for j, spot in enumerate(spots):
                    to = pl.ds(pl.multiple_of(spot, 128), 128)
                    rows = slice(128 * j, 128 * j + 128)
                    queries[to, :WIDE] = wide[rows]
                    queries[to, WIDE:] = tail[rows]
                    residual[to, :] = halves[j // 2][128 * (j % 2) : 128 * (j % 2) + 128, 1280:]

    lane = lax.broadcasted_iota(jnp.int32, (8, 384), 1) // HD
    head = lax.broadcasted_iota(jnp.int32, (8, 384), 0)
    most = jnp.concatenate(largest, axis=1) * 1.01
    most = jnp.where((lane == head) & (head < 5), most, 0.0).astype(BF)
    bounds = lax.dot_general(
        most, jnp.abs(queries[...]), (((1,), (1,)), ((), ())), preferred_element_type=F32
    )
    small = jnp.max(bounds) < 480.0

    def attend(step, shifted):
        row = step * 128 if isinstance(step, int) else pl.multiple_of(step * 128, 128)
        mine = jnp.broadcast_to(ids[0:1, pl.ds(row + 512, 128)], (128, 128)).T[:, 0:1]
        bias = jnp.where(mine == ids[0:1, pl.ds(row, 1152)], 0.0, LOW)
        lane = lax.broadcasted_iota(jnp.int32, (128, 128), 1)
        for slab in range(3):
            span = slice(128 * slab, 128 * slab + 128)
            query = queries[pl.ds(row, 128), span] * BF(0.125)
            mask = bias
            if slab < 2:
                none = jnp.zeros_like(query)
                query = jnp.concatenate(
                    [jnp.where(lane < HD, query, none), jnp.where(lane < HD, none, query)], axis=0
                )
                mask = jnp.concatenate([bias, bias], axis=0)
            scores = lax.dot_general(
                query,
                keys[pl.ds(row, 1152), span],
                (((1,), (1,)), ((), ())),
                preferred_element_type=F32,
            )
            scores = scores + mask
            if shifted:
                scores = scores - jnp.max(scores, axis=-1, keepdims=True)
            raised = jnp.exp(scores).astype(BF)
            out = jnp.dot(
                raised,
                values[pl.ds(row, 1152), 256 * slab : 256 * slab + 256],
                preferred_element_type=F32,
            )
            out = out[:, :128] / out[:, 128:]
            if slab < 2:
                context = jnp.where(lane < HD, out[:128], out[128:])
                stem = residual[pl.ds(row, 128), span].astype(F32)
                memory[pl.ds(row, 128), span] = (stem + context).astype(BF)
            else:
                stem = residual[pl.ds(row, 128), WIDE:GROUP].astype(F32)
                memory[pl.ds(row, 128), WIDE:] = (stem + out[:, HD:]).astype(BF)

    @pl.when(small)
    def _():
        for step in range(4):
            attend(step, False)

    @pl.when(jnp.logical_not(small))
    def _():
        lax.fori_loop(0, 4, lambda step, carry: (attend(step, True), carry)[1], 0)

    near[...] = memory[pl.ds(pl.multiple_of(256 * x, 256), 256), :]
    away[...] = memory[pl.ds(pl.multiple_of(256 * (1 - x), 256), 256), :]


def encoder(places, layers, ids, parts, depth):
    operands = layers + [ids] + parts
    return pl.pallas_call(
        functools.partial(encoder_kernel, len(parts), depth),
        out_shape=(
            jax.ShapeDtypeStruct((512, GROUP), BF),
            jax.ShapeDtypeStruct((256, GROUP), BF),
            jax.ShapeDtypeStruct((256, GROUP), BF),
        ),
        in_specs=[SMEM] + [VMEM] * len(operands),
        out_specs=(VMEM, VMEM, VMEM),
        scratch_shapes=[
            pltpu.VMEM((1280, 1024), BF),
            pltpu.VMEM((512, 384), BF),
            pltpu.VMEM((512, 384), BF),
            pltpu.VMEM((1536, 384), BF),
            pltpu.VMEM((1536, 768), BF),
        ],
        cost_estimate=CHEAP,
        compiler_params=pltpu.CompilerParams(vmem_limit_bytes=24 * 1024 * 1024),
    )(places, *operands)


def cross_kernel(base, table, tokens, asked, memory, beside, *refs):
    outs, out = refs[:-1], refs[-1]
    count = asked.shape[0]
    me = table[base + 2]
    spot = lax.broadcasted_iota(jnp.int32, (count, HD), 1)
    order = lax.broadcasted_iota(jnp.int32, (count, 1), 0)
    owner = (order // 2 * 2) ^ me
    bias = []
    for half in range(2):
        for b in range(4):
            block = table[base + half] + b
            ask = jnp.sum(jnp.where(spot == block, asked[...], 0.0), axis=-1, keepdims=True)
            allowed = (ask > 0.5) | (owner == block)
            bias.append(jnp.broadcast_to(jnp.where(allowed, 0.0, LOW), (count, 128)))
    bias = jnp.concatenate(bias, axis=1)
    bias = jnp.concatenate([bias] * 5, axis=0)
    query = tokens[...].astype(BF)
    cross = jnp.concatenate(
        [
            lax.dot_general(
                query, held[...], (((1,), (1,)), ((), ())), preferred_element_type=F32
            )
            for held in (memory, beside)
        ],
        axis=1,
    )
    cross = jnp.where(bias < 0.0, LOW, cross)
    top = jnp.max(cross, axis=-1, keepdims=True)
    raised = jnp.where(bias < 0.0, 0.0, jnp.exp(cross - top))
    den = jnp.sum(raised, axis=-1, keepdims=True)
    raised = raised.astype(BF)
    out[...] = jnp.dot(raised[:, :512], memory[...], preferred_element_type=F32) + jnp.dot(
        raised[:, 512:], beside[...], preferred_element_type=F32
    )
    lane = lax.broadcasted_iota(jnp.int32, (count, HD), 1)
    for h in range(5):
        rows = slice(count * h, count * h + count)
        stats = jnp.where(lane == 0, top[rows], den[rows])
        both = jnp.concatenate([out[rows, HD * h : HD * h + HD], stats], axis=1)
        for i, owned in enumerate(outs):
            owned[8 * h : 8 * h + 8, :] = both[8 * i : 8 * i + 8]


def cross_partial(base, table, tokens, asked, memory, beside):
    count = asked.shape[0]
    return pl.pallas_call(
        functools.partial(cross_kernel, base),
        out_shape=(jax.ShapeDtypeStruct((40, 128), F32),) * (count // 8),
        in_specs=[SMEM] + [VMEM] * 4,
        out_specs=(VMEM,) * (count // 8),
        scratch_shapes=[pltpu.VMEM((5 * count, GROUP), F32)],
        cost_estimate=CHEAP,
        compiler_params=pltpu.CompilerParams(vmem_limit_bytes=12 * 1024 * 1024),
    )(table, tokens, asked, memory, beside)


def merge_kernel(*refs):
    parts, outs, out = refs[:-5], refs[-5:-1], refs[-1]
    tops = [part[:, HD : HD + 1] for part in parts]
    best = functools.reduce(jnp.maximum, tops)
    total = jnp.zeros((40, 128), F32)
    for top, part in zip(tops, parts):
        total = total + jnp.exp(top - best) * part[...]
    final = total[:, :HD] / total[:, HD + 1 : HD + 2]
    heads = [final[8 * h : 8 * h + 8] for h in range(5)] + [jnp.zeros((8, HD), F32)]
    for slab in range(3):
        out[:, 128 * slab : 128 * slab + 128] = jnp.concatenate(heads[2 * slab : 2 * slab + 2], axis=1)
    for i in range(4):
        outs[i][...] = out[2 * i : 2 * i + 2, :].astype(BF)


def merge(parts):
    return pl.pallas_call(
        merge_kernel,
        out_shape=(jax.ShapeDtypeStruct((2, 384), BF),) * 4,
        in_specs=[VMEM] * len(parts),
        out_specs=(VMEM,) * 4,
        scratch_shapes=[pltpu.VMEM((8, 384), F32)],
        cost_estimate=CHEAP,
        compiler_params=pltpu.CompilerParams(vmem_limit_bytes=4 * 1024 * 1024),
    )(*parts)


def gather_kernel(side, rows, table, *refs):
    pieces, out = refs[:4], refs[4]
    high, x = table[side], table[6]
    start = pl.multiple_of(rows * high, rows) if pieces[0].shape[0] > rows else 0
    flip = jnp.broadcast_to(x, (rows, HD)) == 1
    held = [piece[pl.ds(start, rows), :] for piece in pieces]
    for i, piece in enumerate(held):
        group = (2 * high + x) ^ i
        out[:, pl.ds(pl.multiple_of(WIDE * group, 128), WIDE)] = piece[:, :WIDE]
    for i in range(2):
        first, second = [piece[:, WIDE:GROUP] for piece in held[2 * i : 2 * i + 2]]
        tail = jnp.concatenate([jnp.where(flip, second, first), jnp.where(flip, first, second)], axis=1)
        out[:, pl.ds(pl.multiple_of(1024 + 128 * (high ^ i), 128), 128)] = tail


def gather_groups(side, rows, table, pieces):
    return pl.pallas_call(
        functools.partial(gather_kernel, side, rows),
        out_shape=jax.ShapeDtypeStruct((rows, 1280), BF),
        in_specs=[SMEM] + [VMEM] * 4,
        out_specs=VMEM,
        cost_estimate=CHEAP,
        compiler_params=pltpu.CompilerParams(vmem_limit_bytes=4 * 1024 * 1024),
    )(table, *pieces)


def on_device(stem, norm_gain, qkv_weight, segment_ids, dec_queries, stretch_mask):
    n = lax.axis_size("tm")
    layers = n // 4
    me = lax.axis_index("tm")
    z, x, c = me // 4, (me // 2) % 2, me % 2
    p, k = z % 2, z // 2
    quarter = 2 * k + c
    group = 2 * p + x
    depth = qkv_weight.shape[0]

    utts = lax.axis_size("utt")
    moved = lax.axis_index("utt") % 2
    direct = depth % 16 == 0 and layers == 4 and utts % 2 == 0
    gain = norm_gain.reshape(1, -1)
    table = [128 * (2 * x + c), 128 * (2 * x + 1 - c), 128 * (2 - 2 * x + c), 128 * (3 - 2 * x - c)]
    table += [group, p, x, c]
    table += [512 * (p - c + 1), 512 * (2 - p - c), 1024 * c, 0, x == moved, 4 * quarter - 4, z]
    sources = [me, me ^ 1, me ^ 2, me ^ 3] if direct else [jnp.int32(0)]
    for side in (2 * moved, 2 - 2 * moved) if direct else ():
        for core in (c, 1 - c):
            sources += [4 * (z ^ turn) + side + core for turn in (1, 2, 3)]
    table = scalars(table + sources + [4 * quarter, 4 * (quarter ^ 1), me])
    base = 15 + len(sources)

    steps = [1 if i % 2 else -1 for i in range(layers)]
    near_route = [
        (4 * i + j, 4 * (i + s) + j)
        for i, s in enumerate(steps)
        for j in range(4)
        if 0 <= i + s < layers
    ]
    near = send(stem, near_route)
    pair = swap(stem, n, 4)
    if direct:
        def trade(block):
            return lax.ppermute(block, "utt", [(u, u ^ 1) for u in range(utts)])

        mine, theirs = pack(
            table, qkv_weight, dec_queries, stretch_mask, segment_ids.reshape(1, -1)
        )
        across = swap(theirs, n, 2)
        mine_c, across_c = swap(mine, n, 1), swap(across, n, 1)
        ready = load(table, mine, mine_c, after(across, near, pair), across_c)
        relayed = swap(after(near, ready[0]), n, 4)
        stem_x = swap(after(stem, across), n, 2)
        here = {turn: swap(ready[turn % 2], n, 4 * turn) for turn in (3, 2, 1)}
        pair_x = swap(after(pair, ready[0]), n, 2)
        halo = jnp.where((z == 1) | (z == 2), near, relayed)
        halo_x = swap(after(halo, pair_x, *here.values()), n, 2)
        joined = join([after(here[1], halo), here[2], here[3]])
        traded = trade(joined)
        ids, tokens, asked = prepare(table, ready[0], joined, n)
        own_half = norm_half(table, gain, stem, stem_x)
        pair_half = norm_half(table, gain, pair, pair_x)
        halo_half = norm_half(table, gain, halo, after(halo_x, ids), False)
        own_c, pair_c = swap(own_half, n, 1), swap(pair_half, n, 1)
        halo_c, joined_c = swap(after(halo_half, traded), n, 1), swap(joined, n, 1)
        layered = [own_half, own_c, pair_half, pair_c, halo_half, halo_c]
        weights = [mine, mine_c, across, across_c, joined, joined_c]
        weights += [traded, swap(after(traded, own_c, pair_c, joined_c), n, 1)]
    else:
        stem_x = swap(stem, n, 2)
        far = swap(near, n, 4)
        left = jnp.where(p == 0, near, far)
        right = jnp.where(p == 0, far, near)
        left_x, right_x = swap(left, n, 2), swap(right, n, 2)
        left = norm_half(table, gain, left, left_x, False)
        right = norm_half(table, gain, right, right_x, False)
        halo = [jnp.where(c == 0, left, right), swap(jnp.where(c == 0, right, left), n, 1)]
        own = norm_half(table, gain, stem, stem_x)
        other = norm_half(table, gain, pair, swap(pair, n, 2))
        layered = [own, swap(own, n, 1), other, swap(other, n, 1)] + halo
        whole = lax.all_gather(qkv_weight, "tm", axis=0, tiled=True)
        grouped = jnp.stack([weight_group(whole, g) for g in range(4)])
        weights = [lax.dynamic_index_in_dim(grouped, group, 0, keepdims=False)]
        weights = [jnp.pad(weights[0], ((0, 0), (0, HD)))]
        depth = whole.shape[0]
        packed = jnp.stack([token_group(dec_queries, stretch_mask, g) for g in range(4)])
        every = lax.all_gather(packed, "tm", axis=0)
        every = lax.dynamic_index_in_dim(every, group, 1, keepdims=False)
        every = jnp.take(every, jnp.arange(0, n, 2, dtype=jnp.int32) ^ me, axis=0)
        every = every.reshape(n // 2, 6, 2, HD).transpose(1, 0, 2, 3).reshape(6, n, HD).astype(F32)
        asked = every[5]
        tokens = jnp.concatenate(
            [jnp.pad(every[h] * 0.125, ((0, 0), (HD * h, GROUP - HD - HD * h))) for h in range(5)]
        )
        marks = lax.all_gather(segment_ids, "tm", axis=0, tiled=True).astype(F32)
        marks = jnp.pad(marks, (512, 512))
        marks = lax.dynamic_slice_in_dim(marks, 512 * quarter, 1536, 0)
        ids = jnp.broadcast_to(marks[None], (8, 1536))
    held, stay, leave = encoder(table, layered, ids, weights, depth)

    partial = cross_partial(base, table, tokens, asked, held, swap(held, n, 1))
    owned = [partial[0]] + [swap(partial[i], n, 8 * i) for i in range(1, n // 8)]

    got = []
    for turn, rows in enumerate((after(stay, partial[0]), leave)):
        route = [
            (
                8 * (d // 8) + 4 * (d // 4 % 2) + (d & 2) + (d & 1),
                8 * (d // 8) + 4 * (d & 1) + ((d & 2) ^ (2 * turn)) + (d // 4 % 2),
            )
            for d in range(n)
        ]
        got.append(after(send(rows, route), owned[1]))
    memory = gather_groups(7, 128, table, got + [swap(part, n, 1) for part in got])

    final = merge(owned)
    final = [final[0]] + [swap(final[i], n, 2 * i) for i in (1, 2, 3)]
    final[0] = after(final[0], memory)
    cross_out = gather_groups(5, 2, table, final)
    return (memory, cross_out)


def solution(mesh):
    placed = (
        P(("utt", "tm"), None),
        P(),
        P("tm", None),
        P(("utt", "tm")),
        P(("utt", "tm"), None),
        P(("utt", "tm"), None),
    )
    return jax.shard_map(
        on_device,
        mesh=mesh,
        in_specs=placed,
        out_specs=(P(("utt", "tm"), None), P(("utt", "tm"), None)),
        check_vma=False,
    )
```

```python
import functools

import jax
import jax.numpy as jnp
from jax import lax
from jax.experimental import pallas as pl
from jax.experimental.pallas import tpu as pltpu
from jax.sharding import PartitionSpec as P

HD = 64
WIDE = 256
GROUP = 320
BF = jnp.bfloat16
F32 = jnp.float32
LOW = -1e30
CHEAP = pl.CostEstimate(flops=1, bytes_accessed=1, transcendentals=0)
VMEM = pl.BlockSpec(memory_space=pltpu.VMEM)
SMEM = pl.BlockSpec(memory_space=pltpu.SMEM)


def send(block, route):
    return lax.ppermute(block, "tm", route)


def swap(block, n, mask):
    return send(block, [(d, d ^ mask) for d in range(n)])


def after(value, *awaited):
    return lax.optimization_barrier((value, *awaited))[0]


def scalars(values):
    return jnp.stack([jnp.asarray(v, jnp.int32) for v in values])


def group_of(array, g):
    return array[:, WIDE * g : WIDE * g + WIDE], array[:, 1024 + HD * g : 1024 + HD * g + HD]


def weight_group(weight, g):
    width = weight.shape[1] // 3
    parts = [group_of(weight[:, i * width : (i + 1) * width], g) for i in range(3)]
    (q0, q1), (k0, k1), (v0, v1) = parts
    return jnp.concatenate([q0, k0, v0, k1, v1, q1], axis=1)


def token_group(queries, mask, g):
    wide, tail = group_of(queries, g)
    heads = [wide[:, HD * i : HD * i + HD] for i in range(4)] + [tail]
    asked = jnp.pad(mask.astype(BF), ((0, 0), (0, HD - mask.shape[1])))
    return jnp.concatenate(heads + [asked], axis=0)


def pack_kernel(table, *refs):
    mine, theirs = refs[4:6]
    weight, queries, mask, segments = held = refs[6:10]
    copies = [pltpu.make_async_copy(refs[i], held[i], refs[10].at[i]) for i in range(4)]
    for copy in copies:
        copy.start()
    for copy in copies:
        copy.wait()
    rows, width = weight.shape[0], weight.shape[1] // 3
    blocks = mask.shape[1]
    ids = segments[...]
    digits = [lax.shift_right_logical(ids, 7).astype(F32), (ids & 127).astype(F32)]
    asked = mask[...].astype(F32)
    if blocks < HD:
        asked = jnp.concatenate([asked, jnp.zeros((2, HD - blocks), F32)], axis=1)
    rest = [asked] + [d[:, HD * i : HD * i + HD] for d in digits for i in range(2)]
    rest.append(jnp.zeros((rows - 16, HD), F32))
    for turn, outs in enumerate((mine, theirs)):
        column = table[6] if turn == 0 else 1 - table[6]
        for p in range(2):
            out = outs.at[p]
            wide = pl.multiple_of(WIDE * (2 * p + column), 128)
            tails = []
            for i in range(4):
                source = weight if i < 3 else queries
                at = width * i if i < 3 else 0
                slab = source[:, at + 1024 + 128 * p : at + 1152 + 128 * p].astype(F32)
                odd = jnp.broadcast_to(column, (slab.shape[0], HD)) == 1
                tails.append(jnp.where(odd, slab[:, HD:], slab[:, :HD]))
                if i < 3:
                    out[:, WIDE * i : WIDE * i + WIDE] = weight[
                        :, pl.ds(pl.multiple_of(at + wide, 128), WIDE)
                    ]
            out[:, 3 * WIDE : 896] = jnp.concatenate(tails[1:3], axis=1).astype(BF)
            asking = queries[:, pl.ds(wide, WIDE)].astype(F32)
            heads = [asking[:, HD * h : HD * h + HD] for h in range(4)] + [tails[3]]
            lanes = jnp.concatenate(heads + rest, axis=0)
            out[:, 896:] = jnp.concatenate([tails[0], lanes], axis=1).astype(BF)


def pack(table, weight, queries, mask, segments):
    shape = jax.ShapeDtypeStruct((2, weight.shape[0], 1024), BF)
    given = (weight, queries, mask, segments)
    return pl.pallas_call(
        pack_kernel,
        out_shape=(shape, shape),
        in_specs=[SMEM] + [pl.BlockSpec(memory_space=pl.ANY)] * 4,
        out_specs=(VMEM,) * 2,
        scratch_shapes=[pltpu.VMEM(a.shape, a.dtype) for a in given] + [pltpu.SemaphoreType.DMA((4,))],
        cost_estimate=CHEAP,
        compiler_params=pltpu.CompilerParams(vmem_limit_bytes=8 * 1024 * 1024),
    )(table, weight, queries, mask, segments)


def load_kernel(table, *refs):
    held, outs = refs[:4], refs[4:]
    x, c, p = table[6], table[7], table[5]
    own = jnp.broadcast_to(table[12], outs[0].shape) == 1
    flip_c = jnp.broadcast_to(c, (16, 128)) == 1
    flip_x = jnp.broadcast_to(x, (16, 128)) == 1
    for a in range(2):
        mine, mine_c, across, across_c = [h[pl.ds(p ^ a, 1)][0] for h in held]
        out = outs[a]
        out[...] = jnp.where(own, mine, across)
        lanes = [part[:16, 896:] for part in (mine, mine_c, across, across_c)]
        rows = []
        for first, second in (lanes[:2], lanes[2:]):
            rows.append((jnp.where(flip_c, second, first), jnp.where(flip_c, first, second)))
        low = [jnp.where(flip_x, there, here) for here, there in zip(*rows)]
        high = [jnp.where(flip_x, here, there) for here, there in zip(*rows)]
        lane = lax.broadcasted_iota(jnp.int32, (16, 128), 1)
        for j, found in enumerate(low + high):
            out[16 * j : 16 * j + 16, 896:] = jnp.where(
                lane < HD, out[16 * j : 16 * j + 16, 896:], found
            )


def load(table, *held):
    rows = held[0].shape[1]
    return pl.pallas_call(
        load_kernel,
        out_shape=(jax.ShapeDtypeStruct((rows, 1024), BF),) * 2,
        in_specs=[SMEM] + [VMEM] * 4,
        out_specs=(VMEM,) * 2,
        cost_estimate=CHEAP,
        compiler_params=pltpu.CompilerParams(vmem_limit_bytes=8 * 1024 * 1024),
    )(table, *held)


def norm_kernel(table, gain, here, across, out):
    group = table[4]
    for i, block in enumerate((here, across)):
        rows = slice(128 * i, 128 * i + 128)
        values = block[...].astype(F32)
        mean = jnp.mean(values, axis=-1, keepdims=True)
        centred = values - mean
        var = jnp.mean(centred * centred, axis=-1, keepdims=True)
        out[rows, :1280] = (centred * lax.rsqrt(var + 1e-05) * gain[...]).astype(BF)
        if out.shape[1] > 1280:
            out[rows, 1280 : 1280 + WIDE] = block[:, pl.ds(pl.multiple_of(group * WIDE, 128), WIDE)]
            slab = block[:, pl.ds(pl.multiple_of(1024 + group // 2 * 128, 128), 128)]
            odd = jnp.broadcast_to(lax.rem(group, 2), (128, HD)) == 1
            tail = jnp.where(odd, slab[:, HD:], slab[:, :HD])
            out[rows, 1280 + WIDE :] = jnp.concatenate([tail, jnp.zeros_like(tail)], axis=1)


def norm_half(table, gain, here, across, kept=True):
    return pl.pallas_call(
        norm_kernel,
        out_shape=jax.ShapeDtypeStruct((256, 1664 if kept else 1280), BF),
        in_specs=[SMEM] + [VMEM] * 3,
        out_specs=VMEM,
        cost_estimate=CHEAP,
        compiler_params=pltpu.CompilerParams(vmem_limit_bytes=8 * 1024 * 1024),
    )(table, gain, here, across)


def prepare_kernel(table, *refs):
    first_part, joined, (ids, tokens, asked) = refs[0], refs[1], refs[2:]
    depth = joined.shape[0] // 3
    first, x, core, z = table[13], table[6], table[7], table[14]
    count = asked.shape[0]
    ids[...] = jnp.zeros_like(ids)
    tokens[...] = jnp.zeros_like(tokens)
    flip_c = jnp.broadcast_to(core, (2, HD)) == 1
    flip_x = jnp.broadcast_to(x, (2, HD)) == 1
    for turn in range(4):
        top = depth * (turn - 1)
        part = joined[top : top + 64, 896:] if turn else first_part[:64, 896:]
        lanes = part.astype(F32)[:, HD:]
        for h in range(6):
            rows = [lanes[16 * j + 2 * h : 16 * j + 2 * h + 2] for j in range(4)]
            low = jnp.where(flip_c, rows[1], rows[0])
            high = jnp.where(flip_c, rows[3], rows[2])
            for dx in range(2):
                found = jnp.where(flip_x, low, high) if dx else jnp.where(flip_x, high, low)
                at = 4 * turn + 2 * dx
                if h < 5:
                    tokens[count * h + at : count * h + at + 2, HD * h : HD * h + HD] = found * 0.125
                else:
                    asked[at : at + 2, :] = found
        for j in range(4):
            marks = lanes[16 * j + 12 : 16 * j + 14] * 128.0 + lanes[16 * j + 14 : 16 * j + 16]
            block = 4 * (z ^ turn) + j - first

            @pl.when((block >= 0) & (block < 12))
            def _():
                ids[0:1, pl.ds(pl.multiple_of(block * 128, 128), 128)] = jnp.concatenate(
                    [marks[0:1], marks[1:2]], axis=1
                )


def prepare(table, own, joined, count):
    return pl.pallas_call(
        prepare_kernel,
        out_shape=(
            jax.ShapeDtypeStruct((8, 1536), F32),
            jax.ShapeDtypeStruct((5 * count, GROUP), F32),
            jax.ShapeDtypeStruct((count, HD), F32),
        ),
        in_specs=[SMEM] + [VMEM] * 2,
        out_specs=(VMEM,) * 3,
        cost_estimate=CHEAP,
        compiler_params=pltpu.CompilerParams(vmem_limit_bytes=8 * 1024 * 1024),
    )(table, own, joined)


def join_kernel(*refs):
    parts, out = refs[:-1], refs[-1]
    rows = parts[0].shape[0]
    for i, part in enumerate(parts):
        out[rows * i : rows * i + rows, :] = part[...]


def join(parts):
    rows = parts[0].shape[0]
    return pl.pallas_call(
        join_kernel,
        out_shape=jax.ShapeDtypeStruct((rows * len(parts), 1024), BF),
        in_specs=[VMEM] * len(parts),
        out_specs=VMEM,
        cost_estimate=CHEAP,
        compiler_params=pltpu.CompilerParams(vmem_limit_bytes=4 * 1024 * 1024),
    )(*parts)


def encoder_kernel(n_parts, depth, places, *refs):
    layers = [refs[2 * i : 2 * i + 2] for i in range(3)]
    ids = refs[6]
    parts = refs[7 : 7 + n_parts]
    memory, near, away, weight, residual, queries, keys, values = refs[7 + n_parts :]
    x = places[6]
    at = 15
    for part in parts:
        rows = [part[pl.ds(places[5], 1)][0]] if len(part.shape) == 3 else [
            part[s * depth : s * depth + depth, :] for s in range(part.shape[0] // depth)
        ]
        for found in rows:
            weight[pl.ds(pl.multiple_of(places[at] * depth, 16), depth), :] = found
            at += 1

    for slab in range(3):
        values[:, 256 * slab + 128 : 256 * slab + 256] = jnp.ones((1536, 128), BF)
    spots = [places[i] for i in (0, 2, 1, 3)]
    largest = [jnp.zeros((1, 256), F32), jnp.zeros((1, 128), F32)]
    for i, halves in enumerate(layers):
        place = places[8 + i]
        normed = jnp.concatenate([half[:, :1280] for half in halves], axis=0)
        found = jnp.dot(normed, weight[:, 256:896], preferred_element_type=F32)
        for j, lanes in enumerate((slice(0, 256), slice(512, 640))):
            largest[j] = jnp.maximum(
                largest[j], jnp.max(jnp.abs(found[:, lanes]), axis=0, keepdims=True)
            )
        found = found.astype(BF)
        for j, spot in enumerate(spots):
            to = pl.ds(pl.multiple_of(place + spot, 128), 128)
            block = found[128 * j : 128 * j + 128]
            keys[to, :256] = block[:, :256]
            keys[to, 256:] = block[:, 512:]
            for slab in range(3):
                values[to, 256 * slab : 256 * slab + 128] = block[:, 256 + 128 * slab : 384 + 128 * slab]
        if i < 2:

            @pl.when(place == 512)
            def _():
                normed = jnp.concatenate([half[:, :1280] for half in halves], axis=0)
                wide = jnp.dot(normed, weight[:, :WIDE], preferred_element_type=F32).astype(BF)
                tail = jnp.dot(normed, weight[:, 896:], preferred_element_type=F32).astype(BF)
                lane = lax.broadcasted_iota(jnp.int32, tail.shape, 1)
                tail = jnp.where(lane < HD, tail, jnp.zeros_like(tail))
                for j, spot in enumerate(spots):
                    to = pl.ds(pl.multiple_of(spot, 128), 128)
                    rows = slice(128 * j, 128 * j + 128)
                    queries[to, :WIDE] = wide[rows]
                    queries[to, WIDE:] = tail[rows]
                    residual[to, :] = halves[j // 2][128 * (j % 2) : 128 * (j % 2) + 128, 1280:]

    lane = lax.broadcasted_iota(jnp.int32, (8, 384), 1) // HD
    head = lax.broadcasted_iota(jnp.int32, (8, 384), 0)
    most = jnp.concatenate(largest, axis=1) * 1.01
    most = jnp.where((lane == head) & (head < 5), most, 0.0).astype(BF)
    bounds = lax.dot_general(
        most, jnp.abs(queries[...]), (((1,), (1,)), ((), ())), preferred_element_type=F32
    )
    small = jnp.max(bounds) < 480.0

    def attend(step, shifted):
        row = step * 128 if isinstance(step, int) else pl.multiple_of(step * 128, 128)
        mine = jnp.broadcast_to(ids[0:1, pl.ds(row + 512, 128)], (128, 128)).T[:, 0:1]
        bias = jnp.where(mine == ids[0:1, pl.ds(row, 1152)], 0.0, LOW)
        lane = lax.broadcasted_iota(jnp.int32, (128, 128), 1)
        for slab in range(3):
            span = slice(128 * slab, 128 * slab + 128)
            query = queries[pl.ds(row, 128), span] * BF(0.125)
            mask = bias
            if slab < 2:
                none = jnp.zeros_like(query)
                query = jnp.concatenate(
                    [jnp.where(lane < HD, query, none), jnp.where(lane < HD, none, query)], axis=0
                )
                mask = jnp.concatenate([bias, bias], axis=0)
            scores = lax.dot_general(
                query,
                keys[pl.ds(row, 1152), span],
                (((1,), (1,)), ((), ())),
                preferred_element_type=F32,
            )
            scores = scores + mask
            if shifted:
                scores = scores - jnp.max(scores, axis=-1, keepdims=True)
            raised = jnp.exp(scores).astype(BF)
            out = jnp.dot(
                raised,
                values[pl.ds(row, 1152), 256 * slab : 256 * slab + 256],
                preferred_element_type=F32,
            )
            out = out[:, :128] / out[:, 128:]
            if slab < 2:
                context = jnp.where(lane < HD, out[:128], out[128:])
                stem = residual[pl.ds(row, 128), span].astype(F32)
                memory[pl.ds(row, 128), span] = (stem + context).astype(BF)
            else:
                stem = residual[pl.ds(row, 128), WIDE:GROUP].astype(F32)
                memory[pl.ds(row, 128), WIDE:] = (stem + out[:, HD:]).astype(BF)

    @pl.when(small)
    def _():
        for step in range(4):
            attend(step, False)

    @pl.when(jnp.logical_not(small))
    def _():
        lax.fori_loop(0, 4, lambda step, carry: (attend(step, True), carry)[1], 0)

    near[...] = memory[pl.ds(pl.multiple_of(256 * x, 256), 256), :]
    away[...] = memory[pl.ds(pl.multiple_of(256 * (1 - x), 256), 256), :]


def encoder(places, layers, ids, parts, depth):
    operands = layers + [ids] + parts
    return pl.pallas_call(
        functools.partial(encoder_kernel, len(parts), depth),
        out_shape=(
            jax.ShapeDtypeStruct((512, GROUP), BF),
            jax.ShapeDtypeStruct((256, GROUP), BF),
            jax.ShapeDtypeStruct((256, GROUP), BF),
        ),
        in_specs=[SMEM] + [VMEM] * len(operands),
        out_specs=(VMEM, VMEM, VMEM),
        scratch_shapes=[
            pltpu.VMEM((1280, 1024), BF),
            pltpu.VMEM((512, 384), BF),
            pltpu.VMEM((512, 384), BF),
            pltpu.VMEM((1536, 384), BF),
            pltpu.VMEM((1536, 768), BF),
        ],
        cost_estimate=CHEAP,
        compiler_params=pltpu.CompilerParams(vmem_limit_bytes=24 * 1024 * 1024),
    )(places, *operands)


def cross_kernel(base, table, tokens, asked, memory, beside, *refs):
    outs, out = refs[:-1], refs[-1]
    count = asked.shape[0]
    me = table[base + 2]
    spot = lax.broadcasted_iota(jnp.int32, (count, HD), 1)
    order = lax.broadcasted_iota(jnp.int32, (count, 1), 0)
    owner = (order // 2 * 2) ^ me
    bias = []
    for half in range(2):
        for b in range(4):
            block = table[base + half] + b
            ask = jnp.sum(jnp.where(spot == block, asked[...], 0.0), axis=-1, keepdims=True)
            allowed = (ask > 0.5) | (owner == block)
            bias.append(jnp.broadcast_to(jnp.where(allowed, 0.0, LOW), (count, 128)))
    bias = jnp.concatenate(bias, axis=1)
    bias = jnp.concatenate([bias] * 5, axis=0)
    query = tokens[...].astype(BF)
    cross = jnp.concatenate(
        [
            lax.dot_general(
                query, held[...], (((1,), (1,)), ((), ())), preferred_element_type=F32
            )
            for held in (memory, beside)
        ],
        axis=1,
    )
    cross = jnp.where(bias < 0.0, LOW, cross)
    top = jnp.max(cross, axis=-1, keepdims=True)
    raised = jnp.where(bias < 0.0, 0.0, jnp.exp(cross - top))
    den = jnp.sum(raised, axis=-1, keepdims=True)
    raised = raised.astype(BF)
    out[...] = jnp.dot(raised[:, :512], memory[...], preferred_element_type=F32) + jnp.dot(
        raised[:, 512:], beside[...], preferred_element_type=F32
    )
    lane = lax.broadcasted_iota(jnp.int32, (count, HD), 1)
    for h in range(5):
        rows = slice(count * h, count * h + count)
        stats = jnp.where(lane == 0, top[rows], den[rows])
        both = jnp.concatenate([out[rows, HD * h : HD * h + HD], stats], axis=1)
        for i, owned in enumerate(outs):
            owned[8 * h : 8 * h + 8, :] = both[8 * i : 8 * i + 8]


def cross_partial(base, table, tokens, asked, memory, beside):
    count = asked.shape[0]
    return pl.pallas_call(
        functools.partial(cross_kernel, base),
        out_shape=(jax.ShapeDtypeStruct((40, 128), F32),) * (count // 8),
        in_specs=[SMEM] + [VMEM] * 4,
        out_specs=(VMEM,) * (count // 8),
        scratch_shapes=[pltpu.VMEM((5 * count, GROUP), F32)],
        cost_estimate=CHEAP,
        compiler_params=pltpu.CompilerParams(vmem_limit_bytes=12 * 1024 * 1024),
    )(table, tokens, asked, memory, beside)


def merge_kernel(*refs):
    parts, outs, out = refs[:-5], refs[-5:-1], refs[-1]
    tops = [part[:, HD : HD + 1] for part in parts]
    best = functools.reduce(jnp.maximum, tops)
    total = jnp.zeros((40, 128), F32)
    for top, part in zip(tops, parts):
        total = total + jnp.exp(top - best) * part[...]
    final = total[:, :HD] / total[:, HD + 1 : HD + 2]
    heads = [final[8 * h : 8 * h + 8] for h in range(5)] + [jnp.zeros((8, HD), F32)]
    for slab in range(3):
        out[:, 128 * slab : 128 * slab + 128] = jnp.concatenate(heads[2 * slab : 2 * slab + 2], axis=1)
    for i in range(4):
        outs[i][...] = out[2 * i : 2 * i + 2, :].astype(BF)


def merge(parts):
    return pl.pallas_call(
        merge_kernel,
        out_shape=(jax.ShapeDtypeStruct((2, 384), BF),) * 4,
        in_specs=[VMEM] * len(parts),
        out_specs=(VMEM,) * 4,
        scratch_shapes=[pltpu.VMEM((8, 384), F32)],
        cost_estimate=CHEAP,
        compiler_params=pltpu.CompilerParams(vmem_limit_bytes=4 * 1024 * 1024),
    )(*parts)


def gather_kernel(side, rows, table, *refs):
    pieces, out = refs[:4], refs[4]
    high, x = table[side], table[6]
    start = pl.multiple_of(rows * high, rows) if pieces[0].shape[0] > rows else 0
    flip = jnp.broadcast_to(x, (rows, HD)) == 1
    held = [piece[pl.ds(start, rows), :] for piece in pieces]
    for i, piece in enumerate(held):
        group = (2 * high + x) ^ i
        out[:, pl.ds(pl.multiple_of(WIDE * group, 128), WIDE)] = piece[:, :WIDE]
    for i in range(2):
        first, second = [piece[:, WIDE:GROUP] for piece in held[2 * i : 2 * i + 2]]
        tail = jnp.concatenate([jnp.where(flip, second, first), jnp.where(flip, first, second)], axis=1)
        out[:, pl.ds(pl.multiple_of(1024 + 128 * (high ^ i), 128), 128)] = tail


def gather_groups(side, rows, table, pieces):
    return pl.pallas_call(
        functools.partial(gather_kernel, side, rows),
        out_shape=jax.ShapeDtypeStruct((rows, 1280), BF),
        in_specs=[SMEM] + [VMEM] * 4,
        out_specs=VMEM,
        cost_estimate=CHEAP,
        compiler_params=pltpu.CompilerParams(vmem_limit_bytes=4 * 1024 * 1024),
    )(table, *pieces)


def on_device(stem, norm_gain, qkv_weight, segment_ids, dec_queries, stretch_mask):
    n = lax.axis_size("tm")
    layers = n // 4
    me = lax.axis_index("tm")
    z, x, c = me // 4, (me // 2) % 2, me % 2
    p, k = z % 2, z // 2
    quarter = 2 * k + c
    group = 2 * p + x
    depth = qkv_weight.shape[0]

    utts = lax.axis_size("utt")
    moved = lax.axis_index("utt") % 2
    direct = depth % 16 == 0 and layers == 4 and utts % 2 == 0
    gain = norm_gain.reshape(1, -1)
    table = [128 * (2 * x + c), 128 * (2 * x + 1 - c), 128 * (2 - 2 * x + c), 128 * (3 - 2 * x - c)]
    table += [group, p, x, c]
    table += [512 * (p - c + 1), 512 * (2 - p - c), 1024 * c, 0, x == moved, 4 * quarter - 4, z]
    sources = [me, me ^ 1, me ^ 2, me ^ 3] if direct else [jnp.int32(0)]
    for side in (2 * moved, 2 - 2 * moved) if direct else ():
        for core in (c, 1 - c):
            sources += [4 * (z ^ turn) + side + core for turn in (1, 2, 3)]
    table = scalars(table + sources + [4 * quarter, 4 * (quarter ^ 1), me])
    base = 15 + len(sources)

    steps = [1 if i % 2 else -1 for i in range(layers)]
    near_route = [
        (4 * i + j, 4 * (i + s) + j)
        for i, s in enumerate(steps)
        for j in range(4)
        if 0 <= i + s < layers
    ]
    near = send(stem, near_route)
    pair = swap(stem, n, 4)
    if direct:
        def trade(block):
            return lax.ppermute(block, "utt", [(u, u ^ 1) for u in range(utts)])

        mine, theirs = pack(
            table, qkv_weight, dec_queries, stretch_mask, segment_ids.reshape(1, -1)
        )
        across = swap(theirs, n, 2)
        mine_c, across_c = swap(mine, n, 1), swap(across, n, 1)
        near = send(after(stem, mine_c), near_route)
        ready = load(table, mine, mine_c, after(across, near, pair), across_c)
        relayed = swap(after(near, ready[0]), n, 4)
        stem_x = swap(after(stem, across), n, 2)
        here = {turn: swap(ready[turn % 2], n, 4 * turn) for turn in (3, 2)}
        here[1] = swap(after(ready[1], stem_x), n, 4)
        pair_x = swap(after(pair, ready[0]), n, 2)
        halo = jnp.where((z == 1) | (z == 2), near, relayed)
        halo_x = swap(after(halo, pair_x, *here.values()), n, 2)
        joined = join([after(here[1], halo), here[2], here[3]])
        traded = trade(joined)
        ids, tokens, asked = prepare(table, ready[0], joined, n)
        own_half = norm_half(table, gain, stem, stem_x)
        pair_half = norm_half(table, gain, pair, pair_x)
        halo_half = norm_half(table, gain, halo, after(halo_x, ids), False)
        own_c, pair_c = swap(own_half, n, 1), swap(pair_half, n, 1)
        halo_c, joined_c = swap(after(halo_half, traded), n, 1), swap(joined, n, 1)
        layered = [own_half, own_c, pair_half, pair_c, halo_half, halo_c]
        weights = [mine, mine_c, across, across_c, joined, joined_c]
        weights += [traded, swap(after(traded, own_c, pair_c, joined_c), n, 1)]
    else:
        stem_x = swap(stem, n, 2)
        far = swap(near, n, 4)
        left = jnp.where(p == 0, near, far)
        right = jnp.where(p == 0, far, near)
        left_x, right_x = swap(left, n, 2), swap(right, n, 2)
        left = norm_half(table, gain, left, left_x, False)
        right = norm_half(table, gain, right, right_x, False)
        halo = [jnp.where(c == 0, left, right), swap(jnp.where(c == 0, right, left), n, 1)]
        own = norm_half(table, gain, stem, stem_x)
        other = norm_half(table, gain, pair, swap(pair, n, 2))
        layered = [own, swap(own, n, 1), other, swap(other, n, 1)] + halo
        whole = lax.all_gather(qkv_weight, "tm", axis=0, tiled=True)
        grouped = jnp.stack([weight_group(whole, g) for g in range(4)])
        weights = [lax.dynamic_index_in_dim(grouped, group, 0, keepdims=False)]
        weights = [jnp.pad(weights[0], ((0, 0), (0, HD)))]
        depth = whole.shape[0]
        packed = jnp.stack([token_group(dec_queries, stretch_mask, g) for g in range(4)])
        every = lax.all_gather(packed, "tm", axis=0)
        every = lax.dynamic_index_in_dim(every, group, 1, keepdims=False)
        every = jnp.take(every, jnp.arange(0, n, 2, dtype=jnp.int32) ^ me, axis=0)
        every = every.reshape(n // 2, 6, 2, HD).transpose(1, 0, 2, 3).reshape(6, n, HD).astype(F32)
        asked = every[5]
        tokens = jnp.concatenate(
            [jnp.pad(every[h] * 0.125, ((0, 0), (HD * h, GROUP - HD - HD * h))) for h in range(5)]
        )
        marks = lax.all_gather(segment_ids, "tm", axis=0, tiled=True).astype(F32)
        marks = jnp.pad(marks, (512, 512))
        marks = lax.dynamic_slice_in_dim(marks, 512 * quarter, 1536, 0)
        ids = jnp.broadcast_to(marks[None], (8, 1536))
    held, stay, leave = encoder(table, layered, ids, weights, depth)

    partial = cross_partial(base, table, tokens, asked, held, swap(held, n, 1))
    owned = [partial[0]] + [swap(partial[i], n, 8 * i) for i in range(1, n // 8)]

    got = []
    for turn, rows in enumerate((stay, leave)):
        route = [
            (
                8 * (d // 8) + 4 * (d // 4 % 2) + (d & 2) + (d & 1),
                8 * (d // 8) + 4 * (d & 1) + ((d & 2) ^ (2 * turn)) + (d // 4 % 2),
            )
            for d in range(n)
        ]
        got.append(after(send(rows, route), owned[1]))
    memory = gather_groups(7, 128, table, got + [swap(part, n, 1) for part in got])

    final = merge(owned)
    final = [final[0]] + [swap(final[i], n, 2 * i) for i in (1, 2, 3)]
    final[0] = after(final[0], memory)
    cross_out = gather_groups(5, 2, table, final)
    return (memory, cross_out)


def solution(mesh):
    placed = (
        P(("utt", "tm"), None),
        P(),
        P("tm", None),
        P(("utt", "tm")),
        P(("utt", "tm"), None),
        P(("utt", "tm"), None),
    )
    return jax.shard_map(
        on_device,
        mesh=mesh,
        in_specs=placed,
        out_specs=(P(("utt", "tm"), None), P(("utt", "tm"), None)),
        check_vma=False,
    )
```
